32 devices in a mesh: row: 8 (over y, x, core), col: 4 (over z).
Axes of the slice: x: 2, y: 2, z: 4, core: 2. Of those that a mesh axis runs over, the one named last changes fastest.
Arguments:
- alignment_features: float32 [32, 256, 256], P('col', 'row'), may hold values from -6 to 6
- residue_couplings: float32 [256, 256, 128], P('row', 'col'), may hold values from -6 to 6
- chain_indicator: int32 [32], replicated, may hold values from 0 to 1, as said below
- alignment_result_adjoint: float32 [32, 256, 256], P('col', 'row'), may hold values from -6 to 6
- coupling_result_adjoint: float32 [256, 256, 128], P('row', 'col'), may hold values from -6 to 6
- vertical_probe_matrix: float32 [256, 256], replicated, may hold values from -0.375 to 0.375
- vertical_lookup_matrix: float32 [256, 256], replicated, may hold values from -0.375 to 0.375
- vertical_content_matrix: float32 [256, 256], replicated, may hold values from -0.375 to 0.375
- vertical_result_matrix: float32 [256, 256], replicated, may hold values from -0.75 to 0.75
- horizontal_probe_matrix: float32 [256, 256], replicated, may hold values from -0.375 to 0.375
- horizontal_lookup_matrix: float32 [256, 256], replicated, may hold values from -0.375 to 0.375
- horizontal_content_matrix: float32 [256, 256], replicated, may hold values from -0.375 to 0.375
- coupling_offset_matrix: float32 [128, 8], replicated, may hold values from -0.5 to 0.5
- horizontal_result_matrix: float32 [256, 256], replicated, may hold values from -0.75 to 0.75
- tensor_source_matrix: float32 [256, 32], replicated, may hold values from -0.375 to 0.375
- tensor_target_matrix: float32 [256, 32], replicated, may hold values from -0.375 to 0.375
- tensor_result_matrix: float32 [1024, 128], replicated, may hold values from -0.1875 to 0.1875
- source_side_matrix: float32 [128, 128], replicated, may hold values from -0.5 to 0.5
- source_side_switch: float32 [128, 128], replicated, may hold values from -0.5 to 0.5
- target_side_matrix: float32 [128, 128], replicated, may hold values from -0.5 to 0.5
- target_side_switch: float32 [128, 128], replicated, may hold values from -0.5 to 0.5
- trilateral_result_switch: float32 [128, 128], replicated, may hold values from -0.5 to 0.5
- trilateral_result_matrix: float32 [128, 128], replicated, may hold values from -0.5 to 0.5
Outputs:
- msa_out: float32 [32, 256, 256], P('col', 'row')
- pair_out: float32 [256, 256, 128], P('row', 'col')
- alignment_adjoint: float32 [32, 256, 256], P('col', 'row')
- coupling_adjoint: float32 [256, 256, 128], P('row', 'col')
- vertical_probe_adjoint: float32 [256, 256], replicated
- vertical_lookup_adjoint: float32 [256, 256], replicated
- vertical_content_adjoint: float32 [256, 256], replicated
- column_projection_gradient: float32 [256, 256], replicated
- g_query: float32 [256, 256], replicated
- g_key: float32 [256, 256], replicated
- g_value: float32 [256, 256], replicated
- g_bias: float32 [128, 8], replicated
- row_output_gradient: float32 [256, 256], replicated
- tensor_source_adjoint: float32 [256, 32], replicated
- tensor_target_adjoint: float32 [256, 32], replicated
- g_outer: float32 [1024, 128], replicated
- g_left: float32 [128, 128], replicated
- g_left_gate: float32 [128, 128], replicated
- g_right: float32 [128, 128], replicated
- g_right_gate: float32 [128, 128], replicated
- g_tri_gate: float32 [128, 128], replicated
- g_tri_out: float32 [128, 128], replicated
The draws below stay inside these ranges and needn't reach their ends.
Inputs may be any that keep to these rules, and one draw needn't show every extreme that they name: `chain_indicator`: the first sequence is always present.
All inputs are finite; a program needn't handle non-finite values.
Results may differ from the reference program's by a relative error of at most 0.0003.
Values sent between devices are 32-bit elements; how exact they have to be, the bound alone decides.
No kernel may reach another device: no remote copies, remote signals or barrier semaphores. Data moves between devices by JAX's collectives and lax.ppermute only.
A program may use at most 448 MiB of HBM per device.

```python
import jax
import jax.numpy as jnp
from jax import lax

ALIGNED_FEATURES = 256
CP = 128
FOCUS_GROUPS = 8
SUBSPACE_SIZE = 32
PRODUCT_FEATURES = 32
AMINO_SPAN = 256
ALIGNED_CHAINS = 32


def draw_chain_indicator(key, part):
    key = jax.random.fold_in(key, 7)
    selected_entries = jax.random.randint(key, (ALIGNED_CHAINS,), 0, 2)
    foremost = jnp.arange(ALIGNED_CHAINS) == 0
    return jnp.where(foremost, 1, selected_entries).astype(jnp.int32)


def block_levels(key, dims, split, least, largest):
    factor_of = 1.0
    for position, shards_of in split:
        steps = jax.random.uniform(jax.random.fold_in(jax.random.fold_in(key, 6), position), (shards_of,), jnp.float32, least / len(split), largest / len(split))
        factor_of = factor_of * jnp.repeat(jnp.exp(steps), dims[position] // shards_of).reshape((-1,) + (1,) * (len(dims) - 1 - position))
    return factor_of


def normal_values(stream_key, dims, deviation, most, shards=(), held_as=jnp.bfloat16):
    loudness = block_levels(stream_key, dims, shards, -0.22, 0.18) if shards else 1.0
    array = jax.random.normal(stream_key, dims, jnp.float32) * deviation * loudness
    return jnp.minimum(jnp.maximum(array, -most), most).astype(held_as)


def setup_inputs(seed: int = 0) -> dict:
    streams_of = jax.random.split(jax.random.key(seed), 24)
    return {
        "alignment_features": normal_values(streams_of[0], (ALIGNED_CHAINS, AMINO_SPAN, ALIGNED_FEATURES), 1.0, 6.0, ((0, 4), (1, 8)), jnp.float32),
        "residue_couplings": normal_values(streams_of[1], (AMINO_SPAN, AMINO_SPAN, CP), 1.0, 6.0, ((0, 8), (1, 4)), jnp.float32),
        "chain_indicator": draw_chain_indicator(jax.random.fold_in(streams_of[23], 71), 0),
        "alignment_result_adjoint": normal_values(streams_of[3], (ALIGNED_CHAINS, AMINO_SPAN, ALIGNED_FEATURES), 1.0, 6.0, ((0, 4), (1, 8)), jnp.float32),
        "coupling_result_adjoint": normal_values(streams_of[4], (AMINO_SPAN, AMINO_SPAN, CP), 1.0, 6.0, ((0, 8), (1, 4)), jnp.float32),
        "vertical_probe_matrix": normal_values(streams_of[5], (ALIGNED_FEATURES, FOCUS_GROUPS * SUBSPACE_SIZE), ALIGNED_FEATURES ** -0.5, 0.375, (), jnp.float32),
        "vertical_lookup_matrix": normal_values(streams_of[6], (ALIGNED_FEATURES, FOCUS_GROUPS * SUBSPACE_SIZE), ALIGNED_FEATURES ** -0.5, 0.375, (), jnp.float32),
        "vertical_content_matrix": normal_values(streams_of[7], (ALIGNED_FEATURES, FOCUS_GROUPS * SUBSPACE_SIZE), ALIGNED_FEATURES ** -0.5, 0.375, (), jnp.float32),
        "vertical_result_matrix": normal_values(streams_of[8], (FOCUS_GROUPS * SUBSPACE_SIZE, ALIGNED_FEATURES), (FOCUS_GROUPS * SUBSPACE_SIZE // 4) ** -0.5, 0.75, (), jnp.float32),
        "horizontal_probe_matrix": normal_values(streams_of[9], (ALIGNED_FEATURES, FOCUS_GROUPS * SUBSPACE_SIZE), ALIGNED_FEATURES ** -0.5, 0.375, (), jnp.float32),
        "horizontal_lookup_matrix": normal_values(streams_of[10], (ALIGNED_FEATURES, FOCUS_GROUPS * SUBSPACE_SIZE), ALIGNED_FEATURES ** -0.5, 0.375, (), jnp.float32),
        "horizontal_content_matrix": normal_values(streams_of[11], (ALIGNED_FEATURES, FOCUS_GROUPS * SUBSPACE_SIZE), ALIGNED_FEATURES ** -0.5, 0.375, (), jnp.float32),
        "coupling_offset_matrix": normal_values(streams_of[12], (CP, FOCUS_GROUPS), CP ** -0.5, 0.5, (), jnp.float32),
        "horizontal_result_matrix": normal_values(streams_of[13], (FOCUS_GROUPS * SUBSPACE_SIZE, ALIGNED_FEATURES), (FOCUS_GROUPS * SUBSPACE_SIZE // 4) ** -0.5, 0.75, (), jnp.float32),
        "tensor_source_matrix": normal_values(streams_of[14], (ALIGNED_FEATURES, PRODUCT_FEATURES), ALIGNED_FEATURES ** -0.5, 0.375, (), jnp.float32),
        "tensor_target_matrix": normal_values(streams_of[15], (ALIGNED_FEATURES, PRODUCT_FEATURES), ALIGNED_FEATURES ** -0.5, 0.375, (), jnp.float32),
        "tensor_result_matrix": normal_values(streams_of[16], (PRODUCT_FEATURES * PRODUCT_FEATURES, CP), (PRODUCT_FEATURES * PRODUCT_FEATURES) ** -0.5, 0.1875, (), jnp.float32),
        "source_side_matrix": normal_values(streams_of[17], (CP, CP), CP ** -0.5, 0.5, (), jnp.float32),
        "source_side_switch": normal_values(streams_of[18], (CP, CP), CP ** -0.5, 0.5, (), jnp.float32),
        "target_side_matrix": normal_values(streams_of[19], (CP, CP), CP ** -0.5, 0.5, (), jnp.float32),
        "target_side_switch": normal_values(streams_of[20], (CP, CP), CP ** -0.5, 0.5, (), jnp.float32),
        "trilateral_result_switch": normal_values(streams_of[21], (CP, CP), CP ** -0.5, 0.5, (), jnp.float32),
        "trilateral_result_matrix": normal_values(streams_of[22], (CP, CP), CP ** -0.5, 0.5, (), jnp.float32),
    }


@jax.custom_vjp
def low(v):
    return lax.optimization_barrier(v.astype(jnp.bfloat16)).astype(jnp.float32)

@jax.custom_vjp
def low_back(v):
    return v

def low_keep(v):
    return (low(v), None)

def low_pass(kept, grad):
    return (grad,)

def back_keep(v):
    return (v, None)

def back_low(kept, grad):
    return (low(grad),)
low.defvjp(low_keep, low_pass)
low_back.defvjp(back_keep, back_low)
highest = lax.Precision.HIGHEST

def standardize_features(tensor):
    average = lax.optimization_barrier(jnp.mean(tensor, axis=-1, keepdims=True))
    centered = tensor - average
    spread = lax.optimization_barrier(jnp.mean(centered * centered, axis=-1, keepdims=True))
    return centered * lax.rsqrt(spread + 1e-05)

def affine_map(tensor, weight):
    return jnp.einsum('...a,ab->...b', tensor, weight, precision=highest)

def evaluate_module(alignment_share, coupling_share, parameter_mapping, chain_exists):
    vertical_probe_matrix, vertical_lookup_matrix, vertical_content_matrix, vertical_result_matrix, horizontal_probe_matrix, horizontal_lookup_matrix, horizontal_content_matrix, coupling_offset_matrix, horizontal_result_matrix, tensor_source_matrix, tensor_target_matrix, tensor_result_matrix, source_side_matrix, source_side_switch, target_side_matrix, target_side_switch, trilateral_result_switch, trilateral_result_matrix = parameter_mapping
    overall_stack_count, chain_span = (alignment_share.shape[0], alignment_share.shape[1])
    group_count = coupling_offset_matrix.shape[1]
    group_span = horizontal_probe_matrix.shape[1] // group_count
    standardized_initial = standardize_features(alignment_share)
    col_q = affine_map(standardized_initial, vertical_probe_matrix).reshape(overall_stack_count, chain_span, group_count, group_span)
    col_k = affine_map(standardized_initial, vertical_lookup_matrix).reshape(overall_stack_count, chain_span, group_count, group_span)
    col_v = affine_map(standardized_initial, vertical_content_matrix).reshape(overall_stack_count, chain_span, group_count, group_span)
    col_scores = jnp.einsum('sihd,tihd->ihst', col_q, col_k, precision=highest) * group_span ** (-0.5)
    col_scores = jnp.where(chain_exists[None, None, None, :] > 0, col_scores, -1000000000.0)
    col_weights = jax.nn.softmax(col_scores, axis=-1)
    vertical_blend = jnp.einsum('ihst,tihd->sihd', col_weights, col_v, precision=highest)
    vertical_alignment = alignment_share + affine_map(vertical_blend.reshape(overall_stack_count, chain_span, group_count * group_span), vertical_result_matrix)
    standardized = standardize_features(vertical_alignment)
    split_q = affine_map(standardized, horizontal_probe_matrix).reshape(overall_stack_count, chain_span, group_count, group_span)
    split_k = affine_map(standardized, horizontal_lookup_matrix).reshape(overall_stack_count, chain_span, group_count, group_span)
    split_v = affine_map(standardized, horizontal_content_matrix).reshape(overall_stack_count, chain_span, group_count, group_span)
    coupling_offset_slices = affine_map(coupling_share, coupling_offset_matrix)
    scores = jnp.einsum('sihd,sjhd->shij', split_q, split_k, precision=highest) * group_span ** (-0.5)
    scores = scores + jnp.transpose(coupling_offset_slices, (2, 0, 1))[None]
    weights_soft = jax.nn.softmax(scores, axis=-1)
    softmax_blend = jnp.einsum('shij,sjhd->sihd', weights_soft, split_v, precision=highest)
    revised_alignment = vertical_alignment + affine_map(softmax_blend.reshape(overall_stack_count, chain_span, group_count * group_span), horizontal_result_matrix)
    standardized_revised = standardize_features(revised_alignment)
    left_edge_rows = affine_map(standardized_revised, tensor_source_matrix) * chain_exists[:, None, None]
    right_edge_rows = affine_map(standardized_revised, tensor_target_matrix)
    outer_prod = jnp.einsum('sip,sjq->ijpq', left_edge_rows, right_edge_rows, precision=highest)
    outer_prod = outer_prod.reshape(chain_span, chain_span, -1) / jnp.sum(chain_exists)
    pair_mid = coupling_share + affine_map(outer_prod, tensor_result_matrix)
    normed_pair = standardize_features(pair_mid)
    left_edge = jax.nn.sigmoid(affine_map(normed_pair, source_side_switch)) * affine_map(normed_pair, source_side_matrix)
    right_edge = jax.nn.sigmoid(affine_map(normed_pair, target_side_switch)) * affine_map(normed_pair, target_side_matrix)
    triangle = jnp.einsum('ikc,jkc->ijc', left_edge, right_edge, precision=highest)
    revised_couplings = pair_mid + jax.nn.sigmoid(affine_map(normed_pair, trilateral_result_switch)) * affine_map(standardize_features(triangle), trilateral_result_matrix)
    return (revised_alignment, revised_couplings)

def reference(alignment_features, residue_couplings, chain_indicator, alignment_result_adjoint, coupling_result_adjoint, vertical_probe_matrix, vertical_lookup_matrix, vertical_content_matrix, vertical_result_matrix, horizontal_probe_matrix, horizontal_lookup_matrix, horizontal_content_matrix, coupling_offset_matrix, horizontal_result_matrix, tensor_source_matrix, tensor_target_matrix, tensor_result_matrix, source_side_matrix, source_side_switch, target_side_matrix, target_side_switch, trilateral_result_switch, trilateral_result_matrix):
    chain_exists = chain_indicator.astype(jnp.float32)
    parameter_mapping = (vertical_probe_matrix, vertical_lookup_matrix, vertical_content_matrix, vertical_result_matrix, horizontal_probe_matrix, horizontal_lookup_matrix, horizontal_content_matrix, coupling_offset_matrix, horizontal_result_matrix, tensor_source_matrix, tensor_target_matrix, tensor_result_matrix, source_side_matrix, source_side_switch, target_side_matrix, target_side_switch, trilateral_result_switch, trilateral_result_matrix)

    def execute_module(alignment_share, coupling_share, parameter_bundle):
        return evaluate_module(alignment_share, coupling_share, parameter_bundle, chain_exists)
    (revised_alignment, revised_couplings), reverse_mapping = jax.vjp(execute_module, alignment_features, residue_couplings, parameter_mapping)
    alignment_adjoint, coupling_adjoint, adjoint_sequence_items = reverse_mapping((alignment_result_adjoint, coupling_result_adjoint))
    return (revised_alignment, revised_couplings, alignment_adjoint, coupling_adjoint, adjoint_sequence_items[0], adjoint_sequence_items[1], adjoint_sequence_items[2], adjoint_sequence_items[3], adjoint_sequence_items[4], adjoint_sequence_items[5], adjoint_sequence_items[6], adjoint_sequence_items[7], adjoint_sequence_items[8], adjoint_sequence_items[9], adjoint_sequence_items[10], adjoint_sequence_items[11], adjoint_sequence_items[12], adjoint_sequence_items[13], adjoint_sequence_items[14], adjoint_sequence_items[15], adjoint_sequence_items[16], adjoint_sequence_items[17])
```

```python
import jax
import jax.numpy as jnp
from jax import lax
from jax.sharding import PartitionSpec as P

precise = lax.Precision.HIGH
everyone = ("row", "col")


def standardize_features(tensor):
    average = jnp.mean(tensor, axis=-1, keepdims=True)
    centered = tensor - average
    spread = jnp.mean(centered * centered, axis=-1, keepdims=True)
    return centered * lax.rsqrt(spread + 1e-05)


def affine_map(tensor, weight):
    return jnp.einsum("...a,ab->...b", tensor, weight, precision=precise)


def exchange(chunks, axis):
    shape = chunks.shape
    flat = chunks.reshape(shape[0], -1, 128)
    return lax.all_to_all(flat, axis, 0, 0, tiled=True).reshape(shape)


def collect(block, axis, count):
    return exchange(jnp.broadcast_to(block[None], (count,) + block.shape), axis)


def per_device(mesh_rows, mesh_cols, *arguments):
    (
        alignment_features,
        residue_couplings,
        chain_indicator,
        alignment_result_adjoint,
        coupling_result_adjoint,
        *weights,
    ) = arguments
    devices = mesh_rows * mesh_cols
    present = chain_indicator.astype(jnp.float32)
    total_count = jnp.sum(present)
    chains = present.shape[0]
    rows_here, cols_here, pair_width = residue_couplings.shape
    span = rows_here * mesh_rows
    slim = span // devices
    heads = weights[7].shape[1]
    head_width = weights[4].shape[1] // heads
    chain_groups = devices // heads
    group_chains = chains // chain_groups
    scale = head_width ** (-0.5)
    channels_here = pair_width // devices

    def to_slim(x):
        return lax.all_to_all(x, "col", 1, 0, tiled=True)

    def from_slim(x):
        return lax.all_to_all(x, "col", 0, 1, tiled=True)

    def head_chunks(x):
        kinds = x.shape[0]
        x = x.reshape(kinds, chain_groups, group_chains, slim, heads, head_width)
        x = jnp.transpose(x, (4, 1, 0, 2, 3, 5))
        return x.reshape(devices, kinds, group_chains, slim, head_width)

    def channel_chunks(x):
        x = jnp.transpose(x, (3, 0, 1, 2))
        x = x.reshape(devices, channels_here, *x.shape[1:])
        return jnp.transpose(x, (0, 2, 1, 3, 4))

    def whole_maps(x):
        x = x.reshape(mesh_rows, mesh_cols, *x.shape[1:])
        x = jnp.transpose(x, (2, 3, 0, 4, 1, 5))
        return x.reshape(x.shape[0], x.shape[1], span, span)

    def tile_chunks(x):
        x = x.reshape(channels_here, mesh_rows, rows_here, mesh_cols, cols_here)
        return jnp.transpose(x, (1, 3, 0, 2, 4)).reshape(
            devices, channels_here, rows_here, cols_here
        )

    def forward(alignment_features, residue_couplings, weights):
        (
            vertical_probe_matrix,
            vertical_lookup_matrix,
            vertical_content_matrix,
            vertical_result_matrix,
            horizontal_probe_matrix,
            horizontal_lookup_matrix,
            horizontal_content_matrix,
            coupling_offset_matrix,
            horizontal_result_matrix,
            tensor_source_matrix,
            tensor_target_matrix,
            tensor_result_matrix,
            source_side_matrix,
            source_side_switch,
            target_side_matrix,
            target_side_switch,
            trilateral_result_switch,
            trilateral_result_matrix,
        ) = weights
        bias = affine_map(residue_couplings, coupling_offset_matrix)
        bias = jnp.transpose(bias, (2, 0, 1))
        bias = jnp.broadcast_to(
            bias[:, None], (heads, chain_groups, rows_here, cols_here)
        ).reshape(devices, rows_here, cols_here)
        bias = exchange(bias, everyone).reshape(mesh_rows, mesh_cols, rows_here, cols_here)
        bias = jnp.transpose(bias, (0, 2, 1, 3)).reshape(span, span)

        stripe = to_slim(alignment_features)
        standardized = standardize_features(stripe)
        split = lambda x: x.reshape(chains, slim, heads, head_width)
        col_q = split(affine_map(standardized, vertical_probe_matrix))
        col_k = split(affine_map(standardized, vertical_lookup_matrix))
        col_v = split(affine_map(standardized, vertical_content_matrix))
        col_scores = jnp.einsum("sihd,tihd->ihst", col_q, col_k, precision=precise) * scale
        col_scores = jnp.where(present[None, None, None, :] > 0, col_scores, -1000000000.0)
        col_weights = jax.nn.softmax(col_scores, axis=-1)
        blend = jnp.einsum("ihst,tihd->sihd", col_weights, col_v, precision=precise)
        msa_col = stripe + affine_map(
            blend.reshape(chains, slim, heads * head_width), vertical_result_matrix
        )

        standardized = standardize_features(msa_col)
        qkv = jnp.stack(
            [
                affine_map(standardized, horizontal_probe_matrix),
                affine_map(standardized, horizontal_lookup_matrix),
                affine_map(standardized, horizontal_content_matrix),
            ]
        )
        qkv = exchange(head_chunks(qkv), everyone)
        qkv = jnp.transpose(qkv, (1, 2, 0, 3, 4)).reshape(3, group_chains, span, head_width)
        scores = jnp.einsum("sid,sjd->sij", qkv[0], qkv[1], precision=precise) * scale
        weights_soft = jax.nn.softmax(scores + bias[None], axis=-1)
        blend = jnp.einsum("sij,sjd->sid", weights_soft, qkv[2], precision=precise)
        blend = blend.reshape(group_chains, devices, slim, head_width)
        blend = exchange(jnp.transpose(blend, (1, 0, 2, 3)), everyone)
        blend = blend.reshape(heads, chains, slim, head_width)
        blend = jnp.transpose(blend, (1, 2, 0, 3)).reshape(chains, slim, heads * head_width)
        msa_out = msa_col + affine_map(blend, horizontal_result_matrix)

        standardized = standardize_features(msa_out)
        left_rows = affine_map(standardized, tensor_source_matrix) * present[:, None, None]
        right_rows = affine_map(standardized, tensor_target_matrix)
        features = left_rows.shape[-1]
        left_rows = collect(left_rows, "col", mesh_cols)
        left_rows = jnp.transpose(left_rows, (1, 0, 2, 3)).reshape(chains, rows_here, features)
        turn = [(g, (g % mesh_rows) * mesh_cols + g // mesh_rows) for g in range(devices)]
        right_rows = lax.ppermute(right_rows, everyone, turn)
        right_rows = collect(right_rows, "row", mesh_rows)
        right_rows = jnp.transpose(right_rows, (1, 0, 2, 3)).reshape(chains, cols_here, features)
        outer_prod = jnp.einsum("sip,sjq->ijpq", left_rows, right_rows, precision=precise)
        outer_prod = outer_prod.reshape(rows_here, cols_here, -1) / total_count
        pair_mid = residue_couplings + affine_map(outer_prod, tensor_result_matrix)

        normed_pair = standardize_features(pair_mid)
        left_edge = jax.nn.sigmoid(affine_map(normed_pair, source_side_switch)) * affine_map(
            normed_pair, source_side_matrix
        )
        right_edge = jax.nn.sigmoid(affine_map(normed_pair, target_side_switch)) * affine_map(
            normed_pair, target_side_matrix
        )
        maps = whole_maps(
            exchange(channel_chunks(jnp.stack([left_edge, right_edge])), everyone)
        )
        triangle = jnp.einsum("cik,cjk->cij", maps[0], maps[1], precision=precise)
        triangle = exchange(tile_chunks(triangle), everyone)
        triangle = triangle.reshape(pair_width, rows_here, cols_here)
        triangle = jnp.transpose(triangle, (1, 2, 0))
        pair_out = pair_mid + jax.nn.sigmoid(
            affine_map(normed_pair, trilateral_result_switch)
        ) * affine_map(standardize_features(triangle), trilateral_result_matrix)
        return from_slim(msa_out), pair_out

    (msa_out, pair_out), back = jax.vjp(
        forward, alignment_features, residue_couplings, tuple(weights)
    )
    alignment_adjoint, coupling_adjoint, weight_adjoints = back(
        (alignment_result_adjoint, coupling_result_adjoint)
    )
    early = weight_adjoints[4:]
    late = weight_adjoints[:4]
    sizes = [w.size for w in early]
    flat = jnp.concatenate([w.reshape(-1) for w in early])
    flat = lax.psum(flat.reshape(-1, 128), everyone).reshape(-1)
    summed_early, start = [], 0
    for w, size in zip(early, sizes):
        summed_early.append(lax.slice(flat, (start,), (start + size,)).reshape(w.shape))
        start += size
    stacked = jnp.concatenate(late, axis=0)
    parts = exchange(stacked.reshape(devices, -1, 128), everyone).sum(0)
    stacked = collect(parts, everyone, devices).reshape(stacked.shape)
    summed_late = jnp.split(stacked, 4, axis=0)
    return (
        msa_out,
        pair_out,
        alignment_adjoint,
        coupling_adjoint,
        *summed_late,
        *summed_early,
    )


def solution(mesh):
    mesh_rows, mesh_cols = mesh.shape["row"], mesh.shape["col"]

    def local(*arguments):
        return per_device(mesh_rows, mesh_cols, *arguments)

    whole = P()
    msa = P("col", "row", None)
    pair = P("row", "col", None)
    return jax.shard_map(
        local,
        mesh=mesh,
        in_specs=(msa, pair, whole, msa, pair) + (whole,) * 18,
        out_specs=(msa, pair, msa, pair) + (whole,) * 18,
        check_vma=False,
    )
```

```python
import functools

import jax
import jax.numpy as jnp
from jax import lax
from jax.experimental import pallas as pl
from jax.experimental.pallas import tpu as pltpu
from jax.sharding import PartitionSpec as P

bf16, f32 = jnp.bfloat16, jnp.float32
NN = ((1,), (0,))
NT = ((1,), (1,))
TN = ((0,), (0,))


def one_pass(a, b, dims=NN):
    return lax.dot_general(a, b, (dims, ((), ())), preferred_element_type=f32)


def halves(x):
    high = x.astype(bf16)
    return high, (x - high.astype(f32)).astype(bf16)


def dot3(a, b, dims=NN):
    a_high, a_low = a if isinstance(a, tuple) else halves(a)
    b_high, b_low = b if isinstance(b, tuple) else halves(b)
    return one_pass(a_high, b_high, dims) + (
        one_pass(a_high, b_low, dims) + one_pass(a_low, b_high, dims)
    )


def rounded(pair, rows):
    return pair[0][rows], pair[1][rows]


def iota(shape, dim):
    return lax.broadcasted_iota(jnp.int32, shape, dim)


def norm_parts(x):
    centered = x - jnp.mean(x, axis=-1, keepdims=True)
    inverse = lax.rsqrt(jnp.mean(centered * centered, axis=-1, keepdims=True) + 1e-05)
    return centered * inverse, inverse


def norm_back(normed, inverse, grad):
    return inverse * (
        grad
        - jnp.mean(grad, axis=-1, keepdims=True)
        - normed * jnp.mean(grad * normed, axis=-1, keepdims=True)
    )


def spread_tables(chains):
    groups = chains // 4
    shape = (128, 256)
    spread = [
        jnp.where(
            ((iota(shape, 0) >> 5) == s) & ((iota(shape, 0) & 31) == (iota(shape, 1) >> 3)), 1.0, 0.0
        ).astype(bf16)
        for s in range(4)
    ]
    shape = (chains * 8, chains)
    chain = iota(shape, 0) >> 3
    lift = jnp.where(iota(shape, 1) == (chain & 3) * groups + (chain >> 2), 1.0, 0.0).astype(bf16)
    shape = (chains * 8, 256)
    same = (iota(shape, 0) & 7) == (iota(shape, 1) & 7)
    return spread, lift, same


def spread_left(left_ref, spread, high_ref, low_ref):
    left_high, left_low = halves(left_ref[...])
    for s in range(4):
        high_ref[s] = one_pass(left_high, spread[s])
        low_ref[s] = one_pass(left_low, spread[s])


def block_left(high_ref, low_ref, i, chains, lift, same):
    groups = chains // 4
    rows = pl.ds(pl.multiple_of(i * groups, groups), groups)
    out = []
    for ref in (high_ref, low_ref):
        slab = ref[:, rows, :].reshape(chains, 256).astype(bf16)
        out.append(jnp.where(same, one_pass(lift, slab), 0.0).astype(bf16))
    return tuple(out)


def outer_weights(ref):
    whole = ref[...].reshape(32, 4, 8, 128)
    return [halves(whole[:, g].reshape(256, 128)) for g in range(4)]


def edges_kernel(
    cols, chains, left_ref, right_ref, outer_ref, pair_ref, sides_ref, mid_ref, edge_ref, high_ref, low_ref
):
    spread, lift, same = spread_tables(chains)
    spread_left(left_ref, spread, high_ref, low_ref)
    right = halves(right_ref[...])
    outer = outer_weights(outer_ref)
    sides = halves(sides_ref[...])

    def step(t, carry):
        tiles, places = [], four_rows(t, cols)
        for u in range(4):
            i = 2 * t + u // 2 + 16 * (u % 2)
            block = block_left(high_ref, low_ref, i, chains, lift, same)
            tiles.append(halves(dot3(right, block)))
        update = jnp.zeros((4 * cols, 128), f32)
        for g in range(4):
            rows = slice(g * cols, (g + 1) * cols)
            part = tuple(jnp.concatenate([x[n][rows] for x in tiles], 0) for n in range(2))
            update = update + dot3(part, outer[g])
        mid = update + read_rows(pair_ref, places)
        write_rows(mid_ref, places, mid)
        normed, _ = norm_parts(mid)
        logits = dot3(normed, sides)
        write_turned(edge_ref, t, jax.nn.sigmoid(logits[:, :256]) * logits[:, 256:])
        return carry

    lax.fori_loop(0, 8, step, 0)


def call_edges(left, right, outer, pair, sides, cols):
    chains = left.shape[0] // 32 * 4
    rows = pair.shape[0]
    return pl.pallas_call(
        functools.partial(edges_kernel, cols, chains),
        out_shape=(
            jax.ShapeDtypeStruct((rows, 128), f32),
            jax.ShapeDtypeStruct((256, 16, 128), f32),
        ),
        scratch_shapes=[pltpu.VMEM((4, left.shape[0], 256), f32)] * 2,
        compiler_params=pltpu.CompilerParams(vmem_limit_bytes=56 * 2**20),
        name="edges",
    )(left, right, outer, pair, sides)


def join_tiles(chunks, mesh_rows, mesh_cols, out_ref):
    plain = chunks.reshape(mesh_rows * mesh_cols * 16, 128)
    rolled = pltpu.roll(plain, 64, 1)
    first = iota((16, 128), 1) < 64
    for r in range(mesh_rows):
        for t in range(mesh_cols // 2):
            even = slice((r * mesh_cols + 2 * t) * 16, (r * mesh_cols + 2 * t + 1) * 16)
            odd = slice((r * mesh_cols + 2 * t + 1) * 16, (r * mesh_cols + 2 * t + 2) * 16)
            lanes = slice(t * 128, (t + 1) * 128)
            out_ref[r * 32 : r * 32 + 16, lanes] = jnp.where(first, plain[even], rolled[odd])
            out_ref[r * 32 + 16 : r * 32 + 32, lanes] = jnp.where(first, rolled[even], plain[odd])


def cut_tiles(whole, mesh_rows, mesh_cols, store):
    first = iota((16, 128), 1) < 64
    for t in range(mesh_cols // 2):
        plain = whole[:, t * 128 : (t + 1) * 128]
        rolled = pltpu.roll(plain, 64, 1)
        for r in range(mesh_rows):
            low = slice(r * 32, r * 32 + 16)
            high = slice(r * 32 + 16, r * 32 + 32)
            store(r * mesh_cols + 2 * t, jnp.where(first, plain[low], rolled[high]))
            store(r * mesh_cols + 2 * t + 1, jnp.where(first, rolled[low], plain[high]))


def triangle_kernel(mesh_rows, mesh_cols, edge_ref, out_ref, left_ref, right_ref):
    join_tiles(edge_ref[:, 0, 0], mesh_rows, mesh_cols, left_ref)
    join_tiles(edge_ref[:, 1, 0], mesh_rows, mesh_cols, right_ref)

    def store(d, tile):
        out_ref[d, 0] = tile

    cut_tiles(dot3(left_ref[...], right_ref[...], NT), mesh_rows, mesh_cols, store)


def call_triangle(edges, mesh_rows, mesh_cols):
    devices, _, channels = edges.shape[:3]
    span = mesh_rows * 32
    return pl.pallas_call(
        functools.partial(triangle_kernel, mesh_rows, mesh_cols),
        grid=(channels,),
        in_specs=[pl.BlockSpec((devices, 2, 1, 16, 128), lambda n: (0, 0, n, 0, 0))],
        out_specs=pl.BlockSpec((devices, 1, 16, 128), lambda n: (0, n, 0, 0)),
        out_shape=jax.ShapeDtypeStruct((devices, channels, 16, 128), f32),
        scratch_shapes=[pltpu.VMEM((span, span), f32)] * 2,
        compiler_params=pltpu.CompilerParams(vmem_limit_bytes=56 * 2**20),
        name="triangle",
    )(edges)


def triangle_back_kernel(
    mesh_rows, mesh_cols, edge_ref, grad_ref, out_ref, left_ref, right_ref, whole_ref
):
    join_tiles(edge_ref[:, 0, 0], mesh_rows, mesh_cols, left_ref)
    join_tiles(edge_ref[:, 1, 0], mesh_rows, mesh_cols, right_ref)
    join_tiles(grad_ref[:, 0], mesh_rows, mesh_cols, whole_ref)

    def store(kind):
        def put(d, tile):
            out_ref[d, kind, 0] = tile

        return put

    whole = whole_ref[...]
    cut_tiles(dot3(whole, right_ref[...]), mesh_rows, mesh_cols, store(0))
    cut_tiles(dot3(jnp.transpose(whole), left_ref[...]), mesh_rows, mesh_cols, store(1))


def call_triangle_back(edges, grad, mesh_rows, mesh_cols):
    devices, _, channels = edges.shape[:3]
    span = mesh_rows * 32
    both = pl.BlockSpec((devices, 2, 1, 16, 128), lambda n: (0, 0, n, 0, 0))
    return pl.pallas_call(
        functools.partial(triangle_back_kernel, mesh_rows, mesh_cols),
        grid=(channels,),
        in_specs=[both, pl.BlockSpec((devices, 1, 16, 128), lambda n: (0, n, 0, 0))],
        out_specs=both,
        out_shape=jax.ShapeDtypeStruct(edges.shape, f32),
        scratch_shapes=[pltpu.VMEM((span, span), f32)] * 3,
        compiler_params=pltpu.CompilerParams(vmem_limit_bytes=56 * 2**20),
        name="triangle_back",
    )(edges, grad)


def four_rows(t, cols):
    return [
        pl.ds(pl.multiple_of((2 * t + u // 2 + 16 * (u % 2)) * cols, cols), cols) for u in range(4)
    ]


def read_rows(ref, places):
    return jnp.concatenate([ref[p, :] for p in places], 0)


def write_rows(ref, places, value):
    size = value.shape[0] // len(places)
    for u, p in enumerate(places):
        ref[p, :] = value[u * size : (u + 1) * size]


def read_turned(ref, t):
    parts = []
    for v in range(2):
        tile = ref[:, pl.ds(2 * t + v, 1), :]
        parts.append(jnp.transpose(tile.reshape(tile.shape[0], 128)))
    return jnp.concatenate(parts, 0)


def write_turned(ref, t, value):
    for v in range(2):
        turned = jnp.transpose(value[v * 128 : (v + 1) * 128])
        ref[:, pl.ds(2 * t + v, 1), :] = turned[:, None, :]


def finish_kernel(
    cols, tri_ref, mid_ref, grad_ref, gate_ref, proj_ref, out_ref, dtri_ref, dlogit_ref, dproj_ref
):
    gate_w = halves(gate_ref[...])
    proj_w = halves(proj_ref[...])
    dproj_ref[...] = jnp.zeros_like(dproj_ref)

    def step(t, carry):
        places = four_rows(t, cols)
        mid = read_rows(mid_ref, places)
        grad = read_rows(grad_ref, places)
        normed, _ = norm_parts(mid)
        tri, tri_inverse = norm_parts(read_turned(tri_ref, t))
        tri_halves = halves(tri)
        gate = jax.nn.sigmoid(dot3(normed, gate_w))
        value = dot3(tri_halves, proj_w)
        write_rows(out_ref, places, mid + gate * value)
        dvalue = halves(grad * gate)
        write_rows(dlogit_ref, places, grad * value * gate * (1.0 - gate))
        dproj_ref[...] += dot3(halves(jnp.transpose(tri)), dvalue)
        write_turned(dtri_ref, t, norm_back(tri, tri_inverse, dot3(dvalue, proj_w, NT)))
        return carry

    lax.fori_loop(0, 8, step, 0)


def call_finish(tri, mid, grad, gate, proj, cols):
    rows = mid.shape[0]
    return pl.pallas_call(
        functools.partial(finish_kernel, cols),
        out_shape=(
            jax.ShapeDtypeStruct((rows, 128), f32),
            jax.ShapeDtypeStruct((128, 16, 128), f32),
            jax.ShapeDtypeStruct((rows, 128), f32),
            jax.ShapeDtypeStruct((128, 128), f32),
        ),
        compiler_params=pltpu.CompilerParams(vmem_limit_bytes=56 * 2**20),
        name="finish",
    )(tri, mid, grad, gate, proj)


def edges_back_kernel(
    cols,
    chains,
    dedge_ref,
    mid_ref,
    grad_ref,
    dlogit_ref,
    sides_ref,
    left_ref,
    right_ref,
    outer_ref,
    dmid_ref,
    dsides_ref,
    douter_ref,
    dleft_ref,
    dright_ref,
    high_ref,
    low_ref,
    dslab_ref,
):
    groups = chains // 4
    spread, lift, same = spread_tables(chains)
    spread_left(left_ref, spread, high_ref, low_ref)
    right = halves(right_ref[...])
    right_turned = halves(jnp.transpose(right_ref[...]))
    shape = (chains, chains * 8)
    chain = iota(shape, 1) >> 3
    drop = jnp.where(iota(shape, 0) == (chain & 3) * groups + (chain >> 2), 1.0, 0.0).astype(bf16)
    outer = outer_weights(outer_ref)
    sides = halves(sides_ref[...])
    dsides_ref[...] = jnp.zeros_like(dsides_ref)
    douter_ref[...] = jnp.zeros_like(douter_ref)
    dright_ref[...] = jnp.zeros_like(dright_ref)

    def step(t, carry):
        places = four_rows(t, cols)
        normed, inverse = norm_parts(read_rows(mid_ref, places))
        logits = dot3(normed, rounded(sides, (slice(None), slice(0, 512))))
        gate, value = jax.nn.sigmoid(logits[:, :256]), logits[:, 256:]
        dedge = read_turned(dedge_ref, t)
        dlogits = halves(
            jnp.concatenate(
                [
                    dedge * value * gate * (1.0 - gate),
                    dedge * gate,
                    read_rows(dlogit_ref, places),
                ],
                1,
            )
        )
        dsides_ref[...] += dot3(halves(jnp.transpose(normed)), dlogits)
        dmid = read_rows(grad_ref, places) + norm_back(normed, inverse, dot3(dlogits, sides, NT))
        write_rows(dmid_ref, places, dmid)
        dmid_turned = halves(jnp.transpose(dmid))
        dmid = halves(dmid)
        dprod = [halves(dot3(dmid, outer[g], NT)) for g in range(4)]
        prods = []
        for u in range(4):
            i = 2 * t + u // 2 + 16 * (u % 2)
            block = block_left(high_ref, low_ref, i, chains, lift, same)
            prods.append(halves(dot3(right, block)))
            rows = slice(u * cols, (u + 1) * cols)
            here = tuple(jnp.concatenate([dprod[g][n][rows] for g in range(4)], 0) for n in range(2))
            dright_ref[...] += dot3(here, block, NT)
            dblock = halves(jnp.where(same, dot3(right_turned, here), 0.0))
            dslab = one_pass(drop, dblock[0]) + one_pass(drop, dblock[1])
            place = pl.ds(pl.multiple_of(i * groups, groups), groups)
            dslab_ref[:, place, :] = dslab.reshape(4, groups, 256)
        for g in range(4):
            rows = slice(g * cols, (g + 1) * cols)
            part = tuple(jnp.concatenate([x[n][rows] for x in prods], 0) for n in range(2))
            douter_ref[:, g * 256 : (g + 1) * 256] += dot3(dmid_turned, part)
        return carry

    lax.fori_loop(0, 8, step, 0)
    dleft = jnp.zeros(dleft_ref.shape, f32)
    for s in range(4):
        high, low = halves(dslab_ref[s])
        dleft = dleft + (one_pass(high, spread[s], NT) + one_pass(low, spread[s], NT))
    dleft_ref[...] = dleft


def call_edges_back(dedge, mid, grad, dlogit, sides, left, right, outer, cols):
    chains = left.shape[0] // 32 * 4
    rows = mid.shape[0]
    return pl.pallas_call(
        functools.partial(edges_back_kernel, cols, chains),
        out_shape=(
            jax.ShapeDtypeStruct((rows, 128), f32),
            jax.ShapeDtypeStruct((128, 640), f32),
            jax.ShapeDtypeStruct((128, 1024), f32),
            jax.ShapeDtypeStruct(left.shape, f32),
            jax.ShapeDtypeStruct(right.shape, f32),
        ),
        scratch_shapes=[pltpu.VMEM((4, left.shape[0], 256), f32)] * 3,
        compiler_params=pltpu.CompilerParams(vmem_limit_bytes=56 * 2**20),
        name="edges_back",
    )(dedge, mid, grad, dlogit, sides, left, right, outer)


precise = lax.Precision.HIGH
everyone = ("row", "col")


def standardize_features(tensor):
    average = jnp.mean(tensor, axis=-1, keepdims=True)
    centered = tensor - average
    spread = jnp.mean(centered * centered, axis=-1, keepdims=True)
    return centered * lax.rsqrt(spread + 1e-05)


def affine_map(tensor, weight):
    return jnp.einsum("...a,ab->...b", tensor, weight, precision=precise)


def exchange(chunks, axis):
    shape = chunks.shape
    flat = chunks.reshape(shape[0], -1, 128)
    return lax.all_to_all(flat, axis, 0, 0, tiled=True).reshape(shape)


def collect(block, axis, count):
    return exchange(jnp.broadcast_to(block[None], (count,) + block.shape), axis)


def per_device(mesh_rows, mesh_cols, *arguments):
    (
        alignment_features,
        residue_couplings,
        chain_indicator,
        alignment_result_adjoint,
        coupling_result_adjoint,
        *weights,
    ) = arguments
    devices = mesh_rows * mesh_cols
    present = chain_indicator.astype(jnp.float32)
    total_count = jnp.sum(present)
    chains = present.shape[0]
    rows_here, cols_here, pair_width = residue_couplings.shape
    span = rows_here * mesh_rows
    slim = span // devices
    heads = weights[7].shape[1]
    head_width = weights[4].shape[1] // heads
    chain_groups = devices // heads
    group_chains = chains // chain_groups
    scale = head_width ** (-0.5)
    channels_here = pair_width // devices
    pair_rows = rows_here * cols_here

    def to_slim(x):
        return lax.all_to_all(x, "col", 1, 0, tiled=True)

    def from_slim(x):
        return lax.all_to_all(x, "col", 0, 1, tiled=True)

    def head_chunks(x):
        kinds = x.shape[0]
        x = x.reshape(kinds, chain_groups, group_chains, slim, heads, head_width)
        x = jnp.transpose(x, (4, 1, 0, 2, 3, 5))
        return x.reshape(devices, kinds, group_chains, slim, head_width)

    def msa_side(alignment_features, residue_couplings, weights):
        (
            vertical_probe_matrix,
            vertical_lookup_matrix,
            vertical_content_matrix,
            vertical_result_matrix,
            horizontal_probe_matrix,
            horizontal_lookup_matrix,
            horizontal_content_matrix,
            coupling_offset_matrix,
            horizontal_result_matrix,
            tensor_source_matrix,
            tensor_target_matrix,
        ) = weights
        bias = affine_map(residue_couplings, coupling_offset_matrix)
        bias = jnp.transpose(bias, (2, 0, 1))
        bias = jnp.broadcast_to(
            bias[:, None], (heads, chain_groups, rows_here, cols_here)
        ).reshape(devices, rows_here, cols_here)
        bias = exchange(bias, everyone).reshape(mesh_rows, mesh_cols, rows_here, cols_here)
        bias = jnp.transpose(bias, (0, 2, 1, 3)).reshape(span, span)

        stripe = to_slim(alignment_features)
        standardized = standardize_features(stripe)
        split = lambda x: x.reshape(chains, slim, heads, head_width)
        col_q = split(affine_map(standardized, vertical_probe_matrix))
        col_k = split(affine_map(standardized, vertical_lookup_matrix))
        col_v = split(affine_map(standardized, vertical_content_matrix))
        col_scores = jnp.einsum("sihd,tihd->ihst", col_q, col_k, precision=precise) * scale
        col_scores = jnp.where(present[None, None, None, :] > 0, col_scores, -1000000000.0)
        col_weights = jax.nn.softmax(col_scores, axis=-1)
        blend = jnp.einsum("ihst,tihd->sihd", col_weights, col_v, precision=precise)
        msa_col = stripe + affine_map(
            blend.reshape(chains, slim, heads * head_width), vertical_result_matrix
        )

        standardized = standardize_features(msa_col)
        qkv = jnp.stack(
            [
                affine_map(standardized, horizontal_probe_matrix),
                affine_map(standardized, horizontal_lookup_matrix),
                affine_map(standardized, horizontal_content_matrix),
            ]
        )
        qkv = exchange(head_chunks(qkv), everyone)
        qkv = jnp.transpose(qkv, (1, 2, 0, 3, 4)).reshape(3, group_chains, span, head_width)
        scores = jnp.einsum("sid,sjd->sij", qkv[0], qkv[1], precision=precise) * scale
        weights_soft = jax.nn.softmax(scores + bias[None], axis=-1)
        blend = jnp.einsum("sij,sjd->sid", weights_soft, qkv[2], precision=precise)
        blend = blend.reshape(group_chains, devices, slim, head_width)
        blend = exchange(jnp.transpose(blend, (1, 0, 2, 3)), everyone)
        blend = blend.reshape(heads, chains, slim, head_width)
        blend = jnp.transpose(blend, (1, 2, 0, 3)).reshape(chains, slim, heads * head_width)
        msa_out = msa_col + affine_map(blend, horizontal_result_matrix)

        standardized = standardize_features(msa_out)
        left_rows = affine_map(standardized, tensor_source_matrix)
        left_rows = left_rows * (present / total_count)[:, None, None]
        right_rows = affine_map(standardized, tensor_target_matrix)
        left_rows = left_rows.reshape(chains // 4, 4, slim, 32)
        left_rows = jnp.transpose(left_rows, (2, 0, 1, 3)).reshape(slim, chains // 4, 128)
        left_rows = collect(left_rows, "col", mesh_cols).reshape(-1, 128)
        right_rows = right_rows.reshape(chains // 16, 16, slim, 4, 8)
        right_rows = jnp.transpose(right_rows, (3, 0, 2, 1, 4)).reshape(-1, 128)
        turn = [(g, (g % mesh_rows) * mesh_cols + g // mesh_rows) for g in range(devices)]
        right_rows = lax.ppermute(right_rows, everyone, turn)
        right_rows = collect(right_rows, "row", mesh_rows)
        right_rows = right_rows.reshape(mesh_rows, 4, chains // 16, slim, 128)
        right_rows = jnp.transpose(right_rows, (1, 0, 3, 2, 4))
        return from_slim(msa_out), left_rows, right_rows.reshape(4 * cols_here, chains * 8)

    (
        tensor_result_matrix,
        source_side_matrix,
        source_side_switch,
        target_side_matrix,
        target_side_switch,
        trilateral_result_switch,
        trilateral_result_matrix,
    ) = weights[11:]

    def interleave(left, right):
        shape = (pair_width, devices, channels_here)
        both = jnp.stack([left.reshape(shape), right.reshape(shape)], 2)
        return both.reshape(pair_width, 2 * pair_width)

    def separate(both):
        both = both.reshape(pair_width, devices, 2, channels_here)
        return (
            both[:, :, 0].reshape(pair_width, pair_width),
            both[:, :, 1].reshape(pair_width, pair_width),
        )

    def total(parts):
        return lax.psum(jnp.concatenate(parts, axis=0), everyone)

    sides = jnp.concatenate(
        [
            interleave(source_side_switch, target_side_switch),
            interleave(source_side_matrix, target_side_matrix),
            trilateral_result_switch,
        ],
        1,
    )
    (msa_out, left_rows, right_rows), msa_back = jax.vjp(
        msa_side, alignment_features, residue_couplings, tuple(weights[:11])
    )
    pair_flat = residue_couplings.reshape(pair_rows, pair_width)
    grad_flat = coupling_result_adjoint.reshape(pair_rows, pair_width)
    pair_mid, edges = call_edges(
        left_rows, right_rows, tensor_result_matrix, pair_flat, sides[:, : 4 * pair_width], cols_here
    )
    edges = exchange(edges.reshape(devices, 2, channels_here, 16, 128), everyone)
    triangle = exchange(call_triangle(edges, mesh_rows, mesh_cols), everyone)
    pair_out, d_triangle, d_logit, g_tri_out = call_finish(
        triangle.reshape(pair_width, 16, 128),
        pair_mid,
        grad_flat,
        trilateral_result_switch,
        trilateral_result_matrix,
        cols_here,
    )
    d_triangle = exchange(d_triangle.reshape(devices, channels_here, 16, 128), everyone)
    d_edges = exchange(call_triangle_back(edges, d_triangle, mesh_rows, mesh_cols), everyone)
    d_mid, d_sides, d_outer, d_left, d_right = call_edges_back(
        d_edges.reshape(2 * pair_width, 16, 128),
        pair_mid,
        grad_flat,
        d_logit,
        sides,
        left_rows,
        right_rows,
        tensor_result_matrix,
        cols_here,
    )
    parts = [g_tri_out] + [d_sides[:, n : n + 128] for n in range(0, 640, 128)]
    parts += [d_outer[:, n : n + 128] for n in range(0, 1024, 128)]
    summed = jnp.split(total(parts), 14, axis=0)
    g_tri_out, g_tri_gate = summed[0], summed[5]
    g_left_gate, g_right_gate = separate(jnp.concatenate(summed[1:3], 1))
    g_left, g_right = separate(jnp.concatenate(summed[3:5], 1))
    g_outer = jnp.concatenate(summed[6:], 1).reshape(pair_width, 4, 32, 8)
    g_outer = jnp.transpose(g_outer, (2, 1, 3, 0)).reshape(1024, pair_width)

    alignment_adjoint, coupling_adjoint, msa_adjoints = msa_back(
        (alignment_result_adjoint, d_left, d_right)
    )
    coupling_adjoint = coupling_adjoint + d_mid.reshape(rows_here, cols_here, pair_width)
    wide = [w for w in msa_adjoints if w.shape == (256, 256)]
    thin = jnp.concatenate(
        [msa_adjoints[9], msa_adjoints[10], jnp.pad(msa_adjoints[7], ((0, 128), (0, 24)))], 1
    )
    thin = jnp.concatenate([thin, jnp.zeros((256, 160), jnp.float32)], 1)
    stacked = jnp.concatenate(wide + [thin], axis=0)
    parts = exchange(stacked.reshape(devices, -1, 128), everyone).sum(0)
    stacked = collect(parts, everyone, devices).reshape(stacked.shape)
    summed = jnp.split(stacked, 9, axis=0)
    return (
        msa_out,
        pair_out.reshape(rows_here, cols_here, pair_width),
        alignment_adjoint,
        coupling_adjoint,
        *summed[:7],
        summed[8][:128, 64:72],
        summed[7],
        summed[8][:, :32],
        summed[8][:, 32:64],
        g_outer,
        g_left,
        g_left_gate,
        g_right,
        g_right_gate,
        g_tri_gate,
        g_tri_out,
    )


def solution(mesh):
    mesh_rows, mesh_cols = mesh.shape["row"], mesh.shape["col"]

    def local(*arguments):
        return per_device(mesh_rows, mesh_cols, *arguments)

    whole = P()
    msa = P("col", "row", None)
    pair = P("row", "col", None)
    return jax.shard_map(
        local,
        mesh=mesh,
        in_specs=(msa, pair, whole, msa, pair) + (whole,) * 18,
        out_specs=(msa, pair, msa, pair) + (whole,) * 18,
        check_vma=False,
    )
```

```python
import functools

import jax
import jax.numpy as jnp
from jax import lax
from jax.experimental import pallas as pl
from jax.experimental.pallas import tpu as pltpu
from jax.sharding import PartitionSpec as P

bf16, f32 = jnp.bfloat16, jnp.float32
NN = ((1,), (0,))
NT = ((1,), (1,))
TN = ((0,), (0,))


def one_pass(a, b, dims=NN):
    return lax.dot_general(a, b, (dims, ((), ())), preferred_element_type=f32)


def halves(x):
    high = x.astype(bf16)
    return high, (x - high.astype(f32)).astype(bf16)


def dot3(a, b, dims=NN):
    a_high, a_low = a if isinstance(a, tuple) else halves(a)
    b_high, b_low = b if isinstance(b, tuple) else halves(b)
    return one_pass(a_high, b_high, dims) + (
        one_pass(a_high, b_low, dims) + one_pass(a_low, b_high, dims)
    )


def rounded(pair, rows):
    return pair[0][rows], pair[1][rows]


def iota(shape, dim):
    return lax.broadcasted_iota(jnp.int32, shape, dim)


def norm_parts(x):
    centered = x - jnp.mean(x, axis=-1, keepdims=True)
    inverse = lax.rsqrt(jnp.mean(centered * centered, axis=-1, keepdims=True) + 1e-05)
    return centered * inverse, inverse


def norm_back(normed, inverse, grad):
    return inverse * (
        grad
        - jnp.mean(grad, axis=-1, keepdims=True)
        - normed * jnp.mean(grad * normed, axis=-1, keepdims=True)
    )


def spread_tables(chains):
    groups = chains // 4
    shape = (128, 256)
    spread = [
        jnp.where(
            ((iota(shape, 0) >> 5) == s) & ((iota(shape, 0) & 31) == (iota(shape, 1) >> 3)), 1.0, 0.0
        ).astype(bf16)
        for s in range(4)
    ]
    shape = (chains * 8, chains)
    chain = iota(shape, 0) >> 3
    lift = jnp.where(iota(shape, 1) == (chain & 3) * groups + (chain >> 2), 1.0, 0.0).astype(bf16)
    shape = (chains * 8, 256)
    same = (iota(shape, 0) & 7) == (iota(shape, 1) & 7)
    return spread, lift, same


def spread_left(left_ref, spread, high_ref, low_ref):
    left_high, left_low = halves(left_ref[...])
    for s in range(4):
        high_ref[s] = one_pass(left_high, spread[s])
        low_ref[s] = one_pass(left_low, spread[s])


def block_left(high_ref, low_ref, i, chains, lift, same):
    groups = chains // 4
    rows = pl.ds(pl.multiple_of(i * groups, groups), groups)
    out = []
    for ref in (high_ref, low_ref):
        slab = ref[:, rows, :].reshape(chains, 256).astype(bf16)
        out.append(jnp.where(same, one_pass(lift, slab), 0.0).astype(bf16))
    return tuple(out)


def join_right(ref, out_ref):
    cols = ref.shape[0] * 8
    for g in range(4):
        for n in range(ref.shape[2]):
            out_ref[g * cols : (g + 1) * cols, n * 128 : (n + 1) * 128] = ref[:, g, n].reshape(
                cols, 128
            )


def cut_right(ref, out_ref):
    cols = out_ref.shape[0] * 8
    for g in range(4):
        for n in range(out_ref.shape[2]):
            tile = ref[g * cols : (g + 1) * cols, n * 128 : (n + 1) * 128]
            out_ref[:, g, n] = tile.reshape(-1, 8, 128)


def outer_weights(ref):
    whole = ref[...].reshape(32, 4, 8, 128)
    return [halves(whole[:, g].reshape(256, 128)) for g in range(4)]


def edges_kernel(
    cols, chains, left_ref, right_ref, outer_ref, pair_ref, sides_ref, mid_ref, edge_ref, high_ref, low_ref, whole_ref
):
    spread, lift, same = spread_tables(chains)
    spread_left(left_ref, spread, high_ref, low_ref)
    join_right(right_ref, whole_ref)
    right = halves(whole_ref[...])
    outer = outer_weights(outer_ref)
    sides = halves(sides_ref[...])

    def step(t, carry):
        tiles, places = [], four_rows(t, cols)
        for u in range(4):
            i = 2 * t + u // 2 + 16 * (u % 2)
            block = block_left(high_ref, low_ref, i, chains, lift, same)
            tiles.append(halves(dot3(right, block)))
        update = jnp.zeros((4 * cols, 128), f32)
        for g in range(4):
            rows = slice(g * cols, (g + 1) * cols)
            part = tuple(jnp.concatenate([x[n][rows] for x in tiles], 0) for n in range(2))
            update = update + dot3(part, outer[g])
        mid = update + read_rows(pair_ref, places)
        write_rows(mid_ref, places, mid)
        normed, _ = norm_parts(mid)
        logits = dot3(normed, sides)
        write_turned(edge_ref, t, jax.nn.sigmoid(logits[:, :256]) * logits[:, 256:])
        return carry

    lax.fori_loop(0, 8, step, 0)


def call_edges(left, right, outer, pair, sides, cols):
    chains = left.shape[0] // 32 * 4
    rows = pair.shape[0]
    return pl.pallas_call(
        functools.partial(edges_kernel, cols, chains),
        out_shape=(
            jax.ShapeDtypeStruct((rows, 128), f32),
            jax.ShapeDtypeStruct((256, 16, 128), f32),
        ),
        scratch_shapes=[pltpu.VMEM((4, left.shape[0], 256), f32)] * 2
        + [pltpu.VMEM((4 * cols, chains * 8), f32)],
        compiler_params=pltpu.CompilerParams(vmem_limit_bytes=56 * 2**20),
        name="edges",
    )(left, right, outer, pair, sides)


def join_tiles(chunks, mesh_rows, mesh_cols, out_ref):
    plain = chunks.reshape(mesh_rows * mesh_cols * 16, 128)
    rolled = pltpu.roll(plain, 64, 1)
    first = iota((16, 128), 1) < 64
    for r in range(mesh_rows):
        for t in range(mesh_cols // 2):
            even = slice((r * mesh_cols + 2 * t) * 16, (r * mesh_cols + 2 * t + 1) * 16)
            odd = slice((r * mesh_cols + 2 * t + 1) * 16, (r * mesh_cols + 2 * t + 2) * 16)
            lanes = slice(t * 128, (t + 1) * 128)
            out_ref[r * 32 : r * 32 + 16, lanes] = jnp.where(first, plain[even], rolled[odd])
            out_ref[r * 32 + 16 : r * 32 + 32, lanes] = jnp.where(first, rolled[even], plain[odd])


def cut_tiles(whole, mesh_rows, mesh_cols, store):
    first = iota((16, 128), 1) < 64
    for t in range(mesh_cols // 2):
        plain = whole[:, t * 128 : (t + 1) * 128]
        rolled = pltpu.roll(plain, 64, 1)
        for r in range(mesh_rows):
            low = slice(r * 32, r * 32 + 16)
            high = slice(r * 32 + 16, r * 32 + 32)
            store(r * mesh_cols + 2 * t, jnp.where(first, plain[low], rolled[high]))
            store(r * mesh_cols + 2 * t + 1, jnp.where(first, rolled[low], plain[high]))


def triangle_kernel(mesh_rows, mesh_cols, edge_ref, out_ref, left_ref, right_ref):
    join_tiles(edge_ref[:, 0, 0], mesh_rows, mesh_cols, left_ref)
    join_tiles(edge_ref[:, 1, 0], mesh_rows, mesh_cols, right_ref)

    def store(d, tile):
        out_ref[d, 0] = tile

    cut_tiles(dot3(left_ref[...], right_ref[...], NT), mesh_rows, mesh_cols, store)


def call_triangle(edges, mesh_rows, mesh_cols):
    devices, _, channels = edges.shape[:3]
    span = mesh_rows * 32
    return pl.pallas_call(
        functools.partial(triangle_kernel, mesh_rows, mesh_cols),
        grid=(channels,),
        in_specs=[pl.BlockSpec((devices, 2, 1, 16, 128), lambda n: (0, 0, n, 0, 0))],
        out_specs=pl.BlockSpec((devices, 1, 16, 128), lambda n: (0, n, 0, 0)),
        out_shape=jax.ShapeDtypeStruct((devices, channels, 16, 128), f32),
        scratch_shapes=[pltpu.VMEM((span, span), f32)] * 2,
        compiler_params=pltpu.CompilerParams(vmem_limit_bytes=56 * 2**20),
        name="triangle",
    )(edges)


def triangle_back_kernel(
    mesh_rows, mesh_cols, edge_ref, grad_ref, out_ref, left_ref, right_ref, whole_ref
):
    join_tiles(edge_ref[:, 0, 0], mesh_rows, mesh_cols, left_ref)
    join_tiles(edge_ref[:, 1, 0], mesh_rows, mesh_cols, right_ref)
    join_tiles(grad_ref[:, 0], mesh_rows, mesh_cols, whole_ref)

    def store(kind):
        def put(d, tile):
            out_ref[d, kind, 0] = tile

        return put

    whole = whole_ref[...]
    cut_tiles(dot3(whole, right_ref[...]), mesh_rows, mesh_cols, store(0))
    cut_tiles(dot3(jnp.transpose(whole), left_ref[...]), mesh_rows, mesh_cols, store(1))


def call_triangle_back(edges, grad, mesh_rows, mesh_cols):
    devices, _, channels = edges.shape[:3]
    span = mesh_rows * 32
    both = pl.BlockSpec((devices, 2, 1, 16, 128), lambda n: (0, 0, n, 0, 0))
    return pl.pallas_call(
        functools.partial(triangle_back_kernel, mesh_rows, mesh_cols),
        grid=(channels,),
        in_specs=[both, pl.BlockSpec((devices, 1, 16, 128), lambda n: (0, n, 0, 0))],
        out_specs=both,
        out_shape=jax.ShapeDtypeStruct(edges.shape, f32),
        scratch_shapes=[pltpu.VMEM((span, span), f32)] * 3,
        compiler_params=pltpu.CompilerParams(vmem_limit_bytes=56 * 2**20),
        name="triangle_back",
    )(edges, grad)


def four_rows(t, cols):
    return [
        pl.ds(pl.multiple_of((2 * t + u // 2 + 16 * (u % 2)) * cols, cols), cols) for u in range(4)
    ]


def read_rows(ref, places):
    return jnp.concatenate([ref[p, :] for p in places], 0)


def write_rows(ref, places, value):
    size = value.shape[0] // len(places)
    for u, p in enumerate(places):
        ref[p, :] = value[u * size : (u + 1) * size]


def read_turned(ref, t):
    parts = []
    for v in range(2):
        tile = ref[:, pl.ds(2 * t + v, 1), :]
        parts.append(jnp.transpose(tile.reshape(tile.shape[0], 128)))
    return jnp.concatenate(parts, 0)


def write_turned(ref, t, value):
    for v in range(2):
        turned = jnp.transpose(value[v * 128 : (v + 1) * 128])
        ref[:, pl.ds(2 * t + v, 1), :] = turned[:, None, :]


def finish_kernel(
    cols, tri_ref, mid_ref, grad_ref, gate_ref, proj_ref, out_ref, dtri_ref, dlogit_ref, dproj_ref
):
    gate_w = halves(gate_ref[...])
    proj_w = halves(proj_ref[...])
    dproj_ref[...] = jnp.zeros_like(dproj_ref)

    def step(t, carry):
        places = four_rows(t, cols)
        mid = read_rows(mid_ref, places)
        grad = read_rows(grad_ref, places)
        normed, _ = norm_parts(mid)
        tri, tri_inverse = norm_parts(read_turned(tri_ref, t))
        tri_halves = halves(tri)
        gate = jax.nn.sigmoid(dot3(normed, gate_w))
        value = dot3(tri_halves, proj_w)
        write_rows(out_ref, places, mid + gate * value)
        dvalue = halves(grad * gate)
        write_rows(dlogit_ref, places, grad * value * gate * (1.0 - gate))
        dproj_ref[...] += dot3(halves(jnp.transpose(tri)), dvalue)
        write_turned(dtri_ref, t, norm_back(tri, tri_inverse, dot3(dvalue, proj_w, NT)))
        return carry

    lax.fori_loop(0, 8, step, 0)


def call_finish(tri, mid, grad, gate, proj, cols):
    rows = mid.shape[0]
    return pl.pallas_call(
        functools.partial(finish_kernel, cols),
        out_shape=(
            jax.ShapeDtypeStruct((rows, 128), f32),
            jax.ShapeDtypeStruct((128, 16, 128), f32),
            jax.ShapeDtypeStruct((rows, 128), f32),
            jax.ShapeDtypeStruct((128, 128), f32),
        ),
        compiler_params=pltpu.CompilerParams(vmem_limit_bytes=56 * 2**20),
        name="finish",
    )(tri, mid, grad, gate, proj)


def edges_back_kernel(
    cols,
    chains,
    dedge_ref,
    mid_ref,
    grad_ref,
    dlogit_ref,
    sides_ref,
    left_ref,
    right_ref,
    outer_ref,
    dmid_ref,
    dsides_ref,
    douter_ref,
    dleft_ref,
    dright_ref,
    high_ref,
    low_ref,
    dslab_ref,
    whole_ref,
    dwhole_ref,
):
    groups = chains // 4
    spread, lift, same = spread_tables(chains)
    spread_left(left_ref, spread, high_ref, low_ref)
    join_right(right_ref, whole_ref)
    right = halves(whole_ref[...])
    right_turned = halves(jnp.transpose(whole_ref[...]))
    shape = (chains, chains * 8)
    chain = iota(shape, 1) >> 3
    drop = jnp.where(iota(shape, 0) == (chain & 3) * groups + (chain >> 2), 1.0, 0.0).astype(bf16)
    outer = outer_weights(outer_ref)
    sides = halves(sides_ref[...])
    dsides_ref[...] = jnp.zeros_like(dsides_ref)
    douter_ref[...] = jnp.zeros_like(douter_ref)
    dwhole_ref[...] = jnp.zeros_like(dwhole_ref)

    def step(t, carry):
        places = four_rows(t, cols)
        normed, inverse = norm_parts(read_rows(mid_ref, places))
        logits = dot3(normed, rounded(sides, (slice(None), slice(0, 512))))
        gate, value = jax.nn.sigmoid(logits[:, :256]), logits[:, 256:]
        dedge = read_turned(dedge_ref, t)
        dlogits = halves(
            jnp.concatenate(
                [
                    dedge * value * gate * (1.0 - gate),
                    dedge * gate,
                    read_rows(dlogit_ref, places),
                ],
                1,
            )
        )
        dsides_ref[...] += dot3(halves(jnp.transpose(normed)), dlogits)
        dmid = read_rows(grad_ref, places) + norm_back(normed, inverse, dot3(dlogits, sides, NT))
        write_rows(dmid_ref, places, dmid)
        dmid_turned = halves(jnp.transpose(dmid))
        dmid = halves(dmid)
        dprod = [halves(dot3(dmid, outer[g], NT)) for g in range(4)]
        prods = []
        for u in range(4):
            i = 2 * t + u // 2 + 16 * (u % 2)
            block = block_left(high_ref, low_ref, i, chains, lift, same)
            prods.append(halves(dot3(right, block)))
            rows = slice(u * cols, (u + 1) * cols)
            here = tuple(jnp.concatenate([dprod[g][n][rows] for g in range(4)], 0) for n in range(2))
            dwhole_ref[...] += dot3(here, block, NT)
            dblock = halves(jnp.where(same, dot3(right_turned, here), 0.0))
            dslab = one_pass(drop, dblock[0]) + one_pass(drop, dblock[1])
            place = pl.ds(pl.multiple_of(i * groups, groups), groups)
            dslab_ref[:, place, :] = dslab.reshape(4, groups, 256)
        for g in range(4):
            rows = slice(g * cols, (g + 1) * cols)
            part = tuple(jnp.concatenate([x[n][rows] for x in prods], 0) for n in range(2))
            douter_ref[:, g * 256 : (g + 1) * 256] += dot3(dmid_turned, part)
        return carry

    lax.fori_loop(0, 8, step, 0)
    dleft = jnp.zeros(dleft_ref.shape, f32)
    for s in range(4):
        high, low = halves(dslab_ref[s])
        dleft = dleft + (one_pass(high, spread[s], NT) + one_pass(low, spread[s], NT))
    dleft_ref[...] = dleft
    cut_right(dwhole_ref, dright_ref)


def call_edges_back(dedge, mid, grad, dlogit, sides, left, right, outer, cols):
    chains = left.shape[0] // 32 * 4
    rows = mid.shape[0]
    return pl.pallas_call(
        functools.partial(edges_back_kernel, cols, chains),
        out_shape=(
            jax.ShapeDtypeStruct((rows, 128), f32),
            jax.ShapeDtypeStruct((128, 640), f32),
            jax.ShapeDtypeStruct((128, 1024), f32),
            jax.ShapeDtypeStruct(left.shape, f32),
            jax.ShapeDtypeStruct(right.shape, f32),
        ),
        scratch_shapes=[pltpu.VMEM((4, left.shape[0], 256), f32)] * 3
        + [pltpu.VMEM((4 * cols, chains * 8), f32)] * 2,
        compiler_params=pltpu.CompilerParams(vmem_limit_bytes=56 * 2**20),
        name="edges_back",
    )(dedge, mid, grad, dlogit, sides, left, right, outer)


def pack_heads(y, store):
    lane = iota((1, 1, 128), 2) >> 5
    for tile in range(y.shape[1] // 128):
        part = y[:, tile * 128 : (tile + 1) * 128]
        turned = [part] + [pltpu.roll(part, 32 * n, 1) for n in range(1, 4)]
        turned = [x.reshape(-1, 4, 8, 128) for x in turned]
        for head in range(4):
            out = turned[-head % 4][:, 0]
            for chain in range(1, 4):
                out = jnp.where(lane == chain, turned[(chain - head) % 4][:, chain], out)
            store(tile * 4 + head, out)


def unpack_heads(load, heads):
    lane = iota((1, 1, 128), 2) >> 5
    tiles = []
    for tile in range(heads // 4):
        turned = []
        for head in range(4):
            part = load(tile * 4 + head)
            flat = part.reshape(-1, 128)
            turned.append(
                [part] + [pltpu.roll(flat, 32 * n, 1).reshape(part.shape) for n in range(1, 4)]
            )
        chains = []
        for chain in range(4):
            out = turned[0][-chain % 4]
            for head in range(1, 4):
                out = jnp.where(lane == head, turned[head][(head - chain) % 4], out)
            chains.append(out[:, None])
        tiles.append(jnp.concatenate(chains, 1).reshape(-1, 128))
    return jnp.concatenate(tiles, 1)


def head_lanes(tile, n):
    return jnp.where((iota((1, 128), 1) >> 5) == n, tile, 0.0)


def soft(scores, seen=None):
    if seen is not None:
        scores = jnp.where(seen, scores, -1e30)
    weights = jnp.exp(scores - jnp.max(scores, axis=-1, keepdims=True))
    if seen is not None:
        weights = jnp.where(seen, weights, 0.0)
    return weights * (1.0 / jnp.sum(weights, axis=-1, keepdims=True))


def soft_back(weights, grad):
    return weights * (grad - jnp.sum(weights * grad, axis=-1, keepdims=True))


def stripe_seen(present_ref):
    tokens = present_ref.shape[1]
    shape = (tokens, tokens)
    same = (iota(shape, 0) & 7) == (iota(shape, 1) & 7)
    return same & (present_ref[...] > 0.0)


def column_attention(q, k, v, seen):
    weights, tiles = [], []
    for tile in range(q.shape[1] // 128):
        lanes = slice(tile * 128, (tile + 1) * 128)
        keys, values = halves(k[:, lanes]), halves(v[:, lanes])
        blend = 0.0
        for n in range(4):
            weights.append(soft(dot3(head_lanes(q[:, lanes], n), keys, NT), seen))
            blend = blend + head_lanes(dot3(weights[-1], values), n)
        tiles.append(blend)
    return weights, jnp.concatenate(tiles, 1)


def columns_kernel(
    scale, x_ref, present_ref, q_ref, k_ref, v_ref, o_ref, q2_ref, k2_ref, v2_ref, out_ref, qkv_ref
):
    x = x_ref[...]
    normed, _ = norm_parts(x)
    normed = halves(normed)
    q, k, v = (dot3(normed, halves(w[...])) for w in (q_ref, k_ref, v_ref))
    _, blend = column_attention(q * scale, k, v, stripe_seen(present_ref))
    out = x + dot3(blend, halves(o_ref[...]))
    out_ref[...] = out
    normed, _ = norm_parts(out)
    normed = halves(normed)
    groups = qkv_ref.shape[0] // 8

    def store(kind):
        def put(head, value):
            place = slice(head * groups, (head + 1) * groups)
            qkv_ref[place, kind] = value.reshape(groups, -1, 8, 128)

        return put

    for kind, w in enumerate((q2_ref, k2_ref, v2_ref)):
        pack_heads(dot3(normed, halves(w[...])), store(kind))


def params():
    return pltpu.CompilerParams(vmem_limit_bytes=56 * 2**20)


def call_columns(x, present, weights, devices, group_chains, scale):
    return pl.pallas_call(
        functools.partial(columns_kernel, scale),
        out_shape=(
            jax.ShapeDtypeStruct(x.shape, f32),
            jax.ShapeDtypeStruct((devices, 3, group_chains // 4, 8, 128), f32),
        ),
        compiler_params=params(),
        name="columns",
    )(x, present, *weights)


def rows_kernel(mesh_rows, mesh_cols, scale, qkv_ref, bias_ref, out_ref, whole_ref):
    join_tiles(bias_ref[...], mesh_rows, mesh_cols, whole_ref)
    bias = whole_ref[...]
    for half in range(qkv_ref.shape[2]):
        q, k, v = (qkv_ref[:, kind, half].reshape(-1, 128) for kind in range(3))
        k, v, q = halves(k), halves(v), q * scale
        blend = 0.0
        for n in range(4):
            weights = soft(dot3(head_lanes(q, n), k, NT) + bias)
            blend = blend + head_lanes(dot3(weights, v), n)
        out_ref[:, half] = blend.reshape(-1, 8, 128)


def call_rows(qkv, bias, mesh_rows, mesh_cols, scale):
    devices, _, parts = qkv.shape[:3]
    span = mesh_rows * 32
    return pl.pallas_call(
        functools.partial(rows_kernel, mesh_rows, mesh_cols, scale),
        out_shape=jax.ShapeDtypeStruct((devices, parts, 8, 128), f32),
        scratch_shapes=[pltpu.VMEM((span, span), f32)],
        compiler_params=params(),
        name="rows",
    )(qkv, bias)


def load_heads(ref, kind=None):
    def load(head):
        groups = ref.shape[0] // 8
        place = slice(head * groups, (head + 1) * groups)
        part = ref[place] if kind is None else ref[place, kind]
        return part.reshape(-1, 8, 128)

    return load


def rows_out_kernel(blend_ref, mid_ref, share_ref, o_ref, sides_ref, out_ref, left_ref, right_ref):
    blend = unpack_heads(load_heads(blend_ref), 8)
    out = mid_ref[...] + dot3(blend, halves(o_ref[...]))
    out_ref[...] = out
    normed, _ = norm_parts(out)
    wide = dot3(normed, halves(sides_ref[...]))
    left = (wide[:, :128] * share_ref[...]).reshape(-1, 4, 8, 128)
    lane = iota((1, 1, 128), 2)
    packed = left[:, 0]
    for chain in range(1, 4):
        packed = jnp.where((lane >> 5) == chain, left[:, chain], packed)
    for n in range(packed.shape[0]):
        left_ref[:, n, :] = packed[n]
    for g in range(4):
        right = wide[:, (g + 1) * 128 : (g + 2) * 128].reshape(-1, 16, 8, 128)
        packed = right[:, 0]
        for chain in range(1, 16):
            packed = jnp.where((lane >> 3) == chain, right[:, chain], packed)
        right_ref[g] = packed


def call_rows_out(blend, mid, share, weight, sides):
    chains = mid.shape[0] // 8
    return pl.pallas_call(
        rows_out_kernel,
        out_shape=(
            jax.ShapeDtypeStruct(mid.shape, f32),
            jax.ShapeDtypeStruct((8, chains // 4, 128), f32),
            jax.ShapeDtypeStruct((4, chains // 16, 8, 128), f32),
        ),
        compiler_params=params(),
        name="rows_out",
    )(blend, mid, share, weight, sides)


def rows_out_back_kernel(
    dleft_ref,
    dright_ref,
    grad_ref,
    out_ref,
    blend_ref,
    share_ref,
    o_ref,
    sides_ref,
    dout_ref,
    dblend_ref,
    sum_ref,
):
    lane = iota((1, 1, 128), 2)
    chains = grad_ref.shape[0] // 8
    dleft = jnp.sum(dleft_ref[...], axis=0)
    dleft = jnp.concatenate([dleft[:, n][None] for n in range(chains // 4)], 0)
    wide = [jnp.where((lane >> 5) == n, dleft, 0.0)[:, None] for n in range(4)]
    wide = [jnp.concatenate(wide, 1).reshape(-1, 128) * share_ref[...]]
    dright = dright_ref[...]
    for g in range(4):
        part = [jnp.where((lane >> 3) == n, dright[g], 0.0)[:, None] for n in range(16)]
        wide.append(jnp.concatenate(part, 1).reshape(-1, 128))
    wide = halves(jnp.concatenate(wide, 1))
    normed, inverse = norm_parts(out_ref[...])
    dsides = halves(dot3(halves(jnp.transpose(normed)), wide))
    shape = (640, 128)
    place, spot = iota(shape, 0) - 128, iota(shape, 1)
    target = jnp.where(place < 0, place & 31, 32 + ((place >> 7) << 3) + (place & 7))
    fold = jnp.where(target == spot, 1.0, 0.0).astype(bf16)
    sum_ref[512:768, :] = one_pass(dsides[0], fold) + one_pass(dsides[1], fold)
    dout = grad_ref[...] + norm_back(normed, inverse, dot3(wide, halves(sides_ref[...]), NT))
    dout_ref[...] = dout
    dout = halves(dout)
    groups = dblend_ref.shape[0] // 8

    def store(head, value):
        dblend_ref[head * groups : (head + 1) * groups] = value.reshape(groups, -1, 8, 128)

    pack_heads(dot3(dout, halves(o_ref[...]), NT), store)
    blend = unpack_heads(load_heads(blend_ref), 8)
    write_tall(sum_ref, 0, dot3(halves(jnp.transpose(blend)), dout))


def call_rows_out_back(dleft, dright, grad, out, blend, share, weight, sides):
    return pl.pallas_call(
        rows_out_back_kernel,
        out_shape=(
            jax.ShapeDtypeStruct(grad.shape, f32),
            jax.ShapeDtypeStruct(blend.shape, f32),
            jax.ShapeDtypeStruct((768, 128), f32),
        ),
        compiler_params=params(),
        name="rows_out_back",
    )(dleft, dright, grad, out, blend, share, weight, sides)


def rows_back_kernel(
    mesh_rows, mesh_cols, scale, qkv_ref, bias_ref, dblend_ref, dqkv_ref, dbias_ref, whole_ref
):
    join_tiles(bias_ref[...], mesh_rows, mesh_cols, whole_ref)
    bias = whole_ref[...]
    dbias = 0.0
    for half in range(qkv_ref.shape[2]):
        q, k, v = (qkv_ref[:, kind, half].reshape(-1, 128) for kind in range(3))
        k, v, q = halves(k), halves(v), q * scale
        grad = dblend_ref[:, half].reshape(-1, 128)
        dq, dk, dv = 0.0, 0.0, 0.0
        for n in range(4):
            query, dblend = halves(head_lanes(q, n)), halves(head_lanes(grad, n))
            weights = soft(dot3(query, k, NT) + bias)
            dv = dv + dot3(halves(jnp.transpose(weights)), dblend)
            dscores = soft_back(weights, dot3(dblend, v, NT))
            dbias = dbias + dscores
            dk = dk + dot3(halves(jnp.transpose(dscores)), query)
            dq = dq + head_lanes(dot3(dscores, k), n)
        for kind, value in enumerate((dq * scale, dk, dv)):
            dqkv_ref[:, kind, half] = value.reshape(-1, 8, 128)

    def store(d, tile):
        dbias_ref[d] = tile

    cut_tiles(dbias, mesh_rows, mesh_cols, store)


def call_rows_back(qkv, bias, dblend, mesh_rows, mesh_cols, scale):
    span = mesh_rows * 32
    return pl.pallas_call(
        functools.partial(rows_back_kernel, mesh_rows, mesh_cols, scale),
        out_shape=(
            jax.ShapeDtypeStruct(qkv.shape, f32),
            jax.ShapeDtypeStruct(bias.shape, f32),
        ),
        scratch_shapes=[pltpu.VMEM((span, span), f32)],
        compiler_params=params(),
        name="rows_back",
    )(qkv, bias, dblend)


def write_tall(ref, n, value):
    height, tiles = value.shape[0], value.shape[1] // 128
    for t in range(tiles):
        start = (n * tiles + t) * height
        ref[start : start + height, :] = value[:, t * 128 : (t + 1) * 128]


def projections_back(normed, inverse, grads, weight_refs, sum_ref):
    turned = halves(jnp.transpose(normed))
    dnormed = 0.0
    for n, (grad, w) in enumerate(zip(grads, weight_refs)):
        grad = halves(grad)
        write_tall(sum_ref, n, dot3(turned, grad))
        dnormed = dnormed + dot3(grad, halves(w[...]), NT)
    return norm_back(normed, inverse, dnormed)


def rows_in_back_kernel(
    dqkv_ref, mid_ref, grad_ref, q_ref, k_ref, v_ref, dmid_ref, sum_ref
):
    grads = [unpack_heads(load_heads(dqkv_ref, kind), 8) for kind in range(3)]
    normed, inverse = norm_parts(mid_ref[...])
    dmid_ref[...] = grad_ref[...] + projections_back(
        normed, inverse, grads, (q_ref, k_ref, v_ref), sum_ref
    )


def call_rows_in_back(dqkv, mid, grad, weights):
    return pl.pallas_call(
        rows_in_back_kernel,
        out_shape=(
            jax.ShapeDtypeStruct(mid.shape, f32),
            jax.ShapeDtypeStruct((sum(w.size for w in weights) // 128, 128), f32),
        ),
        compiler_params=params(),
        name="rows_in_back",
    )(dqkv, mid, grad, *weights)


def columns_back_kernel(
    scale,
    x_ref,
    present_ref,
    grad_ref,
    q_ref,
    k_ref,
    v_ref,
    o_ref,
    dx_ref,
    sum_ref,
):
    normed, inverse = norm_parts(x_ref[...])
    normed_halves = halves(normed)
    q, k, v = (dot3(normed_halves, halves(w[...])) for w in (q_ref, k_ref, v_ref))
    q = q * scale
    weights, blend = column_attention(q, k, v, stripe_seen(present_ref))
    grad = grad_ref[...]
    grad_halves = halves(grad)
    write_tall(sum_ref, 3, dot3(halves(jnp.transpose(blend)), grad_halves))
    dblend = dot3(grad_halves, halves(o_ref[...]), NT)
    tiles = [[], [], []]
    for tile in range(q.shape[1] // 128):
        lanes = slice(tile * 128, (tile + 1) * 128)
        keys, values = halves(k[:, lanes]), halves(v[:, lanes])
        dq, dk, dv = 0.0, 0.0, 0.0
        for n in range(4):
            query = halves(head_lanes(q[:, lanes], n))
            dhead = halves(head_lanes(dblend[:, lanes], n))
            share = weights[tile * 4 + n]
            dv = dv + dot3(halves(jnp.transpose(share)), dhead)
            dscores = soft_back(share, dot3(dhead, values, NT))
            dk = dk + dot3(halves(jnp.transpose(dscores)), query)
            dq = dq + head_lanes(dot3(dscores, keys), n)
        for kind, value in enumerate((dq * scale, dk, dv)):
            tiles[kind].append(value)
    grads = [jnp.concatenate(t, 1) for t in tiles]
    dx_ref[...] = grad + projections_back(
        normed, inverse, grads, (q_ref, k_ref, v_ref), sum_ref
    )


def call_columns_back(x, present, grad, weights, scale):
    return pl.pallas_call(
        functools.partial(columns_back_kernel, scale),
        out_shape=(
            jax.ShapeDtypeStruct(x.shape, f32),
            jax.ShapeDtypeStruct((sum(w.size for w in weights) // 128, 128), f32),
        ),
        compiler_params=params(),
        name="columns_back",
    )(x, present, grad, *weights)


def bias_kernel(cols, pair_ref, weight_ref, out_ref):
    weight = halves(weight_ref[...])

    def step(t, carry):
        rows = halves(read_rows(pair_ref, four_rows(t, cols)))
        heads = dot3(weight, rows, NT)
        for v in range(2):
            tile = heads[:, v * 128 : (v + 1) * 128][:, None, :]
            for g in range(out_ref.shape[1]):
                out_ref[:, g, pl.ds(2 * t + v, 1), :] = tile
        return carry

    lax.fori_loop(0, 8, step, 0)


def call_bias(pair, weight, copies, cols):
    return pl.pallas_call(
        functools.partial(bias_kernel, cols),
        out_shape=jax.ShapeDtypeStruct((weight.shape[0], copies, 16, 128), f32),
        compiler_params=params(),
        name="bias",
    )(pair, weight)


def bias_back_kernel(cols, dbias_ref, pair_ref, dmid_ref, weight_ref, out_ref, dweight_ref, sum_ref):
    weight = halves(weight_ref[...])
    sum_ref[...] = jnp.sum(dbias_ref[...], axis=1)
    dweight_ref[...] = jnp.zeros_like(dweight_ref)

    def step(t, carry):
        places = four_rows(t, cols)
        heads = [sum_ref[:, pl.ds(2 * t + v, 1), :].reshape(-1, 128) for v in range(2)]
        heads = jnp.concatenate(heads, 1)
        dweight_ref[...] += dot3(heads, read_rows(pair_ref, places))
        dpair = dot3(jnp.transpose(heads), weight)
        write_rows(out_ref, places, read_rows(dmid_ref, places) + dpair)
        return carry

    lax.fori_loop(0, 8, step, 0)


def call_bias_back(dbias, pair, dmid, weight, cols):
    return pl.pallas_call(
        functools.partial(bias_back_kernel, cols),
        out_shape=(
            jax.ShapeDtypeStruct(pair.shape, f32),
            jax.ShapeDtypeStruct(weight.shape, f32),
        ),
        scratch_shapes=[pltpu.VMEM((dbias.shape[0], 16, 128), f32)],
        compiler_params=params(),
        name="bias_back",
    )(dbias, pair, dmid, weight)


precise = lax.Precision.HIGH
everyone = ("half", "core", "col")
row = ("half", "core")
chips = ("half", "col")


def affine_map(tensor, weight):
    return jnp.einsum("...a,ab->...b", tensor, weight, precision=precise)


def exchange(chunks, axis):
    shape = chunks.shape
    flat = chunks.reshape(shape[0], -1, 128)
    return lax.all_to_all(flat, axis, 0, 0, tiled=True).reshape(shape)


def collect(block, axis, count):
    return exchange(jnp.broadcast_to(block[None], (count,) + block.shape), axis)


def tall(weight):
    return jnp.concatenate([weight[:, :128], weight[:, 128:]], 0)


def wide(tall_weight):
    return jnp.concatenate([tall_weight[:256], tall_weight[256:]], 1)


def cut(whole, count):
    size = whole.shape[0] // count
    return [whole[n * size : (n + 1) * size] for n in range(count)]


class Layout:
    def __init__(self, mesh_rows, mesh_cols, pair, chains, heads, head_width):
        self.mesh_rows, self.mesh_cols = mesh_rows, mesh_cols
        self.devices = mesh_rows * mesh_cols
        self.rows_here, self.cols_here, self.pair_width = pair
        self.span = self.rows_here * mesh_rows
        self.slim = self.span // self.devices
        self.chains, self.heads, self.head_width = chains, heads, head_width
        self.chain_groups = self.devices // heads
        self.group_chains = chains // self.chain_groups
        self.channels_here = self.pair_width // self.devices
        self.scale = head_width ** (-0.5)
        self.turn = [
            (g, (g % mesh_rows) * mesh_cols + g // mesh_rows) for g in range(self.devices)
        ]
        self.turn_back = [(b, a) for a, b in self.turn]

    def to_slim(self, x):
        return lax.all_to_all(x, "col", 1, 0, tiled=True)

    def from_slim(self, x):
        return lax.all_to_all(x, "col", 0, 1, tiled=True)


def msa_plain(size, alignment_features, residue_couplings, present, weights):
    chains, slim, heads, head_width = size.chains, size.slim, size.heads, size.head_width
    devices, groups, group_chains = size.devices, size.chain_groups, size.group_chains
    rows_here, cols_here, span = size.rows_here, size.cols_here, size.span
    mesh_rows, mesh_cols = size.mesh_rows, size.mesh_cols
    bias = jnp.transpose(affine_map(residue_couplings, weights[7]), (2, 0, 1))
    bias = jnp.broadcast_to(bias[:, None], (heads, groups, rows_here, cols_here))
    bias = exchange(bias.reshape(devices, rows_here, cols_here), everyone)
    bias = bias.reshape(mesh_rows, mesh_cols, rows_here, cols_here)
    bias = jnp.transpose(bias, (0, 2, 1, 3)).reshape(span, span)

    stripe = size.to_slim(alignment_features)
    normed, _ = norm_parts(stripe)
    col_q, col_k, col_v = (
        affine_map(normed, w).reshape(chains, slim, heads, head_width) for w in weights[:3]
    )
    scores = jnp.einsum("sihd,tihd->ihst", col_q, col_k, precision=precise) * size.scale
    scores = jnp.where(present[None, None, None, :] > 0, scores, -1000000000.0)
    blend = jnp.einsum(
        "ihst,tihd->sihd", jax.nn.softmax(scores, axis=-1), col_v, precision=precise
    )
    msa_col = stripe + affine_map(blend.reshape(chains, slim, heads * head_width), weights[3])

    normed, _ = norm_parts(msa_col)
    qkv = jnp.stack([affine_map(normed, w) for w in weights[4:7]])
    qkv = qkv.reshape(3, groups, group_chains, slim, heads, head_width)
    qkv = jnp.transpose(qkv, (4, 1, 0, 2, 3, 5))
    qkv = exchange(qkv.reshape(devices, 3, group_chains, slim, head_width), everyone)
    qkv = jnp.transpose(qkv, (1, 2, 0, 3, 4)).reshape(3, group_chains, span, head_width)
    scores = jnp.einsum("sid,sjd->sij", qkv[0], qkv[1], precision=precise) * size.scale
    shares = jax.nn.softmax(scores + bias[None], axis=-1)
    blend = jnp.einsum("sij,sjd->sid", shares, qkv[2], precision=precise)
    blend = blend.reshape(group_chains, devices, slim, head_width)
    blend = exchange(jnp.transpose(blend, (1, 0, 2, 3)), everyone)
    blend = blend.reshape(heads, chains, slim, head_width)
    blend = jnp.transpose(blend, (1, 2, 0, 3)).reshape(chains, slim, heads * head_width)
    msa_out = msa_col + affine_map(blend, weights[8])

    normed, _ = norm_parts(msa_out)
    left = affine_map(normed, weights[9]) * (present / jnp.sum(present))[:, None, None]
    left = jnp.transpose(left.reshape(chains // 4, 4, slim, 32), (2, 0, 1, 3))
    left = collect(left.reshape(slim, chains // 4, 128), "col", mesh_cols).reshape(-1, 128)
    right = affine_map(normed, weights[10]).reshape(chains // 16, 16, slim, 4, 8)
    right = jnp.transpose(right, (3, 0, 2, 1, 4)).reshape(-1, 128)
    right = collect(lax.ppermute(right, everyone, size.turn), row, mesh_rows)
    right = right.reshape(mesh_rows, 4, chains // 16, slim, 128)
    right = jnp.transpose(right, (1, 0, 3, 2, 4)).reshape(4, cols_here // 8, 8, chains // 16, 128)
    return size.from_slim(msa_out), left, jnp.transpose(right, (1, 0, 3, 2, 4))


def msa_forward(size, alignment_features, residue_couplings, present, weights):
    chains, slim, devices = size.chains, size.slim, size.devices
    mesh_rows, mesh_cols = size.mesh_rows, size.mesh_cols
    pair_flat = residue_couplings.reshape(-1, size.pair_width)
    tokens = chains * slim
    seen = jnp.repeat(present, slim)[None]
    share = jnp.repeat(present / jnp.sum(present), slim)[:, None]
    sides = jnp.concatenate(
        [
            jnp.tile(weights[9], (1, 4)),
            jnp.broadcast_to(weights[10].reshape(-1, 4, 1, 8), (256, 4, 16, 8)).reshape(256, 512),
        ],
        1,
    )
    offset = jnp.transpose(weights[7])
    stripe = size.to_slim(alignment_features).reshape(tokens, -1)
    bias = call_bias(pair_flat, offset, size.chain_groups, size.cols_here)
    bias = exchange(bias.reshape(devices, 16, 128), everyone)
    msa_col, qkv = call_columns(
        stripe, seen, weights[:7], devices, size.group_chains, size.scale
    )
    qkv = exchange(qkv, everyone)
    blend = call_rows(qkv, bias, mesh_rows, mesh_cols, size.scale)
    blend = exchange(blend, everyone)
    msa_out, left, right = call_rows_out(blend, msa_col, share, weights[8], sides)
    right = collect(lax.ppermute(right, everyone, size.turn), row, mesh_rows)
    left = collect(left, "col", mesh_cols).reshape(-1, 128)

    def back(grad_out, d_left, d_right, d_mid):
        grad = size.to_slim(grad_out).reshape(tokens, -1)
        d_right = exchange(d_right, row).sum(0)
        d_right = lax.ppermute(d_right, everyone, size.turn_back)
        d_left = exchange(d_left.reshape(mesh_cols, slim, -1, 128), "col")
        d_out, d_blend, first_sums = call_rows_out_back(
            d_left, d_right, grad, msa_out, blend, share, weights[8], sides
        )
        d_blend = exchange(d_blend, everyone)
        d_qkv, d_bias = call_rows_back(qkv, bias, d_blend, mesh_rows, mesh_cols, size.scale)
        d_qkv = exchange(d_qkv, everyone)
        d_bias = exchange(d_bias, everyone)
        d_col, second_sums = call_rows_in_back(d_qkv, msa_col, d_out, weights[4:7])
        d_stripe, col_sums = call_columns_back(stripe, seen, d_col, weights[:4], size.scale)
        d_pair, d_offset = call_bias_back(
            d_bias.reshape(size.heads, size.chain_groups, 16, 128),
            pair_flat,
            d_mid,
            offset,
            size.cols_here,
        )
        d_features = size.from_slim(d_stripe.reshape(chains, slim, -1))
        row_sums = jnp.concatenate([second_sums, first_sums, d_offset], 0)
        return d_features, d_pair, col_sums, row_sums

    return (size.from_slim(msa_out.reshape(chains, slim, -1)), left, right), back


def msa_plain_forward(size, alignment_features, residue_couplings, present, weights):
    outputs, pull = jax.vjp(
        lambda x, y, w: msa_plain(size, x, y, present, w),
        alignment_features,
        residue_couplings,
        weights,
    )

    def back(grad_out, d_left, d_right, d_mid):
        d_features, d_pair, d_weights = pull((grad_out, d_left, d_right))
        d_pair = d_pair.reshape(-1, size.pair_width) + d_mid
        col_sums = jnp.concatenate([tall(w) for w in d_weights[:4]], 0)
        thin = jnp.pad(jnp.concatenate(d_weights[9:11], 1), ((0, 0), (0, 64)))
        row_sums = [tall(d_weights[n]) for n in (4, 5, 6, 8)]
        row_sums = jnp.concatenate(row_sums + [thin, jnp.transpose(d_weights[7])], 0)
        return d_features, d_pair, col_sums, row_sums

    return outputs, back


def per_device(mesh_rows, mesh_cols, *arguments):
    (
        alignment_features,
        residue_couplings,
        chain_indicator,
        alignment_result_adjoint,
        coupling_result_adjoint,
        *weights,
    ) = arguments
    present = chain_indicator.astype(jnp.float32)
    heads = weights[7].shape[1]
    size = Layout(
        mesh_rows,
        mesh_cols,
        residue_couplings.shape,
        present.shape[0],
        heads,
        weights[4].shape[1] // heads,
    )
    devices, channels_here = size.devices, size.channels_here
    cols_here, pair_width = size.cols_here, size.pair_width
    (
        tensor_result_matrix,
        source_side_matrix,
        source_side_switch,
        target_side_matrix,
        target_side_switch,
        trilateral_result_switch,
        trilateral_result_matrix,
    ) = weights[11:]

    def interleave(left, right):
        shape = (pair_width, devices, channels_here)
        both = jnp.stack([left.reshape(shape), right.reshape(shape)], 2)
        return both.reshape(pair_width, 2 * pair_width)

    def separate(both):
        both = both.reshape(pair_width, devices, 2, channels_here)
        return (
            both[:, :, 0].reshape(pair_width, pair_width),
            both[:, :, 1].reshape(pair_width, pair_width),
        )

    core = lax.axis_index("core")
    swap = [(0, 1), (1, 0)]

    def scatter_sum(parts):
        pad = -parts.shape[0] % (devices * 8)
        if pad:
            parts = jnp.pad(parts, ((0, pad), (0, 0)))
        both = parts.reshape(2, -1, 128)
        mine = lax.dynamic_index_in_dim(both, core, 0, False)
        other = lax.dynamic_index_in_dim(both, 1 - core, 0, False)
        mine = mine + lax.ppermute(other, "core", swap)
        return exchange(mine.reshape(devices // 2, -1, 128), chips).sum(0)

    def gather_sum(piece):
        mine = collect(piece, chips, devices // 2).reshape(-1, 128)
        other = lax.ppermute(mine, "core", swap)
        first = core == 0
        return jnp.concatenate(
            [jnp.where(first, mine, other), jnp.where(first, other, mine)], axis=0
        )

    sides = jnp.concatenate(
        [
            interleave(source_side_switch, target_side_switch),
            interleave(source_side_matrix, target_side_matrix),
            trilateral_result_switch,
        ],
        1,
    )
    forward = msa_forward if size.slim == 8 else msa_plain_forward
    (msa_out, left_rows, right_rows), msa_back = forward(
        size, alignment_features, residue_couplings, present, tuple(weights[:11])
    )
    pair_flat = residue_couplings.reshape(-1, pair_width)
    grad_flat = coupling_result_adjoint.reshape(-1, pair_width)
    pair_mid, edges = call_edges(
        left_rows, right_rows, tensor_result_matrix, pair_flat, sides[:, : 4 * pair_width], cols_here
    )
    edges = exchange(edges.reshape(devices, 2, channels_here, 16, 128), everyone)
    triangle = exchange(call_triangle(edges, mesh_rows, mesh_cols), everyone)
    pair_out, d_triangle, d_logit, g_tri_out = call_finish(
        triangle.reshape(pair_width, 16, 128),
        pair_mid,
        grad_flat,
        trilateral_result_switch,
        trilateral_result_matrix,
        cols_here,
    )
    d_triangle = exchange(d_triangle.reshape(devices, channels_here, 16, 128), everyone)
    d_edges = exchange(call_triangle_back(edges, d_triangle, mesh_rows, mesh_cols), everyone)
    d_mid, d_sides, d_outer, d_left, d_right = call_edges_back(
        d_edges.reshape(2 * pair_width, 16, 128),
        pair_mid,
        grad_flat,
        d_logit,
        sides,
        left_rows,
        right_rows,
        tensor_result_matrix,
        cols_here,
    )
    parts = [g_tri_out] + [d_sides[:, n : n + 128] for n in range(0, 640, 128)]
    parts += [d_outer[:, n : n + 128] for n in range(0, 1024, 128)]
    pair_sums = scatter_sum(jnp.concatenate(parts, 0))
    alignment_adjoint, coupling_adjoint, col_sums, row_sums = msa_back(
        alignment_result_adjoint, d_left, d_right, d_mid
    )
    summed = cut(gather_sum(pair_sums)[: 14 * 128], 14)
    g_tri_out, g_tri_gate = summed[0], summed[5]
    g_left_gate, g_right_gate = separate(jnp.concatenate(summed[1:3], 1))
    g_left, g_right = separate(jnp.concatenate(summed[3:5], 1))
    g_outer = jnp.concatenate(summed[6:], 1).reshape(pair_width, 4, 32, 8)
    g_outer = jnp.transpose(g_outer, (2, 1, 3, 0)).reshape(1024, pair_width)

    col_piece, row_piece = scatter_sum(col_sums), scatter_sum(row_sums)
    col_rows = col_piece.shape[0]
    both = collect(jnp.concatenate([col_piece, row_piece], 0), chips, devices // 2)
    other = lax.ppermute(both, "core", swap)
    first = core == 0
    both = jnp.stack([jnp.where(first, both, other), jnp.where(first, other, both)])
    col_sums = both[:, :, :col_rows].reshape(-1, 128)
    row_sums = both[:, :, col_rows:].reshape(-1, 128)
    g_cols = [wide(w) for w in cut(col_sums, 4)]
    g_rows = [wide(w) for w in cut(row_sums[:2048], 4)]
    thin = row_sums[2048:2304]
    return (
        msa_out,
        pair_out.reshape(residue_couplings.shape),
        alignment_adjoint,
        coupling_adjoint.reshape(residue_couplings.shape),
        *g_cols,
        *g_rows[:3],
        jnp.transpose(row_sums[2304 : 2304 + heads]),
        g_rows[3],
        thin[:, :32],
        thin[:, 32:64],
        g_outer,
        g_left,
        g_left_gate,
        g_right,
        g_right_gate,
        g_tri_gate,
        g_tri_out,
    )


def solution(mesh):
    mesh_rows, mesh_cols = mesh.shape["row"], mesh.shape["col"]

    def local(*arguments):
        return per_device(mesh_rows, mesh_cols, *arguments)

    split = jax.sharding.Mesh(
        mesh.devices.reshape(mesh_rows // 2, 2, mesh_cols), ("half", "core", "col")
    )
    whole = P()
    msa = P("col", row, None)
    pair = P(row, "col", None)
    return jax.shard_map(
        local,
        mesh=split,
        in_specs=(msa, pair, whole, msa, pair) + (whole,) * 18,
        out_specs=(msa, pair, msa, pair) + (whole,) * 18,
        check_vma=False,
    )
```

```python
import functools

import jax
import jax.numpy as jnp
from jax import lax
from jax.experimental import pallas as pl
from jax.experimental.pallas import tpu as pltpu
from jax.sharding import PartitionSpec as P

bf16, f32 = jnp.bfloat16, jnp.float32
NN = ((1,), (0,))
NT = ((1,), (1,))
TN = ((0,), (0,))


def one_pass(a, b, dims=NN):
    return lax.dot_general(a, b, (dims, ((), ())), preferred_element_type=f32)


def halves(x):
    high = x.astype(bf16)
    return high, (x - high.astype(f32)).astype(bf16)


def dot3(a, b, dims=NN):
    a_high, a_low = a if isinstance(a, tuple) else halves(a)
    b_high, b_low = b if isinstance(b, tuple) else halves(b)
    return one_pass(a_high, b_high, dims) + (
        one_pass(a_high, b_low, dims) + one_pass(a_low, b_high, dims)
    )


def rounded(pair, rows):
    return pair[0][rows], pair[1][rows]


def iota(shape, dim):
    return lax.broadcasted_iota(jnp.int32, shape, dim)


def norm_parts(x):
    centered = x - jnp.mean(x, axis=-1, keepdims=True)
    inverse = lax.rsqrt(jnp.mean(centered * centered, axis=-1, keepdims=True) + 1e-05)
    return centered * inverse, inverse


def norm_back(normed, inverse, grad):
    return inverse * (
        grad
        - jnp.mean(grad, axis=-1, keepdims=True)
        - normed * jnp.mean(grad * normed, axis=-1, keepdims=True)
    )


def stacked3(a, b, dims=NN):
    a_high, a_low = a if isinstance(a, tuple) else halves(a)
    b_high, b_low = b if isinstance(b, tuple) else halves(b)
    return one_pass(
        jnp.concatenate([a_high, a_low, a_high], dims[0][0]),
        jnp.concatenate([b_high, b_high, b_low], dims[1][0]),
        dims,
    )


def row_of(t, u):
    return 2 * t + u // 2 + 16 * (u % 2)


def same_slot(chains):
    shape = (chains * 8, 256)
    return (iota(shape, 0) & 7) == (iota(shape, 1) & 7)


def blocks_kernel(chains, first_ref, *refs):
    *part_refs, out_ref, left_ref = refs
    groups, count = chains // 4, len(part_refs)
    size = part_refs[0].shape[0]
    t = pl.program_id(0)

    @pl.when(t == 0)
    def _():
        for n, ref in enumerate(part_refs):
            place = lax.rem(first_ref[0] + count - n, count) * size
            left_ref[pl.ds(pl.multiple_of(place, 8), size), :] = ref[...]

    shape = (chains * 8, chains)
    chain = iota(shape, 0) >> 3
    lift = jnp.where(iota(shape, 1) == (chain & 3) * groups + (chain >> 2), 1.0, 0.0).astype(bf16)
    same = same_slot(chains)
    rows = [
        left_ref[pl.ds(pl.multiple_of(row_of(t, u) * groups, groups), groups), :] for u in range(4)
    ]
    rows = jnp.concatenate(halves(jnp.concatenate(rows, 0)), 0)
    shape = (128, 256)
    slabs = []
    for n in range(4):
        spread = ((iota(shape, 0) >> 5) == n) & ((iota(shape, 0) & 31) == (iota(shape, 1) >> 3))
        slabs.append(one_pass(rows, jnp.where(spread, 1.0, 0.0).astype(bf16)))
    for part in range(2):
        for u in range(4):
            place = slice((part * 4 + u) * groups, (part * 4 + u + 1) * groups)
            slab = jnp.concatenate([x[place] for x in slabs], 0).astype(bf16)
            out_ref[0, u, part] = jnp.where(same, one_pass(lift, slab), 0.0).astype(bf16)


def call_blocks(first, parts):
    rows = sum(part.shape[0] for part in parts)
    chains = rows // 32 * 4
    shape = (8, 4, 2, chains * 8, 256)
    return pl.pallas_call(
        functools.partial(blocks_kernel, chains),
        grid=(8,),
        in_specs=[pl.BlockSpec(memory_space=pltpu.SMEM)] + [full(part) for part in parts],
        out_specs=step_block(shape),
        out_shape=jax.ShapeDtypeStruct(shape, bf16),
        scratch_shapes=[pltpu.VMEM((rows, 128), f32)],
        compiler_params=params(),
        name="blocks",
    )(first, *parts)


def join_right(ref, out_ref):
    cols = ref.shape[0] * 8
    for g in range(4):
        for n in range(ref.shape[2]):
            out_ref[g * cols : (g + 1) * cols, n * 128 : (n + 1) * 128] = ref[:, g, n].reshape(
                cols, 128
            )


def cut_right(ref, out_ref):
    cols = out_ref.shape[0] * 8
    for g in range(4):
        for n in range(out_ref.shape[2]):
            tile = ref[g * cols : (g + 1) * cols, n * 128 : (n + 1) * 128]
            out_ref[:, g, n] = tile.reshape(-1, 8, 128)


def outer_weights(ref, out_ref):
    whole = ref[...].reshape(32, 4, 8, 128)
    for g in range(4):
        out_ref[g, 0], out_ref[g, 1] = halves(whole[:, g].reshape(256, 128))


def params():
    return pltpu.CompilerParams(vmem_limit_bytes=56 * 2**20)


def full(array):
    return pl.BlockSpec(array.shape, lambda t, n=len(array.shape): (0,) * n)


def step_block(shape):
    return pl.BlockSpec((1,) + shape[1:], lambda t, n=len(shape): (t,) + (0,) * (n - 1))


def pair_of(ref, *index):
    return ref[(*index, 0)], ref[(*index, 1)]


def edges_kernel(
    cols,
    block_ref,
    right_ref,
    outer_ref,
    pair_ref,
    sides_ref,
    mid_ref,
    edge_ref,
    prod_ref,
    whole_ref,
    right_halves,
    outer_halves,
    sides_halves,
):
    t = pl.program_id(0)

    @pl.when(t == 0)
    def _():
        join_right(right_ref, whole_ref)
        right_halves[0], right_halves[1] = halves(whole_ref[...])
        outer_weights(outer_ref, outer_halves)
        sides_halves[0], sides_halves[1] = halves(sides_ref[...])

    right = pair_of(right_halves)
    places = four_rows(t, cols)
    for u in range(4):
        high, low = halves(stacked3(right, pair_of(block_ref, 0, u)))
        for g in range(4):
            prod_ref[0, g, 0, u * cols : (u + 1) * cols] = high[g * cols : (g + 1) * cols]
            prod_ref[0, g, 1, u * cols : (u + 1) * cols] = low[g * cols : (g + 1) * cols]
    update = 0.0
    for g in range(4):
        update = update + stacked3(pair_of(prod_ref, 0, g), pair_of(outer_halves, g))
    mid = update + read_rows(pair_ref, places)
    write_rows(mid_ref, places, mid)
    normed, _ = norm_parts(mid)
    logits = dot3(normed, pair_of(sides_halves))
    write_turned(edge_ref, t, jax.nn.sigmoid(logits[:, :256]) * logits[:, 256:])


def call_edges(blocks, right, outer, pair, sides, cols):
    rows, depth = pair.shape[0], blocks.shape[3]
    prods = (8, 4, 2, 4 * cols, 256)
    return pl.pallas_call(
        functools.partial(edges_kernel, cols),
        grid=(8,),
        in_specs=[step_block(blocks.shape)] + [full(x) for x in (right, outer, pair, sides)],
        out_specs=(
            pl.BlockSpec((rows, 128), lambda t: (0, 0)),
            pl.BlockSpec((256, 16, 128), lambda t: (0, 0, 0)),
            step_block(prods),
        ),
        out_shape=(
            jax.ShapeDtypeStruct((rows, 128), f32),
            jax.ShapeDtypeStruct((256, 16, 128), f32),
            jax.ShapeDtypeStruct(prods, bf16),
        ),
        scratch_shapes=[
            pltpu.VMEM((4 * cols, depth), f32),
            pltpu.VMEM((2, 4 * cols, depth), bf16),
            pltpu.VMEM((4, 2, 256, 128), bf16),
            pltpu.VMEM((2,) + sides.shape, bf16),
        ],
        compiler_params=params(),
        name="edges",
    )(blocks, right, outer, pair, sides)


def join_tiles(chunks, mesh_rows, mesh_cols, out_ref):
    plain = chunks.reshape(mesh_rows * mesh_cols * 16, 128)
    rolled = pltpu.roll(plain, 64, 1)
    first = iota((16, 128), 1) < 64
    for r in range(mesh_rows):
        for t in range(mesh_cols // 2):
            even = slice((r * mesh_cols + 2 * t) * 16, (r * mesh_cols + 2 * t + 1) * 16)
            odd = slice((r * mesh_cols + 2 * t + 1) * 16, (r * mesh_cols + 2 * t + 2) * 16)
            lanes = slice(t * 128, (t + 1) * 128)
            out_ref[r * 32 : r * 32 + 16, lanes] = jnp.where(first, plain[even], rolled[odd])
            out_ref[r * 32 + 16 : r * 32 + 32, lanes] = jnp.where(first, rolled[even], plain[odd])


def cut_tiles(whole, mesh_rows, mesh_cols, store):
    first = iota((16, 128), 1) < 64
    for t in range(mesh_cols // 2):
        plain = whole[:, t * 128 : (t + 1) * 128]
        rolled = pltpu.roll(plain, 64, 1)
        for r in range(mesh_rows):
            low = slice(r * 32, r * 32 + 16)
            high = slice(r * 32 + 16, r * 32 + 32)
            store(r * mesh_cols + 2 * t, jnp.where(first, plain[low], rolled[high]))
            store(r * mesh_cols + 2 * t + 1, jnp.where(first, rolled[low], plain[high]))


def triangle_kernel(mesh_rows, mesh_cols, edge_ref, out_ref, left_ref, right_ref):
    join_tiles(edge_ref[:, 0, 0], mesh_rows, mesh_cols, left_ref)
    join_tiles(edge_ref[:, 1, 0], mesh_rows, mesh_cols, right_ref)

    def store(d, tile):
        out_ref[d, 0] = tile

    cut_tiles(dot3(left_ref[...], right_ref[...], NT), mesh_rows, mesh_cols, store)


def call_triangle(edges, mesh_rows, mesh_cols):
    devices, _, channels = edges.shape[:3]
    span = mesh_rows * 32
    return pl.pallas_call(
        functools.partial(triangle_kernel, mesh_rows, mesh_cols),
        grid=(channels,),
        in_specs=[pl.BlockSpec((devices, 2, 1, 16, 128), lambda n: (0, 0, n, 0, 0))],
        out_specs=pl.BlockSpec((devices, 1, 16, 128), lambda n: (0, n, 0, 0)),
        out_shape=jax.ShapeDtypeStruct((devices, channels, 16, 128), f32),
        scratch_shapes=[pltpu.VMEM((span, span), f32)] * 2,
        compiler_params=pltpu.CompilerParams(vmem_limit_bytes=56 * 2**20),
        name="triangle",
    )(edges)


def triangle_back_kernel(
    mesh_rows, mesh_cols, edge_ref, grad_ref, out_ref, left_ref, right_ref, whole_ref
):
    join_tiles(edge_ref[:, 0, 0], mesh_rows, mesh_cols, left_ref)
    join_tiles(edge_ref[:, 1, 0], mesh_rows, mesh_cols, right_ref)
    join_tiles(grad_ref[:, 0], mesh_rows, mesh_cols, whole_ref)

    def store(kind):
        def put(d, tile):
            out_ref[d, kind, 0] = tile

        return put

    whole = whole_ref[...]
    cut_tiles(dot3(whole, right_ref[...]), mesh_rows, mesh_cols, store(0))
    cut_tiles(dot3(jnp.transpose(whole), left_ref[...]), mesh_rows, mesh_cols, store(1))


def call_triangle_back(edges, grad, mesh_rows, mesh_cols):
    devices, _, channels = edges.shape[:3]
    span = mesh_rows * 32
    both = pl.BlockSpec((devices, 2, 1, 16, 128), lambda n: (0, 0, n, 0, 0))
    return pl.pallas_call(
        functools.partial(triangle_back_kernel, mesh_rows, mesh_cols),
        grid=(channels,),
        in_specs=[both, pl.BlockSpec((devices, 1, 16, 128), lambda n: (0, n, 0, 0))],
        out_specs=both,
        out_shape=jax.ShapeDtypeStruct(edges.shape, f32),
        scratch_shapes=[pltpu.VMEM((span, span), f32)] * 3,
        compiler_params=pltpu.CompilerParams(vmem_limit_bytes=56 * 2**20),
        name="triangle_back",
    )(edges, grad)


def four_rows(t, cols):
    return [
        pl.ds(pl.multiple_of((2 * t + u // 2 + 16 * (u % 2)) * cols, cols), cols) for u in range(4)
    ]


def read_rows(ref, places):
    return jnp.concatenate([ref[p, :] for p in places], 0)


def write_rows(ref, places, value):
    size = value.shape[0] // len(places)
    for u, p in enumerate(places):
        ref[p, :] = value[u * size : (u + 1) * size]


def read_turned(ref, t):
    parts = []
    for v in range(2):
        tile = ref[:, pl.ds(2 * t + v, 1), :]
        parts.append(jnp.transpose(tile.reshape(tile.shape[0], 128)))
    return jnp.concatenate(parts, 0)


def write_turned(ref, t, value):
    for v in range(2):
        turned = jnp.transpose(value[v * 128 : (v + 1) * 128])
        ref[:, pl.ds(2 * t + v, 1), :] = turned[:, None, :]


def finish_kernel(
    cols, tri_ref, mid_ref, grad_ref, gate_ref, proj_ref, out_ref, dtri_ref, dlogit_ref, dproj_ref
):
    gate_w = halves(gate_ref[...])
    proj_w = halves(proj_ref[...])
    dproj_ref[...] = jnp.zeros_like(dproj_ref)

    def step(t, carry):
        places = four_rows(t, cols)
        mid = read_rows(mid_ref, places)
        grad = read_rows(grad_ref, places)
        normed, _ = norm_parts(mid)
        tri, tri_inverse = norm_parts(read_turned(tri_ref, t))
        tri_halves = halves(tri)
        gate = jax.nn.sigmoid(dot3(normed, gate_w))
        value = dot3(tri_halves, proj_w)
        write_rows(out_ref, places, mid + gate * value)
        dvalue = halves(grad * gate)
        write_rows(dlogit_ref, places, grad * value * gate * (1.0 - gate))
        dproj_ref[...] += dot3(halves(jnp.transpose(tri)), dvalue)
        write_turned(dtri_ref, t, norm_back(tri, tri_inverse, dot3(dvalue, proj_w, NT)))
        return carry

    lax.fori_loop(0, 8, step, 0)


def call_finish(tri, mid, grad, gate, proj, cols):
    rows = mid.shape[0]
    return pl.pallas_call(
        functools.partial(finish_kernel, cols),
        out_shape=(
            jax.ShapeDtypeStruct((rows, 128), f32),
            jax.ShapeDtypeStruct((128, 16, 128), f32),
            jax.ShapeDtypeStruct((rows, 128), f32),
            jax.ShapeDtypeStruct((128, 128), f32),
        ),
        compiler_params=pltpu.CompilerParams(vmem_limit_bytes=56 * 2**20),
        name="finish",
    )(tri, mid, grad, gate, proj)


def edges_back_kernel(
    cols,
    chains,
    dedge_ref,
    mid_ref,
    grad_ref,
    dlogit_ref,
    sides_ref,
    right_ref,
    outer_ref,
    block_ref,
    first_ref,
    dmid_ref,
    dlogits_ref,
    dright_ref,
    *refs,
):
    *dleft_refs, whole_ref, turned_halves, outer_halves, sides_halves, fold_ref, dslab_ref, dleft_ref = (
        refs
    )
    t = pl.program_id(0)

    @pl.when(t == 0)
    def _():
        join_right(right_ref, whole_ref)
        turned_halves[0], turned_halves[1] = halves(jnp.transpose(whole_ref[...]))
        outer_weights(outer_ref, outer_halves)
        sides_halves[0], sides_halves[1] = halves(sides_ref[...])
        shape = (256, 128)
        for u in range(4):
            lane = 64 * (u % 2) + 32 * (u // 2) + (iota(shape, 0) >> 3)
            fold = jnp.where(iota(shape, 1) == lane, 1.0, 0.0).astype(bf16)
            fold_ref[512 * u : 512 * u + 256] = fold
            fold_ref[512 * u + 256 : 512 * u + 512] = fold
        whole_ref[...] = jnp.zeros_like(whole_ref)

    same = same_slot(chains)
    sides = pair_of(sides_halves)
    places = four_rows(t, cols)
    normed, inverse = norm_parts(read_rows(mid_ref, places))
    logits = dot3(normed, rounded(sides, (slice(None), slice(0, 512))))
    gate, value = jax.nn.sigmoid(logits[:, :256]), logits[:, 256:]
    dedge = read_turned(dedge_ref, t)
    dlogits = [
        dedge * value * gate * (1.0 - gate),
        dedge * gate,
        read_rows(dlogit_ref, places),
    ]
    dlogits = halves(jnp.concatenate(dlogits, 1))
    dlogits_ref[0, 0], dlogits_ref[0, 1] = dlogits
    dmid = read_rows(grad_ref, places) + norm_back(normed, inverse, dot3(dlogits, sides, NT))
    write_rows(dmid_ref, places, dmid)
    dmid = halves(dmid)
    dprod = [halves(dot3(dmid, pair_of(outer_halves, g), NT)) for g in range(4)]
    here, diagonal = [], []
    turned = pair_of(turned_halves)
    for u in range(4):
        rows = slice(u * cols, (u + 1) * cols)
        here.append([jnp.concatenate([dprod[g][n][rows] for g in range(4)], 0) for n in range(2)])
        diagonal += halves(jnp.where(same, stacked3(turned, tuple(here[u])), 0.0))
    right_terms = [x for high, low in here for x in (high, low, high)]
    block_terms = [block_ref[0, u, n] for u in range(4) for n in (0, 0, 1)]
    whole_ref[...] += one_pass(
        jnp.concatenate(right_terms, 1), jnp.concatenate(block_terms, 1), NT
    )
    dslab = one_pass(jnp.concatenate(diagonal, 1), fold_ref[...])
    dslab_ref[t] = jnp.sum(dslab.reshape(chains, 8, 128), axis=1)

    @pl.when(t == 7)
    def _():
        cut_right(whole_ref, dright_ref)
        first = iota((chains, 128), 1) < 64
        for n in range(4):
            even, odd = dslab_ref[2 * n], dslab_ref[2 * n + 1]
            dleft_ref[n] = jnp.where(first, even, pltpu.roll(odd, 64, 1))
            dleft_ref[n + 4] = jnp.where(first, pltpu.roll(even, 64, 1), odd)
        count, size = len(dleft_refs), dleft_refs[0].shape[0]
        for n, ref in enumerate(dleft_refs):
            place = lax.rem(first_ref[0] + n, count) * size
            ref[...] = dleft_ref[pl.ds(place, size)]


def call_edges_back(dedge, mid, grad, dlogit, sides, right, outer, blocks, first, count, cols):
    rows, depth = mid.shape[0], blocks.shape[3]
    chains = depth // 8
    dlogits = (8, 2, 4 * cols, 640)
    return pl.pallas_call(
        functools.partial(edges_back_kernel, cols, chains),
        grid=(8,),
        in_specs=[full(x) for x in (dedge, mid, grad, dlogit, sides, right, outer)]
        + [step_block(blocks.shape), pl.BlockSpec(memory_space=pltpu.SMEM)],
        out_specs=(
            pl.BlockSpec((rows, 128), lambda t: (0, 0)),
            step_block(dlogits),
            full(right),
        )
        + (pl.BlockSpec((8 // count, chains, 128), lambda t: (0, 0, 0)),) * count,
        out_shape=(
            jax.ShapeDtypeStruct((rows, 128), f32),
            jax.ShapeDtypeStruct(dlogits, bf16),
            jax.ShapeDtypeStruct(right.shape, f32),
        )
        + (jax.ShapeDtypeStruct((8 // count, chains, 128), f32),) * count,
        scratch_shapes=[
            pltpu.VMEM((4 * cols, depth), f32),
            pltpu.VMEM((2, depth, 4 * cols), bf16),
            pltpu.VMEM((4, 2, 256, 128), bf16),
            pltpu.VMEM((2,) + sides.shape, bf16),
            pltpu.VMEM((2048, 128), bf16),
            pltpu.VMEM((8, chains, 128), f32),
            pltpu.VMEM((8, chains, 128), f32),
        ],
        compiler_params=params(),
        name="edges_back",
    )(dedge, mid, grad, dlogit, sides, right, outer, blocks, first)


def give_halves(core_ref, whole_ref, mine_ref, other_ref):
    mine_ref[...] = whole_ref[core_ref[0]]
    other_ref[...] = whole_ref[1 - core_ref[0]]


def pair_sums_kernel(
    cols,
    shift,
    mid_ref,
    dmid_ref,
    dlogits_ref,
    prod_ref,
    first_ref,
    core_ref,
    mine_ref,
    other_ref,
    sides_ref,
    outer_ref,
    out_ref,
    whole_ref,
):
    t = pl.program_id(0)

    @pl.when(t == 0)
    def _():
        sides_ref[...] = jnp.zeros_like(sides_ref)
        outer_ref[...] = jnp.zeros_like(outer_ref)

    places = four_rows(t, cols)
    normed, _ = norm_parts(read_rows(mid_ref, places))
    sides_ref[...] += stacked3(halves(jnp.transpose(normed)), pair_of(dlogits_ref, 0))
    dmid = halves(jnp.transpose(read_rows(dmid_ref, places)))
    for g in range(4):
        outer_ref[:, g * 256 : (g + 1) * 256] += stacked3(dmid, pair_of(prod_ref, 0, g))

    @pl.when(t == 7)
    def _():
        shape = (256, 256)
        place, width = iota(shape, 0), 1 << shift
        target = (place >> (shift + 1) << shift) + (place & (width - 1))
        target = target + 128 * ((place >> shift) & 1)
        order = jnp.where(iota(shape, 1) == target, 1.0, 0.0).astype(bf16)
        for n in range(2):
            high, low = halves(sides_ref[:, n * 256 : (n + 1) * 256])
            sides = one_pass(high, order) + one_pass(low, order)
            out_ref[n * 256 : n * 256 + 128] = sides[:, :128]
            out_ref[n * 256 + 128 : n * 256 + 256] = sides[:, 128:]
        out_ref[512:640] = sides_ref[:, 512:]
        out_ref[640:768] = first_ref[...]
        for g in range(4):
            tile = jnp.transpose(outer_ref[:, g * 256 : (g + 1) * 256]).reshape(32, 8, 128)
            for p in range(32):
                start = 768 + p * 32 + g * 8
                out_ref[start : start + 8] = tile[p]
        whole_ref[0], whole_ref[1] = out_ref[:896], out_ref[896:]
        give_halves(core_ref, whole_ref, mine_ref, other_ref)


def call_pair_sums(mid, dmid, dlogits, prods, first, core, cols, channels_here):
    return pl.pallas_call(
        functools.partial(pair_sums_kernel, cols, channels_here.bit_length() - 1),
        grid=(8,),
        in_specs=[full(mid), full(dmid), step_block(dlogits.shape), step_block(prods.shape)]
        + [full(first), pl.BlockSpec(memory_space=pltpu.SMEM)],
        out_specs=(pl.BlockSpec((896, 128), lambda t: (0, 0)),) * 2,
        out_shape=(jax.ShapeDtypeStruct((896, 128), f32),) * 2,
        scratch_shapes=[
            pltpu.VMEM((128, 640), f32),
            pltpu.VMEM((128, 1024), f32),
            pltpu.VMEM((1792, 128), f32),
            pltpu.VMEM((2, 896, 128), f32),
        ],
        compiler_params=params(),
        name="pair_sums",
    )(mid, dmid, dlogits, prods, first, core)


def pack_heads(y, store):
    lane = iota((1, 1, 128), 2) >> 5
    for tile in range(y.shape[1] // 128):
        part = y[:, tile * 128 : (tile + 1) * 128]
        turned = [part] + [pltpu.roll(part, 32 * n, 1) for n in range(1, 4)]
        turned = [x.reshape(-1, 4, 8, 128) for x in turned]
        for head in range(4):
            out = turned[-head % 4][:, 0]
            for chain in range(1, 4):
                out = jnp.where(lane == chain, turned[(chain - head) % 4][:, chain], out)
            store(tile * 4 + head, out)


def unpack_heads(load, heads):
    lane = iota((1, 1, 128), 2) >> 5
    tiles = []
    for tile in range(heads // 4):
        turned = []
        for head in range(4):
            part = load(tile * 4 + head)
            flat = part.reshape(-1, 128)
            turned.append(
                [part] + [pltpu.roll(flat, 32 * n, 1).reshape(part.shape) for n in range(1, 4)]
            )
        chains = []
        for chain in range(4):
            out = turned[0][-chain % 4]
            for head in range(1, 4):
                out = jnp.where(lane == head, turned[head][(head - chain) % 4], out)
            chains.append(out[:, None])
        tiles.append(jnp.concatenate(chains, 1).reshape(-1, 128))
    return jnp.concatenate(tiles, 1)


def head_lanes(tile, n):
    return jnp.where((iota((1, 128), 1) >> 5) == n, tile, 0.0)


def soft(scores, seen=None):
    if seen is not None:
        scores = jnp.where(seen, scores, -1e30)
    weights = jnp.exp(scores - jnp.max(scores, axis=-1, keepdims=True))
    if seen is not None:
        weights = jnp.where(seen, weights, 0.0)
    return weights * (1.0 / jnp.sum(weights, axis=-1, keepdims=True))


def soft_back(weights, grad):
    return weights * (grad - jnp.sum(weights * grad, axis=-1, keepdims=True))


def stripe_seen(present_ref):
    tokens = present_ref.shape[1]
    shape = (tokens, tokens)
    same = (iota(shape, 0) & 7) == (iota(shape, 1) & 7)
    return same & (present_ref[...] > 0.0)


def column_attention(q, k, v, seen):
    weights, tiles = [], []
    for tile in range(q.shape[1] // 128):
        lanes = slice(tile * 128, (tile + 1) * 128)
        keys, values = halves(k[:, lanes]), halves(v[:, lanes])
        blend = 0.0
        for n in range(4):
            weights.append(soft(dot3(head_lanes(q[:, lanes], n), keys, NT), seen))
            blend = blend + head_lanes(dot3(weights[-1], values), n)
        tiles.append(blend)
    return weights, jnp.concatenate(tiles, 1)


def columns_kernel(
    scale,
    x_ref,
    present_ref,
    bias_ref,
    q_ref,
    k_ref,
    v_ref,
    o_ref,
    q2_ref,
    k2_ref,
    v2_ref,
    out_ref,
    qkv_ref,
):
    x = x_ref[...]
    normed, _ = norm_parts(x)
    normed = halves(normed)
    q, k, v = (dot3(normed, halves(w[...])) for w in (q_ref, k_ref, v_ref))
    _, blend = column_attention(q * scale, k, v, stripe_seen(present_ref))
    out = x + dot3(blend, halves(o_ref[...]))
    out_ref[...] = out
    normed, _ = norm_parts(out)
    normed = halves(normed)
    groups, size = qkv_ref.shape[0] // 8, (qkv_ref.shape[1] - 16) // 3
    qkv_ref[:, -16:] = bias_ref[...]

    def store(kind):
        def put(head, value):
            place = slice(head * groups, (head + 1) * groups)
            rows = slice(kind * size, (kind + 1) * size)
            qkv_ref[place, rows] = value.reshape(groups, size, 128)

        return put

    for kind, w in enumerate((q2_ref, k2_ref, v2_ref)):
        pack_heads(dot3(normed, halves(w[...])), store(kind))


def call_columns(x, present, bias, weights, group_chains, scale):
    return pl.pallas_call(
        functools.partial(columns_kernel, scale),
        out_shape=(
            jax.ShapeDtypeStruct(x.shape, f32),
            jax.ShapeDtypeStruct((bias.shape[0], 6 * group_chains + 16, 128), f32),
        ),
        compiler_params=params(),
        name="columns",
    )(x, present, bias, *weights)


def packed_parts(ref):
    parts = (ref.shape[1] - 16) // 24
    for half in range(parts):
        places = [(kind * parts + half) * 8 for kind in range(3)]
        yield half, places, [ref[:, p : p + 8].reshape(-1, 128) for p in places]


def rows_kernel(mesh_rows, mesh_cols, scale, qkv_ref, out_ref, whole_ref):
    join_tiles(qkv_ref[:, -16:], mesh_rows, mesh_cols, whole_ref)
    bias = whole_ref[...]
    for half, _, (q, k, v) in packed_parts(qkv_ref):
        k, v, q = halves(k), halves(v), q * scale
        blend = 0.0
        for n in range(4):
            weights = soft(dot3(head_lanes(q, n), k, NT) + bias)
            blend = blend + head_lanes(dot3(weights, v), n)
        out_ref[:, half] = blend.reshape(-1, 8, 128)


def call_rows(qkv, mesh_rows, mesh_cols, scale):
    devices, parts = qkv.shape[0], (qkv.shape[1] - 16) // 24
    span = mesh_rows * 32
    return pl.pallas_call(
        functools.partial(rows_kernel, mesh_rows, mesh_cols, scale),
        out_shape=jax.ShapeDtypeStruct((devices, parts, 8, 128), f32),
        scratch_shapes=[pltpu.VMEM((span, span), f32)],
        compiler_params=params(),
        name="rows",
    )(qkv)


def load_heads(ref, kind=None):
    def load(head):
        groups = ref.shape[0] // 8
        place = slice(head * groups, (head + 1) * groups)
        part = ref[place] if kind is None else ref[place, kind]
        return part.reshape(-1, 8, 128)

    return load


def rows_out_kernel(blend_ref, mid_ref, share_ref, o_ref, sides_ref, out_ref, left_ref, right_ref):
    blend = unpack_heads(load_heads(blend_ref), 8)
    out = mid_ref[...] + dot3(blend, halves(o_ref[...]))
    out_ref[...] = out
    normed, _ = norm_parts(out)
    wide = dot3(normed, halves(sides_ref[...]))
    left = (wide[:, :128] * share_ref[...]).reshape(-1, 4, 8, 128)
    lane = iota((1, 1, 128), 2)
    packed = left[:, 0]
    for chain in range(1, 4):
        packed = jnp.where((lane >> 5) == chain, left[:, chain], packed)
    for n in range(packed.shape[0]):
        left_ref[:, n, :] = packed[n]
    for g in range(4):
        right = wide[:, (g + 1) * 128 : (g + 2) * 128].reshape(-1, 16, 8, 128)
        packed = right[:, 0]
        for chain in range(1, 16):
            packed = jnp.where((lane >> 3) == chain, right[:, chain], packed)
        right_ref[g] = packed


def call_rows_out(blend, mid, share, weight, sides):
    chains = mid.shape[0] // 8
    return pl.pallas_call(
        rows_out_kernel,
        out_shape=(
            jax.ShapeDtypeStruct(mid.shape, f32),
            jax.ShapeDtypeStruct((8, chains // 4, 128), f32),
            jax.ShapeDtypeStruct((4, chains // 16, 8, 128), f32),
        ),
        compiler_params=params(),
        name="rows_out",
    )(blend, mid, share, weight, sides)


def rows_out_back_kernel(*refs):
    *dleft_refs, dright_ref, grad_ref, out_ref, blend_ref, share_ref, o_ref, sides_ref = refs[:-7]
    core_ref, dout_ref, dblend_ref, thin_ref, mine_ref, other_ref, sum_ref = refs[-7:]
    lane = iota((1, 1, 128), 2)
    chains = grad_ref.shape[0] // 8
    dleft = functools.reduce(jnp.add, [ref[...] for ref in dleft_refs])
    shape = (chains * 8, 128)
    slot = iota(shape, 0) & 7
    copy = (chains * 8, chains)
    copy = jnp.where((iota(copy, 0) >> 3) == iota(copy, 1), 1.0, 0.0).astype(bf16)
    left = 0.0
    for n in range(2):
        high, low = halves(dleft[n])
        spot = (slot >> 2 == n) & (slot & 3 == iota(shape, 1) >> 5)
        left = left + jnp.where(spot, one_pass(copy, high) + one_pass(copy, low), 0.0)
    wide = [left * share_ref[...]]
    dright = dright_ref[...]
    for g in range(4):
        part = [jnp.where((lane >> 3) == n, dright[g], 0.0)[:, None] for n in range(16)]
        wide.append(jnp.concatenate(part, 1).reshape(-1, 128))
    wide = halves(jnp.concatenate(wide, 1))
    normed, inverse = norm_parts(out_ref[...])
    dsides = halves(dot3(halves(jnp.transpose(normed)), wide))
    shape = (640, 128)
    place, spot = iota(shape, 0) - 128, iota(shape, 1)
    target = jnp.where(place < 0, place & 31, 32 + ((place >> 7) << 3) + (place & 7))
    fold = jnp.where(target == spot, 1.0, 0.0).astype(bf16)
    thin_ref[...] = one_pass(dsides[0], fold) + one_pass(dsides[1], fold)
    dout = grad_ref[...] + norm_back(normed, inverse, dot3(wide, halves(sides_ref[...]), NT))
    dout_ref[...] = dout
    dout = halves(dout)
    groups = dblend_ref.shape[0] // 8

    def store(head, value):
        dblend_ref[head * groups : (head + 1) * groups] = value.reshape(groups, -1, 8, 128)

    pack_heads(dot3(dout, halves(o_ref[...]), NT), store)
    blend = unpack_heads(load_heads(blend_ref), 8)
    write_halves(sum_ref, 0, dot3(halves(jnp.transpose(blend)), dout))
    give_halves(core_ref, sum_ref, mine_ref, other_ref)


def call_rows_out_back(dlefts, dright, grad, out, blend, share, weight, sides, core):
    shapes, scratch = halves_shapes([weight])
    return pl.pallas_call(
        rows_out_back_kernel,
        out_shape=(
            jax.ShapeDtypeStruct(grad.shape, f32),
            jax.ShapeDtypeStruct(blend.shape, f32),
            jax.ShapeDtypeStruct((256, 128), f32),
        )
        + shapes,
        in_specs=specs(len(dlefts) + 7),
        scratch_shapes=[scratch],
        compiler_params=params(),
        name="rows_out_back",
    )(*dlefts, dright, grad, out, blend, share, weight, sides, core)


def rows_back_kernel(
    mesh_rows, mesh_cols, scale, qkv_ref, dblend_ref, out_ref, whole_ref
):
    join_tiles(qkv_ref[:, -16:], mesh_rows, mesh_cols, whole_ref)
    bias = whole_ref[...]
    dbias = 0.0
    for half, places, (q, k, v) in packed_parts(qkv_ref):
        k, v, q = halves(k), halves(v), q * scale
        grad = dblend_ref[:, half].reshape(-1, 128)
        dq, dk, dv = 0.0, 0.0, 0.0
        for n in range(4):
            query, dblend = halves(head_lanes(q, n)), halves(head_lanes(grad, n))
            weights = soft(dot3(query, k, NT) + bias)
            dv = dv + dot3(halves(jnp.transpose(weights)), dblend)
            dscores = soft_back(weights, dot3(dblend, v, NT))
            dbias = dbias + dscores
            dk = dk + dot3(halves(jnp.transpose(dscores)), query)
            dq = dq + head_lanes(dot3(dscores, k), n)
        for place, value in zip(places, (dq * scale, dk, dv)):
            out_ref[:, place : place + 8] = value.reshape(-1, 8, 128)

    def store(d, tile):
        out_ref[d, -16:] = tile

    cut_tiles(dbias, mesh_rows, mesh_cols, store)


def call_rows_back(qkv, dblend, mesh_rows, mesh_cols, scale):
    span = mesh_rows * 32
    return pl.pallas_call(
        functools.partial(rows_back_kernel, mesh_rows, mesh_cols, scale),
        out_shape=jax.ShapeDtypeStruct(qkv.shape, f32),
        scratch_shapes=[pltpu.VMEM((span, span), f32)],
        compiler_params=params(),
        name="rows_back",
    )(qkv, dblend)


def write_halves(ref, n, value):
    height = value.shape[0]
    for half in range(2):
        ref[half, n * height : (n + 1) * height] = value[:, half * 128 : (half + 1) * 128]


def projections_back(normed, inverse, grads, weight_refs, sum_ref):
    turned = halves(jnp.transpose(normed))
    dnormed = 0.0
    for n, (grad, w) in enumerate(zip(grads, weight_refs)):
        grad = halves(grad)
        write_halves(sum_ref, n, dot3(turned, grad))
        dnormed = dnormed + dot3(grad, halves(w[...]), NT)
    return norm_back(normed, inverse, dnormed)


def rows_in_back_kernel(
    dqkv_ref, mid_ref, grad_ref, q_ref, k_ref, v_ref, core_ref, dmid_ref, mine_ref, other_ref, sum_ref
):
    groups, size = dqkv_ref.shape[0] // 8, (dqkv_ref.shape[1] - 16) // 3

    def load(kind):
        place = slice(kind * size, (kind + 1) * size)
        return lambda head: dqkv_ref[head * groups : (head + 1) * groups, place].reshape(-1, 8, 128)

    grads = [unpack_heads(load(kind), 8) for kind in range(3)]
    normed, inverse = norm_parts(mid_ref[...])
    dmid_ref[...] = grad_ref[...] + projections_back(
        normed, inverse, grads, (q_ref, k_ref, v_ref), sum_ref
    )
    give_halves(core_ref, sum_ref, mine_ref, other_ref)


def halves_shapes(weights):
    rows = sum(w.size for w in weights) // 256
    return (jax.ShapeDtypeStruct((rows, 128), f32),) * 2, pltpu.VMEM((2, rows, 128), f32)


def specs(count):
    vmem = pl.BlockSpec(memory_space=pltpu.VMEM)
    return [vmem] * count + [pl.BlockSpec(memory_space=pltpu.SMEM)]


def call_rows_in_back(dqkv, mid, grad, weights, core):
    shapes, scratch = halves_shapes(weights)
    return pl.pallas_call(
        rows_in_back_kernel,
        in_specs=specs(6),
        out_shape=(jax.ShapeDtypeStruct(mid.shape, f32),) + shapes,
        scratch_shapes=[scratch],
        compiler_params=params(),
        name="rows_in_back",
    )(dqkv, mid, grad, *weights, core)


def columns_back_kernel(
    scale,
    x_ref,
    present_ref,
    grad_ref,
    q_ref,
    k_ref,
    v_ref,
    o_ref,
    core_ref,
    dx_ref,
    mine_ref,
    other_ref,
    sum_ref,
):
    normed, inverse = norm_parts(x_ref[...])
    normed_halves = halves(normed)
    q, k, v = (dot3(normed_halves, halves(w[...])) for w in (q_ref, k_ref, v_ref))
    q = q * scale
    weights, blend = column_attention(q, k, v, stripe_seen(present_ref))
    grad = grad_ref[...]
    grad_halves = halves(grad)
    write_halves(sum_ref, 3, dot3(halves(jnp.transpose(blend)), grad_halves))
    dblend = dot3(grad_halves, halves(o_ref[...]), NT)
    tiles = [[], [], []]
    for tile in range(q.shape[1] // 128):
        lanes = slice(tile * 128, (tile + 1) * 128)
        keys, values = halves(k[:, lanes]), halves(v[:, lanes])
        dq, dk, dv = 0.0, 0.0, 0.0
        for n in range(4):
            query = halves(head_lanes(q[:, lanes], n))
            dhead = halves(head_lanes(dblend[:, lanes], n))
            share = weights[tile * 4 + n]
            dv = dv + dot3(halves(jnp.transpose(share)), dhead)
            dscores = soft_back(share, dot3(dhead, values, NT))
            dk = dk + dot3(halves(jnp.transpose(dscores)), query)
            dq = dq + head_lanes(dot3(dscores, keys), n)
        for kind, value in enumerate((dq * scale, dk, dv)):
            tiles[kind].append(value)
    grads = [jnp.concatenate(t, 1) for t in tiles]
    dx_ref[...] = grad + projections_back(
        normed, inverse, grads, (q_ref, k_ref, v_ref), sum_ref
    )
    give_halves(core_ref, sum_ref, mine_ref, other_ref)


def call_columns_back(x, present, grad, weights, core, scale):
    shapes, scratch = halves_shapes(weights)
    return pl.pallas_call(
        functools.partial(columns_back_kernel, scale),
        in_specs=specs(7),
        out_shape=(jax.ShapeDtypeStruct(x.shape, f32),) + shapes,
        scratch_shapes=[scratch],
        compiler_params=params(),
        name="columns_back",
    )(x, present, grad, *weights, core)


def bias_kernel(cols, pair_ref, weight_ref, out_ref):
    weight = halves(weight_ref[...])

    def step(t, carry):
        rows = halves(read_rows(pair_ref, four_rows(t, cols)))
        heads = dot3(weight, rows, NT)
        for v in range(2):
            tile = heads[:, v * 128 : (v + 1) * 128][:, None, :]
            for g in range(out_ref.shape[1]):
                out_ref[:, g, pl.ds(2 * t + v, 1), :] = tile
        return carry

    lax.fori_loop(0, 8, step, 0)


def call_bias(pair, weight, copies, cols):
    return pl.pallas_call(
        functools.partial(bias_kernel, cols),
        out_shape=jax.ShapeDtypeStruct((weight.shape[0], copies, 16, 128), f32),
        compiler_params=params(),
        name="bias",
    )(pair, weight)


def bias_rows(dbias):
    heads, groups, rows = dbias.shape[:3]
    return pl.BlockSpec((heads, groups, 16, 128), lambda t: (0, 0, rows // 16 - 1, 0))


def head_rows(ref, t):
    heads = [ref[:, pl.ds(2 * t + v, 1), :].reshape(-1, 128) for v in range(2)]
    return jnp.concatenate(heads, 1)


def bias_sums_kernel(
    cols, dbias_ref, pair_ref, thin_ref, core_ref, mine_ref, other_ref, whole_ref, sum_ref, dweight_ref
):
    sum_ref[...] = jnp.sum(dbias_ref[...], axis=1)
    dweight_ref[...] = jnp.zeros_like(dweight_ref)

    def step(t, carry):
        dweight_ref[...] += dot3(head_rows(sum_ref, t), read_rows(pair_ref, four_rows(t, cols)))
        return carry

    lax.fori_loop(0, 8, step, 0)
    whole_ref[0], whole_ref[1] = thin_ref[:128], thin_ref[128:]
    whole_ref[0, :, 64 : 64 + dweight_ref.shape[0]] = jnp.transpose(dweight_ref[...])
    give_halves(core_ref, whole_ref, mine_ref, other_ref)


def call_bias_sums(dbias, pair, thin, core, cols):
    heads = dbias.shape[0]
    return pl.pallas_call(
        functools.partial(bias_sums_kernel, cols),
        grid=(1,),
        in_specs=[bias_rows(dbias), full(pair), full(thin), pl.BlockSpec(memory_space=pltpu.SMEM)],
        out_specs=(pl.BlockSpec((128, 128), lambda t: (0, 0)),) * 2,
        out_shape=(jax.ShapeDtypeStruct((128, 128), f32),) * 2,
        scratch_shapes=[
            pltpu.VMEM((2, 128, 128), f32),
            pltpu.VMEM((heads, 16, 128), f32),
            pltpu.VMEM((heads, 128), f32),
        ],
        compiler_params=params(),
        name="bias_sums",
    )(dbias, pair, thin, core)


def bias_back_kernel(cols, dbias_ref, dmid_ref, weight_ref, out_ref, sum_ref):
    weight = halves(weight_ref[...])
    sum_ref[...] = jnp.sum(dbias_ref[...], axis=1)

    def step(t, carry):
        places = four_rows(t, cols)
        dpair = dot3(jnp.transpose(head_rows(sum_ref, t)), weight)
        write_rows(out_ref, places, read_rows(dmid_ref, places) + dpair)
        return carry

    lax.fori_loop(0, 8, step, 0)


def call_bias_back(dbias, dmid, weight, cols):
    return pl.pallas_call(
        functools.partial(bias_back_kernel, cols),
        grid=(1,),
        in_specs=[bias_rows(dbias), full(dmid), full(weight)],
        out_specs=full(dmid),
        out_shape=jax.ShapeDtypeStruct(dmid.shape, f32),
        scratch_shapes=[pltpu.VMEM((dbias.shape[0], 16, 128), f32)],
        compiler_params=params(),
        name="bias_back",
    )(dbias, dmid, weight)


def spread_sums_kernel(mine_ref, other_ref, core_ref, *outs):
    def place(first, second):
        for half, ref in enumerate((first, second)):
            lanes = slice(half * 128, (half + 1) * 128)
            for n, target in enumerate((0, 1, 2, 3, 4, 5, 6, 8)):
                outs[target][:, lanes] = ref[n * 256 : (n + 1) * 256]
        thin = jnp.transpose(jnp.concatenate([first[2048:2176], second[2048:2176]], 0))
        outs[7][...] = thin[64 : 64 + outs[7].shape[0], :128]
        outs[9][...] = thin[:32]
        outs[10][...] = thin[32:64]
        for n, target in enumerate((13, 15, 12, 14, 16, 17)):
            outs[target][...] = first[2176 + n * 128 : 2304 + n * 128]
        outs[11][:128] = first[2944:3072]
        outs[11][128:] = second[2176:3072]

    @pl.when(core_ref[0] == 0)
    def _():
        place(mine_ref, other_ref)

    @pl.when(core_ref[0] != 0)
    def _():
        place(other_ref, mine_ref)


def call_spread_sums(mine, other, core, shapes):
    thin = (7, 9, 10)
    shapes = [shape[::-1] if n in thin else shape for n, shape in enumerate(shapes)]
    sums = pl.pallas_call(
        spread_sums_kernel,
        in_specs=specs(2),
        out_shape=tuple(jax.ShapeDtypeStruct(shape, f32) for shape in shapes),
        compiler_params=params(),
        name="spread_sums",
    )(mine, other, core)
    return [jnp.transpose(x) if n in thin else x for n, x in enumerate(sums)]


precise = lax.Precision.HIGH
everyone = ("half", "core", "col")
row = ("half", "core")
chips = ("half", "col")


def affine_map(tensor, weight):
    return jnp.einsum("...a,ab->...b", tensor, weight, precision=precise)


def exchange(chunks, axis):
    shape = chunks.shape
    flat = chunks.reshape(shape[0], -1, 128)
    return lax.all_to_all(flat, axis, 0, 0, tiled=True).reshape(shape)


def collect(block, axis, count):
    return exchange(jnp.broadcast_to(block[None], (count,) + block.shape), axis)


def tall(weight):
    return jnp.concatenate([weight[:, :128], weight[:, 128:]], 0)


def together(*arrays):
    return lax.optimization_barrier(arrays)


class Layout:
    def __init__(self, mesh_rows, mesh_cols, pair, chains, heads, head_width):
        self.mesh_rows, self.mesh_cols = mesh_rows, mesh_cols
        self.devices = mesh_rows * mesh_cols
        self.rows_here, self.cols_here, self.pair_width = pair
        self.span = self.rows_here * mesh_rows
        self.slim = self.span // self.devices
        self.chains, self.heads, self.head_width = chains, heads, head_width
        self.chain_groups = self.devices // heads
        self.group_chains = chains // self.chain_groups
        self.channels_here = self.pair_width // self.devices
        self.scale = head_width ** (-0.5)
        self.turn = [
            (g, (g % mesh_rows) * mesh_cols + g // mesh_rows) for g in range(self.devices)
        ]
        self.turn_back = [(b, a) for a, b in self.turn]

        self.swap = [(0, 1), (1, 0)]
        self.core = lax.axis_index("core").reshape(1)

    def to_slim(self, x):
        return lax.all_to_all(x, "col", 1, 0, tiled=True)

    def both_views(self, grad, out):
        count, slim, width = self.mesh_cols, self.slim, grad.shape[2]
        grad = jnp.transpose(grad.reshape(-1, count, slim, width), (1, 0, 2, 3))
        both = jnp.stack([grad, out.reshape(count, -1, slim, width)], 1)
        return both.reshape(count, -1, width)

    def change_views(self, both):
        count, slim, width = self.mesh_cols, self.slim, both.shape[2]
        both = lax.all_to_all(both, "col", 0, 0, tiled=True).reshape(count, 2, -1, slim, width)
        out = jnp.transpose(both[:, 1], (1, 0, 2, 3)).reshape(-1, count * slim, width)
        return both[:, 0].reshape(-1, slim, width), out

    def from_slim_permuted(self, x):
        count, slim = self.mesh_cols, x.shape[1]
        here = lax.axis_index("col")
        blocks = x.reshape(count, -1, slim, x.shape[2])
        out = jnp.zeros((blocks.shape[1], count * slim, x.shape[2]), f32)
        for n in range(count):
            block = lax.dynamic_index_in_dim(blocks, lax.rem(here + n, count), 0, False)
            if n:
                block = lax.ppermute(block, "col", [(s, (s + n) % count) for s in range(count)])
            source = lax.rem(here + count - n, count)
            out = lax.dynamic_update_slice_in_dim(out, block, source * slim, 1)
        return out

    def from_others(self, arrays):
        count = self.mesh_cols
        return [
            lax.ppermute(x, "col", [(s, (s + n) % count) for s in range(count)]) if n else x
            for n, x in enumerate(arrays)
        ]

    def sum_all(self, mine, *beside):
        half = self.mesh_rows // 2
        part = exchange(mine.reshape(half, -1, 128), "half").sum(0)
        part = exchange(part.reshape(self.mesh_cols, -1, 128), "col").sum(0)
        part, *beside = together(part, *beside)
        part = collect(part, "col", self.mesh_cols).reshape(-1, 128)
        return collect(part, "half", half).reshape(-1, 128), *beside


def msa_plain(size, alignment_features, residue_couplings, present, weights):
    chains, slim, heads, head_width = size.chains, size.slim, size.heads, size.head_width
    devices, groups, group_chains = size.devices, size.chain_groups, size.group_chains
    rows_here, cols_here, span = size.rows_here, size.cols_here, size.span
    mesh_rows, mesh_cols = size.mesh_rows, size.mesh_cols
    bias = jnp.transpose(affine_map(residue_couplings, weights[7]), (2, 0, 1))
    bias = jnp.broadcast_to(bias[:, None], (heads, groups, rows_here, cols_here))
    bias = exchange(bias.reshape(devices, rows_here, cols_here), everyone)
    bias = bias.reshape(mesh_rows, mesh_cols, rows_here, cols_here)
    bias = jnp.transpose(bias, (0, 2, 1, 3)).reshape(span, span)

    stripe = size.to_slim(alignment_features)
    normed, _ = norm_parts(stripe)
    col_q, col_k, col_v = (
        affine_map(normed, w).reshape(chains, slim, heads, head_width) for w in weights[:3]
    )
    scores = jnp.einsum("sihd,tihd->ihst", col_q, col_k, precision=precise) * size.scale
    scores = jnp.where(present[None, None, None, :] > 0, scores, -1000000000.0)
    blend = jnp.einsum(
        "ihst,tihd->sihd", jax.nn.softmax(scores, axis=-1), col_v, precision=precise
    )
    msa_col = stripe + affine_map(blend.reshape(chains, slim, heads * head_width), weights[3])

    normed, _ = norm_parts(msa_col)
    qkv = jnp.stack([affine_map(normed, w) for w in weights[4:7]])
    qkv = qkv.reshape(3, groups, group_chains, slim, heads, head_width)
    qkv = jnp.transpose(qkv, (4, 1, 0, 2, 3, 5))
    qkv = exchange(qkv.reshape(devices, 3, group_chains, slim, head_width), everyone)
    qkv = jnp.transpose(qkv, (1, 2, 0, 3, 4)).reshape(3, group_chains, span, head_width)
    scores = jnp.einsum("sid,sjd->sij", qkv[0], qkv[1], precision=precise) * size.scale
    shares = jax.nn.softmax(scores + bias[None], axis=-1)
    blend = jnp.einsum("sij,sjd->sid", shares, qkv[2], precision=precise)
    blend = blend.reshape(group_chains, devices, slim, head_width)
    blend = exchange(jnp.transpose(blend, (1, 0, 2, 3)), everyone)
    blend = blend.reshape(heads, chains, slim, head_width)
    blend = jnp.transpose(blend, (1, 2, 0, 3)).reshape(chains, slim, heads * head_width)
    msa_out = msa_col + affine_map(blend, weights[8])

    normed, _ = norm_parts(msa_out)
    left = affine_map(normed, weights[9]) * (present / jnp.sum(present))[:, None, None]
    left = jnp.transpose(left.reshape(chains // 4, 4, slim, 32), (2, 0, 1, 3))
    left = collect(left.reshape(slim, chains // 4, 128), "col", mesh_cols).reshape(-1, 128)
    right = affine_map(normed, weights[10]).reshape(chains // 16, 16, slim, 4, 8)
    right = jnp.transpose(right, (3, 0, 2, 1, 4)).reshape(-1, 128)
    right = collect(lax.ppermute(right, everyone, size.turn), row, mesh_rows)
    right = right.reshape(mesh_rows, 4, chains // 16, slim, 128)
    right = jnp.transpose(right, (1, 0, 3, 2, 4)).reshape(4, cols_here // 8, 8, chains // 16, 128)
    return msa_out, [left], jnp.transpose(right, (1, 0, 3, 2, 4))


def msa_forward(size, alignment_features, residue_couplings, present, weights):
    chains, slim, devices = size.chains, size.slim, size.devices
    mesh_rows, mesh_cols = size.mesh_rows, size.mesh_cols
    pair_flat = residue_couplings.reshape(-1, size.pair_width)
    tokens = chains * slim
    seen = jnp.repeat(present, slim)[None]
    share = jnp.repeat(present / jnp.sum(present), slim)[:, None]
    sides = jnp.concatenate(
        [
            jnp.tile(weights[9], (1, 4)),
            jnp.broadcast_to(weights[10].reshape(-1, 4, 1, 8), (256, 4, 16, 8)).reshape(256, 512),
        ],
        1,
    )
    offset = jnp.transpose(weights[7])
    stripe = size.to_slim(alignment_features).reshape(tokens, -1)
    bias = call_bias(pair_flat, offset, size.chain_groups, size.cols_here)
    bias = bias.reshape(devices, 16, 128)
    msa_col, qkv = call_columns(stripe, seen, bias, weights[:7], size.group_chains, size.scale)
    qkv = exchange(qkv, everyone)
    blend = call_rows(qkv, mesh_rows, mesh_cols, size.scale)
    blend = exchange(blend, everyone)
    msa_out, left, right = call_rows_out(blend, msa_col, share, weights[8], sides)
    left = size.from_others([left.reshape(-1, 128)] * mesh_cols)
    right, *left = together(lax.ppermute(right, everyone, size.turn), *left)
    right = collect(right, row, mesh_rows)

    def back(grad, d_lefts, d_right, d_mid, pair_sums):
        d_lefts = size.from_others(d_lefts)
        d_right = exchange(d_right, row).sum(0)
        d_right = lax.ppermute(d_right, everyone, size.turn_back)
        d_out, d_blend, thin, *out_sums = call_rows_out_back(
            d_lefts,
            d_right,
            grad.reshape(tokens, -1),
            msa_out,
            blend,
            share,
            weights[8],
            sides,
            size.core,
        )
        d_mid, d_blend = together(d_mid, d_blend)
        pair_sums = pair_sums(d_mid)
        d_blend, *pair_sums = together(exchange(d_blend, everyone), *pair_sums)
        d_qkv = call_rows_back(qkv, d_blend, mesh_rows, mesh_cols, size.scale)
        d_qkv = exchange(d_qkv, everyone)
        d_col, *in_sums = call_rows_in_back(d_qkv, msa_col, d_out, weights[4:7], size.core)
        d_stripe, *col_sums = call_columns_back(
            stripe, seen, d_col, weights[:4], size.core, size.scale
        )
        d_bias = d_qkv.reshape(size.heads, size.chain_groups, -1, 128)
        thin_sums = call_bias_sums(d_bias, pair_flat, thin, size.core, size.cols_here)
        d_pair = call_bias_back(d_bias, d_mid, offset, size.cols_here)
        d_features = size.from_slim_permuted(d_stripe.reshape(chains, slim, -1))
        return d_features, d_pair, col_sums, in_sums, out_sums, thin_sums, pair_sums

    return (msa_out.reshape(chains, slim, -1), left, right), back


def msa_plain_forward(size, alignment_features, residue_couplings, present, weights):
    chains, rows_here = size.chains, size.rows_here
    outputs, pull = jax.vjp(
        lambda x, y, w: msa_plain(size, x, y, present, w),
        alignment_features,
        residue_couplings,
        weights,
    )

    def back(grad, d_lefts, d_right, d_mid, pair_sums):
        d_left = d_lefts[0].reshape(rows_here // 4, chains // 4, 4, 4, 32)
        d_left = jnp.transpose(d_left, (0, 3, 1, 2, 4)).reshape(-1, 128)
        d_features, d_pair, d_weights = pull((grad, [d_left], d_right))
        d_pair = d_pair.reshape(-1, size.pair_width) + d_mid
        thin = [d_weights[9], d_weights[10], jnp.pad(d_weights[7], ((0, 128), (0, 0)))]
        thin = jnp.pad(jnp.concatenate(thin, 1), ((0, 0), (0, 64 - size.heads)))
        core = size.core[0]
        pick = lambda x, n: lax.dynamic_index_in_dim(x, n, 0, False)
        own = lambda x: (pick(x, core), pick(x, 1 - core))
        cut = lambda ws: own(
            jnp.stack([jnp.concatenate([w[:, n : n + 128] for w in ws], 0) for n in (0, 128)])
        )
        return (
            d_features,
            d_pair,
            cut(d_weights[:4]),
            cut(d_weights[4:7]),
            cut(d_weights[8:9]),
            own(thin.reshape(2, -1, 128)),
            pair_sums(d_mid),
        )

    return outputs, back


def per_device(mesh_rows, mesh_cols, *arguments):
    (
        alignment_features,
        residue_couplings,
        chain_indicator,
        alignment_result_adjoint,
        coupling_result_adjoint,
        *weights,
    ) = arguments
    present = chain_indicator.astype(jnp.float32)
    heads = weights[7].shape[1]
    size = Layout(
        mesh_rows,
        mesh_cols,
        residue_couplings.shape,
        present.shape[0],
        heads,
        weights[4].shape[1] // heads,
    )
    devices, channels_here = size.devices, size.channels_here
    cols_here, pair_width = size.cols_here, size.pair_width
    (
        tensor_result_matrix,
        source_side_matrix,
        source_side_switch,
        target_side_matrix,
        target_side_switch,
        trilateral_result_switch,
        trilateral_result_matrix,
    ) = weights[11:]

    def interleave(left, right):
        shape = (pair_width, devices, channels_here)
        both = jnp.stack([left.reshape(shape), right.reshape(shape)], 2)
        return both.reshape(pair_width, 2 * pair_width)

    sides = jnp.concatenate(
        [
            interleave(source_side_switch, target_side_switch),
            interleave(source_side_matrix, target_side_matrix),
            trilateral_result_switch,
        ],
        1,
    )
    forward = msa_forward if size.slim == 8 else msa_plain_forward
    (msa_slim, left_rows, right_rows), msa_back = forward(
        size, alignment_features, residue_couplings, present, tuple(weights[:11])
    )
    pair_flat = residue_couplings.reshape(-1, pair_width)
    grad_flat = coupling_result_adjoint.reshape(-1, pair_width)
    count = len(left_rows)
    first = (lax.axis_index("col") if count > 1 else jnp.int32(0)).reshape(1)
    blocks = call_blocks(first, left_rows)
    pair_mid, edges, prods = call_edges(
        blocks, right_rows, tensor_result_matrix, pair_flat, sides[:, : 4 * pair_width], cols_here
    )
    edges = exchange(edges.reshape(devices, 2, channels_here, 16, 128), everyone)
    triangle = exchange(call_triangle(edges, mesh_rows, mesh_cols), everyone)
    pair_out, d_triangle, d_logit, g_tri_out = call_finish(
        triangle.reshape(pair_width, 16, 128),
        pair_mid,
        grad_flat,
        trilateral_result_switch,
        trilateral_result_matrix,
        cols_here,
    )
    views = (alignment_result_adjoint, msa_slim)
    *views, d_triangle = together(*views, d_triangle)
    views = size.both_views(*views)
    d_triangle = exchange(d_triangle.reshape(devices, channels_here, 16, 128), everyone)
    d_edges = exchange(call_triangle_back(edges, d_triangle, mesh_rows, mesh_cols), everyone)
    d_edges, views = together(d_edges, views)
    msa_grad, msa_out = size.change_views(views)
    d_mid, d_logits, d_right, *d_lefts = call_edges_back(
        d_edges.reshape(2 * pair_width, 16, 128),
        pair_mid,
        grad_flat,
        d_logit,
        sides,
        right_rows,
        tensor_result_matrix,
        blocks,
        first,
        count,
        cols_here,
    )
    d_right, msa_grad, msa_out = together(d_right, msa_grad, msa_out)

    def pair_sums(d_mid):
        return call_pair_sums(
            pair_mid, d_mid, d_logits, prods, g_tri_out, size.core, cols_here, channels_here
        )

    alignment_adjoint, coupling_adjoint, *sums = msa_back(
        msa_grad, d_lefts, d_right, d_mid, pair_sums
    )
    mine = [kept + lax.ppermute(given, "core", size.swap) for kept, given in sums]
    mine, alignment_adjoint, coupling_adjoint = size.sum_all(
        jnp.concatenate(mine, 0), alignment_adjoint, coupling_adjoint
    )
    other = lax.ppermute(mine, "core", size.swap)
    summed = call_spread_sums(mine, other, size.core, [w.shape for w in weights])
    return (
        msa_out,
        pair_out.reshape(residue_couplings.shape),
        alignment_adjoint,
        coupling_adjoint.reshape(residue_couplings.shape),
        *summed,
    )


def solution(mesh):
    mesh_rows, mesh_cols = mesh.shape["row"], mesh.shape["col"]

    def local(*arguments):
        return per_device(mesh_rows, mesh_cols, *arguments)

    split = jax.sharding.Mesh(
        mesh.devices.reshape(mesh_rows // 2, 2, mesh_cols), ("half", "core", "col")
    )
    whole = P()
    msa = P("col", row, None)
    pair = P(row, "col", None)
    return jax.shard_map(
        local,
        mesh=split,
        in_specs=(msa, pair, whole, msa, pair) + (whole,) * 18,
        out_specs=(msa, pair, msa, pair) + (whole,) * 18,
        check_vma=False,
    )
```

```python
import functools

import jax
import jax.numpy as jnp
from jax import lax
from jax.experimental import pallas as pl
from jax.experimental.pallas import tpu as pltpu
from jax.sharding import PartitionSpec as P

bf16, f32 = jnp.bfloat16, jnp.float32
NN = ((1,), (0,))
NT = ((1,), (1,))
TN = ((0,), (0,))


def one_pass(a, b, dims=NN):
    return lax.dot_general(a, b, (dims, ((), ())), preferred_element_type=f32)


def halves(x):
    high = x.astype(bf16)
    return high, (x - high.astype(f32)).astype(bf16)


def dot3(a, b, dims=NN):
    a_high, a_low = a if isinstance(a, tuple) else halves(a)
    b_high, b_low = b if isinstance(b, tuple) else halves(b)
    return one_pass(a_high, b_high, dims) + (
        one_pass(a_high, b_low, dims) + one_pass(a_low, b_high, dims)
    )


def rounded(pair, rows):
    return pair[0][rows], pair[1][rows]


def iota(shape, dim):
    return lax.broadcasted_iota(jnp.int32, shape, dim)


def norm_parts(x):
    centered = x - jnp.mean(x, axis=-1, keepdims=True)
    inverse = lax.rsqrt(jnp.mean(centered * centered, axis=-1, keepdims=True) + 1e-05)
    return centered * inverse, inverse


def norm_back(normed, inverse, grad):
    return inverse * (
        grad
        - jnp.mean(grad, axis=-1, keepdims=True)
        - normed * jnp.mean(grad * normed, axis=-1, keepdims=True)
    )


def stacked3(a, b, dims=NN):
    a_high, a_low = a if isinstance(a, tuple) else halves(a)
    b_high, b_low = b if isinstance(b, tuple) else halves(b)
    return one_pass(
        jnp.concatenate([a_high, a_low, a_high], dims[0][0]),
        jnp.concatenate([b_high, b_high, b_low], dims[1][0]),
        dims,
    )


def row_of(t, u):
    return 2 * t + u // 2 + 16 * (u % 2)


def same_slot(chains):
    shape = (chains * 8, 256)
    return (iota(shape, 0) & 7) == (iota(shape, 1) & 7)


def blocks_kernel(chains, first_ref, *refs):
    *part_refs, out_ref, left_ref = refs
    groups, count = chains // 4, len(part_refs)
    size = part_refs[0].shape[0]
    t = pl.program_id(0)

    @pl.when(t == 0)
    def _():
        for n, ref in enumerate(part_refs):
            place = lax.rem(first_ref[0] + count - n, count) * size
            left_ref[pl.ds(pl.multiple_of(place, 8), size), :] = ref[...]

    shape = (chains * 8, chains)
    chain = iota(shape, 0) >> 3
    lift = jnp.where(iota(shape, 1) == (chain & 3) * groups + (chain >> 2), 1.0, 0.0).astype(bf16)
    same = same_slot(chains)
    rows = [
        left_ref[pl.ds(pl.multiple_of(row_of(t, u) * groups, groups), groups), :] for u in range(4)
    ]
    rows = jnp.concatenate(halves(jnp.concatenate(rows, 0)), 0)
    shape = (128, 256)
    slabs = []
    for n in range(4):
        spread = ((iota(shape, 0) >> 5) == n) & ((iota(shape, 0) & 31) == (iota(shape, 1) >> 3))
        slabs.append(one_pass(rows, jnp.where(spread, 1.0, 0.0).astype(bf16)))
    for part in range(2):
        for u in range(4):
            place = slice((part * 4 + u) * groups, (part * 4 + u + 1) * groups)
            slab = jnp.concatenate([x[place] for x in slabs], 0).astype(bf16)
            out_ref[0, u, part] = jnp.where(same, one_pass(lift, slab), 0.0).astype(bf16)


def call_blocks(first, parts):
    rows = sum(part.shape[0] for part in parts)
    chains = rows // 32 * 4
    shape = (8, 4, 2, chains * 8, 256)
    return pl.pallas_call(
        functools.partial(blocks_kernel, chains),
        grid=(8,),
        in_specs=[pl.BlockSpec(memory_space=pltpu.SMEM)] + [full(part) for part in parts],
        out_specs=step_block(shape),
        out_shape=jax.ShapeDtypeStruct(shape, bf16),
        scratch_shapes=[pltpu.VMEM((rows, 128), f32)],
        compiler_params=params(),
        name="blocks",
    )(first, *parts)


def join_right(ref, out_ref):
    cols = ref.shape[0] * 8
    for g in range(4):
        for n in range(ref.shape[2]):
            out_ref[g * cols : (g + 1) * cols, n * 128 : (n + 1) * 128] = ref[:, g, n].reshape(
                cols, 128
            )


def cut_right(ref, out_ref):
    cols = out_ref.shape[0] * 8
    for g in range(4):
        for n in range(out_ref.shape[2]):
            tile = ref[g * cols : (g + 1) * cols, n * 128 : (n + 1) * 128]
            out_ref[:, g, n] = tile.reshape(-1, 8, 128)


def outer_weights(ref, out_ref):
    whole = ref[...].reshape(32, 4, 8, 128)
    for g in range(4):
        out_ref[g, 0], out_ref[g, 1] = halves(whole[:, g].reshape(256, 128))


def params(mebibytes=56):
    return pltpu.CompilerParams(vmem_limit_bytes=mebibytes * 2**20)


def full(array):
    return pl.BlockSpec(array.shape, lambda t, n=len(array.shape): (0,) * n)


def step_block(shape):
    return pl.BlockSpec((1,) + shape[1:], lambda t, n=len(shape): (t,) + (0,) * (n - 1))


def pair_of(ref, *index):
    return ref[(*index, 0)], ref[(*index, 1)]


def chunk_order(shift):
    shape = (256, 256)
    place, width = iota(shape, 0), 1 << shift
    channel = place & 127
    target = ((channel >> shift) << (shift + 1)) + (channel & (width - 1))
    target = target + ((place >> 7) << shift)
    return jnp.where(iota(shape, 1) == target, 1.0, 0.0).astype(bf16)


def side_halves(shift, refs, out_ref):
    order = chunk_order(shift)
    for n in range(2):
        both = halves(jnp.concatenate([refs[2 * n][...], refs[2 * n + 1][...]], 1))
        for part in range(2):
            out_ref[part, :, n * 256 : (n + 1) * 256] = one_pass(both[part], order).astype(bf16)
    if len(refs) == 5:
        out_ref[0, :, 512:], out_ref[1, :, 512:] = halves(refs[4][...])


def edges_kernel(
    cols,
    shift,
    block_ref,
    right_ref,
    outer_ref,
    pair_ref,
    gate1_ref,
    gate2_ref,
    value1_ref,
    value2_ref,
    mid_ref,
    edge_ref,
    prod_ref,
    whole_ref,
    right_halves,
    outer_halves,
    sides_halves,
):
    t = pl.program_id(0)

    @pl.when(t == 0)
    def _():
        join_right(right_ref, whole_ref)
        right_halves[0], right_halves[1] = halves(whole_ref[...])
        outer_weights(outer_ref, outer_halves)
        side_halves(shift, (gate1_ref, gate2_ref, value1_ref, value2_ref), sides_halves)

    right = pair_of(right_halves)
    places = four_rows(t, cols)
    for u in range(4):
        high, low = halves(stacked3(right, pair_of(block_ref, 0, u)))
        for g in range(4):
            prod_ref[0, g, 0, u * cols : (u + 1) * cols] = high[g * cols : (g + 1) * cols]
            prod_ref[0, g, 1, u * cols : (u + 1) * cols] = low[g * cols : (g + 1) * cols]
    update = 0.0
    for g in range(4):
        update = update + stacked3(pair_of(prod_ref, 0, g), pair_of(outer_halves, g))
    mid = update + read_rows(pair_ref, places)
    write_rows(mid_ref, places, mid)
    normed, _ = norm_parts(mid)
    logits = dot3(normed, pair_of(sides_halves))
    write_turned(edge_ref, t, jax.nn.sigmoid(logits[:, :256]) * logits[:, 256:])


def call_edges(blocks, right, outer, pair, sides, cols, shift):
    rows, depth = pair.shape[0], blocks.shape[3]
    prods = (8, 4, 2, 4 * cols, 256)
    return pl.pallas_call(
        functools.partial(edges_kernel, cols, shift),
        grid=(8,),
        in_specs=[step_block(blocks.shape)] + [full(x) for x in (right, outer, pair, *sides)],
        out_specs=(
            pl.BlockSpec((rows, 128), lambda t: (0, 0)),
            pl.BlockSpec((256, 16, 128), lambda t: (0, 0, 0)),
            step_block(prods),
        ),
        out_shape=(
            jax.ShapeDtypeStruct((rows, 128), f32),
            jax.ShapeDtypeStruct((256, 16, 128), f32),
            jax.ShapeDtypeStruct(prods, bf16),
        ),
        scratch_shapes=[
            pltpu.VMEM((4 * cols, depth), f32),
            pltpu.VMEM((2, 4 * cols, depth), bf16),
            pltpu.VMEM((4, 2, 256, 128), bf16),
            pltpu.VMEM((2, 128, 512), bf16),
        ],
        compiler_params=params(),
        name="edges",
    )(blocks, right, outer, pair, *sides)


def join_tiles(chunks, mesh_rows, mesh_cols, out_ref):
    plain = chunks.reshape(mesh_rows * mesh_cols * 16, 128)
    rolled = pltpu.roll(plain, 64, 1)
    first = iota((16, 128), 1) < 64
    for r in range(mesh_rows):
        for t in range(mesh_cols // 2):
            even = slice((r * mesh_cols + 2 * t) * 16, (r * mesh_cols + 2 * t + 1) * 16)
            odd = slice((r * mesh_cols + 2 * t + 1) * 16, (r * mesh_cols + 2 * t + 2) * 16)
            lanes = slice(t * 128, (t + 1) * 128)
            out_ref[r * 32 : r * 32 + 16, lanes] = jnp.where(first, plain[even], rolled[odd])
            out_ref[r * 32 + 16 : r * 32 + 32, lanes] = jnp.where(first, rolled[even], plain[odd])


def cut_tiles(whole, mesh_rows, mesh_cols, store):
    first = iota((16, 128), 1) < 64
    for t in range(mesh_cols // 2):
        plain = whole[:, t * 128 : (t + 1) * 128]
        rolled = pltpu.roll(plain, 64, 1)
        for r in range(mesh_rows):
            low = slice(r * 32, r * 32 + 16)
            high = slice(r * 32 + 16, r * 32 + 32)
            store(r * mesh_cols + 2 * t, jnp.where(first, plain[low], rolled[high]))
            store(r * mesh_cols + 2 * t + 1, jnp.where(first, rolled[low], plain[high]))


def triangle_kernel(mesh_rows, mesh_cols, edge_ref, out_ref, left_ref, right_ref):
    join_tiles(edge_ref[:, 0, 0], mesh_rows, mesh_cols, left_ref)
    join_tiles(edge_ref[:, 1, 0], mesh_rows, mesh_cols, right_ref)

    def store(d, tile):
        out_ref[d, 0] = tile

    cut_tiles(dot3(left_ref[...], right_ref[...], NT), mesh_rows, mesh_cols, store)


def call_triangle(edges, mesh_rows, mesh_cols):
    devices, _, channels = edges.shape[:3]
    span = mesh_rows * 32
    return pl.pallas_call(
        functools.partial(triangle_kernel, mesh_rows, mesh_cols),
        grid=(channels,),
        in_specs=[pl.BlockSpec((devices, 2, 1, 16, 128), lambda n: (0, 0, n, 0, 0))],
        out_specs=pl.BlockSpec((devices, 1, 16, 128), lambda n: (0, n, 0, 0)),
        out_shape=jax.ShapeDtypeStruct((devices, channels, 16, 128), f32),
        scratch_shapes=[pltpu.VMEM((span, span), f32)] * 2,
        compiler_params=params(32),
        name="triangle",
    )(edges)


def triangle_back_kernel(
    mesh_rows, mesh_cols, edge_ref, grad_ref, out_ref, left_ref, right_ref, whole_ref
):
    join_tiles(edge_ref[:, 0, 0], mesh_rows, mesh_cols, left_ref)
    join_tiles(edge_ref[:, 1, 0], mesh_rows, mesh_cols, right_ref)
    join_tiles(grad_ref[:, 0], mesh_rows, mesh_cols, whole_ref)

    def store(kind):
        def put(d, tile):
            out_ref[d, kind, 0] = tile

        return put

    whole = whole_ref[...]
    cut_tiles(dot3(whole, right_ref[...]), mesh_rows, mesh_cols, store(0))
    cut_tiles(dot3(jnp.transpose(whole), left_ref[...]), mesh_rows, mesh_cols, store(1))


def call_triangle_back(edges, grad, mesh_rows, mesh_cols):
    devices, _, channels = edges.shape[:3]
    span = mesh_rows * 32
    both = pl.BlockSpec((devices, 2, 1, 16, 128), lambda n: (0, 0, n, 0, 0))
    return pl.pallas_call(
        functools.partial(triangle_back_kernel, mesh_rows, mesh_cols),
        grid=(channels,),
        in_specs=[both, pl.BlockSpec((devices, 1, 16, 128), lambda n: (0, n, 0, 0))],
        out_specs=both,
        out_shape=jax.ShapeDtypeStruct(edges.shape, f32),
        scratch_shapes=[pltpu.VMEM((span, span), f32)] * 3,
        compiler_params=params(32),
        name="triangle_back",
    )(edges, grad)


def four_rows(t, cols):
    return [
        pl.ds(pl.multiple_of((2 * t + u // 2 + 16 * (u % 2)) * cols, cols), cols) for u in range(4)
    ]


def read_rows(ref, places):
    return jnp.concatenate([ref[p, :] for p in places], 0)


def write_rows(ref, places, value):
    size = value.shape[0] // len(places)
    for u, p in enumerate(places):
        ref[p, :] = value[u * size : (u + 1) * size]


def read_turned(ref, t):
    parts = []
    for v in range(2):
        tile = ref[:, pl.ds(2 * t + v, 1), :]
        parts.append(jnp.transpose(tile.reshape(tile.shape[0], 128)))
    return jnp.concatenate(parts, 0)


def write_turned(ref, t, value):
    for v in range(2):
        turned = jnp.transpose(value[v * 128 : (v + 1) * 128])
        ref[:, pl.ds(2 * t + v, 1), :] = turned[:, None, :]


def finish_kernel(
    cols, tri_ref, mid_ref, grad_ref, gate_ref, proj_ref, out_ref, dtri_ref, dlogit_ref, dproj_ref
):
    gate_w = halves(gate_ref[...])
    proj_w = halves(proj_ref[...])
    dproj_ref[...] = jnp.zeros_like(dproj_ref)

    def step(t, carry):
        places = four_rows(t, cols)
        mid = read_rows(mid_ref, places)
        grad = read_rows(grad_ref, places)
        normed, _ = norm_parts(mid)
        tri, tri_inverse = norm_parts(read_turned(tri_ref, t))
        tri_halves = halves(tri)
        gate = jax.nn.sigmoid(dot3(normed, gate_w))
        value = dot3(tri_halves, proj_w)
        write_rows(out_ref, places, mid + gate * value)
        dvalue = halves(grad * gate)
        write_rows(dlogit_ref, places, grad * value * gate * (1.0 - gate))
        dproj_ref[...] += dot3(halves(jnp.transpose(tri)), dvalue)
        write_turned(dtri_ref, t, norm_back(tri, tri_inverse, dot3(dvalue, proj_w, NT)))
        return carry

    lax.fori_loop(0, 8, step, 0)


def call_finish(tri, mid, grad, gate, proj, cols):
    rows = mid.shape[0]
    return pl.pallas_call(
        functools.partial(finish_kernel, cols),
        out_shape=(
            jax.ShapeDtypeStruct((rows, 128), f32),
            jax.ShapeDtypeStruct((128, 16, 128), f32),
            jax.ShapeDtypeStruct((rows, 128), f32),
            jax.ShapeDtypeStruct((128, 128), f32),
        ),
        compiler_params=params(32),
        name="finish",
    )(tri, mid, grad, gate, proj)


def edges_back_kernel(
    cols,
    chains,
    shift,
    dedge_ref,
    mid_ref,
    grad_ref,
    dlogit_ref,
    gate1_ref,
    gate2_ref,
    value1_ref,
    value2_ref,
    gate3_ref,
    right_ref,
    outer_ref,
    block_ref,
    first_ref,
    dmid_ref,
    dlogits_ref,
    dright_ref,
    *refs,
):
    *dleft_refs, whole_ref, turned_halves, outer_halves, sides_halves, fold_ref, dslab_ref, dleft_ref = (
        refs
    )
    t = pl.program_id(0)

    @pl.when(t == 0)
    def _():
        join_right(right_ref, whole_ref)
        turned_halves[0], turned_halves[1] = halves(jnp.transpose(whole_ref[...]))
        outer_weights(outer_ref, outer_halves)
        refs = (gate1_ref, gate2_ref, value1_ref, value2_ref, gate3_ref)
        side_halves(shift, refs, sides_halves)
        shape = (256, 128)
        for u in range(4):
            lane = 64 * (u % 2) + 32 * (u // 2) + (iota(shape, 0) >> 3)
            fold = jnp.where(iota(shape, 1) == lane, 1.0, 0.0).astype(bf16)
            fold_ref[512 * u : 512 * u + 256] = fold
            fold_ref[512 * u + 256 : 512 * u + 512] = fold
        whole_ref[...] = jnp.zeros_like(whole_ref)

    same = same_slot(chains)
    sides = pair_of(sides_halves)
    places = four_rows(t, cols)
    normed, inverse = norm_parts(read_rows(mid_ref, places))
    logits = dot3(normed, rounded(sides, (slice(None), slice(0, 512))))
    gate, value = jax.nn.sigmoid(logits[:, :256]), logits[:, 256:]
    dedge = read_turned(dedge_ref, t)
    dlogits = [
        dedge * value * gate * (1.0 - gate),
        dedge * gate,
        read_rows(dlogit_ref, places),
    ]
    dlogits = halves(jnp.concatenate(dlogits, 1))
    dlogits_ref[0, 0], dlogits_ref[0, 1] = dlogits
    dmid = read_rows(grad_ref, places) + norm_back(normed, inverse, dot3(dlogits, sides, NT))
    write_rows(dmid_ref, places, dmid)
    dmid = halves(dmid)
    dprod = [halves(dot3(dmid, pair_of(outer_halves, g), NT)) for g in range(4)]
    here, diagonal = [], []
    turned = pair_of(turned_halves)
    for u in range(4):
        rows = slice(u * cols, (u + 1) * cols)
        here.append([jnp.concatenate([dprod[g][n][rows] for g in range(4)], 0) for n in range(2)])
        diagonal += halves(jnp.where(same, stacked3(turned, tuple(here[u])), 0.0))
    right_terms = [x for high, low in here for x in (high, low, high)]
    block_terms = [block_ref[0, u, n] for u in range(4) for n in (0, 0, 1)]
    whole_ref[...] += one_pass(
        jnp.concatenate(right_terms, 1), jnp.concatenate(block_terms, 1), NT
    )
    dslab = one_pass(jnp.concatenate(diagonal, 1), fold_ref[...])
    dslab_ref[t] = jnp.sum(dslab.reshape(chains, 8, 128), axis=1)

    @pl.when(t == 7)
    def _():
        cut_right(whole_ref, dright_ref)
        first = iota((chains, 128), 1) < 64
        for n in range(4):
            even, odd = dslab_ref[2 * n], dslab_ref[2 * n + 1]
            dleft_ref[n] = jnp.where(first, even, pltpu.roll(odd, 64, 1))
            dleft_ref[n + 4] = jnp.where(first, pltpu.roll(even, 64, 1), odd)
        count, size = len(dleft_refs), dleft_refs[0].shape[0]
        for n, ref in enumerate(dleft_refs):
            place = lax.rem(first_ref[0] + n, count) * size
            ref[...] = dleft_ref[pl.ds(place, size)]


def call_edges_back(
    dedge, mid, grad, dlogit, sides, right, outer, blocks, first, count, cols, shift
):
    rows, depth = mid.shape[0], blocks.shape[3]
    chains = depth // 8
    dlogits = (8, 2, 4 * cols, 640)
    return pl.pallas_call(
        functools.partial(edges_back_kernel, cols, chains, shift),
        grid=(8,),
        in_specs=[full(x) for x in (dedge, mid, grad, dlogit, *sides, right, outer)]
        + [step_block(blocks.shape), pl.BlockSpec(memory_space=pltpu.SMEM)],
        out_specs=(
            pl.BlockSpec((rows, 128), lambda t: (0, 0)),
            step_block(dlogits),
            full(right),
        )
        + (pl.BlockSpec((8 // count, chains, 128), lambda t: (0, 0, 0)),) * count,
        out_shape=(
            jax.ShapeDtypeStruct((rows, 128), f32),
            jax.ShapeDtypeStruct(dlogits, bf16),
            jax.ShapeDtypeStruct(right.shape, f32),
        )
        + (jax.ShapeDtypeStruct((8 // count, chains, 128), f32),) * count,
        scratch_shapes=[
            pltpu.VMEM((4 * cols, depth), f32),
            pltpu.VMEM((2, depth, 4 * cols), bf16),
            pltpu.VMEM((4, 2, 256, 128), bf16),
            pltpu.VMEM((2, 128, 640), bf16),
            pltpu.VMEM((2048, 128), bf16),
            pltpu.VMEM((8, chains, 128), f32),
            pltpu.VMEM((8, chains, 128), f32),
        ],
        compiler_params=params(),
        name="edges_back",
    )(dedge, mid, grad, dlogit, *sides, right, outer, blocks, first)


def give_halves(core_ref, whole_ref, mine_ref, other_ref):
    mine_ref[...] = whole_ref[core_ref[0]]
    other_ref[...] = whole_ref[1 - core_ref[0]]


def side_sums_kernel(
    cols,
    shift,
    mid_ref,
    dlogits_ref,
    first_ref,
    core_ref,
    mine_ref,
    other_ref,
    sides_ref,
    whole_ref,
):
    t = pl.program_id(0)

    @pl.when(t == 0)
    def _():
        sides_ref[...] = jnp.zeros_like(sides_ref)

    normed, _ = norm_parts(read_rows(mid_ref, four_rows(t, cols)))
    sides_ref[...] += stacked3(halves(jnp.transpose(normed)), pair_of(dlogits_ref, 0))

    @pl.when(t == 7)
    def _():
        order = chunk_order(shift)
        for n in range(2):
            high, low = halves(sides_ref[:, n * 256 : (n + 1) * 256])
            sides = one_pass(high, order, NT) + one_pass(low, order, NT)
            for side in range(2):
                place = 2 * n + side
                rows = slice(place % 3 * 128, place % 3 * 128 + 128)
                whole_ref[place // 3, rows] = sides[:, side * 128 : (side + 1) * 128]
        whole_ref[1, 128:256] = sides_ref[:, 512:]
        whole_ref[1, 256:] = first_ref[...]
        give_halves(core_ref, whole_ref, mine_ref, other_ref)


def call_side_sums(mid, dlogits, first, core, cols, shift):
    return pl.pallas_call(
        functools.partial(side_sums_kernel, cols, shift),
        grid=(8,),
        in_specs=[full(mid), step_block(dlogits.shape), full(first)]
        + [pl.BlockSpec(memory_space=pltpu.SMEM)],
        out_specs=(pl.BlockSpec((384, 128), lambda t: (0, 0)),) * 2,
        out_shape=(jax.ShapeDtypeStruct((384, 128), f32),) * 2,
        scratch_shapes=[pltpu.VMEM((128, 640), f32), pltpu.VMEM((2, 384, 128), f32)],
        compiler_params=params(),
        name="side_sums",
    )(mid, dlogits, first, core)


def outer_sums_kernel(
    cols, dmid_ref, prod_ref, core_ref, mine_ref, other_ref, outer_ref, whole_ref
):
    t = pl.program_id(0)

    @pl.when(t == 0)
    def _():
        outer_ref[...] = jnp.zeros_like(outer_ref)

    dmid = halves(jnp.transpose(read_rows(dmid_ref, four_rows(t, cols))))
    for g in range(4):
        outer_ref[:, g * 256 : (g + 1) * 256] += stacked3(dmid, pair_of(prod_ref, 0, g))

    @pl.when(t == 7)
    def _():
        for g in range(4):
            tile = jnp.transpose(outer_ref[:, g * 256 : (g + 1) * 256]).reshape(32, 8, 128)
            for p in range(32):
                start = p % 16 * 32 + g * 8
                whole_ref[p // 16, start : start + 8] = tile[p]
        give_halves(core_ref, whole_ref, mine_ref, other_ref)


def call_outer_sums(dmid, prods, core, cols):
    return pl.pallas_call(
        functools.partial(outer_sums_kernel, cols),
        grid=(8,),
        in_specs=[full(dmid), step_block(prods.shape), pl.BlockSpec(memory_space=pltpu.SMEM)],
        out_specs=(pl.BlockSpec((512, 128), lambda t: (0, 0)),) * 2,
        out_shape=(jax.ShapeDtypeStruct((512, 128), f32),) * 2,
        scratch_shapes=[pltpu.VMEM((128, 1024), f32), pltpu.VMEM((2, 512, 128), f32)],
        compiler_params=params(),
        name="outer_sums",
    )(dmid, prods, core)


def pack_heads(y, store):
    lane = iota((1, 1, 128), 2) >> 5
    for tile in range(y.shape[1] // 128):
        part = y[:, tile * 128 : (tile + 1) * 128]
        turned = [part] + [pltpu.roll(part, 32 * n, 1) for n in range(1, 4)]
        turned = [x.reshape(-1, 4, 8, 128) for x in turned]
        for head in range(4):
            out = turned[-head % 4][:, 0]
            for chain in range(1, 4):
                out = jnp.where(lane == chain, turned[(chain - head) % 4][:, chain], out)
            store(tile * 4 + head, out)


def unpack_heads(load, heads):
    lane = iota((1, 1, 128), 2) >> 5
    tiles = []
    for tile in range(heads // 4):
        turned = []
        for head in range(4):
            part = load(tile * 4 + head)
            flat = part.reshape(-1, 128)
            turned.append(
                [part] + [pltpu.roll(flat, 32 * n, 1).reshape(part.shape) for n in range(1, 4)]
            )
        chains = []
        for chain in range(4):
            out = turned[0][-chain % 4]
            for head in range(1, 4):
                out = jnp.where(lane == head, turned[head][(head - chain) % 4], out)
            chains.append(out[:, None])
        tiles.append(jnp.concatenate(chains, 1).reshape(-1, 128))
    return jnp.concatenate(tiles, 1)


def head_lanes(tile, n):
    return jnp.where((iota((1, 128), 1) >> 5) == n, tile, 0.0)


def soft(scores, seen=None):
    if seen is not None:
        scores = jnp.where(seen, scores, -1e30)
    weights = jnp.exp(scores - jnp.max(scores, axis=-1, keepdims=True))
    if seen is not None:
        weights = jnp.where(seen, weights, 0.0)
    return weights * (1.0 / jnp.sum(weights, axis=-1, keepdims=True))


def soft_back(weights, grad):
    return weights * (grad - jnp.sum(weights * grad, axis=-1, keepdims=True))


def stripe_seen(present_ref):
    tokens = present_ref.shape[1]
    shape = (tokens, tokens)
    same = (iota(shape, 0) & 7) == (iota(shape, 1) & 7)
    return same & (present_ref[...] > 0.0)


def column_attention(q, k, v, seen):
    weights, tiles = [], []
    for tile in range(q.shape[1] // 128):
        lanes = slice(tile * 128, (tile + 1) * 128)
        keys, values = halves(k[:, lanes]), halves(v[:, lanes])
        blend = 0.0
        for n in range(4):
            weights.append(soft(dot3(head_lanes(q[:, lanes], n), keys, NT), seen))
            blend = blend + head_lanes(dot3(weights[-1], values), n)
        tiles.append(blend)
    return weights, jnp.concatenate(tiles, 1)


def columns_kernel(
    scale,
    x_ref,
    present_ref,
    bias_ref,
    q_ref,
    k_ref,
    v_ref,
    o_ref,
    q2_ref,
    k2_ref,
    v2_ref,
    out_ref,
    qkv_ref,
):
    x = x_ref[...]
    normed, _ = norm_parts(x)
    normed = halves(normed)
    q, k, v = (dot3(normed, halves(w[...])) for w in (q_ref, k_ref, v_ref))
    _, blend = column_attention(q * scale, k, v, stripe_seen(present_ref))
    out = x + dot3(blend, halves(o_ref[...]))
    out_ref[...] = out
    normed, _ = norm_parts(out)
    normed = halves(normed)
    groups, size = qkv_ref.shape[0] // 8, (qkv_ref.shape[1] - 16) // 3
    qkv_ref[:, -16:] = bias_ref[...]

    def store(kind):
        def put(head, value):
            place = slice(head * groups, (head + 1) * groups)
            rows = slice(kind * size, (kind + 1) * size)
            qkv_ref[place, rows] = value.reshape(groups, size, 128)

        return put

    for kind, w in enumerate((q2_ref, k2_ref, v2_ref)):
        pack_heads(dot3(normed, halves(w[...])), store(kind))


def call_columns(x, present, bias, weights, group_chains, scale):
    return pl.pallas_call(
        functools.partial(columns_kernel, scale),
        out_shape=(
            jax.ShapeDtypeStruct(x.shape, f32),
            jax.ShapeDtypeStruct((bias.shape[0], 6 * group_chains + 16, 128), f32),
        ),
        compiler_params=params(24),
        name="columns",
    )(x, present, bias, *weights)


def packed_parts(ref):
    parts = (ref.shape[1] - 16) // 24
    for half in range(parts):
        places = [(kind * parts + half) * 8 for kind in range(3)]
        yield half, places, [ref[:, p : p + 8].reshape(-1, 128) for p in places]


def rows_kernel(mesh_rows, mesh_cols, scale, qkv_ref, out_ref, whole_ref):
    join_tiles(qkv_ref[:, -16:], mesh_rows, mesh_cols, whole_ref)
    bias = whole_ref[...]
    for half, _, (q, k, v) in packed_parts(qkv_ref):
        k, v, q = halves(k), halves(v), q * scale
        blend = 0.0
        for n in range(4):
            weights = soft(dot3(head_lanes(q, n), k, NT) + bias)
            blend = blend + head_lanes(dot3(weights, v), n)
        out_ref[:, half] = blend.reshape(-1, 8, 128)


def call_rows(qkv, mesh_rows, mesh_cols, scale):
    devices, parts = qkv.shape[0], (qkv.shape[1] - 16) // 24
    span = mesh_rows * 32
    return pl.pallas_call(
        functools.partial(rows_kernel, mesh_rows, mesh_cols, scale),
        out_shape=jax.ShapeDtypeStruct((devices, parts, 8, 128), f32),
        scratch_shapes=[pltpu.VMEM((span, span), f32)],
        compiler_params=params(24),
        name="rows",
    )(qkv)


def load_heads(ref, kind=None):
    def load(head):
        groups = ref.shape[0] // 8
        place = slice(head * groups, (head + 1) * groups)
        part = ref[place] if kind is None else ref[place, kind]
        return part.reshape(-1, 8, 128)

    return load


def side_copies(source_ref, target_ref):
    both = halves(jnp.concatenate([source_ref[...], target_ref[...]], 0))
    shape = (640, 64)
    place = iota(shape, 0) - 128
    feature = jnp.where(place < 0, place & 31, 32 + ((place >> 7) << 3) + (place & 7))
    copies = jnp.where(iota(shape, 1) == feature, 1.0, 0.0).astype(bf16)
    return tuple(one_pass(copies, part).astype(bf16) for part in both)


def rows_out_kernel(
    blend_ref, mid_ref, share_ref, o_ref, source_ref, target_ref, out_ref, left_ref, right_ref
):
    blend = unpack_heads(load_heads(blend_ref), 8)
    out = mid_ref[...] + dot3(blend, halves(o_ref[...]))
    out_ref[...] = out
    normed, _ = norm_parts(out)
    wide = dot3(normed, side_copies(source_ref, target_ref), NT)
    left = (wide[:, :128] * share_ref[...]).reshape(-1, 4, 8, 128)
    lane = iota((1, 1, 128), 2)
    packed = left[:, 0]
    for chain in range(1, 4):
        packed = jnp.where((lane >> 5) == chain, left[:, chain], packed)
    for n in range(packed.shape[0]):
        left_ref[:, n, :] = packed[n]
    for g in range(4):
        right = wide[:, (g + 1) * 128 : (g + 2) * 128].reshape(-1, 16, 8, 128)
        packed = right[:, 0]
        for chain in range(1, 16):
            packed = jnp.where((lane >> 3) == chain, right[:, chain], packed)
        right_ref[g] = packed


def call_rows_out(blend, mid, share, weight, source, target):
    chains = mid.shape[0] // 8
    return pl.pallas_call(
        rows_out_kernel,
        out_shape=(
            jax.ShapeDtypeStruct(mid.shape, f32),
            jax.ShapeDtypeStruct((8, chains // 4, 128), f32),
            jax.ShapeDtypeStruct((4, chains // 16, 8, 128), f32),
        ),
        compiler_params=params(),
        name="rows_out",
    )(blend, mid, share, weight, source, target)


def rows_out_back_kernel(*refs):
    *dleft_refs, dright_ref, grad_ref, out_ref, blend_ref, share_ref = refs[:-10]
    o_ref, source_ref, target_ref = refs[-10:-7]
    core_ref, dout_ref, dblend_ref, thin_ref, mine_ref, other_ref, sum_ref = refs[-7:]
    lane = iota((1, 1, 128), 2)
    chains = grad_ref.shape[0] // 8
    dleft = functools.reduce(jnp.add, [ref[...] for ref in dleft_refs])
    shape = (chains * 8, 128)
    slot = iota(shape, 0) & 7
    copy = (chains * 8, chains)
    copy = jnp.where((iota(copy, 0) >> 3) == iota(copy, 1), 1.0, 0.0).astype(bf16)
    left = 0.0
    for n in range(2):
        high, low = halves(dleft[n])
        spot = (slot >> 2 == n) & (slot & 3 == iota(shape, 1) >> 5)
        left = left + jnp.where(spot, one_pass(copy, high) + one_pass(copy, low), 0.0)
    wide = [left * share_ref[...]]
    dright = dright_ref[...]
    for g in range(4):
        part = [jnp.where((lane >> 3) == n, dright[g], 0.0)[:, None] for n in range(16)]
        wide.append(jnp.concatenate(part, 1).reshape(-1, 128))
    wide = halves(jnp.concatenate(wide, 1))
    normed, inverse = norm_parts(out_ref[...])
    dsides = halves(dot3(halves(jnp.transpose(normed)), wide))
    shape = (640, 128)
    place, spot = iota(shape, 0) - 128, iota(shape, 1)
    target = jnp.where(place < 0, place & 31, 32 + ((place >> 7) << 3) + (place & 7))
    fold = jnp.where(target == spot, 1.0, 0.0).astype(bf16)
    thin_ref[...] = one_pass(dsides[0], fold) + one_pass(dsides[1], fold)
    dout = grad_ref[...] + norm_back(normed, inverse, dot3(wide, side_copies(source_ref, target_ref)))
    dout_ref[...] = dout
    dout = halves(dout)
    groups = dblend_ref.shape[0] // 8

    def store(head, value):
        dblend_ref[head * groups : (head + 1) * groups] = value.reshape(groups, -1, 8, 128)

    pack_heads(dot3(dout, halves(o_ref[...]), NT), store)
    blend = unpack_heads(load_heads(blend_ref), 8)
    write_halves(sum_ref, 0, dot3(halves(jnp.transpose(blend)), dout))
    give_halves(core_ref, sum_ref, mine_ref, other_ref)


def call_rows_out_back(dlefts, dright, grad, out, blend, share, weight, source, target, core):
    shapes, scratch = halves_shapes([weight])
    return pl.pallas_call(
        rows_out_back_kernel,
        out_shape=(
            jax.ShapeDtypeStruct(grad.shape, f32),
            jax.ShapeDtypeStruct(blend.shape, f32),
            jax.ShapeDtypeStruct((256, 128), f32),
        )
        + shapes,
        in_specs=specs(len(dlefts) + 8),
        scratch_shapes=[scratch],
        compiler_params=params(),
        name="rows_out_back",
    )(*dlefts, dright, grad, out, blend, share, weight, source, target, core)


def rows_back_kernel(
    mesh_rows, mesh_cols, scale, qkv_ref, dblend_ref, out_ref, whole_ref
):
    join_tiles(qkv_ref[:, -16:], mesh_rows, mesh_cols, whole_ref)
    bias = whole_ref[...]
    dbias = 0.0
    for half, places, (q, k, v) in packed_parts(qkv_ref):
        k, v, q = halves(k), halves(v), q * scale
        grad = dblend_ref[:, half].reshape(-1, 128)
        dq, dk, dv = 0.0, 0.0, 0.0
        for n in range(4):
            query, dblend = halves(head_lanes(q, n)), halves(head_lanes(grad, n))
            weights = soft(dot3(query, k, NT) + bias)
            dv = dv + dot3(halves(jnp.transpose(weights)), dblend)
            dscores = soft_back(weights, dot3(dblend, v, NT))
            dbias = dbias + dscores
            dk = dk + dot3(halves(jnp.transpose(dscores)), query)
            dq = dq + head_lanes(dot3(dscores, k), n)
        for place, value in zip(places, (dq * scale, dk, dv)):
            out_ref[:, place : place + 8] = value.reshape(-1, 8, 128)

    def store(d, tile):
        out_ref[d, -16:] = tile

    cut_tiles(dbias, mesh_rows, mesh_cols, store)


def call_rows_back(qkv, dblend, mesh_rows, mesh_cols, scale):
    span = mesh_rows * 32
    return pl.pallas_call(
        functools.partial(rows_back_kernel, mesh_rows, mesh_cols, scale),
        out_shape=jax.ShapeDtypeStruct(qkv.shape, f32),
        scratch_shapes=[pltpu.VMEM((span, span), f32)],
        compiler_params=params(24),
        name="rows_back",
    )(qkv, dblend)


def write_halves(ref, n, value):
    height = value.shape[0]
    for half in range(2):
        ref[half, n * height : (n + 1) * height] = value[:, half * 128 : (half + 1) * 128]


def projections_back(normed, inverse, grads, weight_refs, sum_ref):
    turned = halves(jnp.transpose(normed))
    dnormed = 0.0
    for n, (grad, w) in enumerate(zip(grads, weight_refs)):
        grad = halves(grad)
        write_halves(sum_ref, n, dot3(turned, grad))
        dnormed = dnormed + dot3(grad, halves(w[...]), NT)
    return norm_back(normed, inverse, dnormed)


def rows_in_back_kernel(
    dqkv_ref, mid_ref, grad_ref, q_ref, k_ref, v_ref, core_ref, dmid_ref, mine_ref, other_ref, sum_ref
):
    groups, size = dqkv_ref.shape[0] // 8, (dqkv_ref.shape[1] - 16) // 3

    def load(kind):
        place = slice(kind * size, (kind + 1) * size)
        return lambda head: dqkv_ref[head * groups : (head + 1) * groups, place].reshape(-1, 8, 128)

    grads = [unpack_heads(load(kind), 8) for kind in range(3)]
    normed, inverse = norm_parts(mid_ref[...])
    dmid_ref[...] = grad_ref[...] + projections_back(
        normed, inverse, grads, (q_ref, k_ref, v_ref), sum_ref
    )
    give_halves(core_ref, sum_ref, mine_ref, other_ref)


def halves_shapes(weights):
    rows = sum(w.size for w in weights) // 256
    return (jax.ShapeDtypeStruct((rows, 128), f32),) * 2, pltpu.VMEM((2, rows, 128), f32)


def specs(count):
    vmem = pl.BlockSpec(memory_space=pltpu.VMEM)
    return [vmem] * count + [pl.BlockSpec(memory_space=pltpu.SMEM)]


def call_rows_in_back(dqkv, mid, grad, weights, core):
    shapes, scratch = halves_shapes(weights)
    return pl.pallas_call(
        rows_in_back_kernel,
        in_specs=specs(6),
        out_shape=(jax.ShapeDtypeStruct(mid.shape, f32),) + shapes,
        scratch_shapes=[scratch],
        compiler_params=params(24),
        name="rows_in_back",
    )(dqkv, mid, grad, *weights, core)


def columns_back_kernel(
    scale,
    x_ref,
    present_ref,
    grad_ref,
    q_ref,
    k_ref,
    v_ref,
    o_ref,
    core_ref,
    dx_ref,
    mine_ref,
    other_ref,
    sum_ref,
):
    normed, inverse = norm_parts(x_ref[...])
    normed_halves = halves(normed)
    q, k, v = (dot3(normed_halves, halves(w[...])) for w in (q_ref, k_ref, v_ref))
    q = q * scale
    weights, blend = column_attention(q, k, v, stripe_seen(present_ref))
    grad = grad_ref[...]
    grad_halves = halves(grad)
    write_halves(sum_ref, 3, dot3(halves(jnp.transpose(blend)), grad_halves))
    dblend = dot3(grad_halves, halves(o_ref[...]), NT)
    tiles = [[], [], []]
    for tile in range(q.shape[1] // 128):
        lanes = slice(tile * 128, (tile + 1) * 128)
        keys, values = halves(k[:, lanes]), halves(v[:, lanes])
        dq, dk, dv = 0.0, 0.0, 0.0
        for n in range(4):
            query = halves(head_lanes(q[:, lanes], n))
            dhead = halves(head_lanes(dblend[:, lanes], n))
            share = weights[tile * 4 + n]
            dv = dv + dot3(halves(jnp.transpose(share)), dhead)
            dscores = soft_back(share, dot3(dhead, values, NT))
            dk = dk + dot3(halves(jnp.transpose(dscores)), query)
            dq = dq + head_lanes(dot3(dscores, keys), n)
        for kind, value in enumerate((dq * scale, dk, dv)):
            tiles[kind].append(value)
    grads = [jnp.concatenate(t, 1) for t in tiles]
    dx_ref[...] = grad + projections_back(
        normed, inverse, grads, (q_ref, k_ref, v_ref), sum_ref
    )
    give_halves(core_ref, sum_ref, mine_ref, other_ref)


def call_columns_back(x, present, grad, weights, core, scale):
    shapes, scratch = halves_shapes(weights)
    return pl.pallas_call(
        functools.partial(columns_back_kernel, scale),
        in_specs=specs(7),
        out_shape=(jax.ShapeDtypeStruct(x.shape, f32),) + shapes,
        scratch_shapes=[scratch],
        compiler_params=params(24),
        name="columns_back",
    )(x, present, grad, *weights, core)


def bias_kernel(cols, pair_ref, weight_ref, out_ref):
    weight = halves(weight_ref[...])

    def step(t, carry):
        rows = halves(read_rows(pair_ref, four_rows(t, cols)))
        heads = dot3(weight, rows, NT)
        for v in range(2):
            tile = heads[:, v * 128 : (v + 1) * 128][:, None, :]
            for g in range(out_ref.shape[1]):
                out_ref[:, g, pl.ds(2 * t + v, 1), :] = tile
        return carry

    lax.fori_loop(0, 8, step, 0)


def call_bias(pair, weight, copies, cols):
    return pl.pallas_call(
        functools.partial(bias_kernel, cols),
        out_shape=jax.ShapeDtypeStruct((weight.shape[0], copies, 16, 128), f32),
        compiler_params=params(24),
        name="bias",
    )(pair, weight)


def bias_rows(dbias):
    heads, groups, rows = dbias.shape[:3]
    return pl.BlockSpec((heads, groups, 16, 128), lambda t: (0, 0, rows // 16 - 1, 0))


def head_rows(ref, t):
    heads = [ref[:, pl.ds(2 * t + v, 1), :].reshape(-1, 128) for v in range(2)]
    return jnp.concatenate(heads, 1)


def bias_sums_kernel(
    cols, dbias_ref, pair_ref, thin_ref, core_ref, mine_ref, other_ref, whole_ref, sum_ref, dweight_ref
):
    sum_ref[...] = jnp.sum(dbias_ref[...], axis=1)
    dweight_ref[...] = jnp.zeros_like(dweight_ref)

    def step(t, carry):
        dweight_ref[...] += dot3(head_rows(sum_ref, t), read_rows(pair_ref, four_rows(t, cols)))
        return carry

    lax.fori_loop(0, 8, step, 0)
    whole_ref[0], whole_ref[1] = thin_ref[:128], thin_ref[128:]
    whole_ref[0, :, 64 : 64 + dweight_ref.shape[0]] = jnp.transpose(dweight_ref[...])
    give_halves(core_ref, whole_ref, mine_ref, other_ref)


def call_bias_sums(dbias, pair, thin, core, cols):
    heads = dbias.shape[0]
    return pl.pallas_call(
        functools.partial(bias_sums_kernel, cols),
        grid=(1,),
        in_specs=[bias_rows(dbias), full(pair), full(thin), pl.BlockSpec(memory_space=pltpu.SMEM)],
        out_specs=(pl.BlockSpec((128, 128), lambda t: (0, 0)),) * 2,
        out_shape=(jax.ShapeDtypeStruct((128, 128), f32),) * 2,
        scratch_shapes=[
            pltpu.VMEM((2, 128, 128), f32),
            pltpu.VMEM((heads, 16, 128), f32),
            pltpu.VMEM((heads, 128), f32),
        ],
        compiler_params=params(24),
        name="bias_sums",
    )(dbias, pair, thin, core)


def bias_back_kernel(cols, dbias_ref, dmid_ref, weight_ref, out_ref, sum_ref):
    weight = halves(weight_ref[...])
    sum_ref[...] = jnp.sum(dbias_ref[...], axis=1)

    def step(t, carry):
        places = four_rows(t, cols)
        dpair = dot3(jnp.transpose(head_rows(sum_ref, t)), weight)
        write_rows(out_ref, places, read_rows(dmid_ref, places) + dpair)
        return carry

    lax.fori_loop(0, 8, step, 0)


def call_bias_back(dbias, dmid, weight, cols):
    return pl.pallas_call(
        functools.partial(bias_back_kernel, cols),
        grid=(1,),
        in_specs=[bias_rows(dbias), full(dmid), full(weight)],
        out_specs=full(dmid),
        out_shape=jax.ShapeDtypeStruct(dmid.shape, f32),
        scratch_shapes=[pltpu.VMEM((dbias.shape[0], 16, 128), f32)],
        compiler_params=params(24),
        name="bias_back",
    )(dbias, dmid, weight)


def spread_sums_kernel(mine_ref, other_ref, core_ref, *outs):
    def place(first, second):
        for half, ref in enumerate((first, second)):
            lanes = slice(half * 128, (half + 1) * 128)
            for n, target in enumerate((0, 1, 2, 3, 4, 5, 6, 8)):
                outs[target][:, lanes] = ref[n * 256 : (n + 1) * 256]
        thin = jnp.transpose(jnp.concatenate([first[2048:2176], second[2048:2176]], 0))
        outs[7][...] = thin[64 : 64 + outs[7].shape[0], :128]
        outs[9][...] = thin[:32]
        outs[10][...] = thin[32:64]
        for half, ref in enumerate((first, second)):
            for n, target in enumerate(((13, 15, 12), (14, 16, 17))[half]):
                outs[target][...] = ref[2176 + n * 128 : 2304 + n * 128]
            outs[11][half * 512 : (half + 1) * 512] = ref[2560:3072]

    @pl.when(core_ref[0] == 0)
    def _():
        place(mine_ref, other_ref)

    @pl.when(core_ref[0] != 0)
    def _():
        place(other_ref, mine_ref)


def call_spread_sums(mine, other, core, shapes):
    thin = (7, 9, 10)
    shapes = [shape[::-1] if n in thin else shape for n, shape in enumerate(shapes)]
    sums = pl.pallas_call(
        spread_sums_kernel,
        in_specs=specs(2),
        out_shape=tuple(jax.ShapeDtypeStruct(shape, f32) for shape in shapes),
        compiler_params=params(24),
        name="spread_sums",
    )(mine, other, core)
    return [jnp.transpose(x) if n in thin else x for n, x in enumerate(sums)]


precise = lax.Precision.HIGH
everyone = ("half", "core", "col")
row = ("half", "core")
chips = ("half", "col")


def affine_map(tensor, weight):
    return jnp.einsum("...a,ab->...b", tensor, weight, precision=precise)


def exchange(chunks, axis):
    shape = chunks.shape
    flat = chunks.reshape(shape[0], -1, 128)
    return lax.all_to_all(flat, axis, 0, 0, tiled=True).reshape(shape)


def collect(block, axis, count):
    return exchange(jnp.broadcast_to(block[None], (count,) + block.shape), axis)


def tall(weight):
    return jnp.concatenate([weight[:, :128], weight[:, 128:]], 0)


def together(*arrays):
    return lax.optimization_barrier(arrays)


class Layout:
    def __init__(self, mesh_rows, mesh_cols, pair, chains, heads, head_width):
        self.mesh_rows, self.mesh_cols = mesh_rows, mesh_cols
        self.devices = mesh_rows * mesh_cols
        self.rows_here, self.cols_here, self.pair_width = pair
        self.span = self.rows_here * mesh_rows
        self.slim = self.span // self.devices
        self.chains, self.heads, self.head_width = chains, heads, head_width
        self.chain_groups = self.devices // heads
        self.group_chains = chains // self.chain_groups
        self.channels_here = self.pair_width // self.devices
        self.scale = head_width ** (-0.5)
        self.turn = [
            (g, (g % mesh_rows) * mesh_cols + g // mesh_rows) for g in range(self.devices)
        ]
        self.turn_back = [(b, a) for a, b in self.turn]

        self.swap = [(0, 1), (1, 0)]
        self.core = lax.axis_index("core").reshape(1)

    def to_slim(self, x):
        return lax.all_to_all(x, "col", 1, 0, tiled=True)

    def both_views(self, grad, out):
        count, slim, width = self.mesh_cols, self.slim, grad.shape[2]
        grad = jnp.transpose(grad.reshape(-1, count, slim, width), (1, 0, 2, 3))
        both = jnp.stack([grad, out.reshape(count, -1, slim, width)], 1)
        return both.reshape(count, -1, width)

    def split_views(self, both):
        count, slim, width = self.mesh_cols, self.slim, both.shape[2]
        both = both.reshape(count, 2, -1, slim, width)
        out = jnp.transpose(both[:, 1], (1, 0, 2, 3)).reshape(-1, count * slim, width)
        return both[:, 0].reshape(-1, slim, width), out

    def from_slim_permuted(self, x):
        count, slim = self.mesh_cols, x.shape[1]
        here = lax.axis_index("col")
        blocks = x.reshape(count, -1, slim, x.shape[2])
        out = jnp.zeros((blocks.shape[1], count * slim, x.shape[2]), f32)
        for n in range(count):
            block = lax.dynamic_index_in_dim(blocks, lax.rem(here + n, count), 0, False)
            if n:
                block = lax.ppermute(block, "col", [(s, (s + n) % count) for s in range(count)])
            source = lax.rem(here + count - n, count)
            out = lax.dynamic_update_slice_in_dim(out, block, source * slim, 1)
        return out

    def from_others(self, arrays):
        count = self.mesh_cols
        return [
            lax.ppermute(x, "col", [(s, (s + n) % count) for s in range(count)]) if n else x
            for n, x in enumerate(arrays)
        ]

    def sum_all(self, mine, *beside):
        half = self.mesh_rows // 2
        part = exchange(mine.reshape(half, -1, 128), "half").sum(0)
        part = exchange(part.reshape(self.mesh_cols, -1, 128), "col").sum(0)
        part, *beside = together(part, *beside)
        part = collect(part, "col", self.mesh_cols).reshape(-1, 128)
        return collect(part, "half", half).reshape(-1, 128), *beside


def msa_plain(size, alignment_features, residue_couplings, present, weights):
    chains, slim, heads, head_width = size.chains, size.slim, size.heads, size.head_width
    devices, groups, group_chains = size.devices, size.chain_groups, size.group_chains
    rows_here, cols_here, span = size.rows_here, size.cols_here, size.span
    mesh_rows, mesh_cols = size.mesh_rows, size.mesh_cols
    bias = jnp.transpose(affine_map(residue_couplings, weights[7]), (2, 0, 1))
    bias = jnp.broadcast_to(bias[:, None], (heads, groups, rows_here, cols_here))
    bias = exchange(bias.reshape(devices, rows_here, cols_here), everyone)
    bias = bias.reshape(mesh_rows, mesh_cols, rows_here, cols_here)
    bias = jnp.transpose(bias, (0, 2, 1, 3)).reshape(span, span)

    stripe = size.to_slim(alignment_features)
    normed, _ = norm_parts(stripe)
    col_q, col_k, col_v = (
        affine_map(normed, w).reshape(chains, slim, heads, head_width) for w in weights[:3]
    )
    scores = jnp.einsum("sihd,tihd->ihst", col_q, col_k, precision=precise) * size.scale
    scores = jnp.where(present[None, None, None, :] > 0, scores, -1000000000.0)
    blend = jnp.einsum(
        "ihst,tihd->sihd", jax.nn.softmax(scores, axis=-1), col_v, precision=precise
    )
    msa_col = stripe + affine_map(blend.reshape(chains, slim, heads * head_width), weights[3])

    normed, _ = norm_parts(msa_col)
    qkv = jnp.stack([affine_map(normed, w) for w in weights[4:7]])
    qkv = qkv.reshape(3, groups, group_chains, slim, heads, head_width)
    qkv = jnp.transpose(qkv, (4, 1, 0, 2, 3, 5))
    qkv = exchange(qkv.reshape(devices, 3, group_chains, slim, head_width), everyone)
    qkv = jnp.transpose(qkv, (1, 2, 0, 3, 4)).reshape(3, group_chains, span, head_width)
    scores = jnp.einsum("sid,sjd->sij", qkv[0], qkv[1], precision=precise) * size.scale
    shares = jax.nn.softmax(scores + bias[None], axis=-1)
    blend = jnp.einsum("sij,sjd->sid", shares, qkv[2], precision=precise)
    blend = blend.reshape(group_chains, devices, slim, head_width)
    blend = exchange(jnp.transpose(blend, (1, 0, 2, 3)), everyone)
    blend = blend.reshape(heads, chains, slim, head_width)
    blend = jnp.transpose(blend, (1, 2, 0, 3)).reshape(chains, slim, heads * head_width)
    msa_out = msa_col + affine_map(blend, weights[8])

    normed, _ = norm_parts(msa_out)
    left = affine_map(normed, weights[9]) * (present / jnp.sum(present))[:, None, None]
    left = jnp.transpose(left.reshape(chains // 4, 4, slim, 32), (2, 0, 1, 3))
    left = collect(left.reshape(slim, chains // 4, 128), "col", mesh_cols).reshape(-1, 128)
    right = affine_map(normed, weights[10]).reshape(chains // 16, 16, slim, 4, 8)
    right = jnp.transpose(right, (3, 0, 2, 1, 4)).reshape(-1, 128)
    right = collect(lax.ppermute(right, everyone, size.turn), row, mesh_rows)
    right = right.reshape(mesh_rows, 4, chains // 16, slim, 128)
    right = jnp.transpose(right, (1, 0, 3, 2, 4)).reshape(4, cols_here // 8, 8, chains // 16, 128)
    return msa_out, [left], jnp.transpose(right, (1, 0, 3, 2, 4))


def msa_forward(size, alignment_features, residue_couplings, present, weights):
    chains, slim, devices = size.chains, size.slim, size.devices
    mesh_rows, mesh_cols = size.mesh_rows, size.mesh_cols
    pair_flat = residue_couplings.reshape(-1, size.pair_width)
    tokens = chains * slim
    seen = jnp.repeat(present, slim)[None]
    share = jnp.repeat(present / jnp.sum(present), slim)[:, None]
    source, target = jnp.transpose(weights[9]), jnp.transpose(weights[10])
    offset = jnp.transpose(weights[7])
    stripe = size.to_slim(alignment_features).reshape(tokens, -1)
    bias = call_bias(pair_flat, offset, size.chain_groups, size.cols_here)
    bias = bias.reshape(devices, 16, 128)
    msa_col, qkv = call_columns(stripe, seen, bias, weights[:7], size.group_chains, size.scale)
    qkv = exchange(qkv, everyone)
    blend = call_rows(qkv, mesh_rows, mesh_cols, size.scale)
    blend = exchange(blend, everyone)
    msa_out, left, right = call_rows_out(blend, msa_col, share, weights[8], source, target)
    left = size.from_others([left.reshape(-1, 128)] * mesh_cols)
    right, *left = together(lax.ppermute(right, everyone, size.turn), *left)
    right = collect(right, row, mesh_rows)

    def back(grad, d_lefts, d_right, d_mid, pair_mid, side_sums, outer_sums):
        d_lefts = size.from_others(d_lefts)
        d_right = exchange(d_right, row).sum(0)
        d_right = lax.ppermute(d_right, everyone, size.turn_back)
        d_out, d_blend, thin, *out_sums = call_rows_out_back(
            d_lefts,
            d_right,
            grad.reshape(tokens, -1),
            msa_out,
            blend,
            share,
            weights[8],
            source,
            target,
            size.core,
        )
        d_mid, d_blend = together(d_mid, d_blend)
        outer_sums = outer_sums(d_mid)
        d_blend, *outer_sums = together(exchange(d_blend, everyone), *outer_sums)
        d_qkv = call_rows_back(qkv, d_blend, mesh_rows, mesh_cols, size.scale)
        pair_mid, d_qkv = together(pair_mid, d_qkv)
        side_sums = side_sums(pair_mid)
        d_qkv, *side_sums = together(exchange(d_qkv, everyone), *side_sums)
        d_col, *in_sums = call_rows_in_back(d_qkv, msa_col, d_out, weights[4:7], size.core)
        d_stripe, *col_sums = call_columns_back(
            stripe, seen, d_col, weights[:4], size.core, size.scale
        )
        d_bias = d_qkv.reshape(size.heads, size.chain_groups, -1, 128)
        thin_sums = call_bias_sums(d_bias, pair_flat, thin, size.core, size.cols_here)
        d_pair = call_bias_back(d_bias, d_mid, offset, size.cols_here)
        d_features = size.from_slim_permuted(d_stripe.reshape(chains, slim, -1))
        return d_features, d_pair, col_sums, in_sums, out_sums, thin_sums, side_sums, outer_sums

    return (msa_out.reshape(chains, slim, -1), left, right), back


def msa_plain_forward(size, alignment_features, residue_couplings, present, weights):
    chains, rows_here = size.chains, size.rows_here
    outputs, pull = jax.vjp(
        lambda x, y, w: msa_plain(size, x, y, present, w),
        alignment_features,
        residue_couplings,
        weights,
    )

    def back(grad, d_lefts, d_right, d_mid, pair_mid, side_sums, outer_sums):
        d_left = d_lefts[0].reshape(rows_here // 4, chains // 4, 4, 4, 32)
        d_left = jnp.transpose(d_left, (0, 3, 1, 2, 4)).reshape(-1, 128)
        d_features, d_pair, d_weights = pull((grad, [d_left], d_right))
        d_pair = d_pair.reshape(-1, size.pair_width) + d_mid
        thin = [d_weights[9], d_weights[10], jnp.pad(d_weights[7], ((0, 128), (0, 0)))]
        thin = jnp.pad(jnp.concatenate(thin, 1), ((0, 0), (0, 64 - size.heads)))
        core = size.core[0]
        pick = lambda x, n: lax.dynamic_index_in_dim(x, n, 0, False)
        own = lambda x: (pick(x, core), pick(x, 1 - core))
        cut = lambda ws: own(
            jnp.stack([jnp.concatenate([w[:, n : n + 128] for w in ws], 0) for n in (0, 128)])
        )
        return (
            d_features,
            d_pair,
            cut(d_weights[:4]),
            cut(d_weights[4:7]),
            cut(d_weights[8:9]),
            own(thin.reshape(2, -1, 128)),
            side_sums(pair_mid),
            outer_sums(d_mid),
        )

    return outputs, back


def per_device(mesh_rows, mesh_cols, *arguments):
    (
        alignment_features,
        residue_couplings,
        chain_indicator,
        alignment_result_adjoint,
        coupling_result_adjoint,
        *weights,
    ) = arguments
    present = chain_indicator.astype(jnp.float32)
    heads = weights[7].shape[1]
    size = Layout(
        mesh_rows,
        mesh_cols,
        residue_couplings.shape,
        present.shape[0],
        heads,
        weights[4].shape[1] // heads,
    )
    devices, channels_here = size.devices, size.channels_here
    cols_here, pair_width = size.cols_here, size.pair_width
    (
        tensor_result_matrix,
        source_side_matrix,
        source_side_switch,
        target_side_matrix,
        target_side_switch,
        trilateral_result_switch,
        trilateral_result_matrix,
    ) = weights[11:]

    sides = (source_side_switch, target_side_switch, source_side_matrix, target_side_matrix)
    shift = channels_here.bit_length() - 1
    forward = msa_forward if size.slim == 8 else msa_plain_forward
    (msa_slim, left_rows, right_rows), msa_back = forward(
        size, alignment_features, residue_couplings, present, tuple(weights[:11])
    )
    pair_flat = residue_couplings.reshape(-1, pair_width)
    grad_flat = coupling_result_adjoint.reshape(-1, pair_width)
    count = len(left_rows)
    first = (lax.axis_index("col") if count > 1 else jnp.int32(0)).reshape(1)
    blocks = call_blocks(first, left_rows)
    pair_mid, edges, prods = call_edges(
        blocks, right_rows, tensor_result_matrix, pair_flat, sides, cols_here, shift
    )
    edges = exchange(edges.reshape(devices, 2, channels_here, 16, 128), everyone)
    triangle = exchange(call_triangle(edges, mesh_rows, mesh_cols), everyone)
    pair_out, d_triangle, d_logit, g_tri_out = call_finish(
        triangle.reshape(pair_width, 16, 128),
        pair_mid,
        grad_flat,
        trilateral_result_switch,
        trilateral_result_matrix,
        cols_here,
    )
    views = (alignment_result_adjoint, msa_slim)
    *views, d_triangle = together(*views, d_triangle)
    views = size.both_views(*views)
    d_triangle = exchange(d_triangle.reshape(devices, channels_here, 16, 128), everyone)
    d_edges = exchange(call_triangle_back(edges, d_triangle, mesh_rows, mesh_cols), everyone)
    d_edges, views = together(d_edges, views)
    views = lax.all_to_all(views, "col", 0, 0, tiled=True)
    d_mid, d_logits, d_right, *d_lefts = call_edges_back(
        d_edges.reshape(2 * pair_width, 16, 128),
        pair_mid,
        grad_flat,
        d_logit,
        (*sides, trilateral_result_switch),
        right_rows,
        tensor_result_matrix,
        blocks,
        first,
        count,
        cols_here,
        shift,
    )
    d_right, views = together(d_right, views)
    msa_grad, msa_out = size.split_views(views)

    def side_sums(pair_mid):
        return call_side_sums(pair_mid, d_logits, g_tri_out, size.core, cols_here, shift)

    def outer_sums(d_mid):
        return call_outer_sums(d_mid, prods, size.core, cols_here)

    alignment_adjoint, coupling_adjoint, *sums = msa_back(
        msa_grad, d_lefts, d_right, d_mid, pair_mid, side_sums, outer_sums
    )
    mine = [kept + lax.ppermute(given, "core", size.swap) for kept, given in sums]
    mine, alignment_adjoint, coupling_adjoint = size.sum_all(
        jnp.concatenate(mine, 0), alignment_adjoint, coupling_adjoint
    )
    other = lax.ppermute(mine, "core", size.swap)
    summed = call_spread_sums(mine, other, size.core, [w.shape for w in weights])
    return (
        msa_out,
        pair_out.reshape(residue_couplings.shape),
        alignment_adjoint,
        coupling_adjoint.reshape(residue_couplings.shape),
        *summed,
    )


def solution(mesh):
    mesh_rows, mesh_cols = mesh.shape["row"], mesh.shape["col"]

    def local(*arguments):
        return per_device(mesh_rows, mesh_cols, *arguments)

    split = jax.sharding.Mesh(
        mesh.devices.reshape(mesh_rows // 2, 2, mesh_cols), ("half", "core", "col")
    )
    whole = P()
    msa = P("col", row, None)
    pair = P(row, "col", None)
    return jax.shard_map(
        local,
        mesh=split,
        in_specs=(msa, pair, whole, msa, pair) + (whole,) * 18,
        out_specs=(msa, pair, msa, pair) + (whole,) * 18,
        check_vma=False,
    )
```

```python
import functools

import jax
import jax.numpy as jnp
from jax import lax
from jax.experimental import pallas as pl
from jax.experimental.pallas import tpu as pltpu
from jax.sharding import PartitionSpec as P

bf16, f32 = jnp.bfloat16, jnp.float32
NN = ((1,), (0,))
NT = ((1,), (1,))
TN = ((0,), (0,))


def one_pass(a, b, dims=NN):
    return lax.dot_general(a, b, (dims, ((), ())), preferred_element_type=f32)


def halves(x):
    high = x.astype(bf16)
    return high, (x - high.astype(f32)).astype(bf16)


def dot3(a, b, dims=NN):
    a_high, a_low = a if isinstance(a, tuple) else halves(a)
    b_high, b_low = b if isinstance(b, tuple) else halves(b)
    return one_pass(a_high, b_high, dims) + (
        one_pass(a_high, b_low, dims) + one_pass(a_low, b_high, dims)
    )


def rounded(pair, rows):
    return pair[0][rows], pair[1][rows]


def iota(shape, dim):
    return lax.broadcasted_iota(jnp.int32, shape, dim)


def norm_parts(x):
    centered = x - jnp.mean(x, axis=-1, keepdims=True)
    inverse = lax.rsqrt(jnp.mean(centered * centered, axis=-1, keepdims=True) + 1e-05)
    return centered * inverse, inverse


def norm_back(normed, inverse, grad):
    return inverse * (
        grad
        - jnp.mean(grad, axis=-1, keepdims=True)
        - normed * jnp.mean(grad * normed, axis=-1, keepdims=True)
    )


def stacked3(a, b, dims=NN):
    a_high, a_low = a if isinstance(a, tuple) else halves(a)
    b_high, b_low = b if isinstance(b, tuple) else halves(b)
    return one_pass(
        jnp.concatenate([a_high, a_low, a_high], dims[0][0]),
        jnp.concatenate([b_high, b_high, b_low], dims[1][0]),
        dims,
    )


def row_of(t, u):
    return 2 * t + u // 2 + 16 * (u % 2)


def same_slot(chains):
    shape = (chains * 8, 256)
    return (iota(shape, 0) & 7) == (iota(shape, 1) & 7)


def blocks_kernel(chains, first_ref, *refs):
    *part_refs, out_ref, left_ref = refs
    groups, count = chains // 4, len(part_refs)
    size = part_refs[0].shape[0]
    t = pl.program_id(0)

    @pl.when(t == 0)
    def _():
        for n, ref in enumerate(part_refs):
            place = lax.rem(first_ref[0] + count - n, count) * size
            left_ref[pl.ds(pl.multiple_of(place, 8), size), :] = ref[...]

    shape = (chains * 8, chains)
    chain = iota(shape, 0) >> 3
    lift = jnp.where(iota(shape, 1) == (chain & 3) * groups + (chain >> 2), 1.0, 0.0).astype(bf16)
    same = same_slot(chains)
    rows = [
        left_ref[pl.ds(pl.multiple_of(row_of(t, u) * groups, groups), groups), :] for u in range(4)
    ]
    rows = jnp.concatenate(halves(jnp.concatenate(rows, 0)), 0)
    shape = (128, 256)
    slabs = []
    for n in range(4):
        spread = ((iota(shape, 0) >> 5) == n) & ((iota(shape, 0) & 31) == (iota(shape, 1) >> 3))
        slabs.append(one_pass(rows, jnp.where(spread, 1.0, 0.0).astype(bf16)))
    for part in range(2):
        for u in range(4):
            place = slice((part * 4 + u) * groups, (part * 4 + u + 1) * groups)
            slab = jnp.concatenate([x[place] for x in slabs], 0).astype(bf16)
            out_ref[0, u, part] = jnp.where(same, one_pass(lift, slab), 0.0).astype(bf16)


def call_blocks(first, parts):
    rows = sum(part.shape[0] for part in parts)
    chains = rows // 32 * 4
    shape = (8, 4, 2, chains * 8, 256)
    return pl.pallas_call(
        functools.partial(blocks_kernel, chains),
        grid=(8,),
        in_specs=[pl.BlockSpec(memory_space=pltpu.SMEM)] + [full(part) for part in parts],
        out_specs=step_block(shape),
        out_shape=jax.ShapeDtypeStruct(shape, bf16),
        scratch_shapes=[pltpu.VMEM((rows, 128), f32)],
        compiler_params=params(),
        name="blocks",
    )(first, *parts)


def join_right(ref, out_ref):
    cols = ref.shape[0] * 8
    for g in range(4):
        for n in range(ref.shape[2]):
            out_ref[g * cols : (g + 1) * cols, n * 128 : (n + 1) * 128] = ref[:, g, n].reshape(
                cols, 128
            )


def cut_right(ref, out_ref):
    cols = out_ref.shape[0] * 8
    for g in range(4):
        for n in range(out_ref.shape[2]):
            tile = ref[g * cols : (g + 1) * cols, n * 128 : (n + 1) * 128]
            out_ref[:, g, n] = tile.reshape(-1, 8, 128)


def outer_weights(ref, out_ref):
    whole = ref[...].reshape(32, 4, 8, 128)
    for g in range(4):
        out_ref[g, 0], out_ref[g, 1] = halves(whole[:, g].reshape(256, 128))


def params(mebibytes=56):
    return pltpu.CompilerParams(vmem_limit_bytes=mebibytes * 2**20)


def full(array):
    return pl.BlockSpec(array.shape, lambda t, n=len(array.shape): (0,) * n)


def step_block(shape):
    return pl.BlockSpec((1,) + shape[1:], lambda t, n=len(shape): (t,) + (0,) * (n - 1))


def pair_of(ref, *index):
    return ref[(*index, 0)], ref[(*index, 1)]


def chunk_order(shift):
    shape = (256, 256)
    place, width = iota(shape, 0), 1 << shift
    channel = place & 127
    target = ((channel >> shift) << (shift + 1)) + (channel & (width - 1))
    target = target + ((place >> 7) << shift)
    return jnp.where(iota(shape, 1) == target, 1.0, 0.0).astype(bf16)


def side_halves(shift, refs, out_ref):
    order = chunk_order(shift)
    for n in range(2):
        both = halves(jnp.concatenate([refs[2 * n][...], refs[2 * n + 1][...]], 1))
        for part in range(2):
            out_ref[part, :, n * 256 : (n + 1) * 256] = one_pass(both[part], order).astype(bf16)
    if len(refs) == 5:
        out_ref[0, :, 512:], out_ref[1, :, 512:] = halves(refs[4][...])


def edges_kernel(
    cols,
    shift,
    block_ref,
    right_ref,
    outer_ref,
    pair_ref,
    gate1_ref,
    gate2_ref,
    value1_ref,
    value2_ref,
    mid_ref,
    edge_ref,
    prod_ref,
    whole_ref,
    right_halves,
    outer_halves,
    sides_halves,
):
    t = pl.program_id(0)

    @pl.when(t == 0)
    def _():
        join_right(right_ref, whole_ref)
        right_halves[0], right_halves[1] = halves(whole_ref[...])
        outer_weights(outer_ref, outer_halves)
        side_halves(shift, (gate1_ref, gate2_ref, value1_ref, value2_ref), sides_halves)

    right = pair_of(right_halves)
    places = four_rows(t, cols)
    for u in range(4):
        high, low = halves(stacked3(right, pair_of(block_ref, 0, u)))
        for g in range(4):
            prod_ref[0, g, 0, u * cols : (u + 1) * cols] = high[g * cols : (g + 1) * cols]
            prod_ref[0, g, 1, u * cols : (u + 1) * cols] = low[g * cols : (g + 1) * cols]
    update = 0.0
    for g in range(4):
        update = update + dot3(pair_of(prod_ref, 0, g), pair_of(outer_halves, g))
    mid = update + read_rows(pair_ref, places)
    write_rows(mid_ref, places, mid)
    normed, _ = norm_parts(mid)
    logits = stacked3(normed, pair_of(sides_halves))
    write_turned(edge_ref, t, jax.nn.sigmoid(logits[:, :256]) * logits[:, 256:])


def call_edges(blocks, right, outer, pair, sides, cols, shift):
    rows, depth = pair.shape[0], blocks.shape[3]
    prods = (8, 4, 2, 4 * cols, 256)
    return pl.pallas_call(
        functools.partial(edges_kernel, cols, shift),
        grid=(8,),
        in_specs=[step_block(blocks.shape)] + [full(x) for x in (right, outer, pair, *sides)],
        out_specs=(
            pl.BlockSpec((rows, 128), lambda t: (0, 0)),
            pl.BlockSpec((256, 16, 128), lambda t: (0, 0, 0)),
            step_block(prods),
        ),
        out_shape=(
            jax.ShapeDtypeStruct((rows, 128), f32),
            jax.ShapeDtypeStruct((256, 16, 128), f32),
            jax.ShapeDtypeStruct(prods, bf16),
        ),
        scratch_shapes=[
            pltpu.VMEM((4 * cols, depth), f32),
            pltpu.VMEM((2, 4 * cols, depth), bf16),
            pltpu.VMEM((4, 2, 256, 128), bf16),
            pltpu.VMEM((2, 128, 512), bf16),
        ],
        compiler_params=params(),
        name="edges",
    )(blocks, right, outer, pair, *sides)


def join_tiles(chunks, mesh_rows, mesh_cols, out_ref):
    plain = chunks.reshape(mesh_rows * mesh_cols * 16, 128)
    rolled = pltpu.roll(plain, 64, 1)
    first = iota((16, 128), 1) < 64
    for r in range(mesh_rows):
        for t in range(mesh_cols // 2):
            even = slice((r * mesh_cols + 2 * t) * 16, (r * mesh_cols + 2 * t + 1) * 16)
            odd = slice((r * mesh_cols + 2 * t + 1) * 16, (r * mesh_cols + 2 * t + 2) * 16)
            lanes = slice(t * 128, (t + 1) * 128)
            out_ref[r * 32 : r * 32 + 16, lanes] = jnp.where(first, plain[even], rolled[odd])
            out_ref[r * 32 + 16 : r * 32 + 32, lanes] = jnp.where(first, rolled[even], plain[odd])


def cut_tiles(whole, mesh_rows, mesh_cols, store):
    first = iota((16, 128), 1) < 64
    for t in range(mesh_cols // 2):
        plain = whole[:, t * 128 : (t + 1) * 128]
        rolled = pltpu.roll(plain, 64, 1)
        for r in range(mesh_rows):
            low = slice(r * 32, r * 32 + 16)
            high = slice(r * 32 + 16, r * 32 + 32)
            store(r * mesh_cols + 2 * t, jnp.where(first, plain[low], rolled[high]))
            store(r * mesh_cols + 2 * t + 1, jnp.where(first, rolled[low], plain[high]))


def triangle_kernel(mesh_rows, mesh_cols, edge_ref, out_ref, left_ref, right_ref):
    join_tiles(edge_ref[:, 0, 0], mesh_rows, mesh_cols, left_ref)
    join_tiles(edge_ref[:, 1, 0], mesh_rows, mesh_cols, right_ref)

    def store(d, tile):
        out_ref[d, 0] = tile

    cut_tiles(dot3(left_ref[...], right_ref[...], NT), mesh_rows, mesh_cols, store)


def call_triangle(edges, mesh_rows, mesh_cols):
    devices, _, channels = edges.shape[:3]
    span = mesh_rows * 32
    return pl.pallas_call(
        functools.partial(triangle_kernel, mesh_rows, mesh_cols),
        grid=(channels,),
        in_specs=[pl.BlockSpec((devices, 2, 1, 16, 128), lambda n: (0, 0, n, 0, 0))],
        out_specs=pl.BlockSpec((devices, 1, 16, 128), lambda n: (0, n, 0, 0)),
        out_shape=jax.ShapeDtypeStruct((devices, channels, 16, 128), f32),
        scratch_shapes=[pltpu.VMEM((span, span), f32)] * 2,
        compiler_params=params(32),
        name="triangle",
    )(edges)


def triangle_back_kernel(
    mesh_rows, mesh_cols, edge_ref, grad_ref, out_ref, left_ref, right_ref, whole_ref
):
    join_tiles(edge_ref[:, 0, 0], mesh_rows, mesh_cols, left_ref)
    join_tiles(edge_ref[:, 1, 0], mesh_rows, mesh_cols, right_ref)
    join_tiles(grad_ref[:, 0], mesh_rows, mesh_cols, whole_ref)

    def store(kind):
        def put(d, tile):
            out_ref[d, kind, 0] = tile

        return put

    whole = whole_ref[...]
    cut_tiles(dot3(whole, right_ref[...]), mesh_rows, mesh_cols, store(0))
    cut_tiles(dot3(jnp.transpose(whole), left_ref[...]), mesh_rows, mesh_cols, store(1))


def call_triangle_back(edges, grad, mesh_rows, mesh_cols):
    devices, _, channels = edges.shape[:3]
    span = mesh_rows * 32
    both = pl.BlockSpec((devices, 2, 1, 16, 128), lambda n: (0, 0, n, 0, 0))
    return pl.pallas_call(
        functools.partial(triangle_back_kernel, mesh_rows, mesh_cols),
        grid=(channels,),
        in_specs=[both, pl.BlockSpec((devices, 1, 16, 128), lambda n: (0, n, 0, 0))],
        out_specs=both,
        out_shape=jax.ShapeDtypeStruct(edges.shape, f32),
        scratch_shapes=[pltpu.VMEM((span, span), f32)] * 3,
        compiler_params=params(32),
        name="triangle_back",
    )(edges, grad)


def four_rows(t, cols):
    return [
        pl.ds(pl.multiple_of((2 * t + u // 2 + 16 * (u % 2)) * cols, cols), cols) for u in range(4)
    ]


def read_rows(ref, places):
    return jnp.concatenate([ref[p, :] for p in places], 0)


def write_rows(ref, places, value):
    size = value.shape[0] // len(places)
    for u, p in enumerate(places):
        ref[p, :] = value[u * size : (u + 1) * size]


def read_turned(ref, t):
    parts = []
    for v in range(2):
        tile = ref[:, pl.ds(2 * t + v, 1), :]
        parts.append(jnp.transpose(tile.reshape(tile.shape[0], 128)))
    return jnp.concatenate(parts, 0)


def write_turned(ref, t, value):
    for v in range(2):
        turned = jnp.transpose(value[v * 128 : (v + 1) * 128])
        ref[:, pl.ds(2 * t + v, 1), :] = turned[:, None, :]


def finish_kernel(
    cols, tri_ref, mid_ref, grad_ref, gate_ref, proj_ref, out_ref, dtri_ref, dlogit_ref, dproj_ref
):
    gate_w = halves(gate_ref[...])
    proj_w = halves(proj_ref[...])
    dproj_ref[...] = jnp.zeros_like(dproj_ref)

    def step(t, carry):
        places = four_rows(t, cols)
        mid = read_rows(mid_ref, places)
        grad = read_rows(grad_ref, places)
        normed, _ = norm_parts(mid)
        tri, tri_inverse = norm_parts(read_turned(tri_ref, t))
        tri_halves = halves(tri)
        gate = jax.nn.sigmoid(dot3(normed, gate_w))
        value = dot3(tri_halves, proj_w)
        write_rows(out_ref, places, mid + gate * value)
        dvalue = halves(grad * gate)
        write_rows(dlogit_ref, places, grad * value * gate * (1.0 - gate))
        dproj_ref[...] += stacked3(halves(jnp.transpose(tri)), dvalue)
        write_turned(dtri_ref, t, norm_back(tri, tri_inverse, stacked3(dvalue, proj_w, NT)))
        return carry

    lax.fori_loop(0, 8, step, 0)


def call_finish(tri, mid, grad, gate, proj, cols):
    rows = mid.shape[0]
    return pl.pallas_call(
        functools.partial(finish_kernel, cols),
        out_shape=(
            jax.ShapeDtypeStruct((rows, 128), f32),
            jax.ShapeDtypeStruct((128, 16, 128), f32),
            jax.ShapeDtypeStruct((rows, 128), f32),
            jax.ShapeDtypeStruct((128, 128), f32),
        ),
        compiler_params=params(32),
        name="finish",
    )(tri, mid, grad, gate, proj)


def edges_back_kernel(
    cols,
    chains,
    shift,
    dedge_ref,
    mid_ref,
    grad_ref,
    dlogit_ref,
    gate1_ref,
    gate2_ref,
    value1_ref,
    value2_ref,
    gate3_ref,
    right_ref,
    outer_ref,
    block_ref,
    first_ref,
    dmid_ref,
    dlogits_ref,
    dright_ref,
    *refs,
):
    *dleft_refs, whole_ref, turned_halves, outer_halves, sides_halves, fold_ref, dslab_ref, dleft_ref = (
        refs
    )
    t = pl.program_id(0)

    @pl.when(t == 0)
    def _():
        join_right(right_ref, whole_ref)
        turned_halves[0], turned_halves[1] = halves(jnp.transpose(whole_ref[...]))
        outer_weights(outer_ref, outer_halves)
        refs = (gate1_ref, gate2_ref, value1_ref, value2_ref, gate3_ref)
        side_halves(shift, refs, sides_halves)
        shape = (256, 128)
        for u in range(4):
            lane = 64 * (u % 2) + 32 * (u // 2) + (iota(shape, 0) >> 3)
            fold = jnp.where(iota(shape, 1) == lane, 1.0, 0.0).astype(bf16)
            fold_ref[512 * u : 512 * u + 256] = fold
            fold_ref[512 * u + 256 : 512 * u + 512] = fold
        whole_ref[...] = jnp.zeros_like(whole_ref)

    same = same_slot(chains)
    sides = pair_of(sides_halves)
    places = four_rows(t, cols)
    normed, inverse = norm_parts(read_rows(mid_ref, places))
    logits = stacked3(normed, rounded(sides, (slice(None), slice(0, 512))))
    gate, value = jax.nn.sigmoid(logits[:, :256]), logits[:, 256:]
    dedge = read_turned(dedge_ref, t)
    dlogits = [
        dedge * value * gate * (1.0 - gate),
        dedge * gate,
        read_rows(dlogit_ref, places),
    ]
    dlogits = halves(jnp.concatenate(dlogits, 1))
    dlogits_ref[0, 0], dlogits_ref[0, 1] = dlogits
    dmid = read_rows(grad_ref, places) + norm_back(normed, inverse, dot3(dlogits, sides, NT))
    write_rows(dmid_ref, places, dmid)
    dmid = halves(dmid)
    dprod = [halves(stacked3(dmid, pair_of(outer_halves, g), NT)) for g in range(4)]
    here, diagonal = [], []
    turned = pair_of(turned_halves)
    for u in range(4):
        rows = slice(u * cols, (u + 1) * cols)
        here.append([jnp.concatenate([dprod[g][n][rows] for g in range(4)], 0) for n in range(2)])
        diagonal += halves(jnp.where(same, stacked3(turned, tuple(here[u])), 0.0))
    right_terms = [x for high, low in here for x in (high, low, high)]
    block_terms = [block_ref[0, u, n] for u in range(4) for n in (0, 0, 1)]
    whole_ref[...] += one_pass(
        jnp.concatenate(right_terms, 1), jnp.concatenate(block_terms, 1), NT
    )
    dslab = one_pass(jnp.concatenate(diagonal, 1), fold_ref[...])
    dslab_ref[t] = jnp.sum(dslab.reshape(chains, 8, 128), axis=1)

    @pl.when(t == 7)
    def _():
        cut_right(whole_ref, dright_ref)
        first = iota((chains, 128), 1) < 64
        for n in range(4):
            even, odd = dslab_ref[2 * n], dslab_ref[2 * n + 1]
            dleft_ref[n] = jnp.where(first, even, pltpu.roll(odd, 64, 1))
            dleft_ref[n + 4] = jnp.where(first, pltpu.roll(even, 64, 1), odd)
        count, size = len(dleft_refs), dleft_refs[0].shape[0]
        for n, ref in enumerate(dleft_refs):
            place = lax.rem(first_ref[0] + n, count) * size
            ref[...] = dleft_ref[pl.ds(place, size)]


def call_edges_back(
    dedge, mid, grad, dlogit, sides, right, outer, blocks, first, count, cols, shift
):
    rows, depth = mid.shape[0], blocks.shape[3]
    chains = depth // 8
    dlogits = (8, 2, 4 * cols, 640)
    return pl.pallas_call(
        functools.partial(edges_back_kernel, cols, chains, shift),
        grid=(8,),
        in_specs=[full(x) for x in (dedge, mid, grad, dlogit, *sides, right, outer)]
        + [step_block(blocks.shape), pl.BlockSpec(memory_space=pltpu.SMEM)],
        out_specs=(
            pl.BlockSpec((rows, 128), lambda t: (0, 0)),
            step_block(dlogits),
            full(right),
        )
        + (pl.BlockSpec((8 // count, chains, 128), lambda t: (0, 0, 0)),) * count,
        out_shape=(
            jax.ShapeDtypeStruct((rows, 128), f32),
            jax.ShapeDtypeStruct(dlogits, bf16),
            jax.ShapeDtypeStruct(right.shape, f32),
        )
        + (jax.ShapeDtypeStruct((8 // count, chains, 128), f32),) * count,
        scratch_shapes=[
            pltpu.VMEM((4 * cols, depth), f32),
            pltpu.VMEM((2, depth, 4 * cols), bf16),
            pltpu.VMEM((4, 2, 256, 128), bf16),
            pltpu.VMEM((2, 128, 640), bf16),
            pltpu.VMEM((2048, 128), bf16),
            pltpu.VMEM((8, chains, 128), f32),
            pltpu.VMEM((8, chains, 128), f32),
        ],
        compiler_params=params(),
        name="edges_back",
    )(dedge, mid, grad, dlogit, *sides, right, outer, blocks, first)


def give_halves(core_ref, whole_ref, mine_ref, other_ref):
    mine_ref[...] = whole_ref[core_ref[0]]
    other_ref[...] = whole_ref[1 - core_ref[0]]


def side_sums_kernel(
    cols,
    shift,
    mid_ref,
    dlogits_ref,
    first_ref,
    core_ref,
    mine_ref,
    other_ref,
    sides_ref,
    whole_ref,
):
    t = pl.program_id(0)

    @pl.when(t == 0)
    def _():
        sides_ref[...] = jnp.zeros_like(sides_ref)

    normed, _ = norm_parts(read_rows(mid_ref, four_rows(t, cols)))
    sides_ref[...] += stacked3(halves(jnp.transpose(normed)), pair_of(dlogits_ref, 0))

    @pl.when(t == 7)
    def _():
        order = chunk_order(shift)
        for n in range(2):
            high, low = halves(sides_ref[:, n * 256 : (n + 1) * 256])
            sides = one_pass(high, order, NT) + one_pass(low, order, NT)
            for side in range(2):
                place = 2 * n + side
                rows = slice(place % 3 * 128, place % 3 * 128 + 128)
                whole_ref[place // 3, rows] = sides[:, side * 128 : (side + 1) * 128]
        whole_ref[1, 128:256] = sides_ref[:, 512:]
        whole_ref[1, 256:] = first_ref[...]
        give_halves(core_ref, whole_ref, mine_ref, other_ref)


def call_side_sums(mid, dlogits, first, core, cols, shift):
    return pl.pallas_call(
        functools.partial(side_sums_kernel, cols, shift),
        grid=(8,),
        in_specs=[full(mid), step_block(dlogits.shape), full(first)]
        + [pl.BlockSpec(memory_space=pltpu.SMEM)],
        out_specs=(pl.BlockSpec((384, 128), lambda t: (0, 0)),) * 2,
        out_shape=(jax.ShapeDtypeStruct((384, 128), f32),) * 2,
        scratch_shapes=[pltpu.VMEM((128, 640), f32), pltpu.VMEM((2, 384, 128), f32)],
        compiler_params=params(),
        name="side_sums",
    )(mid, dlogits, first, core)


def outer_sums_kernel(
    cols, dmid_ref, prod_ref, core_ref, mine_ref, other_ref, outer_ref, whole_ref
):
    t = pl.program_id(0)

    @pl.when(t == 0)
    def _():
        outer_ref[...] = jnp.zeros_like(outer_ref)

    dmid = halves(jnp.transpose(read_rows(dmid_ref, four_rows(t, cols))))
    for g in range(4):
        outer_ref[:, g * 256 : (g + 1) * 256] += stacked3(dmid, pair_of(prod_ref, 0, g))

    @pl.when(t == 7)
    def _():
        for g in range(4):
            tile = jnp.transpose(outer_ref[:, g * 256 : (g + 1) * 256]).reshape(32, 8, 128)
            for p in range(32):
                start = p % 16 * 32 + g * 8
                whole_ref[p // 16, start : start + 8] = tile[p]
        give_halves(core_ref, whole_ref, mine_ref, other_ref)


def call_outer_sums(dmid, prods, core, cols):
    return pl.pallas_call(
        functools.partial(outer_sums_kernel, cols),
        grid=(8,),
        in_specs=[full(dmid), step_block(prods.shape), pl.BlockSpec(memory_space=pltpu.SMEM)],
        out_specs=(pl.BlockSpec((512, 128), lambda t: (0, 0)),) * 2,
        out_shape=(jax.ShapeDtypeStruct((512, 128), f32),) * 2,
        scratch_shapes=[pltpu.VMEM((128, 1024), f32), pltpu.VMEM((2, 512, 128), f32)],
        compiler_params=params(),
        name="outer_sums",
    )(dmid, prods, core)


def pack_heads(y, store):
    lane = iota((1, 1, 128), 2) >> 5
    for tile in range(y.shape[1] // 128):
        part = y[:, tile * 128 : (tile + 1) * 128]
        turned = [part] + [pltpu.roll(part, 32 * n, 1) for n in range(1, 4)]
        turned = [x.reshape(-1, 4, 8, 128) for x in turned]
        for head in range(4):
            out = turned[-head % 4][:, 0]
            for chain in range(1, 4):
                out = jnp.where(lane == chain, turned[(chain - head) % 4][:, chain], out)
            store(tile * 4 + head, out)


def unpack_heads(load, heads):
    lane = iota((1, 1, 128), 2) >> 5
    tiles = []
    for tile in range(heads // 4):
        turned = []
        for head in range(4):
            part = load(tile * 4 + head)
            flat = part.reshape(-1, 128)
            turned.append(
                [part] + [pltpu.roll(flat, 32 * n, 1).reshape(part.shape) for n in range(1, 4)]
            )
        chains = []
        for chain in range(4):
            out = turned[0][-chain % 4]
            for head in range(1, 4):
                out = jnp.where(lane == head, turned[head][(head - chain) % 4], out)
            chains.append(out[:, None])
        tiles.append(jnp.concatenate(chains, 1).reshape(-1, 128))
    return jnp.concatenate(tiles, 1)


def head_lanes(tile, n):
    return jnp.where((iota((1, 128), 1) >> 5) == n, tile, 0.0)


def stack_heads(tile):
    return jnp.concatenate([head_lanes(tile, n) for n in range(4)], 0)


def join_heads(stacked):
    size = stacked.shape[0] // 4
    lane = iota((1, 128), 1) >> 5
    out = stacked[:size]
    for n in range(1, 4):
        out = jnp.where(lane == n, stacked[n * size : (n + 1) * size], out)
    return out


def soft(scores, seen=None):
    if seen is not None:
        scores = jnp.where(seen, scores, -1e30)
    weights = jnp.exp(scores - jnp.max(scores, axis=-1, keepdims=True))
    if seen is not None:
        weights = jnp.where(seen, weights, 0.0)
    return weights * (1.0 / jnp.sum(weights, axis=-1, keepdims=True))


def soft_back(weights, grad):
    return weights * (grad - jnp.sum(weights * grad, axis=-1, keepdims=True))


def stripe_seen(present_ref):
    tokens = present_ref.shape[1]
    shape = (tokens, tokens)
    same = (iota(shape, 0) & 7) == (iota(shape, 1) & 7)
    return same & (present_ref[...] > 0.0)


def column_attention(q, k, v, seen):
    weights, tiles = [], []
    for tile in range(q.shape[1] // 128):
        lanes = slice(tile * 128, (tile + 1) * 128)
        keys, values = halves(k[:, lanes]), halves(v[:, lanes])
        blend = 0.0
        for n in range(4):
            weights.append(soft(dot3(head_lanes(q[:, lanes], n), keys, NT), seen))
            blend = blend + head_lanes(dot3(weights[-1], values), n)
        tiles.append(blend)
    return weights, jnp.concatenate(tiles, 1)


def columns_kernel(
    scale,
    x_ref,
    present_ref,
    bias_ref,
    q_ref,
    k_ref,
    v_ref,
    o_ref,
    q2_ref,
    k2_ref,
    v2_ref,
    out_ref,
    qkv_ref,
):
    x = x_ref[...]
    normed, _ = norm_parts(x)
    normed = halves(normed)
    q, k, v = (dot3(normed, halves(w[...])) for w in (q_ref, k_ref, v_ref))
    _, blend = column_attention(q * scale, k, v, stripe_seen(present_ref))
    out = x + dot3(blend, halves(o_ref[...]))
    out_ref[...] = out
    normed, _ = norm_parts(out)
    normed = halves(normed)
    groups, size = qkv_ref.shape[0] // 8, (qkv_ref.shape[1] - 16) // 3
    qkv_ref[:, -16:] = bias_ref[...]

    def store(kind):
        def put(head, value):
            place = slice(head * groups, (head + 1) * groups)
            rows = slice(kind * size, (kind + 1) * size)
            qkv_ref[place, rows] = value.reshape(groups, size, 128)

        return put

    for kind, w in enumerate((q2_ref, k2_ref, v2_ref)):
        pack_heads(dot3(normed, halves(w[...])), store(kind))


def call_columns(x, present, bias, weights, group_chains, scale):
    return pl.pallas_call(
        functools.partial(columns_kernel, scale),
        out_shape=(
            jax.ShapeDtypeStruct(x.shape, f32),
            jax.ShapeDtypeStruct((bias.shape[0], 6 * group_chains + 16, 128), f32),
        ),
        compiler_params=params(24),
        name="columns",
    )(x, present, bias, *weights)


def packed_parts(ref):
    parts = (ref.shape[1] - 16) // 24
    for half in range(parts):
        places = [(kind * parts + half) * 8 for kind in range(3)]
        yield half, places, [ref[:, p : p + 8].reshape(-1, 128) for p in places]


def rows_kernel(mesh_rows, mesh_cols, scale, qkv_ref, out_ref, whole_ref):
    join_tiles(qkv_ref[:, -16:], mesh_rows, mesh_cols, whole_ref)
    bias = whole_ref[...]
    for half, _, (q, k, v) in packed_parts(qkv_ref):
        k, v, q = halves(k), halves(v), q * scale
        blend = 0.0
        for n in range(4):
            weights = soft(dot3(head_lanes(q, n), k, NT) + bias)
            blend = blend + head_lanes(dot3(weights, v), n)
        out_ref[:, half] = blend.reshape(-1, 8, 128)


def call_rows(qkv, mesh_rows, mesh_cols, scale):
    devices, parts = qkv.shape[0], (qkv.shape[1] - 16) // 24
    span = mesh_rows * 32
    return pl.pallas_call(
        functools.partial(rows_kernel, mesh_rows, mesh_cols, scale),
        out_shape=jax.ShapeDtypeStruct((devices, parts, 8, 128), f32),
        scratch_shapes=[pltpu.VMEM((span, span), f32)],
        compiler_params=params(24),
        name="rows",
    )(qkv)


def load_heads(ref, kind=None):
    def load(head):
        groups = ref.shape[0] // 8
        place = slice(head * groups, (head + 1) * groups)
        part = ref[place] if kind is None else ref[place, kind]
        return part.reshape(-1, 8, 128)

    return load


def side_copies(source_ref, target_ref):
    both = halves(jnp.concatenate([source_ref[...], target_ref[...]], 0))
    shape = (640, 64)
    place = iota(shape, 0) - 128
    feature = jnp.where(place < 0, place & 31, 32 + ((place >> 7) << 3) + (place & 7))
    copies = jnp.where(iota(shape, 1) == feature, 1.0, 0.0).astype(bf16)
    return tuple(one_pass(copies, part).astype(bf16) for part in both)


def rows_out_kernel(
    blend_ref, mid_ref, share_ref, o_ref, source_ref, target_ref, out_ref, left_ref, right_ref
):
    blend = unpack_heads(load_heads(blend_ref), 8)
    out = mid_ref[...] + dot3(blend, halves(o_ref[...]))
    out_ref[...] = out
    normed, _ = norm_parts(out)
    wide = dot3(normed, side_copies(source_ref, target_ref), NT)
    left = (wide[:, :128] * share_ref[...]).reshape(-1, 4, 8, 128)
    lane = iota((1, 1, 128), 2)
    packed = left[:, 0]
    for chain in range(1, 4):
        packed = jnp.where((lane >> 5) == chain, left[:, chain], packed)
    for n in range(packed.shape[0]):
        left_ref[:, n, :] = packed[n]
    for g in range(4):
        right = wide[:, (g + 1) * 128 : (g + 2) * 128].reshape(-1, 16, 8, 128)
        packed = right[:, 0]
        for chain in range(1, 16):
            packed = jnp.where((lane >> 3) == chain, right[:, chain], packed)
        right_ref[g] = packed


def call_rows_out(blend, mid, share, weight, source, target):
    chains = mid.shape[0] // 8
    return pl.pallas_call(
        rows_out_kernel,
        out_shape=(
            jax.ShapeDtypeStruct(mid.shape, f32),
            jax.ShapeDtypeStruct((8, chains // 4, 128), f32),
            jax.ShapeDtypeStruct((4, chains // 16, 8, 128), f32),
        ),
        compiler_params=params(),
        name="rows_out",
    )(blend, mid, share, weight, source, target)


def rows_out_back_kernel(*refs):
    *dleft_refs, dright_ref, grad_ref, out_ref, blend_ref, share_ref = refs[:-10]
    o_ref, source_ref, target_ref = refs[-10:-7]
    core_ref, dout_ref, dblend_ref, thin_ref, mine_ref, other_ref, sum_ref = refs[-7:]
    lane = iota((1, 1, 128), 2)
    chains = grad_ref.shape[0] // 8
    dleft = functools.reduce(jnp.add, [ref[...] for ref in dleft_refs])
    shape = (chains * 8, 128)
    slot = iota(shape, 0) & 7
    copy = (chains * 8, chains)
    copy = jnp.where((iota(copy, 0) >> 3) == iota(copy, 1), 1.0, 0.0).astype(bf16)
    left = 0.0
    for n in range(2):
        high, low = halves(dleft[n])
        spot = (slot >> 2 == n) & (slot & 3 == iota(shape, 1) >> 5)
        left = left + jnp.where(spot, one_pass(copy, high) + one_pass(copy, low), 0.0)
    wide = [left * share_ref[...]]
    dright = dright_ref[...]
    for g in range(4):
        part = [jnp.where((lane >> 3) == n, dright[g], 0.0)[:, None] for n in range(16)]
        wide.append(jnp.concatenate(part, 1).reshape(-1, 128))
    wide = halves(jnp.concatenate(wide, 1))
    normed, inverse = norm_parts(out_ref[...])
    dsides = halves(dot3(halves(jnp.transpose(normed)), wide))
    shape = (640, 128)
    place, spot = iota(shape, 0) - 128, iota(shape, 1)
    target = jnp.where(place < 0, place & 31, 32 + ((place >> 7) << 3) + (place & 7))
    fold = jnp.where(target == spot, 1.0, 0.0).astype(bf16)
    thin_ref[...] = one_pass(dsides[0], fold) + one_pass(dsides[1], fold)
    dout = grad_ref[...] + norm_back(normed, inverse, dot3(wide, side_copies(source_ref, target_ref)))
    dout_ref[...] = dout
    dout = halves(dout)
    groups = dblend_ref.shape[0] // 8

    def store(head, value):
        dblend_ref[head * groups : (head + 1) * groups] = value.reshape(groups, -1, 8, 128)

    pack_heads(dot3(dout, halves(o_ref[...]), NT), store)
    blend = unpack_heads(load_heads(blend_ref), 8)
    write_halves(sum_ref, 0, dot3(halves(jnp.transpose(blend)), dout))
    give_halves(core_ref, sum_ref, mine_ref, other_ref)


def call_rows_out_back(dlefts, dright, grad, out, blend, share, weight, source, target, core):
    shapes, scratch = halves_shapes([weight])
    return pl.pallas_call(
        rows_out_back_kernel,
        out_shape=(
            jax.ShapeDtypeStruct(grad.shape, f32),
            jax.ShapeDtypeStruct(blend.shape, f32),
            jax.ShapeDtypeStruct((256, 128), f32),
        )
        + shapes,
        in_specs=specs(len(dlefts) + 8),
        scratch_shapes=[scratch],
        compiler_params=params(),
        name="rows_out_back",
    )(*dlefts, dright, grad, out, blend, share, weight, source, target, core)


def rows_back_kernel(
    mesh_rows, mesh_cols, scale, qkv_ref, dblend_ref, out_ref, whole_ref
):
    join_tiles(qkv_ref[:, -16:], mesh_rows, mesh_cols, whole_ref)
    bias = jnp.concatenate([whole_ref[...]] * 4, 0)
    span = whole_ref.shape[0]
    dbias = 0.0
    for half, places, (q, k, v) in packed_parts(qkv_ref):
        k, query = halves(k), halves(stack_heads(q * scale))
        dblend = halves(stack_heads(dblend_ref[:, half].reshape(-1, 128)))
        weights = soft(dot3(query, k, NT) + bias)
        dv = dot3(halves(jnp.transpose(weights)), dblend)
        dscores = soft_back(weights, dot3(dblend, halves(v), NT))
        for n in range(4):
            dbias = dbias + dscores[n * span : (n + 1) * span]
        dk = dot3(halves(jnp.transpose(dscores)), query)
        dq = join_heads(dot3(dscores, k))
        for place, value in zip(places, (dq * scale, dk, dv)):
            out_ref[:, place : place + 8] = value.reshape(-1, 8, 128)

    def store(d, tile):
        out_ref[d, -16:] = tile

    cut_tiles(dbias, mesh_rows, mesh_cols, store)


def call_rows_back(qkv, dblend, mesh_rows, mesh_cols, scale):
    span = mesh_rows * 32
    return pl.pallas_call(
        functools.partial(rows_back_kernel, mesh_rows, mesh_cols, scale),
        out_shape=jax.ShapeDtypeStruct(qkv.shape, f32),
        scratch_shapes=[pltpu.VMEM((span, span), f32)],
        compiler_params=params(24),
        name="rows_back",
    )(qkv, dblend)


def write_halves(ref, n, value):
    height = value.shape[0]
    for half in range(2):
        ref[half, n * height : (n + 1) * height] = value[:, half * 128 : (half + 1) * 128]


def projections_back(normed, inverse, grads, weight_refs, sum_ref):
    turned = halves(jnp.transpose(normed))
    dnormed = 0.0
    for n, (grad, w) in enumerate(zip(grads, weight_refs)):
        grad = halves(grad)
        write_halves(sum_ref, n, dot3(turned, grad))
        dnormed = dnormed + dot3(grad, halves(w[...]), NT)
    return norm_back(normed, inverse, dnormed)


def rows_in_back_kernel(
    dqkv_ref, mid_ref, grad_ref, q_ref, k_ref, v_ref, core_ref, dmid_ref, mine_ref, other_ref, sum_ref
):
    groups, size = dqkv_ref.shape[0] // 8, (dqkv_ref.shape[1] - 16) // 3

    def load(kind):
        place = slice(kind * size, (kind + 1) * size)
        return lambda head: dqkv_ref[head * groups : (head + 1) * groups, place].reshape(-1, 8, 128)

    grads = [unpack_heads(load(kind), 8) for kind in range(3)]
    normed, inverse = norm_parts(mid_ref[...])
    dmid_ref[...] = grad_ref[...] + projections_back(
        normed, inverse, grads, (q_ref, k_ref, v_ref), sum_ref
    )
    give_halves(core_ref, sum_ref, mine_ref, other_ref)


def halves_shapes(weights):
    rows = sum(w.size for w in weights) // 256
    return (jax.ShapeDtypeStruct((rows, 128), f32),) * 2, pltpu.VMEM((2, rows, 128), f32)


def specs(count):
    vmem = pl.BlockSpec(memory_space=pltpu.VMEM)
    return [vmem] * count + [pl.BlockSpec(memory_space=pltpu.SMEM)]


def call_rows_in_back(dqkv, mid, grad, weights, core):
    shapes, scratch = halves_shapes(weights)
    return pl.pallas_call(
        rows_in_back_kernel,
        in_specs=specs(6),
        out_shape=(jax.ShapeDtypeStruct(mid.shape, f32),) + shapes,
        scratch_shapes=[scratch],
        compiler_params=params(24),
        name="rows_in_back",
    )(dqkv, mid, grad, *weights, core)


def columns_back_kernel(
    scale,
    x_ref,
    present_ref,
    grad_ref,
    q_ref,
    k_ref,
    v_ref,
    o_ref,
    core_ref,
    dx_ref,
    mine_ref,
    other_ref,
    sum_ref,
):
    normed, inverse = norm_parts(x_ref[...])
    normed_halves = halves(normed)
    q, k, v = (dot3(normed_halves, halves(w[...])) for w in (q_ref, k_ref, v_ref))
    q = q * scale
    weights, blend = column_attention(q, k, v, stripe_seen(present_ref))
    grad = grad_ref[...]
    grad_halves = halves(grad)
    write_halves(sum_ref, 3, dot3(halves(jnp.transpose(blend)), grad_halves))
    dblend = dot3(grad_halves, halves(o_ref[...]), NT)
    tiles = [[], [], []]
    for tile in range(q.shape[1] // 128):
        lanes = slice(tile * 128, (tile + 1) * 128)
        keys, values = halves(k[:, lanes]), halves(v[:, lanes])
        dq, dk, dv = 0.0, 0.0, 0.0
        for n in range(4):
            query = halves(head_lanes(q[:, lanes], n))
            dhead = halves(head_lanes(dblend[:, lanes], n))
            share = weights[tile * 4 + n]
            dv = dv + dot3(halves(jnp.transpose(share)), dhead)
            dscores = soft_back(share, dot3(dhead, values, NT))
            dk = dk + dot3(halves(jnp.transpose(dscores)), query)
            dq = dq + head_lanes(dot3(dscores, keys), n)
        for kind, value in enumerate((dq * scale, dk, dv)):
            tiles[kind].append(value)
    grads = [jnp.concatenate(t, 1) for t in tiles]
    dx_ref[...] = grad + projections_back(
        normed, inverse, grads, (q_ref, k_ref, v_ref), sum_ref
    )
    give_halves(core_ref, sum_ref, mine_ref, other_ref)


def call_columns_back(x, present, grad, weights, core, scale):
    shapes, scratch = halves_shapes(weights)
    return pl.pallas_call(
        functools.partial(columns_back_kernel, scale),
        in_specs=specs(7),
        out_shape=(jax.ShapeDtypeStruct(x.shape, f32),) + shapes,
        scratch_shapes=[scratch],
        compiler_params=params(24),
        name="columns_back",
    )(x, present, grad, *weights, core)


def bias_kernel(cols, pair_ref, weight_ref, out_ref):
    weight = halves(weight_ref[...])

    def step(t, carry):
        rows = halves(read_rows(pair_ref, four_rows(t, cols)))
        heads = dot3(weight, rows, NT)
        for v in range(2):
            tile = heads[:, v * 128 : (v + 1) * 128][:, None, :]
            for g in range(out_ref.shape[1]):
                out_ref[:, g, pl.ds(2 * t + v, 1), :] = tile
        return carry

    lax.fori_loop(0, 8, step, 0)


def call_bias(pair, weight, copies, cols):
    return pl.pallas_call(
        functools.partial(bias_kernel, cols),
        out_shape=jax.ShapeDtypeStruct((weight.shape[0], copies, 16, 128), f32),
        compiler_params=params(24),
        name="bias",
    )(pair, weight)


def bias_rows(dbias):
    heads, groups, rows = dbias.shape[:3]
    return pl.BlockSpec((heads, groups, 16, 128), lambda t: (0, 0, rows // 16 - 1, 0))


def head_rows(ref, t):
    heads = [ref[:, pl.ds(2 * t + v, 1), :].reshape(-1, 128) for v in range(2)]
    return jnp.concatenate(heads, 1)


def bias_sums_kernel(
    cols, dbias_ref, pair_ref, thin_ref, core_ref, mine_ref, other_ref, whole_ref, sum_ref, dweight_ref
):
    sum_ref[...] = jnp.sum(dbias_ref[...], axis=1)
    dweight_ref[...] = jnp.zeros_like(dweight_ref)

    def step(t, carry):
        dweight_ref[...] += dot3(head_rows(sum_ref, t), read_rows(pair_ref, four_rows(t, cols)))
        return carry

    lax.fori_loop(0, 8, step, 0)
    whole_ref[0], whole_ref[1] = thin_ref[:128], thin_ref[128:]
    whole_ref[0, :, 64 : 64 + dweight_ref.shape[0]] = jnp.transpose(dweight_ref[...])
    give_halves(core_ref, whole_ref, mine_ref, other_ref)


def call_bias_sums(dbias, pair, thin, core, cols):
    heads = dbias.shape[0]
    return pl.pallas_call(
        functools.partial(bias_sums_kernel, cols),
        grid=(1,),
        in_specs=[bias_rows(dbias), full(pair), full(thin), pl.BlockSpec(memory_space=pltpu.SMEM)],
        out_specs=(pl.BlockSpec((128, 128), lambda t: (0, 0)),) * 2,
        out_shape=(jax.ShapeDtypeStruct((128, 128), f32),) * 2,
        scratch_shapes=[
            pltpu.VMEM((2, 128, 128), f32),
            pltpu.VMEM((heads, 16, 128), f32),
            pltpu.VMEM((heads, 128), f32),
        ],
        compiler_params=params(24),
        name="bias_sums",
    )(dbias, pair, thin, core)


def bias_back_kernel(cols, dbias_ref, dmid_ref, weight_ref, out_ref, sum_ref):
    weight = halves(weight_ref[...])
    sum_ref[...] = jnp.sum(dbias_ref[...], axis=1)

    def step(t, carry):
        places = four_rows(t, cols)
        dpair = dot3(jnp.transpose(head_rows(sum_ref, t)), weight)
        write_rows(out_ref, places, read_rows(dmid_ref, places) + dpair)
        return carry

    lax.fori_loop(0, 8, step, 0)


def call_bias_back(dbias, dmid, weight, cols):
    return pl.pallas_call(
        functools.partial(bias_back_kernel, cols),
        grid=(1,),
        in_specs=[bias_rows(dbias), full(dmid), full(weight)],
        out_specs=full(dmid),
        out_shape=jax.ShapeDtypeStruct(dmid.shape, f32),
        scratch_shapes=[pltpu.VMEM((dbias.shape[0], 16, 128), f32)],
        compiler_params=params(24),
        name="bias_back",
    )(dbias, dmid, weight)


def spread_sums_kernel(
    half, cols, mine_ref, early_ref, other_ref, other_early_ref, place_ref, *refs
):
    *outs, whole_ref = refs
    size = early_ref.shape[0] // (half * cols)
    for part, ref in enumerate((early_ref, other_early_ref)):
        for n in range(half * cols):
            row = lax.rem(place_ref[1] + half - n // cols, half)
            chip = row * cols + lax.rem(place_ref[2] + cols - n % cols, cols)
            target = pl.ds(pl.multiple_of(chip * size, 8), size)
            whole_ref[part, target] = ref[n * size : (n + 1) * size]

    def place(first, second, order):
        for half, ref in enumerate((first, second)):
            lanes = slice(half * 128, (half + 1) * 128)
            for n, target in enumerate((0, 1, 2, 3, 4, 5, 6)):
                outs[target][:, lanes] = ref[n * 256 : (n + 1) * 256]
            outs[8][:, lanes] = whole_ref[order[half], 512:768]
            for n, target in enumerate(((13, 15, 12), (14, 16, 17))[half]):
                outs[target][...] = whole_ref[order[half], 768 + n * 128 : 896 + n * 128]
            outs[11][half * 512 : (half + 1) * 512] = whole_ref[order[half], :512]
        thin = jnp.transpose(jnp.concatenate([first[1792:1920], second[1792:1920]], 0))
        outs[7][...] = thin[64 : 64 + outs[7].shape[0], :128]
        outs[9][...] = thin[:32]
        outs[10][...] = thin[32:64]

    @pl.when(place_ref[0] == 0)
    def _():
        place(mine_ref, other_ref, (0, 1))

    @pl.when(place_ref[0] != 0)
    def _():
        place(other_ref, mine_ref, (1, 0))


def call_spread_sums(mine, early, other, other_early, place, half, cols, shapes):
    thin = (7, 9, 10)
    shapes = [shape[::-1] if n in thin else shape for n, shape in enumerate(shapes)]
    sums = pl.pallas_call(
        functools.partial(spread_sums_kernel, half, cols),
        in_specs=specs(4),
        out_shape=tuple(jax.ShapeDtypeStruct(shape, f32) for shape in shapes),
        scratch_shapes=[pltpu.VMEM((2,) + early.shape, f32)],
        compiler_params=params(24),
        name="spread_sums",
    )(mine, early, other, other_early, place)
    return [jnp.transpose(x) if n in thin else x for n, x in enumerate(sums)]


precise = lax.Precision.HIGH
everyone = ("half", "core", "col")
row = ("half", "core")
chips = ("half", "col")


def affine_map(tensor, weight):
    return jnp.einsum("...a,ab->...b", tensor, weight, precision=precise)


def exchange(chunks, axis):
    shape = chunks.shape
    flat = chunks.reshape(shape[0], -1, 128)
    return lax.all_to_all(flat, axis, 0, 0, tiled=True).reshape(shape)


def collect(block, axis, count):
    return exchange(jnp.broadcast_to(block[None], (count,) + block.shape), axis)


def tall(weight):
    return jnp.concatenate([weight[:, :128], weight[:, 128:]], 0)


def together(*arrays):
    return lax.optimization_barrier(arrays)


class Layout:
    def __init__(self, mesh_rows, mesh_cols, pair, chains, heads, head_width):
        self.mesh_rows, self.mesh_cols = mesh_rows, mesh_cols
        self.devices = mesh_rows * mesh_cols
        self.rows_here, self.cols_here, self.pair_width = pair
        self.span = self.rows_here * mesh_rows
        self.slim = self.span // self.devices
        self.chains, self.heads, self.head_width = chains, heads, head_width
        self.chain_groups = self.devices // heads
        self.group_chains = chains // self.chain_groups
        self.channels_here = self.pair_width // self.devices
        self.scale = head_width ** (-0.5)
        self.turn = [
            (g, (g % mesh_rows) * mesh_cols + g // mesh_rows) for g in range(self.devices)
        ]
        self.turn_back = [(b, a) for a, b in self.turn]

        self.swap = [(0, 1), (1, 0)]
        self.core = lax.axis_index("core").reshape(1)

    def to_slim(self, x):
        return lax.all_to_all(x, "col", 1, 0, tiled=True)

    def both_views(self, grad, out):
        count, slim, width = self.mesh_cols, self.slim, grad.shape[2]
        grad = jnp.transpose(grad.reshape(-1, count, slim, width), (1, 0, 2, 3))
        both = jnp.stack([grad, out.reshape(count, -1, slim, width)], 1)
        return both.reshape(count, -1, width)

    def split_views(self, both):
        count, slim, width = self.mesh_cols, self.slim, both.shape[2]
        both = both.reshape(count, 2, -1, slim, width)
        out = jnp.transpose(both[:, 1], (1, 0, 2, 3)).reshape(-1, count * slim, width)
        return both[:, 0].reshape(-1, slim, width), out

    def from_slim_permuted(self, x):
        count, slim = self.mesh_cols, x.shape[1]
        here = lax.axis_index("col")
        blocks = x.reshape(count, -1, slim, x.shape[2])
        out = jnp.zeros((blocks.shape[1], count * slim, x.shape[2]), f32)
        for n in range(count):
            block = lax.dynamic_index_in_dim(blocks, lax.rem(here + n, count), 0, False)
            if n:
                block = lax.ppermute(block, "col", [(s, (s + n) % count) for s in range(count)])
            source = lax.rem(here + count - n, count)
            out = lax.dynamic_update_slice_in_dim(out, block, source * slim, 1)
        return out

    def from_others(self, arrays, axis="col"):
        count = len(arrays)
        return [
            lax.ppermute(x, axis, [(s, (s + n) % count) for s in range(count)]) if n else x
            for n, x in enumerate(arrays)
        ]

    def share_sum(self, x, axis, count):
        here = lax.axis_index(axis)
        x = x.reshape(count, -1, 128)
        parts = [
            lax.dynamic_index_in_dim(x, lax.rem(here + n, count), 0, False) for n in range(count)
        ]
        return functools.reduce(jnp.add, self.from_others(parts, axis))

    def all_parts(self, x, axis, count):
        return jnp.concatenate(self.from_others([x] * count, axis), 0)

    def core_sum(self, sums):
        sums = [kept + lax.ppermute(given, "core", self.swap) for kept, given in sums]
        return jnp.concatenate(sums, 0)

    def half_sum(self, early):
        early = self.core_sum(early)
        pad = -early.shape[0] % (4 * self.devices)
        early = jnp.pad(early, ((0, pad), (0, 0))) if pad else early
        return self.share_sum(early, "half", self.mesh_rows // 2)

    def sum_all(self, late, early, *beside):
        half, cols = self.mesh_rows // 2, self.mesh_cols
        late, early = together(self.core_sum(late), early)
        late = exchange(late.reshape(half, -1, 128), "half")
        late, early = together(late, self.share_sum(early, "col", cols))
        late = exchange(late.sum(0).reshape(cols, -1, 128), "col")
        late, early, *beside = together(late, self.all_parts(early, "col", cols), *beside)
        late = collect(late.sum(0), "col", cols).reshape(-1, 128)
        late, early = together(late, self.all_parts(early, "half", half))
        late = collect(late, "half", half).reshape(-1, 128)
        late, other_early = together(late, lax.ppermute(early, "core", self.swap))
        return (late, early, lax.ppermute(late, "core", self.swap), other_early), beside


def msa_plain(size, alignment_features, residue_couplings, present, weights):
    chains, slim, heads, head_width = size.chains, size.slim, size.heads, size.head_width
    devices, groups, group_chains = size.devices, size.chain_groups, size.group_chains
    rows_here, cols_here, span = size.rows_here, size.cols_here, size.span
    mesh_rows, mesh_cols = size.mesh_rows, size.mesh_cols
    bias = jnp.transpose(affine_map(residue_couplings, weights[7]), (2, 0, 1))
    bias = jnp.broadcast_to(bias[:, None], (heads, groups, rows_here, cols_here))
    bias = exchange(bias.reshape(devices, rows_here, cols_here), everyone)
    bias = bias.reshape(mesh_rows, mesh_cols, rows_here, cols_here)
    bias = jnp.transpose(bias, (0, 2, 1, 3)).reshape(span, span)

    stripe = size.to_slim(alignment_features)
    normed, _ = norm_parts(stripe)
    col_q, col_k, col_v = (
        affine_map(normed, w).reshape(chains, slim, heads, head_width) for w in weights[:3]
    )
    scores = jnp.einsum("sihd,tihd->ihst", col_q, col_k, precision=precise) * size.scale
    scores = jnp.where(present[None, None, None, :] > 0, scores, -1000000000.0)
    blend = jnp.einsum(
        "ihst,tihd->sihd", jax.nn.softmax(scores, axis=-1), col_v, precision=precise
    )
    msa_col = stripe + affine_map(blend.reshape(chains, slim, heads * head_width), weights[3])

    normed, _ = norm_parts(msa_col)
    qkv = jnp.stack([affine_map(normed, w) for w in weights[4:7]])
    qkv = qkv.reshape(3, groups, group_chains, slim, heads, head_width)
    qkv = jnp.transpose(qkv, (4, 1, 0, 2, 3, 5))
    qkv = exchange(qkv.reshape(devices, 3, group_chains, slim, head_width), everyone)
    qkv = jnp.transpose(qkv, (1, 2, 0, 3, 4)).reshape(3, group_chains, span, head_width)
    scores = jnp.einsum("sid,sjd->sij", qkv[0], qkv[1], precision=precise) * size.scale
    shares = jax.nn.softmax(scores + bias[None], axis=-1)
    blend = jnp.einsum("sij,sjd->sid", shares, qkv[2], precision=precise)
    blend = blend.reshape(group_chains, devices, slim, head_width)
    blend = exchange(jnp.transpose(blend, (1, 0, 2, 3)), everyone)
    blend = blend.reshape(heads, chains, slim, head_width)
    blend = jnp.transpose(blend, (1, 2, 0, 3)).reshape(chains, slim, heads * head_width)
    msa_out = msa_col + affine_map(blend, weights[8])

    normed, _ = norm_parts(msa_out)
    left = affine_map(normed, weights[9]) * (present / jnp.sum(present))[:, None, None]
    left = jnp.transpose(left.reshape(chains // 4, 4, slim, 32), (2, 0, 1, 3))
    left = collect(left.reshape(slim, chains // 4, 128), "col", mesh_cols).reshape(-1, 128)
    right = affine_map(normed, weights[10]).reshape(chains // 16, 16, slim, 4, 8)
    right = jnp.transpose(right, (3, 0, 2, 1, 4)).reshape(-1, 128)
    right = collect(lax.ppermute(right, everyone, size.turn), row, mesh_rows)
    right = right.reshape(mesh_rows, 4, chains // 16, slim, 128)
    right = jnp.transpose(right, (1, 0, 3, 2, 4)).reshape(4, cols_here // 8, 8, chains // 16, 128)
    return msa_out, [left], jnp.transpose(right, (1, 0, 3, 2, 4))


def msa_forward(size, alignment_features, residue_couplings, present, weights):
    chains, slim, devices = size.chains, size.slim, size.devices
    mesh_rows, mesh_cols = size.mesh_rows, size.mesh_cols
    pair_flat = residue_couplings.reshape(-1, size.pair_width)
    tokens = chains * slim
    seen = jnp.repeat(present, slim)[None]
    share = jnp.repeat(present / jnp.sum(present), slim)[:, None]
    source, target = jnp.transpose(weights[9]), jnp.transpose(weights[10])
    offset = jnp.transpose(weights[7])
    stripe = size.to_slim(alignment_features).reshape(tokens, -1)
    bias = call_bias(pair_flat, offset, size.chain_groups, size.cols_here)
    bias = bias.reshape(devices, 16, 128)
    msa_col, qkv = call_columns(stripe, seen, bias, weights[:7], size.group_chains, size.scale)
    qkv = exchange(qkv, everyone)
    blend = call_rows(qkv, mesh_rows, mesh_cols, size.scale)
    blend = exchange(blend, everyone)
    msa_out, left, right = call_rows_out(blend, msa_col, share, weights[8], source, target)
    left = size.from_others([left.reshape(-1, 128)] * mesh_cols)
    right, *left = together(lax.ppermute(right, everyone, size.turn), *left)
    right = collect(right, row, mesh_rows)

    def back(grad, d_lefts, d_right, d_mid, pair_mid, side_sums, outer_sums):
        d_lefts = size.from_others(d_lefts)
        d_right = exchange(d_right, row).sum(0)
        d_right = lax.ppermute(d_right, everyone, size.turn_back)
        d_out, d_blend, thin, *out_sums = call_rows_out_back(
            d_lefts,
            d_right,
            grad.reshape(tokens, -1),
            msa_out,
            blend,
            share,
            weights[8],
            source,
            target,
            size.core,
        )
        d_mid, d_blend = together(d_mid, d_blend)
        outer_sums = outer_sums(d_mid)
        d_blend, *outer_sums = together(exchange(d_blend, everyone), *outer_sums)
        d_qkv = call_rows_back(qkv, d_blend, mesh_rows, mesh_cols, size.scale)
        pair_mid, d_qkv = together(pair_mid, d_qkv)
        side_sums = side_sums(pair_mid)
        early = size.half_sum((outer_sums, out_sums, side_sums))
        d_qkv, early = together(exchange(d_qkv, everyone), early)
        d_col, *in_sums = call_rows_in_back(d_qkv, msa_col, d_out, weights[4:7], size.core)
        d_stripe, *col_sums = call_columns_back(
            stripe, seen, d_col, weights[:4], size.core, size.scale
        )
        d_bias = d_qkv.reshape(size.heads, size.chain_groups, -1, 128)
        thin_sums = call_bias_sums(d_bias, pair_flat, thin, size.core, size.cols_here)
        d_pair = call_bias_back(d_bias, d_mid, offset, size.cols_here)
        d_features = size.from_slim_permuted(d_stripe.reshape(chains, slim, -1))
        late = (col_sums, in_sums, thin_sums)
        return d_features, d_pair, late, early

    return (msa_out.reshape(chains, slim, -1), left, right), back


def msa_plain_forward(size, alignment_features, residue_couplings, present, weights):
    chains, rows_here = size.chains, size.rows_here
    outputs, pull = jax.vjp(
        lambda x, y, w: msa_plain(size, x, y, present, w),
        alignment_features,
        residue_couplings,
        weights,
    )

    def back(grad, d_lefts, d_right, d_mid, pair_mid, side_sums, outer_sums):
        d_left = d_lefts[0].reshape(rows_here // 4, chains // 4, 4, 4, 32)
        d_left = jnp.transpose(d_left, (0, 3, 1, 2, 4)).reshape(-1, 128)
        d_features, d_pair, d_weights = pull((grad, [d_left], d_right))
        d_pair = d_pair.reshape(-1, size.pair_width) + d_mid
        thin = [d_weights[9], d_weights[10], jnp.pad(d_weights[7], ((0, 128), (0, 0)))]
        thin = jnp.pad(jnp.concatenate(thin, 1), ((0, 0), (0, 64 - size.heads)))
        core = size.core[0]
        pick = lambda x, n: lax.dynamic_index_in_dim(x, n, 0, False)
        own = lambda x: (pick(x, core), pick(x, 1 - core))
        cut = lambda ws: own(
            jnp.stack([jnp.concatenate([w[:, n : n + 128] for w in ws], 0) for n in (0, 128)])
        )
        late = (cut(d_weights[:4]), cut(d_weights[4:7]), own(thin.reshape(2, -1, 128)))
        early = (outer_sums(d_mid), cut(d_weights[8:9]), side_sums(pair_mid))
        return d_features, d_pair, late, size.half_sum(early)

    return outputs, back


def per_device(mesh_rows, mesh_cols, *arguments):
    (
        alignment_features,
        residue_couplings,
        chain_indicator,
        alignment_result_adjoint,
        coupling_result_adjoint,
        *weights,
    ) = arguments
    present = chain_indicator.astype(jnp.float32)
    heads = weights[7].shape[1]
    size = Layout(
        mesh_rows,
        mesh_cols,
        residue_couplings.shape,
        present.shape[0],
        heads,
        weights[4].shape[1] // heads,
    )
    devices, channels_here = size.devices, size.channels_here
    cols_here, pair_width = size.cols_here, size.pair_width
    (
        tensor_result_matrix,
        source_side_matrix,
        source_side_switch,
        target_side_matrix,
        target_side_switch,
        trilateral_result_switch,
        trilateral_result_matrix,
    ) = weights[11:]

    sides = (source_side_switch, target_side_switch, source_side_matrix, target_side_matrix)
    shift = channels_here.bit_length() - 1
    forward = msa_forward if size.slim == 8 else msa_plain_forward
    (msa_slim, left_rows, right_rows), msa_back = forward(
        size, alignment_features, residue_couplings, present, tuple(weights[:11])
    )
    pair_flat = residue_couplings.reshape(-1, pair_width)
    grad_flat = coupling_result_adjoint.reshape(-1, pair_width)
    count = len(left_rows)
    first = (lax.axis_index("col") if count > 1 else jnp.int32(0)).reshape(1)
    blocks = call_blocks(first, left_rows)
    pair_mid, edges, prods = call_edges(
        blocks, right_rows, tensor_result_matrix, pair_flat, sides, cols_here, shift
    )
    edges = exchange(edges.reshape(devices, 2, channels_here, 16, 128), everyone)
    triangle = exchange(call_triangle(edges, mesh_rows, mesh_cols), everyone)
    pair_out, d_triangle, d_logit, g_tri_out = call_finish(
        triangle.reshape(pair_width, 16, 128),
        pair_mid,
        grad_flat,
        trilateral_result_switch,
        trilateral_result_matrix,
        cols_here,
    )
    views = (alignment_result_adjoint, msa_slim)
    *views, d_triangle = together(*views, d_triangle)
    views = size.both_views(*views)
    d_triangle = exchange(d_triangle.reshape(devices, channels_here, 16, 128), everyone)
    d_edges = exchange(call_triangle_back(edges, d_triangle, mesh_rows, mesh_cols), everyone)
    d_edges, views = together(d_edges, views)
    views = lax.all_to_all(views, "col", 0, 0, tiled=True)
    d_mid, d_logits, d_right, *d_lefts = call_edges_back(
        d_edges.reshape(2 * pair_width, 16, 128),
        pair_mid,
        grad_flat,
        d_logit,
        (*sides, trilateral_result_switch),
        right_rows,
        tensor_result_matrix,
        blocks,
        first,
        count,
        cols_here,
        shift,
    )
    d_right, views = together(d_right, views)
    msa_grad, msa_out = size.split_views(views)

    def side_sums(pair_mid):
        return call_side_sums(pair_mid, d_logits, g_tri_out, size.core, cols_here, shift)

    def outer_sums(d_mid):
        return call_outer_sums(d_mid, prods, size.core, cols_here)

    alignment_adjoint, coupling_adjoint, late, early = msa_back(
        msa_grad, d_lefts, d_right, d_mid, pair_mid, side_sums, outer_sums
    )
    sums, (alignment_adjoint, coupling_adjoint) = size.sum_all(
        late, early, alignment_adjoint, coupling_adjoint
    )
    place = jnp.stack([lax.axis_index(axis) for axis in ("core", "half", "col")])
    summed = call_spread_sums(*sums, place, mesh_rows // 2, mesh_cols, [w.shape for w in weights])
    return (
        msa_out,
        pair_out.reshape(residue_couplings.shape),
        alignment_adjoint,
        coupling_adjoint.reshape(residue_couplings.shape),
        *summed,
    )


def solution(mesh):
    mesh_rows, mesh_cols = mesh.shape["row"], mesh.shape["col"]

    def local(*arguments):
        return per_device(mesh_rows, mesh_cols, *arguments)

    split = jax.sharding.Mesh(
        mesh.devices.reshape(mesh_rows // 2, 2, mesh_cols), ("half", "core", "col")
    )
    whole = P()
    msa = P("col", row, None)
    pair = P(row, "col", None)
    return jax.shard_map(
        local,
        mesh=split,
        in_specs=(msa, pair, whole, msa, pair) + (whole,) * 18,
        out_specs=(msa, pair, msa, pair) + (whole,) * 18,
        check_vma=False,
    )
```

```python
import functools

import jax
import jax.numpy as jnp
from jax import lax
from jax.experimental import pallas as pl
from jax.experimental.pallas import tpu as pltpu
from jax.sharding import PartitionSpec as P

bf16, f32 = jnp.bfloat16, jnp.float32
NN = ((1,), (0,))
NT = ((1,), (1,))
TN = ((0,), (0,))


def one_pass(a, b, dims=NN):
    return lax.dot_general(a, b, (dims, ((), ())), preferred_element_type=f32)


def halves(x):
    high = x.astype(bf16)
    return high, (x - high.astype(f32)).astype(bf16)


def dot3(a, b, dims=NN):
    a_high, a_low = a if isinstance(a, tuple) else halves(a)
    b_high, b_low = b if isinstance(b, tuple) else halves(b)
    return one_pass(a_high, b_high, dims) + (
        one_pass(a_high, b_low, dims) + one_pass(a_low, b_high, dims)
    )


def rounded(pair, rows):
    return pair[0][rows], pair[1][rows]


def iota(shape, dim):
    return lax.broadcasted_iota(jnp.int32, shape, dim)


def norm_parts(x):
    centered = x - jnp.mean(x, axis=-1, keepdims=True)
    inverse = lax.rsqrt(jnp.mean(centered * centered, axis=-1, keepdims=True) + 1e-05)
    return centered * inverse, inverse


def norm_back(normed, inverse, grad):
    return inverse * (
        grad
        - jnp.mean(grad, axis=-1, keepdims=True)
        - normed * jnp.mean(grad * normed, axis=-1, keepdims=True)
    )


def stacked3(a, b, dims=NN):
    a_high, a_low = a if isinstance(a, tuple) else halves(a)
    b_high, b_low = b if isinstance(b, tuple) else halves(b)
    return one_pass(
        jnp.concatenate([a_high, a_low, a_high], dims[0][0]),
        jnp.concatenate([b_high, b_high, b_low], dims[1][0]),
        dims,
    )


def row_of(t, u):
    return 2 * t + u // 2 + 16 * (u % 2)


def same_slot(chains):
    shape = (chains * 8, 256)
    return (iota(shape, 0) & 7) == (iota(shape, 1) & 7)


def blocks_kernel(chains, first_ref, *refs):
    *part_refs, out_ref, left_ref = refs
    groups, count = chains // 4, len(part_refs)
    size = part_refs[0].shape[0]
    t = pl.program_id(0)

    @pl.when(t == 0)
    def _():
        for n, ref in enumerate(part_refs):
            place = lax.rem(first_ref[0] + count - n, count) * size
            left_ref[pl.ds(pl.multiple_of(place, 8), size), :] = ref[...]

    shape = (chains * 8, chains)
    chain = iota(shape, 0) >> 3
    lift = jnp.where(iota(shape, 1) == (chain & 3) * groups + (chain >> 2), 1.0, 0.0).astype(bf16)
    same = same_slot(chains)
    rows = [
        left_ref[pl.ds(pl.multiple_of(row_of(t, u) * groups, groups), groups), :] for u in range(4)
    ]
    rows = jnp.concatenate(halves(jnp.concatenate(rows, 0)), 0)
    shape = (128, 256)
    slabs = []
    for n in range(4):
        spread = ((iota(shape, 0) >> 5) == n) & ((iota(shape, 0) & 31) == (iota(shape, 1) >> 3))
        slabs.append(one_pass(rows, jnp.where(spread, 1.0, 0.0).astype(bf16)))
    for part in range(2):
        for u in range(4):
            place = slice((part * 4 + u) * groups, (part * 4 + u + 1) * groups)
            slab = jnp.concatenate([x[place] for x in slabs], 0).astype(bf16)
            out_ref[0, u, part] = jnp.where(same, one_pass(lift, slab), 0.0).astype(bf16)


def call_blocks(first, parts):
    rows = sum(part.shape[0] for part in parts)
    chains = rows // 32 * 4
    shape = (8, 4, 2, chains * 8, 256)
    return pl.pallas_call(
        functools.partial(blocks_kernel, chains),
        grid=(8,),
        in_specs=[pl.BlockSpec(memory_space=pltpu.SMEM)] + [full(part) for part in parts],
        out_specs=step_block(shape),
        out_shape=jax.ShapeDtypeStruct(shape, bf16),
        scratch_shapes=[pltpu.VMEM((rows, 128), f32)],
        compiler_params=params(),
        name="blocks",
    )(first, *parts)


def join_right(ref, out_ref):
    cols = ref.shape[0] * 8
    for g in range(4):
        for n in range(ref.shape[2]):
            out_ref[g * cols : (g + 1) * cols, n * 128 : (n + 1) * 128] = ref[:, g, n].reshape(
                cols, 128
            )


def cut_right(ref, out_ref):
    cols = out_ref.shape[0] * 8
    for g in range(4):
        for n in range(out_ref.shape[2]):
            tile = ref[g * cols : (g + 1) * cols, n * 128 : (n + 1) * 128]
            out_ref[:, g, n] = tile.reshape(-1, 8, 128)


def outer_weights(ref, out_ref):
    whole = ref[...].reshape(32, 4, 8, 128)
    for g in range(4):
        out_ref[g, 0], out_ref[g, 1] = halves(whole[:, g].reshape(256, 128))


def params(mebibytes=56):
    return pltpu.CompilerParams(vmem_limit_bytes=mebibytes * 2**20)


def full(array):
    return pl.BlockSpec(array.shape, lambda t, n=len(array.shape): (0,) * n)


def step_block(shape):
    return pl.BlockSpec((1,) + shape[1:], lambda t, n=len(shape): (t,) + (0,) * (n - 1))


def pair_of(ref, *index):
    return ref[(*index, 0)], ref[(*index, 1)]


def chunk_order(shift):
    shape = (256, 256)
    place, width = iota(shape, 0), 1 << shift
    channel = place & 127
    target = ((channel >> shift) << (shift + 1)) + (channel & (width - 1))
    target = target + ((place >> 7) << shift)
    return jnp.where(iota(shape, 1) == target, 1.0, 0.0).astype(bf16)


def side_halves(shift, refs, out_ref):
    order = chunk_order(shift)
    for n in range(2):
        both = halves(jnp.concatenate([refs[2 * n][...], refs[2 * n + 1][...]], 1))
        for part in range(2):
            out_ref[part, :, n * 256 : (n + 1) * 256] = one_pass(both[part], order).astype(bf16)
    if len(refs) == 5:
        out_ref[0, :, 512:], out_ref[1, :, 512:] = halves(refs[4][...])


def prepare_kernel(shift, outer_ref, *refs):
    *side_refs, outer_halves, sides_halves = refs
    outer_weights(outer_ref, outer_halves)
    side_halves(shift, side_refs, sides_halves)


def call_prepare(outer, sides, shift):
    return pl.pallas_call(
        functools.partial(prepare_kernel, shift),
        out_shape=(
            jax.ShapeDtypeStruct((4, 2, 256, 128), bf16),
            jax.ShapeDtypeStruct((2, 128, 640), bf16),
        ),
        compiler_params=params(),
        name="prepare",
    )(outer, *sides)


def edges_kernel(
    cols,
    block_ref,
    right_ref,
    outer_halves,
    sides_halves,
    pair_ref,
    mid_ref,
    edge_ref,
    prod_ref,
    whole_ref,
    right_halves,
):
    t = pl.program_id(0)

    @pl.when(t == 0)
    def _():
        join_right(right_ref, whole_ref)
        right_halves[0], right_halves[1] = halves(whole_ref[...])

    right = pair_of(right_halves)
    places = four_rows(t, cols)
    for u in range(4):
        high, low = halves(stacked3(right, pair_of(block_ref, 0, u)))
        for g in range(4):
            prod_ref[0, g, 0, u * cols : (u + 1) * cols] = high[g * cols : (g + 1) * cols]
            prod_ref[0, g, 1, u * cols : (u + 1) * cols] = low[g * cols : (g + 1) * cols]
    update = 0.0
    for g in range(4):
        update = update + dot3(pair_of(prod_ref, 0, g), pair_of(outer_halves, g))
    mid = update + read_rows(pair_ref, places)
    write_rows(mid_ref, places, mid)
    normed, _ = norm_parts(mid)
    sides = rounded(pair_of(sides_halves), (slice(None), slice(0, 512)))
    logits = stacked3(normed, sides)
    write_turned(edge_ref, t, jax.nn.sigmoid(logits[:, :256]) * logits[:, 256:])


def call_edges(blocks, right, outer, sides, pair, cols):
    rows, depth = pair.shape[0], blocks.shape[3]
    prods = (8, 4, 2, 4 * cols, 256)
    return pl.pallas_call(
        functools.partial(edges_kernel, cols),
        grid=(8,),
        in_specs=[step_block(blocks.shape)] + [full(x) for x in (right, outer, sides, pair)],
        out_specs=(
            pl.BlockSpec((rows, 128), lambda t: (0, 0)),
            pl.BlockSpec((256, 16, 128), lambda t: (0, 0, 0)),
            step_block(prods),
        ),
        out_shape=(
            jax.ShapeDtypeStruct((rows, 128), f32),
            jax.ShapeDtypeStruct((256, 16, 128), f32),
            jax.ShapeDtypeStruct(prods, bf16),
        ),
        scratch_shapes=[
            pltpu.VMEM((4 * cols, depth), f32),
            pltpu.VMEM((2, 4 * cols, depth), bf16),
        ],
        compiler_params=params(),
        name="edges",
    )(blocks, right, outer, sides, pair)


def factors_kernel(cols, mid_ref, sides_halves, out_ref):
    normed, _ = norm_parts(read_rows(mid_ref, four_rows(pl.program_id(0), cols)))
    sides = rounded(pair_of(sides_halves), (slice(None), slice(0, 512)))
    logits = stacked3(normed, sides)
    gate = jax.nn.sigmoid(logits[:, :256])
    out_ref[0, :, :256] = logits[:, 256:] * gate * (1.0 - gate)
    out_ref[0, :, 256:] = gate


def call_factors(mid, sides, cols):
    shape = (8, 4 * cols, 512)
    return pl.pallas_call(
        functools.partial(factors_kernel, cols),
        grid=(8,),
        in_specs=[full(mid), full(sides)],
        out_specs=step_block(shape),
        out_shape=jax.ShapeDtypeStruct(shape, f32),
        compiler_params=params(),
        name="factors",
    )(mid, sides)


def join_tiles(chunks, mesh_rows, mesh_cols, out_ref):
    plain = chunks.reshape(mesh_rows * mesh_cols * 16, 128)
    rolled = pltpu.roll(plain, 64, 1)
    first = iota((16, 128), 1) < 64
    for r in range(mesh_rows):
        for t in range(mesh_cols // 2):
            even = slice((r * mesh_cols + 2 * t) * 16, (r * mesh_cols + 2 * t + 1) * 16)
            odd = slice((r * mesh_cols + 2 * t + 1) * 16, (r * mesh_cols + 2 * t + 2) * 16)
            lanes = slice(t * 128, (t + 1) * 128)
            out_ref[r * 32 : r * 32 + 16, lanes] = jnp.where(first, plain[even], rolled[odd])
            out_ref[r * 32 + 16 : r * 32 + 32, lanes] = jnp.where(first, rolled[even], plain[odd])


def cut_tiles(whole, mesh_rows, mesh_cols, store):
    first = iota((16, 128), 1) < 64
    for t in range(mesh_cols // 2):
        plain = whole[:, t * 128 : (t + 1) * 128]
        rolled = pltpu.roll(plain, 64, 1)
        for r in range(mesh_rows):
            low = slice(r * 32, r * 32 + 16)
            high = slice(r * 32 + 16, r * 32 + 32)
            store(r * mesh_cols + 2 * t, jnp.where(first, plain[low], rolled[high]))
            store(r * mesh_cols + 2 * t + 1, jnp.where(first, rolled[low], plain[high]))


def triangle_kernel(mesh_rows, mesh_cols, edge_ref, out_ref, left_ref, right_ref):
    join_tiles(edge_ref[:, 0, 0], mesh_rows, mesh_cols, left_ref)
    join_tiles(edge_ref[:, 1, 0], mesh_rows, mesh_cols, right_ref)

    def store(d, tile):
        out_ref[d, 0] = tile

    cut_tiles(dot3(left_ref[...], right_ref[...], NT), mesh_rows, mesh_cols, store)


def call_triangle(edges, mesh_rows, mesh_cols):
    devices, _, channels = edges.shape[:3]
    span = mesh_rows * 32
    return pl.pallas_call(
        functools.partial(triangle_kernel, mesh_rows, mesh_cols),
        grid=(channels,),
        in_specs=[pl.BlockSpec((devices, 2, 1, 16, 128), lambda n: (0, 0, n, 0, 0))],
        out_specs=pl.BlockSpec((devices, 1, 16, 128), lambda n: (0, n, 0, 0)),
        out_shape=jax.ShapeDtypeStruct((devices, channels, 16, 128), f32),
        scratch_shapes=[pltpu.VMEM((span, span), f32)] * 2,
        compiler_params=params(32),
        name="triangle",
    )(edges)


def triangle_back_kernel(
    mesh_rows, mesh_cols, edge_ref, grad_ref, out_ref, left_ref, right_ref, whole_ref
):
    join_tiles(edge_ref[:, 0, 0], mesh_rows, mesh_cols, left_ref)
    join_tiles(edge_ref[:, 1, 0], mesh_rows, mesh_cols, right_ref)
    join_tiles(grad_ref[:, 0], mesh_rows, mesh_cols, whole_ref)

    def store(kind):
        def put(d, tile):
            out_ref[d, kind, 0] = tile

        return put

    whole = whole_ref[...]
    cut_tiles(dot3(whole, right_ref[...]), mesh_rows, mesh_cols, store(0))
    cut_tiles(dot3(jnp.transpose(whole), left_ref[...]), mesh_rows, mesh_cols, store(1))


def call_triangle_back(edges, grad, mesh_rows, mesh_cols):
    devices, _, channels = edges.shape[:3]
    span = mesh_rows * 32
    both = pl.BlockSpec((devices, 2, 1, 16, 128), lambda n: (0, 0, n, 0, 0))
    return pl.pallas_call(
        functools.partial(triangle_back_kernel, mesh_rows, mesh_cols),
        grid=(channels,),
        in_specs=[both, pl.BlockSpec((devices, 1, 16, 128), lambda n: (0, n, 0, 0))],
        out_specs=both,
        out_shape=jax.ShapeDtypeStruct(edges.shape, f32),
        scratch_shapes=[pltpu.VMEM((span, span), f32)] * 3,
        compiler_params=params(32),
        name="triangle_back",
    )(edges, grad)


def four_rows(t, cols):
    return [
        pl.ds(pl.multiple_of((2 * t + u // 2 + 16 * (u % 2)) * cols, cols), cols) for u in range(4)
    ]


def read_rows(ref, places):
    return jnp.concatenate([ref[p, :] for p in places], 0)


def write_rows(ref, places, value):
    size = value.shape[0] // len(places)
    for u, p in enumerate(places):
        ref[p, :] = value[u * size : (u + 1) * size]


def read_turned(ref, t):
    parts = []
    for v in range(2):
        tile = ref[:, pl.ds(2 * t + v, 1), :]
        parts.append(jnp.transpose(tile.reshape(tile.shape[0], 128)))
    return jnp.concatenate(parts, 0)


def write_turned(ref, t, value):
    for v in range(2):
        turned = jnp.transpose(value[v * 128 : (v + 1) * 128])
        ref[:, pl.ds(2 * t + v, 1), :] = turned[:, None, :]


def finish_kernel(
    cols, tri_ref, mid_ref, grad_ref, gate_ref, proj_ref, out_ref, dtri_ref, dlogit_ref, dproj_ref
):
    gate_w = halves(gate_ref[...])
    proj_w = halves(proj_ref[...])
    dproj_ref[...] = jnp.zeros_like(dproj_ref)

    def step(t, carry):
        places = four_rows(t, cols)
        mid = read_rows(mid_ref, places)
        grad = read_rows(grad_ref, places)
        normed, _ = norm_parts(mid)
        tri, tri_inverse = norm_parts(read_turned(tri_ref, t))
        tri_halves = halves(tri)
        gate = jax.nn.sigmoid(dot3(normed, gate_w))
        value = dot3(tri_halves, proj_w)
        write_rows(out_ref, places, mid + gate * value)
        dvalue = halves(grad * gate)
        write_rows(dlogit_ref, places, grad * value * gate * (1.0 - gate))
        dproj_ref[...] += stacked3(halves(jnp.transpose(tri)), dvalue)
        write_turned(dtri_ref, t, norm_back(tri, tri_inverse, stacked3(dvalue, proj_w, NT)))
        return carry

    lax.fori_loop(0, 8, step, 0)


def call_finish(tri, mid, grad, gate, proj, cols):
    rows = mid.shape[0]
    return pl.pallas_call(
        functools.partial(finish_kernel, cols),
        out_shape=(
            jax.ShapeDtypeStruct((rows, 128), f32),
            jax.ShapeDtypeStruct((128, 16, 128), f32),
            jax.ShapeDtypeStruct((rows, 128), f32),
            jax.ShapeDtypeStruct((128, 128), f32),
        ),
        compiler_params=params(32),
        name="finish",
    )(tri, mid, grad, gate, proj)


def edges_back_kernel(
    cols,
    chains,
    dedge_ref,
    mid_ref,
    grad_ref,
    dlogit_ref,
    sides_halves,
    right_ref,
    outer_halves,
    factor_ref,
    block_ref,
    first_ref,
    dmid_ref,
    dlogits_ref,
    dright_ref,
    *refs,
):
    *dleft_refs, whole_ref, turned_halves, fold_ref, dslab_ref, dleft_ref = refs
    t = pl.program_id(0)

    @pl.when(t == 0)
    def _():
        join_right(right_ref, whole_ref)
        turned_halves[0], turned_halves[1] = halves(jnp.transpose(whole_ref[...]))
        shape = (256, 128)
        for u in range(4):
            lane = 64 * (u % 2) + 32 * (u // 2) + (iota(shape, 0) >> 3)
            fold = jnp.where(iota(shape, 1) == lane, 1.0, 0.0).astype(bf16)
            fold_ref[512 * u : 512 * u + 256] = fold
            fold_ref[512 * u + 256 : 512 * u + 512] = fold
        whole_ref[...] = jnp.zeros_like(whole_ref)

    same = same_slot(chains)
    sides = pair_of(sides_halves)
    places = four_rows(t, cols)
    normed, inverse = norm_parts(read_rows(mid_ref, places))
    dedge = read_turned(dedge_ref, t)
    dlogits = [
        dedge * factor_ref[0, :, :256],
        dedge * factor_ref[0, :, 256:],
        read_rows(dlogit_ref, places),
    ]
    dlogits = halves(jnp.concatenate(dlogits, 1))
    dlogits_ref[0, 0], dlogits_ref[0, 1] = dlogits
    dmid = read_rows(grad_ref, places) + norm_back(normed, inverse, dot3(dlogits, sides, NT))
    write_rows(dmid_ref, places, dmid)
    dmid = halves(dmid)
    dprod = [halves(stacked3(dmid, pair_of(outer_halves, g), NT)) for g in range(4)]
    here, diagonal = [], []
    turned = pair_of(turned_halves)
    for u in range(4):
        rows = slice(u * cols, (u + 1) * cols)
        here.append([jnp.concatenate([dprod[g][n][rows] for g in range(4)], 0) for n in range(2)])
        diagonal += halves(jnp.where(same, stacked3(turned, tuple(here[u])), 0.0))
    right_terms = [x for high, low in here for x in (high, low, high)]
    block_terms = [block_ref[0, u, n] for u in range(4) for n in (0, 0, 1)]
    whole_ref[...] += one_pass(
        jnp.concatenate(right_terms, 1), jnp.concatenate(block_terms, 1), NT
    )
    dslab = one_pass(jnp.concatenate(diagonal, 1), fold_ref[...])
    dslab_ref[t] = jnp.sum(dslab.reshape(chains, 8, 128), axis=1)

    @pl.when(t == 7)
    def _():
        cut_right(whole_ref, dright_ref)
        first = iota((chains, 128), 1) < 64
        for n in range(4):
            even, odd = dslab_ref[2 * n], dslab_ref[2 * n + 1]
            dleft_ref[n] = jnp.where(first, even, pltpu.roll(odd, 64, 1))
            dleft_ref[n + 4] = jnp.where(first, pltpu.roll(even, 64, 1), odd)
        count, size = len(dleft_refs), dleft_refs[0].shape[0]
        for n, ref in enumerate(dleft_refs):
            place = lax.rem(first_ref[0] + n, count) * size
            ref[...] = dleft_ref[pl.ds(place, size)]


def call_edges_back(
    dedge, mid, grad, dlogit, sides, right, outer, factors, blocks, first, count, cols
):
    rows, depth = mid.shape[0], blocks.shape[3]
    chains = depth // 8
    dlogits = (8, 2, 4 * cols, 640)
    return pl.pallas_call(
        functools.partial(edges_back_kernel, cols, chains),
        grid=(8,),
        in_specs=[full(x) for x in (dedge, mid, grad, dlogit, sides, right, outer)]
        + [step_block(factors.shape), step_block(blocks.shape), pl.BlockSpec(memory_space=pltpu.SMEM)],
        out_specs=(
            pl.BlockSpec((rows, 128), lambda t: (0, 0)),
            step_block(dlogits),
            full(right),
        )
        + (pl.BlockSpec((8 // count, chains, 128), lambda t: (0, 0, 0)),) * count,
        out_shape=(
            jax.ShapeDtypeStruct((rows, 128), f32),
            jax.ShapeDtypeStruct(dlogits, bf16),
            jax.ShapeDtypeStruct(right.shape, f32),
        )
        + (jax.ShapeDtypeStruct((8 // count, chains, 128), f32),) * count,
        scratch_shapes=[
            pltpu.VMEM((4 * cols, depth), f32),
            pltpu.VMEM((2, depth, 4 * cols), bf16),
            pltpu.VMEM((2048, 128), bf16),
            pltpu.VMEM((8, chains, 128), f32),
            pltpu.VMEM((8, chains, 128), f32),
        ],
        compiler_params=params(),
        name="edges_back",
    )(dedge, mid, grad, dlogit, sides, right, outer, factors, blocks, first)


def give_halves(core_ref, whole_ref, mine_ref, other_ref):
    mine_ref[...] = whole_ref[core_ref[0]]
    other_ref[...] = whole_ref[1 - core_ref[0]]


def side_sums_kernel(
    cols,
    shift,
    mid_ref,
    dlogits_ref,
    first_ref,
    core_ref,
    mine_ref,
    other_ref,
    sides_ref,
    whole_ref,
):
    t = pl.program_id(0)

    @pl.when(t == 0)
    def _():
        sides_ref[...] = jnp.zeros_like(sides_ref)

    normed, _ = norm_parts(read_rows(mid_ref, four_rows(t, cols)))
    sides_ref[...] += stacked3(halves(jnp.transpose(normed)), pair_of(dlogits_ref, 0))

    @pl.when(t == 7)
    def _():
        order = chunk_order(shift)
        for n in range(2):
            high, low = halves(sides_ref[:, n * 256 : (n + 1) * 256])
            sides = one_pass(high, order, NT) + one_pass(low, order, NT)
            for side in range(2):
                place = 2 * n + side
                rows = slice(place % 3 * 128, place % 3 * 128 + 128)
                whole_ref[place // 3, rows] = sides[:, side * 128 : (side + 1) * 128]
        whole_ref[1, 128:256] = sides_ref[:, 512:]
        whole_ref[1, 256:] = first_ref[...]
        give_halves(core_ref, whole_ref, mine_ref, other_ref)


def call_side_sums(mid, dlogits, first, core, cols, shift):
    return pl.pallas_call(
        functools.partial(side_sums_kernel, cols, shift),
        grid=(8,),
        in_specs=[full(mid), step_block(dlogits.shape), full(first)]
        + [pl.BlockSpec(memory_space=pltpu.SMEM)],
        out_specs=(pl.BlockSpec((384, 128), lambda t: (0, 0)),) * 2,
        out_shape=(jax.ShapeDtypeStruct((384, 128), f32),) * 2,
        scratch_shapes=[pltpu.VMEM((128, 640), f32), pltpu.VMEM((2, 384, 128), f32)],
        compiler_params=params(),
        name="side_sums",
    )(mid, dlogits, first, core)


def outer_sums_kernel(
    cols, dmid_ref, prod_ref, core_ref, mine_ref, other_ref, outer_ref, whole_ref
):
    t = pl.program_id(0)

    @pl.when(t == 0)
    def _():
        outer_ref[...] = jnp.zeros_like(outer_ref)

    dmid = halves(jnp.transpose(read_rows(dmid_ref, four_rows(t, cols))))
    for g in range(4):
        outer_ref[:, g * 256 : (g + 1) * 256] += stacked3(dmid, pair_of(prod_ref, 0, g))

    @pl.when(t == 7)
    def _():
        for g in range(4):
            tile = jnp.transpose(outer_ref[:, g * 256 : (g + 1) * 256]).reshape(32, 8, 128)
            for p in range(32):
                start = p % 16 * 32 + g * 8
                whole_ref[p // 16, start : start + 8] = tile[p]
        give_halves(core_ref, whole_ref, mine_ref, other_ref)


def call_outer_sums(dmid, prods, core, cols):
    return pl.pallas_call(
        functools.partial(outer_sums_kernel, cols),
        grid=(8,),
        in_specs=[full(dmid), step_block(prods.shape), pl.BlockSpec(memory_space=pltpu.SMEM)],
        out_specs=(pl.BlockSpec((512, 128), lambda t: (0, 0)),) * 2,
        out_shape=(jax.ShapeDtypeStruct((512, 128), f32),) * 2,
        scratch_shapes=[pltpu.VMEM((128, 1024), f32), pltpu.VMEM((2, 512, 128), f32)],
        compiler_params=params(),
        name="outer_sums",
    )(dmid, prods, core)


def pack_heads(y, store):
    lane = iota((1, 1, 128), 2) >> 5
    for tile in range(y.shape[1] // 128):
        part = y[:, tile * 128 : (tile + 1) * 128]
        turned = [part] + [pltpu.roll(part, 32 * n, 1) for n in range(1, 4)]
        turned = [x.reshape(-1, 4, 8, 128) for x in turned]
        for head in range(4):
            out = turned[-head % 4][:, 0]
            for chain in range(1, 4):
                out = jnp.where(lane == chain, turned[(chain - head) % 4][:, chain], out)
            store(tile * 4 + head, out)


def unpack_heads(load, heads):
    lane = iota((1, 1, 128), 2) >> 5
    tiles = []
    for tile in range(heads // 4):
        turned = []
        for head in range(4):
            part = load(tile * 4 + head)
            flat = part.reshape(-1, 128)
            turned.append(
                [part] + [pltpu.roll(flat, 32 * n, 1).reshape(part.shape) for n in range(1, 4)]
            )
        chains = []
        for chain in range(4):
            out = turned[0][-chain % 4]
            for head in range(1, 4):
                out = jnp.where(lane == head, turned[head][(head - chain) % 4], out)
            chains.append(out[:, None])
        tiles.append(jnp.concatenate(chains, 1).reshape(-1, 128))
    return jnp.concatenate(tiles, 1)


def head_lanes(tile, n):
    return jnp.where((iota((1, 128), 1) >> 5) == n, tile, 0.0)


def stack_heads(tile):
    return jnp.concatenate([head_lanes(tile, n) for n in range(4)], 0)


def join_heads(stacked):
    size = stacked.shape[0] // 4
    lane = iota((1, 128), 1) >> 5
    out = stacked[:size]
    for n in range(1, 4):
        out = jnp.where(lane == n, stacked[n * size : (n + 1) * size], out)
    return out


def soft(scores, seen=None):
    if seen is not None:
        scores = jnp.where(seen, scores, -1e30)
    weights = jnp.exp(scores - jnp.max(scores, axis=-1, keepdims=True))
    if seen is not None:
        weights = jnp.where(seen, weights, 0.0)
    return weights * (1.0 / jnp.sum(weights, axis=-1, keepdims=True))


def soft_back(weights, grad):
    return weights * (grad - jnp.sum(weights * grad, axis=-1, keepdims=True))


def stripe_seen(present_ref):
    tokens = present_ref.shape[1]
    shape = (tokens, tokens)
    same = (iota(shape, 0) & 7) == (iota(shape, 1) & 7)
    return same & (present_ref[...] > 0.0)


def column_attention(q, k, v, seen):
    weights, tiles = [], []
    for tile in range(q.shape[1] // 128):
        lanes = slice(tile * 128, (tile + 1) * 128)
        keys, values = halves(k[:, lanes]), halves(v[:, lanes])
        blend = 0.0
        for n in range(4):
            weights.append(soft(dot3(head_lanes(q[:, lanes], n), keys, NT), seen))
            blend = blend + head_lanes(dot3(weights[-1], values), n)
        tiles.append(blend)
    return weights, jnp.concatenate(tiles, 1)


def columns_kernel(
    scale,
    x_ref,
    present_ref,
    bias_ref,
    q_ref,
    k_ref,
    v_ref,
    o_ref,
    q2_ref,
    k2_ref,
    v2_ref,
    out_ref,
    qkv_ref,
):
    x = x_ref[...]
    normed, _ = norm_parts(x)
    normed = halves(normed)
    q, k, v = (dot3(normed, halves(w[...])) for w in (q_ref, k_ref, v_ref))
    _, blend = column_attention(q * scale, k, v, stripe_seen(present_ref))
    out = x + dot3(blend, halves(o_ref[...]))
    out_ref[...] = out
    normed, _ = norm_parts(out)
    normed = halves(normed)
    groups, size = qkv_ref.shape[0] // 8, (qkv_ref.shape[1] - 16) // 3
    qkv_ref[:, -16:] = bias_ref[...]

    def store(kind):
        def put(head, value):
            place = slice(head * groups, (head + 1) * groups)
            rows = slice(kind * size, (kind + 1) * size)
            qkv_ref[place, rows] = value.reshape(groups, size, 128)

        return put

    for kind, w in enumerate((q2_ref, k2_ref, v2_ref)):
        pack_heads(dot3(normed, halves(w[...])), store(kind))


def call_columns(x, present, bias, weights, group_chains, scale):
    return pl.pallas_call(
        functools.partial(columns_kernel, scale),
        out_shape=(
            jax.ShapeDtypeStruct(x.shape, f32),
            jax.ShapeDtypeStruct((bias.shape[0], 6 * group_chains + 16, 128), f32),
        ),
        compiler_params=params(),
        name="columns",
    )(x, present, bias, *weights)


def packed_parts(ref):
    parts = (ref.shape[1] - 16) // 24
    for half in range(parts):
        places = [(kind * parts + half) * 8 for kind in range(3)]
        yield half, places, [ref[:, p : p + 8].reshape(-1, 128) for p in places]


def rows_kernel(mesh_rows, mesh_cols, scale, qkv_ref, out_ref, whole_ref):
    join_tiles(qkv_ref[:, -16:], mesh_rows, mesh_cols, whole_ref)
    bias = whole_ref[...]
    for half, _, (q, k, v) in packed_parts(qkv_ref):
        k, v, q = halves(k), halves(v), q * scale
        blend = 0.0
        for n in range(4):
            weights = soft(dot3(head_lanes(q, n), k, NT) + bias)
            blend = blend + head_lanes(dot3(weights, v), n)
        out_ref[:, half] = blend.reshape(-1, 8, 128)


def call_rows(qkv, mesh_rows, mesh_cols, scale):
    devices, parts = qkv.shape[0], (qkv.shape[1] - 16) // 24
    span = mesh_rows * 32
    return pl.pallas_call(
        functools.partial(rows_kernel, mesh_rows, mesh_cols, scale),
        out_shape=jax.ShapeDtypeStruct((devices, parts, 8, 128), f32),
        scratch_shapes=[pltpu.VMEM((span, span), f32)],
        compiler_params=params(24),
        name="rows",
    )(qkv)


def load_heads(ref, kind=None):
    def load(head):
        groups = ref.shape[0] // 8
        place = slice(head * groups, (head + 1) * groups)
        part = ref[place] if kind is None else ref[place, kind]
        return part.reshape(-1, 8, 128)

    return load


def side_copies(source_ref, target_ref):
    both = halves(jnp.concatenate([source_ref[...], target_ref[...]], 0))
    shape = (640, 64)
    place = iota(shape, 0) - 128
    feature = jnp.where(place < 0, place & 31, 32 + ((place >> 7) << 3) + (place & 7))
    copies = jnp.where(iota(shape, 1) == feature, 1.0, 0.0).astype(bf16)
    return tuple(one_pass(copies, part).astype(bf16) for part in both)


def rows_out_kernel(
    blend_ref, mid_ref, share_ref, o_ref, source_ref, target_ref, out_ref, left_ref, right_ref
):
    blend = unpack_heads(load_heads(blend_ref), 8)
    out = mid_ref[...] + dot3(blend, halves(o_ref[...]))
    out_ref[...] = out
    normed, _ = norm_parts(out)
    wide = dot3(normed, side_copies(source_ref, target_ref), NT)
    left = (wide[:, :128] * share_ref[...]).reshape(-1, 4, 8, 128)
    lane = iota((1, 1, 128), 2)
    packed = left[:, 0]
    for chain in range(1, 4):
        packed = jnp.where((lane >> 5) == chain, left[:, chain], packed)
    for n in range(packed.shape[0]):
        left_ref[:, n, :] = packed[n]
    for g in range(4):
        right = wide[:, (g + 1) * 128 : (g + 2) * 128].reshape(-1, 16, 8, 128)
        packed = right[:, 0]
        for chain in range(1, 16):
            packed = jnp.where((lane >> 3) == chain, right[:, chain], packed)
        right_ref[g] = packed


def call_rows_out(blend, mid, share, weight, source, target):
    chains = mid.shape[0] // 8
    return pl.pallas_call(
        rows_out_kernel,
        out_shape=(
            jax.ShapeDtypeStruct(mid.shape, f32),
            jax.ShapeDtypeStruct((8, chains // 4, 128), f32),
            jax.ShapeDtypeStruct((4, chains // 16, 8, 128), f32),
        ),
        compiler_params=params(),
        name="rows_out",
    )(blend, mid, share, weight, source, target)


def rows_out_back_kernel(*refs):
    *dleft_refs, dright_ref, grad_ref, out_ref, blend_ref, share_ref = refs[:-10]
    o_ref, source_ref, target_ref = refs[-10:-7]
    core_ref, dout_ref, dblend_ref, thin_ref, mine_ref, other_ref, sum_ref = refs[-7:]
    lane = iota((1, 1, 128), 2)
    chains = grad_ref.shape[0] // 8
    dleft = functools.reduce(jnp.add, [ref[...] for ref in dleft_refs])
    shape = (chains * 8, 128)
    slot = iota(shape, 0) & 7
    copy = (chains * 8, chains)
    copy = jnp.where((iota(copy, 0) >> 3) == iota(copy, 1), 1.0, 0.0).astype(bf16)
    left = 0.0
    for n in range(2):
        high, low = halves(dleft[n])
        spot = (slot >> 2 == n) & (slot & 3 == iota(shape, 1) >> 5)
        left = left + jnp.where(spot, one_pass(copy, high) + one_pass(copy, low), 0.0)
    wide = [left * share_ref[...]]
    dright = dright_ref[...]
    for g in range(4):
        part = [jnp.where((lane >> 3) == n, dright[g], 0.0)[:, None] for n in range(16)]
        wide.append(jnp.concatenate(part, 1).reshape(-1, 128))
    wide = halves(jnp.concatenate(wide, 1))
    normed, inverse = norm_parts(out_ref[...])
    dsides = halves(dot3(halves(jnp.transpose(normed)), wide))
    shape = (640, 128)
    place, spot = iota(shape, 0) - 128, iota(shape, 1)
    target = jnp.where(place < 0, place & 31, 32 + ((place >> 7) << 3) + (place & 7))
    fold = jnp.where(target == spot, 1.0, 0.0).astype(bf16)
    thin_ref[...] = one_pass(dsides[0], fold) + one_pass(dsides[1], fold)
    dout = grad_ref[...] + norm_back(normed, inverse, dot3(wide, side_copies(source_ref, target_ref)))
    dout_ref[...] = dout
    dout = halves(dout)
    groups = dblend_ref.shape[0] // 8

    def store(head, value):
        dblend_ref[head * groups : (head + 1) * groups] = value.reshape(groups, -1, 8, 128)

    pack_heads(dot3(dout, halves(o_ref[...]), NT), store)
    blend = unpack_heads(load_heads(blend_ref), 8)
    write_halves(sum_ref, 0, dot3(halves(jnp.transpose(blend)), dout))
    give_halves(core_ref, sum_ref, mine_ref, other_ref)


def call_rows_out_back(dlefts, dright, grad, out, blend, share, weight, source, target, core):
    shapes, scratch = halves_shapes([weight])
    return pl.pallas_call(
        rows_out_back_kernel,
        out_shape=(
            jax.ShapeDtypeStruct(grad.shape, f32),
            jax.ShapeDtypeStruct(blend.shape, f32),
            jax.ShapeDtypeStruct((256, 128), f32),
        )
        + shapes,
        in_specs=specs(len(dlefts) + 8),
        scratch_shapes=[scratch],
        compiler_params=params(),
        name="rows_out_back",
    )(*dlefts, dright, grad, out, blend, share, weight, source, target, core)


def rows_back_kernel(
    mesh_rows, mesh_cols, scale, qkv_ref, dblend_ref, out_ref, whole_ref
):
    join_tiles(qkv_ref[:, -16:], mesh_rows, mesh_cols, whole_ref)
    bias = jnp.concatenate([whole_ref[...]] * 4, 0)
    span = whole_ref.shape[0]
    dbias = 0.0
    for half, places, (q, k, v) in packed_parts(qkv_ref):
        k, query = halves(k), halves(stack_heads(q * scale))
        dblend = halves(stack_heads(dblend_ref[:, half].reshape(-1, 128)))
        weights = soft(dot3(query, k, NT) + bias)
        dv = dot3(halves(jnp.transpose(weights)), dblend)
        dscores = soft_back(weights, dot3(dblend, halves(v), NT))
        for n in range(4):
            dbias = dbias + dscores[n * span : (n + 1) * span]
        dk = dot3(halves(jnp.transpose(dscores)), query)
        dq = join_heads(dot3(dscores, k))
        for place, value in zip(places, (dq * scale, dk, dv)):
            out_ref[:, place : place + 8] = value.reshape(-1, 8, 128)

    def store(d, tile):
        out_ref[d, -16:] = tile

    cut_tiles(dbias, mesh_rows, mesh_cols, store)


def call_rows_back(qkv, dblend, mesh_rows, mesh_cols, scale):
    span = mesh_rows * 32
    return pl.pallas_call(
        functools.partial(rows_back_kernel, mesh_rows, mesh_cols, scale),
        out_shape=jax.ShapeDtypeStruct(qkv.shape, f32),
        scratch_shapes=[pltpu.VMEM((span, span), f32)],
        compiler_params=params(24),
        name="rows_back",
    )(qkv, dblend)


def write_halves(ref, n, value):
    height = value.shape[0]
    for half in range(2):
        ref[half, n * height : (n + 1) * height] = value[:, half * 128 : (half + 1) * 128]


def projections_back(normed, inverse, grads, weight_refs, sum_ref):
    turned = halves(jnp.transpose(normed))
    dnormed = 0.0
    for n, (grad, w) in enumerate(zip(grads, weight_refs)):
        grad = halves(grad)
        write_halves(sum_ref, n, dot3(turned, grad))
        dnormed = dnormed + dot3(grad, halves(w[...]), NT)
    return norm_back(normed, inverse, dnormed)


def rows_in_back_kernel(
    dqkv_ref, mid_ref, grad_ref, q_ref, k_ref, v_ref, core_ref, dmid_ref, mine_ref, other_ref, sum_ref
):
    groups, size = dqkv_ref.shape[0] // 8, (dqkv_ref.shape[1] - 16) // 3

    def load(kind):
        place = slice(kind * size, (kind + 1) * size)
        return lambda head: dqkv_ref[head * groups : (head + 1) * groups, place].reshape(-1, 8, 128)

    grads = [unpack_heads(load(kind), 8) for kind in range(3)]
    normed, inverse = norm_parts(mid_ref[...])
    dmid_ref[...] = grad_ref[...] + projections_back(
        normed, inverse, grads, (q_ref, k_ref, v_ref), sum_ref
    )
    give_halves(core_ref, sum_ref, mine_ref, other_ref)


def halves_shapes(weights):
    rows = sum(w.size for w in weights) // 256
    return (jax.ShapeDtypeStruct((rows, 128), f32),) * 2, pltpu.VMEM((2, rows, 128), f32)


def specs(count):
    vmem = pl.BlockSpec(memory_space=pltpu.VMEM)
    return [vmem] * count + [pl.BlockSpec(memory_space=pltpu.SMEM)]


def call_rows_in_back(dqkv, mid, grad, weights, core):
    shapes, scratch = halves_shapes(weights)
    return pl.pallas_call(
        rows_in_back_kernel,
        in_specs=specs(6),
        out_shape=(jax.ShapeDtypeStruct(mid.shape, f32),) + shapes,
        scratch_shapes=[scratch],
        compiler_params=params(24),
        name="rows_in_back",
    )(dqkv, mid, grad, *weights, core)


def columns_back_kernel(
    scale,
    x_ref,
    present_ref,
    grad_ref,
    q_ref,
    k_ref,
    v_ref,
    o_ref,
    core_ref,
    dx_ref,
    mine_ref,
    other_ref,
    sum_ref,
):
    normed, inverse = norm_parts(x_ref[...])
    normed_halves = halves(normed)
    q, k, v = (dot3(normed_halves, halves(w[...])) for w in (q_ref, k_ref, v_ref))
    q = q * scale
    weights, blend = column_attention(q, k, v, stripe_seen(present_ref))
    grad = grad_ref[...]
    grad_halves = halves(grad)
    write_halves(sum_ref, 3, dot3(halves(jnp.transpose(blend)), grad_halves))
    dblend = dot3(grad_halves, halves(o_ref[...]), NT)
    tiles = [[], [], []]
    for tile in range(q.shape[1] // 128):
        lanes = slice(tile * 128, (tile + 1) * 128)
        keys, values = halves(k[:, lanes]), halves(v[:, lanes])
        dq, dk, dv = 0.0, 0.0, 0.0
        for n in range(4):
            query = halves(head_lanes(q[:, lanes], n))
            dhead = halves(head_lanes(dblend[:, lanes], n))
            share = weights[tile * 4 + n]
            dv = dv + dot3(halves(jnp.transpose(share)), dhead)
            dscores = soft_back(share, dot3(dhead, values, NT))
            dk = dk + dot3(halves(jnp.transpose(dscores)), query)
            dq = dq + head_lanes(dot3(dscores, keys), n)
        for kind, value in enumerate((dq * scale, dk, dv)):
            tiles[kind].append(value)
    grads = [jnp.concatenate(t, 1) for t in tiles]
    dx_ref[...] = grad + projections_back(
        normed, inverse, grads, (q_ref, k_ref, v_ref), sum_ref
    )
    give_halves(core_ref, sum_ref, mine_ref, other_ref)


def call_columns_back(x, present, grad, weights, core, scale):
    shapes, scratch = halves_shapes(weights)
    return pl.pallas_call(
        functools.partial(columns_back_kernel, scale),
        in_specs=specs(7),
        out_shape=(jax.ShapeDtypeStruct(x.shape, f32),) + shapes,
        scratch_shapes=[scratch],
        compiler_params=params(24),
        name="columns_back",
    )(x, present, grad, *weights, core)


def bias_kernel(cols, pair_ref, weight_ref, out_ref):
    weight = halves(weight_ref[...])

    def step(t, carry):
        rows = halves(read_rows(pair_ref, four_rows(t, cols)))
        heads = dot3(weight, rows, NT)
        for v in range(2):
            tile = heads[:, v * 128 : (v + 1) * 128][:, None, :]
            for g in range(out_ref.shape[1]):
                out_ref[:, g, pl.ds(2 * t + v, 1), :] = tile
        return carry

    lax.fori_loop(0, 8, step, 0)


def call_bias(pair, weight, copies, cols):
    return pl.pallas_call(
        functools.partial(bias_kernel, cols),
        out_shape=jax.ShapeDtypeStruct((weight.shape[0], copies, 16, 128), f32),
        compiler_params=params(24),
        name="bias",
    )(pair, weight)


def bias_rows(dbias):
    heads, groups, rows = dbias.shape[:3]
    return pl.BlockSpec((heads, groups, 16, 128), lambda t: (0, 0, rows // 16 - 1, 0))


def head_rows(ref, t):
    heads = [ref[:, pl.ds(2 * t + v, 1), :].reshape(-1, 128) for v in range(2)]
    return jnp.concatenate(heads, 1)


def bias_sums_kernel(
    cols, dbias_ref, pair_ref, thin_ref, core_ref, mine_ref, other_ref, whole_ref, sum_ref, dweight_ref
):
    sum_ref[...] = jnp.sum(dbias_ref[...], axis=1)
    dweight_ref[...] = jnp.zeros_like(dweight_ref)

    def step(t, carry):
        dweight_ref[...] += dot3(head_rows(sum_ref, t), read_rows(pair_ref, four_rows(t, cols)))
        return carry

    lax.fori_loop(0, 8, step, 0)
    whole_ref[0], whole_ref[1] = thin_ref[:128], thin_ref[128:]
    whole_ref[0, :, 64 : 64 + dweight_ref.shape[0]] = jnp.transpose(dweight_ref[...])
    give_halves(core_ref, whole_ref, mine_ref, other_ref)


def call_bias_sums(dbias, pair, thin, core, cols):
    heads = dbias.shape[0]
    return pl.pallas_call(
        functools.partial(bias_sums_kernel, cols),
        grid=(1,),
        in_specs=[bias_rows(dbias), full(pair), full(thin), pl.BlockSpec(memory_space=pltpu.SMEM)],
        out_specs=(pl.BlockSpec((128, 128), lambda t: (0, 0)),) * 2,
        out_shape=(jax.ShapeDtypeStruct((128, 128), f32),) * 2,
        scratch_shapes=[
            pltpu.VMEM((2, 128, 128), f32),
            pltpu.VMEM((heads, 16, 128), f32),
            pltpu.VMEM((heads, 128), f32),
        ],
        compiler_params=params(24),
        name="bias_sums",
    )(dbias, pair, thin, core)


def bias_back_kernel(cols, dbias_ref, dmid_ref, weight_ref, out_ref, sum_ref):
    weight = halves(weight_ref[...])
    sum_ref[...] = jnp.sum(dbias_ref[...], axis=1)

    def step(t, carry):
        places = four_rows(t, cols)
        dpair = dot3(jnp.transpose(head_rows(sum_ref, t)), weight)
        write_rows(out_ref, places, read_rows(dmid_ref, places) + dpair)
        return carry

    lax.fori_loop(0, 8, step, 0)


def call_bias_back(dbias, dmid, weight, cols):
    return pl.pallas_call(
        functools.partial(bias_back_kernel, cols),
        grid=(1,),
        in_specs=[bias_rows(dbias), full(dmid), full(weight)],
        out_specs=full(dmid),
        out_shape=jax.ShapeDtypeStruct(dmid.shape, f32),
        scratch_shapes=[pltpu.VMEM((dbias.shape[0], 16, 128), f32)],
        compiler_params=params(24),
        name="bias_back",
    )(dbias, dmid, weight)


def spread_sums_kernel(
    half, cols, mine_ref, early_ref, other_ref, other_early_ref, place_ref, *refs
):
    *outs, whole_ref = refs
    size = early_ref.shape[0] // (half * cols)
    for part, ref in enumerate((early_ref, other_early_ref)):
        for n in range(half * cols):
            row = lax.rem(place_ref[1] + half - n // cols, half)
            chip = row * cols + lax.rem(place_ref[2] + cols - n % cols, cols)
            target = pl.ds(pl.multiple_of(chip * size, 8), size)
            whole_ref[part, target] = ref[n * size : (n + 1) * size]

    def place(first, second, order):
        for half, ref in enumerate((first, second)):
            lanes = slice(half * 128, (half + 1) * 128)
            for n, target in enumerate((0, 1, 2, 3, 4, 5, 6)):
                outs[target][:, lanes] = ref[n * 256 : (n + 1) * 256]
            outs[8][:, lanes] = whole_ref[order[half], 512:768]
            for n, target in enumerate(((13, 15, 12), (14, 16, 17))[half]):
                outs[target][...] = ref[1920 + n * 128 : 2048 + n * 128]
            outs[11][half * 512 : (half + 1) * 512] = whole_ref[order[half], :512]
        thin = jnp.transpose(jnp.concatenate([first[1792:1920], second[1792:1920]], 0))
        outs[7][...] = thin[64 : 64 + outs[7].shape[0], :128]
        outs[9][...] = thin[:32]
        outs[10][...] = thin[32:64]

    @pl.when(place_ref[0] == 0)
    def _():
        place(mine_ref, other_ref, (0, 1))

    @pl.when(place_ref[0] != 0)
    def _():
        place(other_ref, mine_ref, (1, 0))


def call_spread_sums(mine, early, other, other_early, place, half, cols, shapes):
    thin = (7, 9, 10)
    shapes = [shape[::-1] if n in thin else shape for n, shape in enumerate(shapes)]
    sums = pl.pallas_call(
        functools.partial(spread_sums_kernel, half, cols),
        in_specs=specs(4),
        out_shape=tuple(jax.ShapeDtypeStruct(shape, f32) for shape in shapes),
        scratch_shapes=[pltpu.VMEM((2,) + early.shape, f32)],
        compiler_params=params(24),
        name="spread_sums",
    )(mine, early, other, other_early, place)
    return [jnp.transpose(x) if n in thin else x for n, x in enumerate(sums)]


precise = lax.Precision.HIGH
everyone = ("half", "core", "col")
row = ("half", "core")
chips = ("half", "col")


def affine_map(tensor, weight):
    return jnp.einsum("...a,ab->...b", tensor, weight, precision=precise)


def exchange(chunks, axis):
    shape = chunks.shape
    flat = chunks.reshape(shape[0], -1, 128)
    return lax.all_to_all(flat, axis, 0, 0, tiled=True).reshape(shape)


def collect(block, axis, count):
    return exchange(jnp.broadcast_to(block[None], (count,) + block.shape), axis)


def tall(weight):
    return jnp.concatenate([weight[:, :128], weight[:, 128:]], 0)


def together(*arrays):
    return lax.optimization_barrier(arrays)


class Layout:
    def __init__(self, mesh_rows, mesh_cols, pair, chains, heads, head_width):
        self.mesh_rows, self.mesh_cols = mesh_rows, mesh_cols
        self.devices = mesh_rows * mesh_cols
        self.rows_here, self.cols_here, self.pair_width = pair
        self.span = self.rows_here * mesh_rows
        self.slim = self.span // self.devices
        self.chains, self.heads, self.head_width = chains, heads, head_width
        self.chain_groups = self.devices // heads
        self.group_chains = chains // self.chain_groups
        self.channels_here = self.pair_width // self.devices
        self.scale = head_width ** (-0.5)
        self.turn = [
            (g, (g % mesh_rows) * mesh_cols + g // mesh_rows) for g in range(self.devices)
        ]
        self.turn_back = [(b, a) for a, b in self.turn]

        self.swap = [(0, 1), (1, 0)]
        self.core = lax.axis_index("core").reshape(1)

    def to_slim(self, x):
        return lax.all_to_all(x, "col", 1, 0, tiled=True)

    def both_views(self, grad, out):
        count, slim, width = self.mesh_cols, self.slim, grad.shape[2]
        grad = jnp.transpose(grad.reshape(-1, count, slim, width), (1, 0, 2, 3))
        both = jnp.stack([grad, out.reshape(count, -1, slim, width)], 1)
        return both.reshape(count, -1, width)

    def split_views(self, both):
        count, slim, width = self.mesh_cols, self.slim, both.shape[2]
        both = both.reshape(count, 2, -1, slim, width)
        out = jnp.transpose(both[:, 1], (1, 0, 2, 3)).reshape(-1, count * slim, width)
        return both[:, 0].reshape(-1, slim, width), out

    def from_slim_permuted(self, x):
        count, slim = self.mesh_cols, x.shape[1]
        here = lax.axis_index("col")
        blocks = x.reshape(count, -1, slim, x.shape[2])
        out = jnp.zeros((blocks.shape[1], count * slim, x.shape[2]), f32)
        for n in range(count):
            block = lax.dynamic_index_in_dim(blocks, lax.rem(here + n, count), 0, False)
            if n:
                block = lax.ppermute(block, "col", [(s, (s + n) % count) for s in range(count)])
            source = lax.rem(here + count - n, count)
            out = lax.dynamic_update_slice_in_dim(out, block, source * slim, 1)
        return out

    def from_others(self, arrays, axis="col"):
        count = len(arrays)
        return [
            lax.ppermute(x, axis, [(s, (s + n) % count) for s in range(count)]) if n else x
            for n, x in enumerate(arrays)
        ]

    def share_sum(self, x, axis, count):
        here = lax.axis_index(axis)
        x = x.reshape(count, -1, 128)
        parts = [
            lax.dynamic_index_in_dim(x, lax.rem(here + n, count), 0, False) for n in range(count)
        ]
        return functools.reduce(jnp.add, self.from_others(parts, axis))

    def all_parts(self, x, axis, count):
        return jnp.concatenate(self.from_others([x] * count, axis), 0)

    def core_sum(self, sums):
        sums = [
            part[0] + lax.ppermute(part[1], "core", self.swap) if len(part) == 2 else part[0]
            for part in sums
        ]
        return jnp.concatenate(sums, 0)

    def half_sum(self, early):
        early = self.core_sum(early)
        pad = -early.shape[0] % (4 * self.devices)
        early = jnp.pad(early, ((0, pad), (0, 0))) if pad else early
        return self.share_sum(early, "half", self.mesh_rows // 2)

    def sum_all(self, late, early, *beside):
        half, cols = self.mesh_rows // 2, self.mesh_cols
        late, early = together(self.core_sum(late), early)
        late = exchange(late.reshape(half, -1, 128), "half")
        late, early = together(late, self.share_sum(early, "col", cols))
        late = exchange(late.sum(0).reshape(cols, -1, 128), "col")
        late, early, *beside = together(late, self.all_parts(early, "col", cols), *beside)
        late = collect(late.sum(0), "col", cols).reshape(-1, 128)
        late, early = together(late, self.all_parts(early, "half", half))
        late = collect(late, "half", half).reshape(-1, 128)
        late, other_early = together(late, lax.ppermute(early, "core", self.swap))
        return (late, early, lax.ppermute(late, "core", self.swap), other_early), beside


def msa_plain(size, alignment_features, residue_couplings, present, weights):
    chains, slim, heads, head_width = size.chains, size.slim, size.heads, size.head_width
    devices, groups, group_chains = size.devices, size.chain_groups, size.group_chains
    rows_here, cols_here, span = size.rows_here, size.cols_here, size.span
    mesh_rows, mesh_cols = size.mesh_rows, size.mesh_cols
    bias = jnp.transpose(affine_map(residue_couplings, weights[7]), (2, 0, 1))
    bias = jnp.broadcast_to(bias[:, None], (heads, groups, rows_here, cols_here))
    bias = exchange(bias.reshape(devices, rows_here, cols_here), everyone)
    bias = bias.reshape(mesh_rows, mesh_cols, rows_here, cols_here)
    bias = jnp.transpose(bias, (0, 2, 1, 3)).reshape(span, span)

    stripe = size.to_slim(alignment_features)
    normed, _ = norm_parts(stripe)
    col_q, col_k, col_v = (
        affine_map(normed, w).reshape(chains, slim, heads, head_width) for w in weights[:3]
    )
    scores = jnp.einsum("sihd,tihd->ihst", col_q, col_k, precision=precise) * size.scale
    scores = jnp.where(present[None, None, None, :] > 0, scores, -1000000000.0)
    blend = jnp.einsum(
        "ihst,tihd->sihd", jax.nn.softmax(scores, axis=-1), col_v, precision=precise
    )
    msa_col = stripe + affine_map(blend.reshape(chains, slim, heads * head_width), weights[3])

    normed, _ = norm_parts(msa_col)
    qkv = jnp.stack([affine_map(normed, w) for w in weights[4:7]])
    qkv = qkv.reshape(3, groups, group_chains, slim, heads, head_width)
    qkv = jnp.transpose(qkv, (4, 1, 0, 2, 3, 5))
    qkv = exchange(qkv.reshape(devices, 3, group_chains, slim, head_width), everyone)
    qkv = jnp.transpose(qkv, (1, 2, 0, 3, 4)).reshape(3, group_chains, span, head_width)
    scores = jnp.einsum("sid,sjd->sij", qkv[0], qkv[1], precision=precise) * size.scale
    shares = jax.nn.softmax(scores + bias[None], axis=-1)
    blend = jnp.einsum("sij,sjd->sid", shares, qkv[2], precision=precise)
    blend = blend.reshape(group_chains, devices, slim, head_width)
    blend = exchange(jnp.transpose(blend, (1, 0, 2, 3)), everyone)
    blend = blend.reshape(heads, chains, slim, head_width)
    blend = jnp.transpose(blend, (1, 2, 0, 3)).reshape(chains, slim, heads * head_width)
    msa_out = msa_col + affine_map(blend, weights[8])

    normed, _ = norm_parts(msa_out)
    left = affine_map(normed, weights[9]) * (present / jnp.sum(present))[:, None, None]
    left = jnp.transpose(left.reshape(chains // 4, 4, slim, 32), (2, 0, 1, 3))
    left = collect(left.reshape(slim, chains // 4, 128), "col", mesh_cols).reshape(-1, 128)
    right = affine_map(normed, weights[10]).reshape(chains // 16, 16, slim, 4, 8)
    right = jnp.transpose(right, (3, 0, 2, 1, 4)).reshape(-1, 128)
    right = collect(lax.ppermute(right, everyone, size.turn), row, mesh_rows)
    right = right.reshape(mesh_rows, 4, chains // 16, slim, 128)
    right = jnp.transpose(right, (1, 0, 3, 2, 4)).reshape(4, cols_here // 8, 8, chains // 16, 128)
    return msa_out, [left], jnp.transpose(right, (1, 0, 3, 2, 4))


def msa_forward(size, alignment_features, residue_couplings, present, weights, prepare, raw):
    chains, slim, devices = size.chains, size.slim, size.devices
    mesh_rows, mesh_cols = size.mesh_rows, size.mesh_cols
    pair_flat = residue_couplings.reshape(-1, size.pair_width)
    tokens = chains * slim
    seen = jnp.repeat(present, slim)[None]
    share = jnp.repeat(present / jnp.sum(present), slim)[:, None]
    source, target = jnp.transpose(weights[9]), jnp.transpose(weights[10])
    offset = jnp.transpose(weights[7])
    stripe = size.to_slim(alignment_features).reshape(tokens, -1)
    bias = call_bias(pair_flat, offset, size.chain_groups, size.cols_here)
    bias = bias.reshape(devices, 16, 128)
    msa_col, qkv = call_columns(stripe, seen, bias, weights[:7], size.group_chains, size.scale)
    qkv = exchange(qkv, everyone)
    blend = call_rows(qkv, mesh_rows, mesh_cols, size.scale)
    raw, blend = together(raw, blend)
    blend, ready = together(exchange(blend, everyone), prepare(raw))
    msa_out, left, right = call_rows_out(blend, msa_col, share, weights[8], source, target)
    left = size.from_others([left.reshape(-1, 128)] * mesh_cols)
    right, *left = together(lax.ppermute(right, everyone, size.turn), *left)
    right = collect(right, row, mesh_rows)

    def back(grad, d_lefts, d_right, d_mid, pair_mid, side_sums, outer_sums):
        d_lefts = size.from_others(d_lefts)
        d_right = exchange(d_right, row).sum(0)
        d_right = lax.ppermute(d_right, everyone, size.turn_back)
        d_out, d_blend, thin, *out_sums = call_rows_out_back(
            d_lefts,
            d_right,
            grad.reshape(tokens, -1),
            msa_out,
            blend,
            share,
            weights[8],
            source,
            target,
            size.core,
        )
        d_mid, d_blend = together(d_mid, d_blend)
        outer_sums = outer_sums(d_mid)
        d_blend, *outer_sums = together(exchange(d_blend, everyone), *outer_sums)
        d_qkv = call_rows_back(qkv, d_blend, mesh_rows, mesh_cols, size.scale)
        pair_mid, d_qkv = together(pair_mid, d_qkv)
        side_sums = side_sums(pair_mid)
        early = size.half_sum((outer_sums, out_sums))
        side_sum = size.core_sum([side_sums])
        d_qkv, early, side_sum = together(exchange(d_qkv, everyone), early, side_sum)
        d_col, *in_sums = call_rows_in_back(d_qkv, msa_col, d_out, weights[4:7], size.core)
        d_stripe, *col_sums = call_columns_back(
            stripe, seen, d_col, weights[:4], size.core, size.scale
        )
        d_bias = d_qkv.reshape(size.heads, size.chain_groups, -1, 128)
        thin_sums = call_bias_sums(d_bias, pair_flat, thin, size.core, size.cols_here)
        d_pair = call_bias_back(d_bias, d_mid, offset, size.cols_here)
        d_features = size.from_slim_permuted(d_stripe.reshape(chains, slim, -1))
        late = (col_sums, in_sums, thin_sums, (side_sum,))
        return d_features, d_pair, late, early

    return (msa_out.reshape(chains, slim, -1), left, right), ready, back


def msa_plain_forward(
    size, alignment_features, residue_couplings, present, weights, prepare, raw
):
    chains, rows_here = size.chains, size.rows_here
    outputs, pull = jax.vjp(
        lambda x, y, w: msa_plain(size, x, y, present, w),
        alignment_features,
        residue_couplings,
        weights,
    )

    def back(grad, d_lefts, d_right, d_mid, pair_mid, side_sums, outer_sums):
        d_left = d_lefts[0].reshape(rows_here // 4, chains // 4, 4, 4, 32)
        d_left = jnp.transpose(d_left, (0, 3, 1, 2, 4)).reshape(-1, 128)
        d_features, d_pair, d_weights = pull((grad, [d_left], d_right))
        d_pair = d_pair.reshape(-1, size.pair_width) + d_mid
        thin = [d_weights[9], d_weights[10], jnp.pad(d_weights[7], ((0, 128), (0, 0)))]
        thin = jnp.pad(jnp.concatenate(thin, 1), ((0, 0), (0, 64 - size.heads)))
        core = size.core[0]
        pick = lambda x, n: lax.dynamic_index_in_dim(x, n, 0, False)
        own = lambda x: (pick(x, core), pick(x, 1 - core))
        cut = lambda ws: own(
            jnp.stack([jnp.concatenate([w[:, n : n + 128] for w in ws], 0) for n in (0, 128)])
        )
        late = (cut(d_weights[:4]), cut(d_weights[4:7]), own(thin.reshape(2, -1, 128)))
        late = (*late, side_sums(pair_mid))
        early = (outer_sums(d_mid), cut(d_weights[8:9]))
        return d_features, d_pair, late, size.half_sum(early)

    return outputs, prepare(raw), back


def per_device(mesh_rows, mesh_cols, *arguments):
    (
        alignment_features,
        residue_couplings,
        chain_indicator,
        alignment_result_adjoint,
        coupling_result_adjoint,
        *weights,
    ) = arguments
    present = chain_indicator.astype(jnp.float32)
    heads = weights[7].shape[1]
    size = Layout(
        mesh_rows,
        mesh_cols,
        residue_couplings.shape,
        present.shape[0],
        heads,
        weights[4].shape[1] // heads,
    )
    devices, channels_here = size.devices, size.channels_here
    cols_here, pair_width = size.cols_here, size.pair_width
    (
        tensor_result_matrix,
        source_side_matrix,
        source_side_switch,
        target_side_matrix,
        target_side_switch,
        trilateral_result_switch,
        trilateral_result_matrix,
    ) = weights[11:]

    sides = (source_side_switch, target_side_switch, source_side_matrix, target_side_matrix)
    shift = channels_here.bit_length() - 1
    def prepare(raw):
        return call_prepare(raw[0], raw[1:], shift)

    forward = msa_forward if size.slim == 8 else msa_plain_forward
    (msa_slim, left_rows, right_rows), (outer_halves, sides_halves), msa_back = forward(
        size,
        alignment_features,
        residue_couplings,
        present,
        tuple(weights[:11]),
        prepare,
        (tensor_result_matrix, *sides, trilateral_result_switch),
    )
    pair_flat = residue_couplings.reshape(-1, pair_width)
    grad_flat = coupling_result_adjoint.reshape(-1, pair_width)
    count = len(left_rows)
    first = (lax.axis_index("col") if count > 1 else jnp.int32(0)).reshape(1)
    blocks = call_blocks(first, left_rows)
    pair_mid, edges, prods = call_edges(
        blocks, right_rows, outer_halves, sides_halves, pair_flat, cols_here
    )
    edges = exchange(edges.reshape(devices, 2, channels_here, 16, 128), everyone)
    triangle = exchange(call_triangle(edges, mesh_rows, mesh_cols), everyone)
    pair_out, d_triangle, d_logit, g_tri_out = call_finish(
        triangle.reshape(pair_width, 16, 128),
        pair_mid,
        grad_flat,
        trilateral_result_switch,
        trilateral_result_matrix,
        cols_here,
    )
    views = (alignment_result_adjoint, msa_slim)
    *views, d_triangle = together(*views, d_triangle)
    views = size.both_views(*views)
    d_triangle = exchange(d_triangle.reshape(devices, channels_here, 16, 128), everyone)
    d_edges = call_triangle_back(edges, d_triangle, mesh_rows, mesh_cols)
    d_edges, mid_again = together(d_edges, pair_mid)
    factors = call_factors(mid_again, sides_halves, cols_here)
    d_edges, factors = together(exchange(d_edges, everyone), factors)
    d_edges, views = together(d_edges, views)
    views = lax.all_to_all(views, "col", 0, 0, tiled=True)
    d_mid, d_logits, d_right, *d_lefts = call_edges_back(
        d_edges.reshape(2 * pair_width, 16, 128),
        pair_mid,
        grad_flat,
        d_logit,
        sides_halves,
        right_rows,
        outer_halves,
        factors,
        blocks,
        first,
        count,
        cols_here,
    )
    d_right, views = together(d_right, views)
    msa_grad, msa_out = size.split_views(views)

    def side_sums(pair_mid):
        return call_side_sums(pair_mid, d_logits, g_tri_out, size.core, cols_here, shift)

    def outer_sums(d_mid):
        return call_outer_sums(d_mid, prods, size.core, cols_here)

    alignment_adjoint, coupling_adjoint, late, early = msa_back(
        msa_grad, d_lefts, d_right, d_mid, pair_mid, side_sums, outer_sums
    )
    sums, (alignment_adjoint, coupling_adjoint) = size.sum_all(
        late, early, alignment_adjoint, coupling_adjoint
    )
    place = jnp.stack([lax.axis_index(axis) for axis in ("core", "half", "col")])
    summed = call_spread_sums(*sums, place, mesh_rows // 2, mesh_cols, [w.shape for w in weights])
    return (
        msa_out,
        pair_out.reshape(residue_couplings.shape),
        alignment_adjoint,
        coupling_adjoint.reshape(residue_couplings.shape),
        *summed,
    )


def solution(mesh):
    mesh_rows, mesh_cols = mesh.shape["row"], mesh.shape["col"]

    def local(*arguments):
        return per_device(mesh_rows, mesh_cols, *arguments)

    split = jax.sharding.Mesh(
        mesh.devices.reshape(mesh_rows // 2, 2, mesh_cols), ("half", "core", "col")
    )
    whole = P()
    msa = P("col", row, None)
    pair = P(row, "col", None)
    return jax.shard_map(
        local,
        mesh=split,
        in_specs=(msa, pair, whole, msa, pair) + (whole,) * 18,
        out_specs=(msa, pair, msa, pair) + (whole,) * 18,
        check_vma=False,
    )
```

```python
import functools

import jax
import jax.numpy as jnp
from jax import lax
from jax.experimental import pallas as pl
from jax.experimental.pallas import tpu as pltpu
from jax.sharding import PartitionSpec as P

bf16, f32 = jnp.bfloat16, jnp.float32
NN = ((1,), (0,))
NT = ((1,), (1,))
TN = ((0,), (0,))


def one_pass(a, b, dims=NN):
    return lax.dot_general(a, b, (dims, ((), ())), preferred_element_type=f32)


def halves(x):
    high = x.astype(bf16)
    return high, (x - high.astype(f32)).astype(bf16)


def dot3(a, b, dims=NN):
    a_high, a_low = a if isinstance(a, tuple) else halves(a)
    b_high, b_low = b if isinstance(b, tuple) else halves(b)
    return one_pass(a_high, b_high, dims) + (
        one_pass(a_high, b_low, dims) + one_pass(a_low, b_high, dims)
    )


def rounded(pair, rows):
    return pair[0][rows], pair[1][rows]


def iota(shape, dim):
    return lax.broadcasted_iota(jnp.int32, shape, dim)


def norm_parts(x):
    centered = x - jnp.mean(x, axis=-1, keepdims=True)
    inverse = lax.rsqrt(jnp.mean(centered * centered, axis=-1, keepdims=True) + 1e-05)
    return centered * inverse, inverse


def norm_back(normed, inverse, grad):
    return inverse * (
        grad
        - jnp.mean(grad, axis=-1, keepdims=True)
        - normed * jnp.mean(grad * normed, axis=-1, keepdims=True)
    )


def stacked3(a, b, dims=NN):
    a_high, a_low = a if isinstance(a, tuple) else halves(a)
    b_high, b_low = b if isinstance(b, tuple) else halves(b)
    return one_pass(
        jnp.concatenate([a_high, a_low, a_high], dims[0][0]),
        jnp.concatenate([b_high, b_high, b_low], dims[1][0]),
        dims,
    )


def row_of(t, u):
    return 2 * t + u // 2 + 16 * (u % 2)


def same_slot(chains):
    shape = (chains * 8, 256)
    return (iota(shape, 0) & 7) == (iota(shape, 1) & 7)


def blocks_kernel(chains, first_ref, *refs):
    *part_refs, out_ref, left_ref = refs
    groups, count = chains // 4, len(part_refs)
    size = part_refs[0].shape[0]
    t = pl.program_id(0)

    @pl.when(t == 0)
    def _():
        for n, ref in enumerate(part_refs):
            place = lax.rem(first_ref[0] + count - n, count) * size
            left_ref[pl.ds(pl.multiple_of(place, 8), size), :] = ref[...]

    shape = (chains * 8, chains)
    chain = iota(shape, 0) >> 3
    lift = jnp.where(iota(shape, 1) == (chain & 3) * groups + (chain >> 2), 1.0, 0.0).astype(bf16)
    same = same_slot(chains)
    rows = [
        left_ref[pl.ds(pl.multiple_of(row_of(t, u) * groups, groups), groups), :] for u in range(4)
    ]
    rows = jnp.concatenate(halves(jnp.concatenate(rows, 0)), 0)
    shape = (128, 256)
    slabs = []
    for n in range(4):
        spread = ((iota(shape, 0) >> 5) == n) & ((iota(shape, 0) & 31) == (iota(shape, 1) >> 3))
        slabs.append(one_pass(rows, jnp.where(spread, 1.0, 0.0).astype(bf16)))
    for part in range(2):
        for u in range(4):
            place = slice((part * 4 + u) * groups, (part * 4 + u + 1) * groups)
            slab = jnp.concatenate([x[place] for x in slabs], 0).astype(bf16)
            out_ref[0, u, part] = jnp.where(same, one_pass(lift, slab), 0.0).astype(bf16)


def call_blocks(first, parts):
    rows = sum(part.shape[0] for part in parts)
    chains = rows // 32 * 4
    shape = (8, 4, 2, chains * 8, 256)
    return pl.pallas_call(
        functools.partial(blocks_kernel, chains),
        grid=(8,),
        in_specs=[pl.BlockSpec(memory_space=pltpu.SMEM)] + [full(part) for part in parts],
        out_specs=step_block(shape),
        out_shape=jax.ShapeDtypeStruct(shape, bf16),
        scratch_shapes=[pltpu.VMEM((rows, 128), f32)],
        compiler_params=params(),
        name="blocks",
    )(first, *parts)


def join_right(ref, out_ref):
    cols = ref.shape[0] * 8
    for g in range(4):
        for n in range(ref.shape[2]):
            out_ref[g * cols : (g + 1) * cols, n * 128 : (n + 1) * 128] = ref[:, g, n].reshape(
                cols, 128
            )


def cut_right(ref, out_ref):
    cols = out_ref.shape[0] * 8
    for g in range(4):
        for n in range(out_ref.shape[2]):
            tile = ref[g * cols : (g + 1) * cols, n * 128 : (n + 1) * 128]
            out_ref[:, g, n] = tile.reshape(-1, 8, 128)


def outer_weights(ref, out_ref):
    whole = ref[...].reshape(32, 4, 8, 128)
    for g in range(4):
        out_ref[g, 0], out_ref[g, 1] = halves(whole[:, g].reshape(256, 128))


def params(mebibytes=56):
    return pltpu.CompilerParams(vmem_limit_bytes=mebibytes * 2**20)


def full(array):
    return pl.BlockSpec(array.shape, lambda t, n=len(array.shape): (0,) * n)


def step_block(shape):
    return pl.BlockSpec((1,) + shape[1:], lambda t, n=len(shape): (t,) + (0,) * (n - 1))


def pair_of(ref, *index):
    return ref[(*index, 0)], ref[(*index, 1)]


def chunk_order(shift):
    shape = (256, 256)
    place, width = iota(shape, 0), 1 << shift
    channel = place & 127
    target = ((channel >> shift) << (shift + 1)) + (channel & (width - 1))
    target = target + ((place >> 7) << shift)
    return jnp.where(iota(shape, 1) == target, 1.0, 0.0).astype(bf16)


def side_halves(shift, refs, out_ref):
    order = chunk_order(shift)
    for n in range(2):
        both = halves(jnp.concatenate([refs[2 * n][...], refs[2 * n + 1][...]], 1))
        for part in range(2):
            out_ref[part, :, n * 256 : (n + 1) * 256] = one_pass(both[part], order).astype(bf16)
    if len(refs) == 5:
        out_ref[0, :, 512:], out_ref[1, :, 512:] = halves(refs[4][...])


def prepare_kernel(shift, outer_ref, *refs):
    *side_refs, outer_halves, sides_halves = refs
    outer_weights(outer_ref, outer_halves)
    side_halves(shift, side_refs, sides_halves)


def call_prepare(outer, sides, shift):
    return pl.pallas_call(
        functools.partial(prepare_kernel, shift),
        out_shape=(
            jax.ShapeDtypeStruct((4, 2, 256, 128), bf16),
            jax.ShapeDtypeStruct((2, 128, 640), bf16),
        ),
        compiler_params=params(),
        name="prepare",
    )(outer, *sides)


def edges_kernel(
    cols,
    block_ref,
    right_ref,
    outer_halves,
    sides_halves,
    pair_ref,
    mid_ref,
    edge_ref,
    prod_ref,
    whole_ref,
    right_halves,
):
    t = pl.program_id(0)

    @pl.when(t == 0)
    def _():
        join_right(right_ref, whole_ref)
        right_halves[0], right_halves[1] = halves(whole_ref[...])

    right = pair_of(right_halves)
    places = four_rows(t, cols)
    for u in range(4):
        high, low = halves(stacked3(right, pair_of(block_ref, 0, u)))
        for g in range(4):
            prod_ref[0, g, 0, u * cols : (u + 1) * cols] = high[g * cols : (g + 1) * cols]
            prod_ref[0, g, 1, u * cols : (u + 1) * cols] = low[g * cols : (g + 1) * cols]
    update = 0.0
    for g in range(4):
        update = update + dot3(pair_of(prod_ref, 0, g), pair_of(outer_halves, g))
    mid = update + read_rows(pair_ref, places)
    write_rows(mid_ref, places, mid)
    normed, _ = norm_parts(mid)
    sides = rounded(pair_of(sides_halves), (slice(None), slice(0, 512)))
    logits = stacked3(normed, sides)
    write_turned(edge_ref, t, jax.nn.sigmoid(logits[:, :256]) * logits[:, 256:])


def call_edges(blocks, right, outer, sides, pair, cols):
    rows, depth = pair.shape[0], blocks.shape[3]
    prods = (8, 4, 2, 4 * cols, 256)
    return pl.pallas_call(
        functools.partial(edges_kernel, cols),
        grid=(8,),
        in_specs=[step_block(blocks.shape)] + [full(x) for x in (right, outer, sides, pair)],
        out_specs=(
            pl.BlockSpec((rows, 128), lambda t: (0, 0)),
            pl.BlockSpec((256, 16, 128), lambda t: (0, 0, 0)),
            step_block(prods),
        ),
        out_shape=(
            jax.ShapeDtypeStruct((rows, 128), f32),
            jax.ShapeDtypeStruct((256, 16, 128), f32),
            jax.ShapeDtypeStruct(prods, bf16),
        ),
        scratch_shapes=[
            pltpu.VMEM((4 * cols, depth), f32),
            pltpu.VMEM((2, 4 * cols, depth), bf16),
        ],
        compiler_params=params(),
        name="edges",
    )(blocks, right, outer, sides, pair)


def factors_kernel(cols, mid_ref, sides_halves, out_ref):
    normed, _ = norm_parts(read_rows(mid_ref, four_rows(pl.program_id(0), cols)))
    sides = rounded(pair_of(sides_halves), (slice(None), slice(0, 512)))
    logits = stacked3(normed, sides)
    gate = jax.nn.sigmoid(logits[:, :256])
    out_ref[0, :, :256] = logits[:, 256:] * gate * (1.0 - gate)
    out_ref[0, :, 256:] = gate


def call_factors(mid, sides, cols):
    shape = (8, 4 * cols, 512)
    return pl.pallas_call(
        functools.partial(factors_kernel, cols),
        grid=(8,),
        in_specs=[full(mid), full(sides)],
        out_specs=step_block(shape),
        out_shape=jax.ShapeDtypeStruct(shape, f32),
        compiler_params=params(),
        name="factors",
    )(mid, sides)


def join_tiles(chunks, mesh_rows, mesh_cols, out_ref):
    plain = chunks.reshape(mesh_rows * mesh_cols * 16, 128)
    rolled = pltpu.roll(plain, 64, 1)
    first = iota((16, 128), 1) < 64
    for r in range(mesh_rows):
        for t in range(mesh_cols // 2):
            even = slice((r * mesh_cols + 2 * t) * 16, (r * mesh_cols + 2 * t + 1) * 16)
            odd = slice((r * mesh_cols + 2 * t + 1) * 16, (r * mesh_cols + 2 * t + 2) * 16)
            lanes = slice(t * 128, (t + 1) * 128)
            out_ref[r * 32 : r * 32 + 16, lanes] = jnp.where(first, plain[even], rolled[odd])
            out_ref[r * 32 + 16 : r * 32 + 32, lanes] = jnp.where(first, rolled[even], plain[odd])


def cut_tiles(whole, mesh_rows, mesh_cols, store):
    first = iota((16, 128), 1) < 64
    for t in range(mesh_cols // 2):
        plain = whole[:, t * 128 : (t + 1) * 128]
        rolled = pltpu.roll(plain, 64, 1)
        for r in range(mesh_rows):
            low = slice(r * 32, r * 32 + 16)
            high = slice(r * 32 + 16, r * 32 + 32)
            store(r * mesh_cols + 2 * t, jnp.where(first, plain[low], rolled[high]))
            store(r * mesh_cols + 2 * t + 1, jnp.where(first, rolled[low], plain[high]))


def triangle_kernel(mesh_rows, mesh_cols, edge_ref, out_ref, left_ref, right_ref):
    join_tiles(edge_ref[:, 0, 0], mesh_rows, mesh_cols, left_ref)
    join_tiles(edge_ref[:, 1, 0], mesh_rows, mesh_cols, right_ref)

    def store(d, tile):
        out_ref[d, 0] = tile

    cut_tiles(dot3(left_ref[...], right_ref[...], NT), mesh_rows, mesh_cols, store)


def call_triangle(edges, mesh_rows, mesh_cols):
    devices, _, channels = edges.shape[:3]
    span = mesh_rows * 32
    return pl.pallas_call(
        functools.partial(triangle_kernel, mesh_rows, mesh_cols),
        grid=(channels,),
        in_specs=[pl.BlockSpec((devices, 2, 1, 16, 128), lambda n: (0, 0, n, 0, 0))],
        out_specs=pl.BlockSpec((devices, 1, 16, 128), lambda n: (0, n, 0, 0)),
        out_shape=jax.ShapeDtypeStruct((devices, channels, 16, 128), f32),
        scratch_shapes=[pltpu.VMEM((span, span), f32)] * 2,
        compiler_params=params(32),
        name="triangle",
    )(edges)


def triangle_back_kernel(
    mesh_rows, mesh_cols, edge_ref, grad_ref, out_ref, left_ref, right_ref, whole_ref
):
    join_tiles(edge_ref[:, 0, 0], mesh_rows, mesh_cols, left_ref)
    join_tiles(edge_ref[:, 1, 0], mesh_rows, mesh_cols, right_ref)
    join_tiles(grad_ref[:, 0], mesh_rows, mesh_cols, whole_ref)

    def store(kind):
        def put(d, tile):
            out_ref[d, kind, 0] = tile

        return put

    whole = whole_ref[...]
    cut_tiles(dot3(whole, right_ref[...]), mesh_rows, mesh_cols, store(0))
    cut_tiles(dot3(jnp.transpose(whole), left_ref[...]), mesh_rows, mesh_cols, store(1))


def call_triangle_back(edges, grad, mesh_rows, mesh_cols):
    devices, _, channels = edges.shape[:3]
    span = mesh_rows * 32
    both = pl.BlockSpec((devices, 2, 1, 16, 128), lambda n: (0, 0, n, 0, 0))
    return pl.pallas_call(
        functools.partial(triangle_back_kernel, mesh_rows, mesh_cols),
        grid=(channels,),
        in_specs=[both, pl.BlockSpec((devices, 1, 16, 128), lambda n: (0, n, 0, 0))],
        out_specs=both,
        out_shape=jax.ShapeDtypeStruct(edges.shape, f32),
        scratch_shapes=[pltpu.VMEM((span, span), f32)] * 3,
        compiler_params=params(32),
        name="triangle_back",
    )(edges, grad)


def four_rows(t, cols):
    return [
        pl.ds(pl.multiple_of((2 * t + u // 2 + 16 * (u % 2)) * cols, cols), cols) for u in range(4)
    ]


def read_rows(ref, places):
    return jnp.concatenate([ref[p, :] for p in places], 0)


def write_rows(ref, places, value):
    size = value.shape[0] // len(places)
    for u, p in enumerate(places):
        ref[p, :] = value[u * size : (u + 1) * size]


def read_turned(ref, t):
    parts = []
    for v in range(2):
        tile = ref[:, pl.ds(2 * t + v, 1), :]
        parts.append(jnp.transpose(tile.reshape(tile.shape[0], 128)))
    return jnp.concatenate(parts, 0)


def write_turned(ref, t, value):
    for v in range(2):
        turned = jnp.transpose(value[v * 128 : (v + 1) * 128])
        ref[:, pl.ds(2 * t + v, 1), :] = turned[:, None, :]


def finish_kernel(
    cols, tri_ref, mid_ref, grad_ref, gate_ref, proj_ref, out_ref, dtri_ref, dlogit_ref, dproj_ref
):
    gate_w = halves(gate_ref[...])
    proj_w = halves(proj_ref[...])
    dproj_ref[...] = jnp.zeros_like(dproj_ref)

    def step(t, carry):
        places = four_rows(t, cols)
        mid = read_rows(mid_ref, places)
        grad = read_rows(grad_ref, places)
        normed, _ = norm_parts(mid)
        tri, tri_inverse = norm_parts(read_turned(tri_ref, t))
        tri_halves = halves(tri)
        gate = jax.nn.sigmoid(dot3(normed, gate_w))
        value = dot3(tri_halves, proj_w)
        write_rows(out_ref, places, mid + gate * value)
        dvalue = halves(grad * gate)
        write_rows(dlogit_ref, places, grad * value * gate * (1.0 - gate))
        dproj_ref[...] += stacked3(halves(jnp.transpose(tri)), dvalue)
        write_turned(dtri_ref, t, norm_back(tri, tri_inverse, stacked3(dvalue, proj_w, NT)))
        return carry

    lax.fori_loop(0, 8, step, 0)


def call_finish(tri, mid, grad, gate, proj, cols):
    rows = mid.shape[0]
    return pl.pallas_call(
        functools.partial(finish_kernel, cols),
        out_shape=(
            jax.ShapeDtypeStruct((rows, 128), f32),
            jax.ShapeDtypeStruct((128, 16, 128), f32),
            jax.ShapeDtypeStruct((rows, 128), f32),
            jax.ShapeDtypeStruct((128, 128), f32),
        ),
        compiler_params=params(32),
        name="finish",
    )(tri, mid, grad, gate, proj)


def edges_back_kernel(
    cols,
    chains,
    dedge_ref,
    mid_ref,
    grad_ref,
    dlogit_ref,
    sides_halves,
    right_ref,
    outer_halves,
    factor_ref,
    block_ref,
    first_ref,
    dmid_ref,
    dlogits_ref,
    dright_ref,
    *refs,
):
    *dleft_refs, whole_ref, turned_halves, fold_ref, dslab_ref, dleft_ref = refs
    t = pl.program_id(0)

    @pl.when(t == 0)
    def _():
        join_right(right_ref, whole_ref)
        turned_halves[0], turned_halves[1] = halves(jnp.transpose(whole_ref[...]))
        shape = (256, 128)
        for u in range(4):
            lane = 64 * (u % 2) + 32 * (u // 2) + (iota(shape, 0) >> 3)
            fold = jnp.where(iota(shape, 1) == lane, 1.0, 0.0).astype(bf16)
            fold_ref[512 * u : 512 * u + 256] = fold
            fold_ref[512 * u + 256 : 512 * u + 512] = fold
        whole_ref[...] = jnp.zeros_like(whole_ref)

    same = same_slot(chains)
    sides = pair_of(sides_halves)
    places = four_rows(t, cols)
    normed, inverse = norm_parts(read_rows(mid_ref, places))
    dedge = read_turned(dedge_ref, t)
    dlogits = [
        dedge * factor_ref[0, :, :256],
        dedge * factor_ref[0, :, 256:],
        read_rows(dlogit_ref, places),
    ]
    dlogits = halves(jnp.concatenate(dlogits, 1))
    dlogits_ref[0, 0], dlogits_ref[0, 1] = dlogits
    dmid = read_rows(grad_ref, places) + norm_back(normed, inverse, dot3(dlogits, sides, NT))
    write_rows(dmid_ref, places, dmid)
    dmid = halves(dmid)
    dprod = [halves(stacked3(dmid, pair_of(outer_halves, g), NT)) for g in range(4)]
    here, diagonal = [], []
    turned = pair_of(turned_halves)
    for u in range(4):
        rows = slice(u * cols, (u + 1) * cols)
        here.append([jnp.concatenate([dprod[g][n][rows] for g in range(4)], 0) for n in range(2)])
        diagonal += halves(jnp.where(same, stacked3(turned, tuple(here[u])), 0.0))
    right_terms = [x for high, low in here for x in (high, low, high)]
    block_terms = [block_ref[0, u, n] for u in range(4) for n in (0, 0, 1)]
    whole_ref[...] += one_pass(
        jnp.concatenate(right_terms, 1), jnp.concatenate(block_terms, 1), NT
    )
    dslab = one_pass(jnp.concatenate(diagonal, 1), fold_ref[...])
    dslab_ref[t] = jnp.sum(dslab.reshape(chains, 8, 128), axis=1)

    @pl.when(t == 7)
    def _():
        cut_right(whole_ref, dright_ref)
        first = iota((chains, 128), 1) < 64
        for n in range(4):
            even, odd = dslab_ref[2 * n], dslab_ref[2 * n + 1]
            dleft_ref[n] = jnp.where(first, even, pltpu.roll(odd, 64, 1))
            dleft_ref[n + 4] = jnp.where(first, pltpu.roll(even, 64, 1), odd)
        count, size = len(dleft_refs), dleft_refs[0].shape[0]
        for n, ref in enumerate(dleft_refs):
            place = lax.rem(first_ref[0] + n, count) * size
            ref[...] = dleft_ref[pl.ds(place, size)]


def call_edges_back(
    dedge, mid, grad, dlogit, sides, right, outer, factors, blocks, first, count, cols
):
    rows, depth = mid.shape[0], blocks.shape[3]
    chains = depth // 8
    dlogits = (8, 2, 4 * cols, 640)
    return pl.pallas_call(
        functools.partial(edges_back_kernel, cols, chains),
        grid=(8,),
        in_specs=[full(x) for x in (dedge, mid, grad, dlogit, sides, right, outer)]
        + [step_block(factors.shape), step_block(blocks.shape), pl.BlockSpec(memory_space=pltpu.SMEM)],
        out_specs=(
            pl.BlockSpec((rows, 128), lambda t: (0, 0)),
            step_block(dlogits),
            full(right),
        )
        + (pl.BlockSpec((8 // count, chains, 128), lambda t: (0, 0, 0)),) * count,
        out_shape=(
            jax.ShapeDtypeStruct((rows, 128), f32),
            jax.ShapeDtypeStruct(dlogits, bf16),
            jax.ShapeDtypeStruct(right.shape, f32),
        )
        + (jax.ShapeDtypeStruct((8 // count, chains, 128), f32),) * count,
        scratch_shapes=[
            pltpu.VMEM((4 * cols, depth), f32),
            pltpu.VMEM((2, depth, 4 * cols), bf16),
            pltpu.VMEM((2048, 128), bf16),
            pltpu.VMEM((8, chains, 128), f32),
            pltpu.VMEM((8, chains, 128), f32),
        ],
        compiler_params=params(),
        name="edges_back",
    )(dedge, mid, grad, dlogit, sides, right, outer, factors, blocks, first)


def give_halves(core_ref, whole_ref, mine_ref, other_ref):
    mine_ref[...] = whole_ref[core_ref[0]]
    other_ref[...] = whole_ref[1 - core_ref[0]]


def side_sums_kernel(
    cols,
    shift,
    mid_ref,
    dlogits_ref,
    first_ref,
    core_ref,
    mine_ref,
    other_ref,
    sides_ref,
    whole_ref,
):
    t = pl.program_id(0)

    @pl.when(t == 0)
    def _():
        sides_ref[...] = jnp.zeros_like(sides_ref)

    normed, _ = norm_parts(read_rows(mid_ref, four_rows(t, cols)))
    sides_ref[...] += stacked3(halves(jnp.transpose(normed)), pair_of(dlogits_ref, 0))

    @pl.when(t == 7)
    def _():
        order = chunk_order(shift)
        for n in range(2):
            high, low = halves(sides_ref[:, n * 256 : (n + 1) * 256])
            sides = one_pass(high, order, NT) + one_pass(low, order, NT)
            for side in range(2):
                place = 2 * n + side
                rows = slice(place % 3 * 128, place % 3 * 128 + 128)
                whole_ref[place // 3, rows] = sides[:, side * 128 : (side + 1) * 128]
        whole_ref[1, 128:256] = sides_ref[:, 512:]
        whole_ref[1, 256:] = first_ref[...]
        give_halves(core_ref, whole_ref, mine_ref, other_ref)


def call_side_sums(mid, dlogits, first, core, cols, shift):
    return pl.pallas_call(
        functools.partial(side_sums_kernel, cols, shift),
        grid=(8,),
        in_specs=[full(mid), step_block(dlogits.shape), full(first)]
        + [pl.BlockSpec(memory_space=pltpu.SMEM)],
        out_specs=(pl.BlockSpec((384, 128), lambda t: (0, 0)),) * 2,
        out_shape=(jax.ShapeDtypeStruct((384, 128), f32),) * 2,
        scratch_shapes=[pltpu.VMEM((128, 640), f32), pltpu.VMEM((2, 384, 128), f32)],
        compiler_params=params(),
        name="side_sums",
    )(mid, dlogits, first, core)


def outer_sums_kernel(
    cols, dmid_ref, prod_ref, core_ref, mine_ref, other_ref, outer_ref, whole_ref
):
    t = pl.program_id(0)

    @pl.when(t == 0)
    def _():
        outer_ref[...] = jnp.zeros_like(outer_ref)

    dmid = halves(jnp.transpose(read_rows(dmid_ref, four_rows(t, cols))))
    for g in range(4):
        outer_ref[:, g * 256 : (g + 1) * 256] += stacked3(dmid, pair_of(prod_ref, 0, g))

    @pl.when(t == 7)
    def _():
        for g in range(4):
            tile = jnp.transpose(outer_ref[:, g * 256 : (g + 1) * 256]).reshape(32, 8, 128)
            for p in range(32):
                start = p % 16 * 32 + g * 8
                whole_ref[p // 16, start : start + 8] = tile[p]
        give_halves(core_ref, whole_ref, mine_ref, other_ref)


def call_outer_sums(dmid, prods, core, cols):
    return pl.pallas_call(
        functools.partial(outer_sums_kernel, cols),
        grid=(8,),
        in_specs=[full(dmid), step_block(prods.shape), pl.BlockSpec(memory_space=pltpu.SMEM)],
        out_specs=(pl.BlockSpec((512, 128), lambda t: (0, 0)),) * 2,
        out_shape=(jax.ShapeDtypeStruct((512, 128), f32),) * 2,
        scratch_shapes=[pltpu.VMEM((128, 1024), f32), pltpu.VMEM((2, 512, 128), f32)],
        compiler_params=params(),
        name="outer_sums",
    )(dmid, prods, core)


def pack_heads(y, store):
    lane = iota((1, 1, 128), 2) >> 5
    for tile in range(y.shape[1] // 128):
        part = y[:, tile * 128 : (tile + 1) * 128]
        turned = [part] + [pltpu.roll(part, 32 * n, 1) for n in range(1, 4)]
        turned = [x.reshape(-1, 4, 8, 128) for x in turned]
        for head in range(4):
            out = turned[-head % 4][:, 0]
            for chain in range(1, 4):
                out = jnp.where(lane == chain, turned[(chain - head) % 4][:, chain], out)
            store(tile * 4 + head, out)


def unpack_heads(load, heads):
    lane = iota((1, 1, 128), 2) >> 5
    tiles = []
    for tile in range(heads // 4):
        turned = []
        for head in range(4):
            part = load(tile * 4 + head)
            flat = part.reshape(-1, 128)
            turned.append(
                [part] + [pltpu.roll(flat, 32 * n, 1).reshape(part.shape) for n in range(1, 4)]
            )
        chains = []
        for chain in range(4):
            out = turned[0][-chain % 4]
            for head in range(1, 4):
                out = jnp.where(lane == head, turned[head][(head - chain) % 4], out)
            chains.append(out[:, None])
        tiles.append(jnp.concatenate(chains, 1).reshape(-1, 128))
    return jnp.concatenate(tiles, 1)


def head_lanes(tile, n):
    return jnp.where((iota((1, 128), 1) >> 5) == n, tile, 0.0)


def stack_heads(tile):
    return jnp.concatenate([head_lanes(tile, n) for n in range(4)], 0)


def join_heads(stacked):
    size = stacked.shape[0] // 4
    lane = iota((1, 128), 1) >> 5
    out = stacked[:size]
    for n in range(1, 4):
        out = jnp.where(lane == n, stacked[n * size : (n + 1) * size], out)
    return out


def soft(scores, seen=None):
    if seen is not None:
        scores = jnp.where(seen, scores, -1e30)
    weights = jnp.exp(scores - jnp.max(scores, axis=-1, keepdims=True))
    if seen is not None:
        weights = jnp.where(seen, weights, 0.0)
    return weights * (1.0 / jnp.sum(weights, axis=-1, keepdims=True))


def soft_back(weights, grad):
    return weights * (grad - jnp.sum(weights * grad, axis=-1, keepdims=True))


def stripe_seen(present_ref):
    tokens = present_ref.shape[1]
    shape = (tokens, tokens)
    same = (iota(shape, 0) & 7) == (iota(shape, 1) & 7)
    return same & (present_ref[...] > 0.0)


def column_attention(q, k, v, seen):
    weights, tiles = [], []
    for tile in range(q.shape[1] // 128):
        lanes = slice(tile * 128, (tile + 1) * 128)
        keys, values = halves(k[:, lanes]), halves(v[:, lanes])
        blend = 0.0
        for n in range(4):
            weights.append(soft(dot3(head_lanes(q[:, lanes], n), keys, NT), seen))
            blend = blend + head_lanes(dot3(weights[-1], values), n)
        tiles.append(blend)
    return weights, jnp.concatenate(tiles, 1)


def columns_kernel(
    scale,
    x_ref,
    present_ref,
    bias_ref,
    q_ref,
    k_ref,
    v_ref,
    o_ref,
    q2_ref,
    k2_ref,
    v2_ref,
    out_ref,
    qkv_ref,
):
    x = x_ref[...]
    normed, _ = norm_parts(x)
    normed = halves(normed)
    q, k, v = (dot3(normed, halves(w[...])) for w in (q_ref, k_ref, v_ref))
    _, blend = column_attention(q * scale, k, v, stripe_seen(present_ref))
    out = x + dot3(blend, halves(o_ref[...]))
    out_ref[...] = out
    normed, _ = norm_parts(out)
    normed = halves(normed)
    groups, size = qkv_ref.shape[0] // 8, (qkv_ref.shape[1] - 16) // 3
    qkv_ref[:, -16:] = bias_ref[...]

    def store(kind):
        def put(head, value):
            place = slice(head * groups, (head + 1) * groups)
            rows = slice(kind * size, (kind + 1) * size)
            qkv_ref[place, rows] = value.reshape(groups, size, 128)

        return put

    for kind, w in enumerate((q2_ref, k2_ref, v2_ref)):
        pack_heads(dot3(normed, halves(w[...])), store(kind))


def call_columns(x, present, bias, weights, group_chains, scale):
    return pl.pallas_call(
        functools.partial(columns_kernel, scale),
        out_shape=(
            jax.ShapeDtypeStruct(x.shape, f32),
            jax.ShapeDtypeStruct((bias.shape[0], 6 * group_chains + 16, 128), f32),
        ),
        compiler_params=params(24),
        name="columns",
    )(x, present, bias, *weights)


def packed_parts(ref):
    parts = (ref.shape[1] - 16) // 24
    for half in range(parts):
        places = [(kind * parts + half) * 8 for kind in range(3)]
        yield half, places, [ref[:, p : p + 8].reshape(-1, 128) for p in places]


def rows_kernel(mesh_rows, mesh_cols, scale, qkv_ref, out_ref, whole_ref):
    join_tiles(qkv_ref[:, -16:], mesh_rows, mesh_cols, whole_ref)
    bias = whole_ref[...]
    for half, _, (q, k, v) in packed_parts(qkv_ref):
        k, v, q = halves(k), halves(v), q * scale
        blend = 0.0
        for n in range(4):
            weights = soft(dot3(head_lanes(q, n), k, NT) + bias)
            blend = blend + head_lanes(dot3(weights, v), n)
        out_ref[:, half] = blend.reshape(-1, 8, 128)


def call_rows(qkv, mesh_rows, mesh_cols, scale):
    devices, parts = qkv.shape[0], (qkv.shape[1] - 16) // 24
    span = mesh_rows * 32
    return pl.pallas_call(
        functools.partial(rows_kernel, mesh_rows, mesh_cols, scale),
        out_shape=jax.ShapeDtypeStruct((devices, parts, 8, 128), f32),
        scratch_shapes=[pltpu.VMEM((span, span), f32)],
        compiler_params=params(24),
        name="rows",
    )(qkv)


def load_heads(ref, kind=None):
    def load(head):
        groups = ref.shape[0] // 8
        place = slice(head * groups, (head + 1) * groups)
        part = ref[place] if kind is None else ref[place, kind]
        return part.reshape(-1, 8, 128)

    return load


def side_copies(source_ref, target_ref):
    both = halves(jnp.concatenate([source_ref[...], target_ref[...]], 0))
    shape = (640, 64)
    place = iota(shape, 0) - 128
    feature = jnp.where(place < 0, place & 31, 32 + ((place >> 7) << 3) + (place & 7))
    copies = jnp.where(iota(shape, 1) == feature, 1.0, 0.0).astype(bf16)
    return tuple(one_pass(copies, part).astype(bf16) for part in both)


def rows_out_kernel(
    blend_ref, mid_ref, share_ref, o_ref, source_ref, target_ref, out_ref, left_ref, right_ref
):
    blend = unpack_heads(load_heads(blend_ref), 8)
    out = mid_ref[...] + dot3(blend, halves(o_ref[...]))
    out_ref[...] = out
    normed, _ = norm_parts(out)
    wide = dot3(normed, side_copies(source_ref, target_ref), NT)
    left = (wide[:, :128] * share_ref[...]).reshape(-1, 4, 8, 128)
    lane = iota((1, 1, 128), 2)
    packed = left[:, 0]
    for chain in range(1, 4):
        packed = jnp.where((lane >> 5) == chain, left[:, chain], packed)
    for n in range(packed.shape[0]):
        left_ref[:, n, :] = packed[n]
    for g in range(4):
        right = wide[:, (g + 1) * 128 : (g + 2) * 128].reshape(-1, 16, 8, 128)
        packed = right[:, 0]
        for chain in range(1, 16):
            packed = jnp.where((lane >> 3) == chain, right[:, chain], packed)
        right_ref[g] = packed


def call_rows_out(blend, mid, share, weight, source, target):
    chains = mid.shape[0] // 8
    return pl.pallas_call(
        rows_out_kernel,
        out_shape=(
            jax.ShapeDtypeStruct(mid.shape, f32),
            jax.ShapeDtypeStruct((8, chains // 4, 128), f32),
            jax.ShapeDtypeStruct((4, chains // 16, 8, 128), f32),
        ),
        compiler_params=params(),
        name="rows_out",
    )(blend, mid, share, weight, source, target)


def rows_out_back_kernel(*refs):
    *dleft_refs, dright_ref, grad_ref, out_ref, blend_ref, share_ref = refs[:-10]
    o_ref, source_ref, target_ref = refs[-10:-7]
    core_ref, dout_ref, dblend_ref, thin_ref, mine_ref, other_ref, sum_ref = refs[-7:]
    lane = iota((1, 1, 128), 2)
    chains = grad_ref.shape[0] // 8
    dleft = functools.reduce(jnp.add, [ref[...] for ref in dleft_refs])
    shape = (chains * 8, 128)
    slot = iota(shape, 0) & 7
    copy = (chains * 8, chains)
    copy = jnp.where((iota(copy, 0) >> 3) == iota(copy, 1), 1.0, 0.0).astype(bf16)
    left = 0.0
    for n in range(2):
        high, low = halves(dleft[n])
        spot = (slot >> 2 == n) & (slot & 3 == iota(shape, 1) >> 5)
        left = left + jnp.where(spot, one_pass(copy, high) + one_pass(copy, low), 0.0)
    wide = [left * share_ref[...]]
    dright = dright_ref[...]
    for g in range(4):
        part = [jnp.where((lane >> 3) == n, dright[g], 0.0)[:, None] for n in range(16)]
        wide.append(jnp.concatenate(part, 1).reshape(-1, 128))
    wide = halves(jnp.concatenate(wide, 1))
    normed, inverse = norm_parts(out_ref[...])
    dsides = halves(dot3(halves(jnp.transpose(normed)), wide))
    shape = (640, 128)
    place, spot = iota(shape, 0) - 128, iota(shape, 1)
    target = jnp.where(place < 0, place & 31, 32 + ((place >> 7) << 3) + (place & 7))
    fold = jnp.where(target == spot, 1.0, 0.0).astype(bf16)
    thin_ref[...] = one_pass(dsides[0], fold) + one_pass(dsides[1], fold)
    dout = grad_ref[...] + norm_back(normed, inverse, dot3(wide, side_copies(source_ref, target_ref)))
    dout_ref[...] = dout
    dout = halves(dout)
    groups = dblend_ref.shape[0] // 8

    def store(head, value):
        dblend_ref[head * groups : (head + 1) * groups] = value.reshape(groups, -1, 8, 128)

    pack_heads(dot3(dout, halves(o_ref[...]), NT), store)
    blend = unpack_heads(load_heads(blend_ref), 8)
    write_halves(sum_ref, 0, dot3(halves(jnp.transpose(blend)), dout))
    give_halves(core_ref, sum_ref, mine_ref, other_ref)


def call_rows_out_back(dlefts, dright, grad, out, blend, share, weight, source, target, core):
    shapes, scratch = halves_shapes([weight])
    return pl.pallas_call(
        rows_out_back_kernel,
        out_shape=(
            jax.ShapeDtypeStruct(grad.shape, f32),
            jax.ShapeDtypeStruct(blend.shape, f32),
            jax.ShapeDtypeStruct((256, 128), f32),
        )
        + shapes,
        in_specs=specs(len(dlefts) + 8),
        scratch_shapes=[scratch],
        compiler_params=params(),
        name="rows_out_back",
    )(*dlefts, dright, grad, out, blend, share, weight, source, target, core)


def rows_back_kernel(
    mesh_rows, mesh_cols, scale, qkv_ref, dblend_ref, out_ref, whole_ref
):
    join_tiles(qkv_ref[:, -16:], mesh_rows, mesh_cols, whole_ref)
    bias = jnp.concatenate([whole_ref[...]] * 4, 0)
    span = whole_ref.shape[0]
    dbias = 0.0
    for half, places, (q, k, v) in packed_parts(qkv_ref):
        k, query = halves(k), halves(stack_heads(q * scale))
        dblend = halves(stack_heads(dblend_ref[:, half].reshape(-1, 128)))
        weights = soft(dot3(query, k, NT) + bias)
        dv = dot3(halves(jnp.transpose(weights)), dblend)
        dscores = soft_back(weights, dot3(dblend, halves(v), NT))
        for n in range(4):
            dbias = dbias + dscores[n * span : (n + 1) * span]
        dk = dot3(halves(jnp.transpose(dscores)), query)
        dq = join_heads(dot3(dscores, k))
        for place, value in zip(places, (dq * scale, dk, dv)):
            out_ref[:, place : place + 8] = value.reshape(-1, 8, 128)

    def store(d, tile):
        out_ref[d, -16:] = tile

    cut_tiles(dbias, mesh_rows, mesh_cols, store)


def call_rows_back(qkv, dblend, mesh_rows, mesh_cols, scale):
    span = mesh_rows * 32
    return pl.pallas_call(
        functools.partial(rows_back_kernel, mesh_rows, mesh_cols, scale),
        out_shape=jax.ShapeDtypeStruct(qkv.shape, f32),
        scratch_shapes=[pltpu.VMEM((span, span), f32)],
        compiler_params=params(24),
        name="rows_back",
    )(qkv, dblend)


def write_halves(ref, n, value):
    height = value.shape[0]
    for half in range(2):
        ref[half, n * height : (n + 1) * height] = value[:, half * 128 : (half + 1) * 128]


def projections_back(normed, inverse, grads, weight_refs, sum_ref):
    turned = halves(jnp.transpose(normed))
    dnormed = 0.0
    for n, (grad, w) in enumerate(zip(grads, weight_refs)):
        grad = halves(grad)
        write_halves(sum_ref, n, dot3(turned, grad))
        dnormed = dnormed + dot3(grad, halves(w[...]), NT)
    return norm_back(normed, inverse, dnormed)


def rows_in_back_kernel(
    dqkv_ref, mid_ref, grad_ref, q_ref, k_ref, v_ref, core_ref, dmid_ref, mine_ref, other_ref, sum_ref
):
    groups, size = dqkv_ref.shape[0] // 8, (dqkv_ref.shape[1] - 16) // 3

    def load(kind):
        place = slice(kind * size, (kind + 1) * size)
        return lambda head: dqkv_ref[head * groups : (head + 1) * groups, place].reshape(-1, 8, 128)

    grads = [unpack_heads(load(kind), 8) for kind in range(3)]
    normed, inverse = norm_parts(mid_ref[...])
    dmid_ref[...] = grad_ref[...] + projections_back(
        normed, inverse, grads, (q_ref, k_ref, v_ref), sum_ref
    )
    give_halves(core_ref, sum_ref, mine_ref, other_ref)


def halves_shapes(weights):
    rows = sum(w.size for w in weights) // 256
    return (jax.ShapeDtypeStruct((rows, 128), f32),) * 2, pltpu.VMEM((2, rows, 128), f32)


def specs(count):
    vmem = pl.BlockSpec(memory_space=pltpu.VMEM)
    return [vmem] * count + [pl.BlockSpec(memory_space=pltpu.SMEM)]


def call_rows_in_back(dqkv, mid, grad, weights, core):
    shapes, scratch = halves_shapes(weights)
    return pl.pallas_call(
        rows_in_back_kernel,
        in_specs=specs(6),
        out_shape=(jax.ShapeDtypeStruct(mid.shape, f32),) + shapes,
        scratch_shapes=[scratch],
        compiler_params=params(24),
        name="rows_in_back",
    )(dqkv, mid, grad, *weights, core)


def columns_back_kernel(
    scale,
    x_ref,
    present_ref,
    grad_ref,
    q_ref,
    k_ref,
    v_ref,
    o_ref,
    core_ref,
    dx_ref,
    mine_ref,
    other_ref,
    sum_ref,
):
    normed, inverse = norm_parts(x_ref[...])
    normed_halves = halves(normed)
    q, k, v = (dot3(normed_halves, halves(w[...])) for w in (q_ref, k_ref, v_ref))
    q = q * scale
    weights, blend = column_attention(q, k, v, stripe_seen(present_ref))
    grad = grad_ref[...]
    grad_halves = halves(grad)
    write_halves(sum_ref, 3, dot3(halves(jnp.transpose(blend)), grad_halves))
    dblend = dot3(grad_halves, halves(o_ref[...]), NT)
    tiles = [[], [], []]
    for tile in range(q.shape[1] // 128):
        lanes = slice(tile * 128, (tile + 1) * 128)
        keys, values = halves(k[:, lanes]), halves(v[:, lanes])
        dq, dk, dv = 0.0, 0.0, 0.0
        for n in range(4):
            query = halves(head_lanes(q[:, lanes], n))
            dhead = halves(head_lanes(dblend[:, lanes], n))
            share = weights[tile * 4 + n]
            dv = dv + dot3(halves(jnp.transpose(share)), dhead)
            dscores = soft_back(share, dot3(dhead, values, NT))
            dk = dk + dot3(halves(jnp.transpose(dscores)), query)
            dq = dq + head_lanes(dot3(dscores, keys), n)
        for kind, value in enumerate((dq * scale, dk, dv)):
            tiles[kind].append(value)
    grads = [jnp.concatenate(t, 1) for t in tiles]
    dx_ref[...] = grad + projections_back(
        normed, inverse, grads, (q_ref, k_ref, v_ref), sum_ref
    )
    give_halves(core_ref, sum_ref, mine_ref, other_ref)


def call_columns_back(x, present, grad, weights, core, scale):
    shapes, scratch = halves_shapes(weights)
    return pl.pallas_call(
        functools.partial(columns_back_kernel, scale),
        in_specs=specs(7),
        out_shape=(jax.ShapeDtypeStruct(x.shape, f32),) + shapes,
        scratch_shapes=[scratch],
        compiler_params=params(24),
        name="columns_back",
    )(x, present, grad, *weights, core)


def bias_kernel(cols, pair_ref, weight_ref, out_ref):
    weight = halves(weight_ref[...])

    def step(t, carry):
        rows = halves(read_rows(pair_ref, four_rows(t, cols)))
        heads = dot3(weight, rows, NT)
        for v in range(2):
            tile = heads[:, v * 128 : (v + 1) * 128][:, None, :]
            for g in range(out_ref.shape[1]):
                out_ref[:, g, pl.ds(2 * t + v, 1), :] = tile
        return carry

    lax.fori_loop(0, 8, step, 0)


def call_bias(pair, weight, copies, cols):
    return pl.pallas_call(
        functools.partial(bias_kernel, cols),
        out_shape=jax.ShapeDtypeStruct((weight.shape[0], copies, 16, 128), f32),
        compiler_params=params(24),
        name="bias",
    )(pair, weight)


def bias_rows(dbias):
    heads, groups, rows = dbias.shape[:3]
    return pl.BlockSpec((heads, groups, 16, 128), lambda t: (0, 0, rows // 16 - 1, 0))


def head_rows(ref, t):
    heads = [ref[:, pl.ds(2 * t + v, 1), :].reshape(-1, 128) for v in range(2)]
    return jnp.concatenate(heads, 1)


def bias_sums_kernel(
    cols, dbias_ref, pair_ref, thin_ref, core_ref, mine_ref, other_ref, whole_ref, sum_ref, dweight_ref
):
    sum_ref[...] = jnp.sum(dbias_ref[...], axis=1)
    dweight_ref[...] = jnp.zeros_like(dweight_ref)

    def step(t, carry):
        dweight_ref[...] += dot3(head_rows(sum_ref, t), read_rows(pair_ref, four_rows(t, cols)))
        return carry

    lax.fori_loop(0, 8, step, 0)
    whole_ref[0], whole_ref[1] = thin_ref[:128], thin_ref[128:]
    whole_ref[0, :, 64 : 64 + dweight_ref.shape[0]] = jnp.transpose(dweight_ref[...])
    give_halves(core_ref, whole_ref, mine_ref, other_ref)


def call_bias_sums(dbias, pair, thin, core, cols):
    heads = dbias.shape[0]
    return pl.pallas_call(
        functools.partial(bias_sums_kernel, cols),
        grid=(1,),
        in_specs=[bias_rows(dbias), full(pair), full(thin), pl.BlockSpec(memory_space=pltpu.SMEM)],
        out_specs=(pl.BlockSpec((128, 128), lambda t: (0, 0)),) * 2,
        out_shape=(jax.ShapeDtypeStruct((128, 128), f32),) * 2,
        scratch_shapes=[
            pltpu.VMEM((2, 128, 128), f32),
            pltpu.VMEM((heads, 16, 128), f32),
            pltpu.VMEM((heads, 128), f32),
        ],
        compiler_params=params(24),
        name="bias_sums",
    )(dbias, pair, thin, core)


def bias_back_kernel(cols, dbias_ref, dmid_ref, weight_ref, out_ref, sum_ref):
    weight = halves(weight_ref[...])
    sum_ref[...] = jnp.sum(dbias_ref[...], axis=1)

    def step(t, carry):
        places = four_rows(t, cols)
        dpair = dot3(jnp.transpose(head_rows(sum_ref, t)), weight)
        write_rows(out_ref, places, read_rows(dmid_ref, places) + dpair)
        return carry

    lax.fori_loop(0, 8, step, 0)


def call_bias_back(dbias, dmid, weight, cols):
    return pl.pallas_call(
        functools.partial(bias_back_kernel, cols),
        grid=(1,),
        in_specs=[bias_rows(dbias), full(dmid), full(weight)],
        out_specs=full(dmid),
        out_shape=jax.ShapeDtypeStruct(dmid.shape, f32),
        scratch_shapes=[pltpu.VMEM((dbias.shape[0], 16, 128), f32)],
        compiler_params=params(24),
        name="bias_back",
    )(dbias, dmid, weight)


def spread_sums_kernel(
    half, cols, mine_ref, early_ref, other_ref, other_early_ref, place_ref, *refs
):
    *outs, whole_ref = refs
    size = early_ref.shape[0] // (half * cols)
    for part, ref in enumerate((early_ref, other_early_ref)):
        for n in range(half * cols):
            row = lax.rem(place_ref[1] + half - n // cols, half)
            chip = row * cols + lax.rem(place_ref[2] + cols - n % cols, cols)
            target = pl.ds(pl.multiple_of(chip * size, 8), size)
            whole_ref[part, target] = ref[n * size : (n + 1) * size]

    def place(first, second, order):
        for half, ref in enumerate((first, second)):
            lanes = slice(half * 128, (half + 1) * 128)
            for n, target in enumerate((0, 1, 2, 3, 4, 5, 6)):
                outs[target][:, lanes] = ref[n * 256 : (n + 1) * 256]
            outs[8][:, lanes] = whole_ref[order[half], 512:768]
            for n, target in enumerate(((13, 15, 12), (14, 16, 17))[half]):
                outs[target][...] = ref[1920 + n * 128 : 2048 + n * 128]
            outs[11][half * 512 : (half + 1) * 512] = whole_ref[order[half], :512]
        thin = jnp.transpose(jnp.concatenate([first[1792:1920], second[1792:1920]], 0))
        outs[7][...] = thin[64 : 64 + outs[7].shape[0], :128]
        outs[9][...] = thin[:32]
        outs[10][...] = thin[32:64]

    @pl.when(place_ref[0] == 0)
    def _():
        place(mine_ref, other_ref, (0, 1))

    @pl.when(place_ref[0] != 0)
    def _():
        place(other_ref, mine_ref, (1, 0))


def call_spread_sums(mine, early, other, other_early, place, half, cols, shapes):
    thin = (7, 9, 10)
    shapes = [shape[::-1] if n in thin else shape for n, shape in enumerate(shapes)]
    sums = pl.pallas_call(
        functools.partial(spread_sums_kernel, half, cols),
        in_specs=specs(4),
        out_shape=tuple(jax.ShapeDtypeStruct(shape, f32) for shape in shapes),
        scratch_shapes=[pltpu.VMEM((2,) + early.shape, f32)],
        compiler_params=params(24),
        name="spread_sums",
    )(mine, early, other, other_early, place)
    return [jnp.transpose(x) if n in thin else x for n, x in enumerate(sums)]


precise = lax.Precision.HIGH
everyone = ("half", "core", "col")
row = ("half", "core")
chips = ("half", "col")


def affine_map(tensor, weight):
    return jnp.einsum("...a,ab->...b", tensor, weight, precision=precise)


def exchange(chunks, axis):
    shape = chunks.shape
    flat = chunks.reshape(shape[0], -1, 128)
    return lax.all_to_all(flat, axis, 0, 0, tiled=True).reshape(shape)


def collect(block, axis, count):
    return exchange(jnp.broadcast_to(block[None], (count,) + block.shape), axis)


def tall(weight):
    return jnp.concatenate([weight[:, :128], weight[:, 128:]], 0)


def together(*arrays):
    return lax.optimization_barrier(arrays)


class Layout:
    def __init__(self, mesh_rows, mesh_cols, pair, chains, heads, head_width):
        self.mesh_rows, self.mesh_cols = mesh_rows, mesh_cols
        self.devices = mesh_rows * mesh_cols
        self.rows_here, self.cols_here, self.pair_width = pair
        self.span = self.rows_here * mesh_rows
        self.slim = self.span // self.devices
        self.chains, self.heads, self.head_width = chains, heads, head_width
        self.chain_groups = self.devices // heads
        self.group_chains = chains // self.chain_groups
        self.channels_here = self.pair_width // self.devices
        self.scale = head_width ** (-0.5)
        self.turn = [
            (g, (g % mesh_rows) * mesh_cols + g // mesh_rows) for g in range(self.devices)
        ]
        self.turn_back = [(b, a) for a, b in self.turn]

        self.swap = [(0, 1), (1, 0)]
        self.core = lax.axis_index("core").reshape(1)

    def to_slim(self, x):
        return lax.all_to_all(x, "col", 1, 0, tiled=True)

    def both_views(self, grad, out):
        count, slim, width = self.mesh_cols, self.slim, grad.shape[2]
        grad = jnp.transpose(grad.reshape(-1, count, slim, width), (1, 0, 2, 3))
        both = jnp.stack([grad, out.reshape(count, -1, slim, width)], 1)
        return both.reshape(count, -1, width)

    def split_views(self, both):
        count, slim, width = self.mesh_cols, self.slim, both.shape[2]
        both = both.reshape(count, 2, -1, slim, width)
        out = jnp.transpose(both[:, 1], (1, 0, 2, 3)).reshape(-1, count * slim, width)
        return both[:, 0].reshape(-1, slim, width), out

    def from_slim_permuted(self, x):
        count, slim = self.mesh_cols, x.shape[1]
        here = lax.axis_index("col")
        blocks = x.reshape(count, -1, slim, x.shape[2])
        out = jnp.zeros((blocks.shape[1], count * slim, x.shape[2]), f32)
        for n in range(count):
            block = lax.dynamic_index_in_dim(blocks, lax.rem(here + n, count), 0, False)
            if n:
                block = lax.ppermute(block, "col", [(s, (s + n) % count) for s in range(count)])
            source = lax.rem(here + count - n, count)
            out = lax.dynamic_update_slice_in_dim(out, block, source * slim, 1)
        return out

    def from_others(self, arrays, axis="col"):
        count = len(arrays)
        return [
            lax.ppermute(x, axis, [(s, (s + n) % count) for s in range(count)]) if n else x
            for n, x in enumerate(arrays)
        ]

    def share_sum(self, x, axis, count):
        here = lax.axis_index(axis)
        x = x.reshape(count, -1, 128)
        parts = [
            lax.dynamic_index_in_dim(x, lax.rem(here + n, count), 0, False) for n in range(count)
        ]
        return functools.reduce(jnp.add, self.from_others(parts, axis))

    def all_parts(self, x, axis, count):
        return jnp.concatenate(self.from_others([x] * count, axis), 0)

    def core_sum(self, sums):
        sums = [
            part[0] + lax.ppermute(part[1], "core", self.swap) if len(part) == 2 else part[0]
            for part in sums
        ]
        return jnp.concatenate(sums, 0)

    def half_sum(self, early):
        early = self.core_sum(early)
        pad = -early.shape[0] % (4 * self.devices)
        early = jnp.pad(early, ((0, pad), (0, 0))) if pad else early
        return self.share_sum(early, "half", self.mesh_rows // 2)

    def sum_all(self, late, early, *beside):
        half, cols = self.mesh_rows // 2, self.mesh_cols
        late, early = together(self.core_sum(late), early)
        late = exchange(late.reshape(half, -1, 128), "half")
        late, early = together(late, self.share_sum(early, "col", cols))
        late = exchange(late.sum(0).reshape(cols, -1, 128), "col")
        late, early, *beside = together(late, self.all_parts(early, "col", cols), *beside)
        late = collect(late.sum(0), "col", cols).reshape(-1, 128)
        late, early = together(late, self.all_parts(early, "half", half))
        late = collect(late, "half", half).reshape(-1, 128)
        late, other_early = together(late, lax.ppermute(early, "core", self.swap))
        return (late, early, lax.ppermute(late, "core", self.swap), other_early), beside


def msa_plain(size, alignment_features, residue_couplings, present, weights):
    chains, slim, heads, head_width = size.chains, size.slim, size.heads, size.head_width
    devices, groups, group_chains = size.devices, size.chain_groups, size.group_chains
    rows_here, cols_here, span = size.rows_here, size.cols_here, size.span
    mesh_rows, mesh_cols = size.mesh_rows, size.mesh_cols
    bias = jnp.transpose(affine_map(residue_couplings, weights[7]), (2, 0, 1))
    bias = jnp.broadcast_to(bias[:, None], (heads, groups, rows_here, cols_here))
    bias = exchange(bias.reshape(devices, rows_here, cols_here), everyone)
    bias = bias.reshape(mesh_rows, mesh_cols, rows_here, cols_here)
    bias = jnp.transpose(bias, (0, 2, 1, 3)).reshape(span, span)

    stripe = size.to_slim(alignment_features)
    normed, _ = norm_parts(stripe)
    col_q, col_k, col_v = (
        affine_map(normed, w).reshape(chains, slim, heads, head_width) for w in weights[:3]
    )
    scores = jnp.einsum("sihd,tihd->ihst", col_q, col_k, precision=precise) * size.scale
    scores = jnp.where(present[None, None, None, :] > 0, scores, -1000000000.0)
    blend = jnp.einsum(
        "ihst,tihd->sihd", jax.nn.softmax(scores, axis=-1), col_v, precision=precise
    )
    msa_col = stripe + affine_map(blend.reshape(chains, slim, heads * head_width), weights[3])

    normed, _ = norm_parts(msa_col)
    qkv = jnp.stack([affine_map(normed, w) for w in weights[4:7]])
    qkv = qkv.reshape(3, groups, group_chains, slim, heads, head_width)
    qkv = jnp.transpose(qkv, (4, 1, 0, 2, 3, 5))
    qkv = exchange(qkv.reshape(devices, 3, group_chains, slim, head_width), everyone)
    qkv = jnp.transpose(qkv, (1, 2, 0, 3, 4)).reshape(3, group_chains, span, head_width)
    scores = jnp.einsum("sid,sjd->sij", qkv[0], qkv[1], precision=precise) * size.scale
    shares = jax.nn.softmax(scores + bias[None], axis=-1)
    blend = jnp.einsum("sij,sjd->sid", shares, qkv[2], precision=precise)
    blend = blend.reshape(group_chains, devices, slim, head_width)
    blend = exchange(jnp.transpose(blend, (1, 0, 2, 3)), everyone)
    blend = blend.reshape(heads, chains, slim, head_width)
    blend = jnp.transpose(blend, (1, 2, 0, 3)).reshape(chains, slim, heads * head_width)
    msa_out = msa_col + affine_map(blend, weights[8])

    normed, _ = norm_parts(msa_out)
    left = affine_map(normed, weights[9]) * (present / jnp.sum(present))[:, None, None]
    left = jnp.transpose(left.reshape(chains // 4, 4, slim, 32), (2, 0, 1, 3))
    left = collect(left.reshape(slim, chains // 4, 128), "col", mesh_cols).reshape(-1, 128)
    right = affine_map(normed, weights[10]).reshape(chains // 16, 16, slim, 4, 8)
    right = jnp.transpose(right, (3, 0, 2, 1, 4)).reshape(-1, 128)
    right = collect(lax.ppermute(right, everyone, size.turn), row, mesh_rows)
    right = right.reshape(mesh_rows, 4, chains // 16, slim, 128)
    right = jnp.transpose(right, (1, 0, 3, 2, 4)).reshape(4, cols_here // 8, 8, chains // 16, 128)
    return msa_out, [left], jnp.transpose(right, (1, 0, 3, 2, 4))


def msa_forward(size, alignment_features, residue_couplings, present, weights, prepare, raw):
    chains, slim, devices = size.chains, size.slim, size.devices
    mesh_rows, mesh_cols = size.mesh_rows, size.mesh_cols
    pair_flat = residue_couplings.reshape(-1, size.pair_width)
    tokens = chains * slim
    seen = jnp.repeat(present, slim)[None]
    share = jnp.repeat(present / jnp.sum(present), slim)[:, None]
    source, target = jnp.transpose(weights[9]), jnp.transpose(weights[10])
    offset = jnp.transpose(weights[7])
    stripe = size.to_slim(alignment_features).reshape(tokens, -1)
    bias = call_bias(pair_flat, offset, size.chain_groups, size.cols_here)
    bias = bias.reshape(devices, 16, 128)
    msa_col, qkv = call_columns(stripe, seen, bias, weights[:7], size.group_chains, size.scale)
    qkv = exchange(qkv, everyone)
    blend = call_rows(qkv, mesh_rows, mesh_cols, size.scale)
    raw, blend = together(raw, blend)
    blend, ready = together(exchange(blend, everyone), prepare(raw))
    msa_out, left, right = call_rows_out(blend, msa_col, share, weights[8], source, target)
    left = size.from_others([left.reshape(-1, 128)] * mesh_cols)
    right, *left = together(lax.ppermute(right, everyone, size.turn), *left)
    right = collect(right, row, mesh_rows)

    def back(grad, d_lefts, d_right, d_mid, pair_mid, side_sums, outer_sums):
        d_lefts = size.from_others(d_lefts)
        d_right = exchange(d_right, row).sum(0)
        d_right = lax.ppermute(d_right, everyone, size.turn_back)
        d_out, d_blend, thin, *out_sums = call_rows_out_back(
            d_lefts,
            d_right,
            grad.reshape(tokens, -1),
            msa_out,
            blend,
            share,
            weights[8],
            source,
            target,
            size.core,
        )
        d_mid, d_blend = together(d_mid, d_blend)
        outer_sums = outer_sums(d_mid)
        d_blend, *outer_sums = together(exchange(d_blend, everyone), *outer_sums)
        d_qkv = call_rows_back(qkv, d_blend, mesh_rows, mesh_cols, size.scale)
        pair_mid, d_qkv = together(pair_mid, d_qkv)
        side_sums = side_sums(pair_mid)
        early = size.half_sum((outer_sums, out_sums))
        side_sum = size.core_sum([side_sums])
        d_qkv, early, side_sum = together(exchange(d_qkv, everyone), early, side_sum)
        d_col, *in_sums = call_rows_in_back(d_qkv, msa_col, d_out, weights[4:7], size.core)
        d_stripe, *col_sums = call_columns_back(
            stripe, seen, d_col, weights[:4], size.core, size.scale
        )
        d_bias = d_qkv.reshape(size.heads, size.chain_groups, -1, 128)
        thin_sums = call_bias_sums(d_bias, pair_flat, thin, size.core, size.cols_here)
        d_pair = call_bias_back(d_bias, d_mid, offset, size.cols_here)
        d_features = size.from_slim_permuted(d_stripe.reshape(chains, slim, -1))
        late = (col_sums, in_sums, thin_sums, (side_sum,))
        return d_features, d_pair, late, early

    return (msa_out.reshape(chains, slim, -1), left, right), ready, back


def msa_plain_forward(
    size, alignment_features, residue_couplings, present, weights, prepare, raw
):
    chains, rows_here = size.chains, size.rows_here
    outputs, pull = jax.vjp(
        lambda x, y, w: msa_plain(size, x, y, present, w),
        alignment_features,
        residue_couplings,
        weights,
    )

    def back(grad, d_lefts, d_right, d_mid, pair_mid, side_sums, outer_sums):
        d_left = d_lefts[0].reshape(rows_here // 4, chains // 4, 4, 4, 32)
        d_left = jnp.transpose(d_left, (0, 3, 1, 2, 4)).reshape(-1, 128)
        d_features, d_pair, d_weights = pull((grad, [d_left], d_right))
        d_pair = d_pair.reshape(-1, size.pair_width) + d_mid
        thin = [d_weights[9], d_weights[10], jnp.pad(d_weights[7], ((0, 128), (0, 0)))]
        thin = jnp.pad(jnp.concatenate(thin, 1), ((0, 0), (0, 64 - size.heads)))
        core = size.core[0]
        pick = lambda x, n: lax.dynamic_index_in_dim(x, n, 0, False)
        own = lambda x: (pick(x, core), pick(x, 1 - core))
        cut = lambda ws: own(
            jnp.stack([jnp.concatenate([w[:, n : n + 128] for w in ws], 0) for n in (0, 128)])
        )
        late = (cut(d_weights[:4]), cut(d_weights[4:7]), own(thin.reshape(2, -1, 128)))
        late = (*late, side_sums(pair_mid))
        early = (outer_sums(d_mid), cut(d_weights[8:9]))
        return d_features, d_pair, late, size.half_sum(early)

    return outputs, prepare(raw), back


def per_device(mesh_rows, mesh_cols, *arguments):
    (
        alignment_features,
        residue_couplings,
        chain_indicator,
        alignment_result_adjoint,
        coupling_result_adjoint,
        *weights,
    ) = arguments
    present = chain_indicator.astype(jnp.float32)
    heads = weights[7].shape[1]
    size = Layout(
        mesh_rows,
        mesh_cols,
        residue_couplings.shape,
        present.shape[0],
        heads,
        weights[4].shape[1] // heads,
    )
    devices, channels_here = size.devices, size.channels_here
    cols_here, pair_width = size.cols_here, size.pair_width
    (
        tensor_result_matrix,
        source_side_matrix,
        source_side_switch,
        target_side_matrix,
        target_side_switch,
        trilateral_result_switch,
        trilateral_result_matrix,
    ) = weights[11:]

    sides = (source_side_switch, target_side_switch, source_side_matrix, target_side_matrix)
    shift = channels_here.bit_length() - 1
    def prepare(raw):
        return call_prepare(raw[0], raw[1:], shift)

    forward = msa_forward if size.slim == 8 else msa_plain_forward
    (msa_slim, left_rows, right_rows), (outer_halves, sides_halves), msa_back = forward(
        size,
        alignment_features,
        residue_couplings,
        present,
        tuple(weights[:11]),
        prepare,
        (tensor_result_matrix, *sides, trilateral_result_switch),
    )
    pair_flat = residue_couplings.reshape(-1, pair_width)
    grad_flat = coupling_result_adjoint.reshape(-1, pair_width)
    count = len(left_rows)
    first = (lax.axis_index("col") if count > 1 else jnp.int32(0)).reshape(1)
    blocks = call_blocks(first, left_rows)
    pair_mid, edges, prods = call_edges(
        blocks, right_rows, outer_halves, sides_halves, pair_flat, cols_here
    )
    edges = exchange(edges.reshape(devices, 2, channels_here, 16, 128), everyone)
    triangle = exchange(call_triangle(edges, mesh_rows, mesh_cols), everyone)
    pair_out, d_triangle, d_logit, g_tri_out = call_finish(
        triangle.reshape(pair_width, 16, 128),
        pair_mid,
        grad_flat,
        trilateral_result_switch,
        trilateral_result_matrix,
        cols_here,
    )
    views = (alignment_result_adjoint, msa_slim)
    *views, d_triangle = together(*views, d_triangle)
    views = size.both_views(*views)
    d_triangle = exchange(d_triangle.reshape(devices, channels_here, 16, 128), everyone)
    d_edges = call_triangle_back(edges, d_triangle, mesh_rows, mesh_cols)
    d_edges, mid_again = together(d_edges, pair_mid)
    factors = call_factors(mid_again, sides_halves, cols_here)
    d_edges, factors = together(exchange(d_edges, everyone), factors)
    d_edges, views = together(d_edges, views)
    views = lax.all_to_all(views, "col", 0, 0, tiled=True)
    d_mid, d_logits, d_right, *d_lefts = call_edges_back(
        d_edges.reshape(2 * pair_width, 16, 128),
        pair_mid,
        grad_flat,
        d_logit,
        sides_halves,
        right_rows,
        outer_halves,
        factors,
        blocks,
        first,
        count,
        cols_here,
    )
    d_right, views = together(d_right, views)
    msa_grad, msa_out = size.split_views(views)

    def side_sums(pair_mid):
        return call_side_sums(pair_mid, d_logits, g_tri_out, size.core, cols_here, shift)

    def outer_sums(d_mid):
        return call_outer_sums(d_mid, prods, size.core, cols_here)

    alignment_adjoint, coupling_adjoint, late, early = msa_back(
        msa_grad, d_lefts, d_right, d_mid, pair_mid, side_sums, outer_sums
    )
    sums, (alignment_adjoint, coupling_adjoint) = size.sum_all(
        late, early, alignment_adjoint, coupling_adjoint
    )
    place = jnp.stack([lax.axis_index(axis) for axis in ("core", "half", "col")])
    summed = call_spread_sums(*sums, place, mesh_rows // 2, mesh_cols, [w.shape for w in weights])
    return (
        msa_out,
        pair_out.reshape(residue_couplings.shape),
        alignment_adjoint,
        coupling_adjoint.reshape(residue_couplings.shape),
        *summed,
    )


def solution(mesh):
    mesh_rows, mesh_cols = mesh.shape["row"], mesh.shape["col"]

    def local(*arguments):
        return per_device(mesh_rows, mesh_cols, *arguments)

    split = jax.sharding.Mesh(
        mesh.devices.reshape(mesh_rows // 2, 2, mesh_cols), ("half", "core", "col")
    )
    whole = P()
    msa = P("col", row, None)
    pair = P(row, "col", None)
    return jax.shard_map(
        local,
        mesh=split,
        in_specs=(msa, pair, whole, msa, pair) + (whole,) * 18,
        out_specs=(msa, pair, msa, pair) + (whole,) * 18,
        check_vma=False,
    )
```

```python
import functools

import jax
import jax.numpy as jnp
from jax import lax
from jax.experimental import pallas as pl
from jax.experimental.pallas import tpu as pltpu
from jax.sharding import PartitionSpec as P

bf16, f32 = jnp.bfloat16, jnp.float32
NN = ((1,), (0,))
NT = ((1,), (1,))
TN = ((0,), (0,))


def one_pass(a, b, dims=NN):
    return lax.dot_general(a, b, (dims, ((), ())), preferred_element_type=f32)


def halves(x):
    high = x.astype(bf16)
    return high, (x - high.astype(f32)).astype(bf16)


def dot3(a, b, dims=NN):
    a_high, a_low = a if isinstance(a, tuple) else halves(a)
    b_high, b_low = b if isinstance(b, tuple) else halves(b)
    return one_pass(a_high, b_high, dims) + (
        one_pass(a_high, b_low, dims) + one_pass(a_low, b_high, dims)
    )


def rounded(pair, rows):
    return pair[0][rows], pair[1][rows]


def iota(shape, dim):
    return lax.broadcasted_iota(jnp.int32, shape, dim)


def norm_parts(x):
    centered = x - jnp.mean(x, axis=-1, keepdims=True)
    inverse = lax.rsqrt(jnp.mean(centered * centered, axis=-1, keepdims=True) + 1e-05)
    return centered * inverse, inverse


def norm_back(normed, inverse, grad):
    return inverse * (
        grad
        - jnp.mean(grad, axis=-1, keepdims=True)
        - normed * jnp.mean(grad * normed, axis=-1, keepdims=True)
    )


def stacked3(a, b, dims=NN):
    a_high, a_low = a if isinstance(a, tuple) else halves(a)
    b_high, b_low = b if isinstance(b, tuple) else halves(b)
    return one_pass(
        jnp.concatenate([a_high, a_low, a_high], dims[0][0]),
        jnp.concatenate([b_high, b_high, b_low], dims[1][0]),
        dims,
    )


def tall3(a, b, dims=NN):
    a_high, a_low = a if isinstance(a, tuple) else halves(a)
    b_high, b_low = b if isinstance(b, tuple) else halves(b)
    both = one_pass(jnp.concatenate([a_high, a_low], 0), b_high, dims)
    rows = a_high.shape[0]
    return both[:rows] + both[rows:] + one_pass(a_high, b_low, dims)


def row_of(t, u):
    return 2 * t + u // 2 + 16 * (u % 2)


def same_slot(chains):
    shape = (chains * 8, 256)
    return (iota(shape, 0) & 7) == (iota(shape, 1) & 7)


def blocks_kernel(chains, first_ref, *refs):
    *part_refs, out_ref, left_ref = refs
    groups, count = chains // 4, len(part_refs)
    size = part_refs[0].shape[0]
    t = pl.program_id(0)

    @pl.when(t == 0)
    def _():
        for n, ref in enumerate(part_refs):
            place = lax.rem(first_ref[0] + count - n, count) * size
            left_ref[pl.ds(pl.multiple_of(place, 8), size), :] = ref[...]

    shape = (chains * 8, chains)
    chain = iota(shape, 0) >> 3
    lift = jnp.where(iota(shape, 1) == (chain & 3) * groups + (chain >> 2), 1.0, 0.0).astype(bf16)
    same = same_slot(chains)
    rows = [
        left_ref[pl.ds(pl.multiple_of(row_of(t, u) * groups, groups), groups), :] for u in range(4)
    ]
    rows = jnp.concatenate(halves(jnp.concatenate(rows, 0)), 0)
    shape = (128, 256)
    slabs = []
    for n in range(4):
        spread = ((iota(shape, 0) >> 5) == n) & ((iota(shape, 0) & 31) == (iota(shape, 1) >> 3))
        slabs.append(one_pass(rows, jnp.where(spread, 1.0, 0.0).astype(bf16)))
    for part in range(2):
        for u in range(4):
            place = slice((part * 4 + u) * groups, (part * 4 + u + 1) * groups)
            slab = jnp.concatenate([x[place] for x in slabs], 0).astype(bf16)
            out_ref[0, u, part] = jnp.where(same, one_pass(lift, slab), 0.0).astype(bf16)


def call_blocks(first, parts):
    rows = sum(part.shape[0] for part in parts)
    chains = rows // 32 * 4
    shape = (8, 4, 2, chains * 8, 256)
    return pl.pallas_call(
        functools.partial(blocks_kernel, chains),
        grid=(8,),
        in_specs=[pl.BlockSpec(memory_space=pltpu.SMEM)] + [full(part) for part in parts],
        out_specs=step_block(shape),
        out_shape=jax.ShapeDtypeStruct(shape, bf16),
        scratch_shapes=[pltpu.VMEM((rows, 128), f32)],
        compiler_params=params(),
        name="blocks",
    )(first, *parts)


def join_right(ref, out_ref):
    cols = ref.shape[0] * 8
    for g in range(4):
        for n in range(ref.shape[2]):
            out_ref[g * cols : (g + 1) * cols, n * 128 : (n + 1) * 128] = ref[:, g, n].reshape(
                cols, 128
            )


def cut_right(ref, out_ref):
    cols = out_ref.shape[0] * 8
    for g in range(4):
        for n in range(out_ref.shape[2]):
            tile = ref[g * cols : (g + 1) * cols, n * 128 : (n + 1) * 128]
            out_ref[:, g, n] = tile.reshape(-1, 8, 128)


def outer_weights(ref, out_ref):
    whole = ref[...].reshape(32, 4, 8, 128)
    for g in range(4):
        out_ref[g, 0], out_ref[g, 1] = halves(whole[:, g].reshape(256, 128))


def params(mebibytes=56):
    return pltpu.CompilerParams(vmem_limit_bytes=mebibytes * 2**20)


def full(array):
    return pl.BlockSpec(array.shape, lambda t, n=len(array.shape): (0,) * n)


def step_block(shape):
    return pl.BlockSpec((1,) + shape[1:], lambda t, n=len(shape): (t,) + (0,) * (n - 1))


def pair_of(ref, *index):
    return ref[(*index, 0)], ref[(*index, 1)]


def chunk_order(shift):
    shape = (256, 256)
    place, width = iota(shape, 0), 1 << shift
    channel = place & 127
    target = ((channel >> shift) << (shift + 1)) + (channel & (width - 1))
    target = target + ((place >> 7) << shift)
    return jnp.where(iota(shape, 1) == target, 1.0, 0.0).astype(bf16)


def side_halves(shift, refs, out_ref):
    order = chunk_order(shift)
    for n in range(2):
        both = halves(jnp.concatenate([refs[2 * n][...], refs[2 * n + 1][...]], 1))
        for part in range(2):
            out_ref[part, :, n * 256 : (n + 1) * 256] = one_pass(both[part], order).astype(bf16)
    if len(refs) == 5:
        out_ref[0, :, 512:], out_ref[1, :, 512:] = halves(refs[4][...])


def by_step(array, cols):
    return array.reshape(2, 8, 2 * cols, 128)


def rows_block(cols):
    return pl.BlockSpec((2, 1, 2 * cols, 128), lambda t: (0, t, 0, 0))


def rows_shape(cols):
    return jax.ShapeDtypeStruct((2, 8, 2 * cols, 128), f32)


def read_step(ref, cols):
    return jnp.concatenate(
        [ref[u % 2, 0, u // 2 * cols : (u // 2 + 1) * cols] for u in range(4)], 0
    )


def write_step(ref, cols, value):
    for u in range(4):
        ref[u % 2, 0, u // 2 * cols : (u // 2 + 1) * cols] = value[u * cols : (u + 1) * cols]


def prepare_kernel(shift, outer_ref, *refs):
    *side_refs, outer_halves, sides_halves = refs
    outer_weights(outer_ref, outer_halves)
    side_halves(shift, side_refs, sides_halves)


def call_prepare(outer, sides, shift):
    return pl.pallas_call(
        functools.partial(prepare_kernel, shift),
        out_shape=(
            jax.ShapeDtypeStruct((4, 2, 256, 128), bf16),
            jax.ShapeDtypeStruct((2, 128, 640), bf16),
        ),
        compiler_params=params(),
        name="prepare",
    )(outer, *sides)


def edges_kernel(
    cols,
    block_ref,
    right_ref,
    outer_halves,
    sides_halves,
    pair_ref,
    mid_ref,
    edge_ref,
    prod_ref,
    whole_ref,
    right_halves,
):
    t = pl.program_id(0)

    @pl.when(t == 0)
    def _():
        join_right(right_ref, whole_ref)
        right_halves[0], right_halves[1] = halves(whole_ref[...])

    right = pair_of(right_halves)
    for u in range(4):
        high, low = halves(stacked3(right, pair_of(block_ref, 0, u)))
        for g in range(4):
            prod_ref[0, g, 0, u * cols : (u + 1) * cols] = high[g * cols : (g + 1) * cols]
            prod_ref[0, g, 1, u * cols : (u + 1) * cols] = low[g * cols : (g + 1) * cols]
    update = 0.0
    for g in range(4):
        update = update + dot3(pair_of(prod_ref, 0, g), pair_of(outer_halves, g))
    mid = update + read_step(pair_ref, cols)
    write_step(mid_ref, cols, mid)
    normed, _ = norm_parts(mid)
    sides = rounded(pair_of(sides_halves), (slice(None), slice(0, 512)))
    logits = stacked3(normed, sides)
    write_turned(edge_ref, t, jax.nn.sigmoid(logits[:, :256]) * logits[:, 256:])


def call_edges(blocks, right, outer, sides, pair, cols):
    rows, depth = pair.shape[0], blocks.shape[3]
    prods = (8, 4, 2, 4 * cols, 256)
    mid, edges, products = pl.pallas_call(
        functools.partial(edges_kernel, cols),
        grid=(8,),
        in_specs=[step_block(blocks.shape)] + [full(x) for x in (right, outer, sides)]
        + [rows_block(cols)],
        out_specs=(
            rows_block(cols),
            pl.BlockSpec((256, 16, 128), lambda t: (0, 0, 0)),
            step_block(prods),
        ),
        out_shape=(
            rows_shape(cols),
            jax.ShapeDtypeStruct((256, 16, 128), f32),
            jax.ShapeDtypeStruct(prods, bf16),
        ),
        scratch_shapes=[
            pltpu.VMEM((4 * cols, depth), f32),
            pltpu.VMEM((2, 4 * cols, depth), bf16),
        ],
        compiler_params=params(),
        name="edges",
    )(blocks, right, outer, sides, by_step(pair, cols))
    return mid.reshape(rows, 128), edges, products


def factors_kernel(cols, mid_ref, sides_halves, out_ref):
    normed, _ = norm_parts(read_rows(mid_ref, four_rows(pl.program_id(0), cols)))
    sides = rounded(pair_of(sides_halves), (slice(None), slice(0, 512)))
    logits = stacked3(normed, sides)
    gate = jax.nn.sigmoid(logits[:, :256])
    out_ref[0, :, :256] = logits[:, 256:] * gate * (1.0 - gate)
    out_ref[0, :, 256:] = gate


def call_factors(mid, sides, cols):
    shape = (8, 4 * cols, 512)
    return pl.pallas_call(
        functools.partial(factors_kernel, cols),
        grid=(8,),
        in_specs=[full(mid), full(sides)],
        out_specs=step_block(shape),
        out_shape=jax.ShapeDtypeStruct(shape, f32),
        compiler_params=params(),
        name="factors",
    )(mid, sides)


def join_tiles(chunks, mesh_rows, mesh_cols, out_ref):
    plain = chunks.reshape(mesh_rows * mesh_cols * 16, 128)
    rolled = pltpu.roll(plain, 64, 1)
    first = iota((16, 128), 1) < 64
    for r in range(mesh_rows):
        for t in range(mesh_cols // 2):
            even = slice((r * mesh_cols + 2 * t) * 16, (r * mesh_cols + 2 * t + 1) * 16)
            odd = slice((r * mesh_cols + 2 * t + 1) * 16, (r * mesh_cols + 2 * t + 2) * 16)
            lanes = slice(t * 128, (t + 1) * 128)
            out_ref[r * 32 : r * 32 + 16, lanes] = jnp.where(first, plain[even], rolled[odd])
            out_ref[r * 32 + 16 : r * 32 + 32, lanes] = jnp.where(first, rolled[even], plain[odd])


def cut_tiles(whole, mesh_rows, mesh_cols, store):
    first = iota((16, 128), 1) < 64
    for t in range(mesh_cols // 2):
        plain = whole[:, t * 128 : (t + 1) * 128]
        rolled = pltpu.roll(plain, 64, 1)
        for r in range(mesh_rows):
            low = slice(r * 32, r * 32 + 16)
            high = slice(r * 32 + 16, r * 32 + 32)
            store(r * mesh_cols + 2 * t, jnp.where(first, plain[low], rolled[high]))
            store(r * mesh_cols + 2 * t + 1, jnp.where(first, rolled[low], plain[high]))


def triangle_kernel(mesh_rows, mesh_cols, edge_ref, out_ref, left_ref, right_ref):
    join_tiles(edge_ref[:, 0, 0], mesh_rows, mesh_cols, left_ref)
    join_tiles(edge_ref[:, 1, 0], mesh_rows, mesh_cols, right_ref)

    def store(d, tile):
        out_ref[d, 0] = tile

    cut_tiles(dot3(left_ref[...], right_ref[...], NT), mesh_rows, mesh_cols, store)


def call_triangle(edges, mesh_rows, mesh_cols):
    devices, _, channels = edges.shape[:3]
    span = mesh_rows * 32
    return pl.pallas_call(
        functools.partial(triangle_kernel, mesh_rows, mesh_cols),
        grid=(channels,),
        in_specs=[pl.BlockSpec((devices, 2, 1, 16, 128), lambda n: (0, 0, n, 0, 0))],
        out_specs=pl.BlockSpec((devices, 1, 16, 128), lambda n: (0, n, 0, 0)),
        out_shape=jax.ShapeDtypeStruct((devices, channels, 16, 128), f32),
        scratch_shapes=[pltpu.VMEM((span, span), f32)] * 2,
        compiler_params=params(32),
        name="triangle",
    )(edges)


def triangle_back_kernel(
    mesh_rows, mesh_cols, edge_ref, grad_ref, out_ref, left_ref, right_ref, whole_ref
):
    join_tiles(edge_ref[:, 0, 0], mesh_rows, mesh_cols, left_ref)
    join_tiles(edge_ref[:, 1, 0], mesh_rows, mesh_cols, right_ref)
    join_tiles(grad_ref[:, 0], mesh_rows, mesh_cols, whole_ref)

    def store(kind):
        def put(d, tile):
            out_ref[d, kind, 0] = tile

        return put

    whole = whole_ref[...]
    cut_tiles(dot3(whole, right_ref[...]), mesh_rows, mesh_cols, store(0))
    cut_tiles(dot3(jnp.transpose(whole), left_ref[...]), mesh_rows, mesh_cols, store(1))


def call_triangle_back(edges, grad, mesh_rows, mesh_cols):
    devices, _, channels = edges.shape[:3]
    span = mesh_rows * 32
    both = pl.BlockSpec((devices, 2, 1, 16, 128), lambda n: (0, 0, n, 0, 0))
    return pl.pallas_call(
        functools.partial(triangle_back_kernel, mesh_rows, mesh_cols),
        grid=(channels,),
        in_specs=[both, pl.BlockSpec((devices, 1, 16, 128), lambda n: (0, n, 0, 0))],
        out_specs=both,
        out_shape=jax.ShapeDtypeStruct(edges.shape, f32),
        scratch_shapes=[pltpu.VMEM((span, span), f32)] * 3,
        compiler_params=params(32),
        name="triangle_back",
    )(edges, grad)


def four_rows(t, cols):
    return [
        pl.ds(pl.multiple_of((2 * t + u // 2 + 16 * (u % 2)) * cols, cols), cols) for u in range(4)
    ]


def read_rows(ref, places):
    return jnp.concatenate([ref[p, :] for p in places], 0)


def write_rows(ref, places, value):
    size = value.shape[0] // len(places)
    for u, p in enumerate(places):
        ref[p, :] = value[u * size : (u + 1) * size]


def read_turned(ref, t):
    parts = []
    for v in range(2):
        tile = ref[:, pl.ds(2 * t + v, 1), :]
        parts.append(jnp.transpose(tile.reshape(tile.shape[0], 128)))
    return jnp.concatenate(parts, 0)


def write_turned(ref, t, value):
    for v in range(2):
        turned = jnp.transpose(value[v * 128 : (v + 1) * 128])
        ref[:, pl.ds(2 * t + v, 1), :] = turned[:, None, :]


def finish_kernel(
    cols, tri_ref, mid_ref, grad_ref, gate_ref, proj_ref, out_ref, dtri_ref, dlogit_ref, dproj_ref
):
    gate_w = halves(gate_ref[...])
    proj_w = halves(proj_ref[...])
    dproj_ref[...] = jnp.zeros_like(dproj_ref)

    def step(t, carry):
        places = four_rows(t, cols)
        mid = read_rows(mid_ref, places)
        grad = read_rows(grad_ref, places)
        normed, _ = norm_parts(mid)
        tri, tri_inverse = norm_parts(read_turned(tri_ref, t))
        tri_halves = halves(tri)
        gate = jax.nn.sigmoid(dot3(normed, gate_w))
        value = dot3(tri_halves, proj_w)
        write_rows(out_ref, places, mid + gate * value)
        dvalue = halves(grad * gate)
        write_rows(dlogit_ref, places, grad * value * gate * (1.0 - gate))
        dproj_ref[...] += stacked3(halves(jnp.transpose(tri)), dvalue)
        write_turned(dtri_ref, t, norm_back(tri, tri_inverse, stacked3(dvalue, proj_w, NT)))
        return carry

    lax.fori_loop(0, 8, step, 0)


def call_finish(tri, mid, grad, gate, proj, cols):
    rows = mid.shape[0]
    return pl.pallas_call(
        functools.partial(finish_kernel, cols),
        out_shape=(
            jax.ShapeDtypeStruct((rows, 128), f32),
            jax.ShapeDtypeStruct((128, 16, 128), f32),
            jax.ShapeDtypeStruct((rows, 128), f32),
            jax.ShapeDtypeStruct((128, 128), f32),
        ),
        compiler_params=params(32),
        name="finish",
    )(tri, mid, grad, gate, proj)


def edges_back_kernel(
    cols,
    chains,
    dedge_ref,
    mid_ref,
    grad_ref,
    dlogit_ref,
    sides_halves,
    right_ref,
    outer_halves,
    factor_ref,
    block_ref,
    first_ref,
    dmid_ref,
    dlogits_ref,
    dright_ref,
    *refs,
):
    *dleft_refs, whole_ref, turned_halves, fold_ref, dslab_ref, dleft_ref = refs
    t = pl.program_id(0)

    @pl.when(t == 0)
    def _():
        join_right(right_ref, whole_ref)
        turned_halves[0], turned_halves[1] = halves(jnp.transpose(whole_ref[...]))
        shape = (256, 128)
        for u in range(4):
            lane = 64 * (u % 2) + 32 * (u // 2) + (iota(shape, 0) >> 3)
            fold = jnp.where(iota(shape, 1) == lane, 1.0, 0.0).astype(bf16)
            fold_ref[512 * u : 512 * u + 256] = fold
            fold_ref[512 * u + 256 : 512 * u + 512] = fold
        whole_ref[...] = jnp.zeros_like(whole_ref)

    same = same_slot(chains)
    sides = pair_of(sides_halves)
    normed, inverse = norm_parts(read_step(mid_ref, cols))
    dedge = read_turned(dedge_ref, t)
    dlogits = [
        dedge * factor_ref[0, :, :256],
        dedge * factor_ref[0, :, 256:],
        read_step(dlogit_ref, cols),
    ]
    dlogits = halves(jnp.concatenate(dlogits, 1))
    dlogits_ref[0, 0], dlogits_ref[0, 1] = dlogits
    dmid = read_step(grad_ref, cols) + norm_back(normed, inverse, dot3(dlogits, sides, NT))
    write_step(dmid_ref, cols, dmid)
    dmid = halves(dmid)
    dprod = [halves(stacked3(dmid, pair_of(outer_halves, g), NT)) for g in range(4)]
    here, diagonal = [], []
    turned = pair_of(turned_halves)
    for u in range(4):
        rows = slice(u * cols, (u + 1) * cols)
        here.append([jnp.concatenate([dprod[g][n][rows] for g in range(4)], 0) for n in range(2)])
        diagonal += halves(jnp.where(same, stacked3(turned, tuple(here[u])), 0.0))
    right_terms = [x for high, low in here for x in (high, low, high)]
    block_terms = [block_ref[0, u, n] for u in range(4) for n in (0, 0, 1)]
    whole_ref[...] += one_pass(
        jnp.concatenate(right_terms, 1), jnp.concatenate(block_terms, 1), NT
    )
    dslab = one_pass(jnp.concatenate(diagonal, 1), fold_ref[...])
    dslab_ref[t] = jnp.sum(dslab.reshape(chains, 8, 128), axis=1)

    @pl.when(t == 7)
    def _():
        cut_right(whole_ref, dright_ref)
        first = iota((chains, 128), 1) < 64
        for n in range(4):
            even, odd = dslab_ref[2 * n], dslab_ref[2 * n + 1]
            dleft_ref[n] = jnp.where(first, even, pltpu.roll(odd, 64, 1))
            dleft_ref[n + 4] = jnp.where(first, pltpu.roll(even, 64, 1), odd)
        count, size = len(dleft_refs), dleft_refs[0].shape[0]
        for n, ref in enumerate(dleft_refs):
            place = lax.rem(first_ref[0] + n, count) * size
            ref[...] = dleft_ref[pl.ds(place, size)]


def call_edges_back(
    dedge, mid, grad, dlogit, sides, right, outer, factors, blocks, first, count, cols
):
    rows, depth = mid.shape[0], blocks.shape[3]
    chains = depth // 8
    dlogits = (8, 2, 4 * cols, 640)
    rows_in = [by_step(x, cols) for x in (mid, grad, dlogit)]
    dmid, *others = pl.pallas_call(
        functools.partial(edges_back_kernel, cols, chains),
        grid=(8,),
        in_specs=[full(dedge)]
        + [rows_block(cols)] * 3
        + [full(x) for x in (sides, right, outer)]
        + [step_block(factors.shape), step_block(blocks.shape), pl.BlockSpec(memory_space=pltpu.SMEM)],
        out_specs=(
            rows_block(cols),
            step_block(dlogits),
            full(right),
        )
        + (pl.BlockSpec((8 // count, chains, 128), lambda t: (0, 0, 0)),) * count,
        out_shape=(
            rows_shape(cols),
            jax.ShapeDtypeStruct(dlogits, bf16),
            jax.ShapeDtypeStruct(right.shape, f32),
        )
        + (jax.ShapeDtypeStruct((8 // count, chains, 128), f32),) * count,
        scratch_shapes=[
            pltpu.VMEM((4 * cols, depth), f32),
            pltpu.VMEM((2, depth, 4 * cols), bf16),
            pltpu.VMEM((2048, 128), bf16),
            pltpu.VMEM((8, chains, 128), f32),
            pltpu.VMEM((8, chains, 128), f32),
        ],
        compiler_params=params(),
        name="edges_back",
    )(dedge, *rows_in, sides, right, outer, factors, blocks, first)
    return dmid.reshape(rows, 128), *others


def give_halves(core_ref, whole_ref, mine_ref, other_ref):
    mine_ref[...] = whole_ref[core_ref[0]]
    other_ref[...] = whole_ref[1 - core_ref[0]]


def side_sums_kernel(
    cols,
    shift,
    mid_ref,
    dlogits_ref,
    first_ref,
    core_ref,
    mine_ref,
    other_ref,
    sides_ref,
    whole_ref,
):
    t = pl.program_id(0)

    @pl.when(t == 0)
    def _():
        sides_ref[...] = jnp.zeros_like(sides_ref)

    normed, _ = norm_parts(read_rows(mid_ref, four_rows(t, cols)))
    sides_ref[...] += tall3(halves(jnp.transpose(normed)), pair_of(dlogits_ref, 0))

    @pl.when(t == 7)
    def _():
        order = chunk_order(shift)
        for n in range(2):
            high, low = halves(sides_ref[:, n * 256 : (n + 1) * 256])
            sides = one_pass(high, order, NT) + one_pass(low, order, NT)
            for side in range(2):
                place = 2 * n + side
                rows = slice(place % 3 * 128, place % 3 * 128 + 128)
                whole_ref[place // 3, rows] = sides[:, side * 128 : (side + 1) * 128]
        whole_ref[1, 128:256] = sides_ref[:, 512:]
        whole_ref[1, 256:] = first_ref[...]
        give_halves(core_ref, whole_ref, mine_ref, other_ref)


def call_side_sums(mid, dlogits, first, core, cols, shift):
    return pl.pallas_call(
        functools.partial(side_sums_kernel, cols, shift),
        grid=(8,),
        in_specs=[full(mid), step_block(dlogits.shape), full(first)]
        + [pl.BlockSpec(memory_space=pltpu.SMEM)],
        out_specs=(pl.BlockSpec((384, 128), lambda t: (0, 0)),) * 2,
        out_shape=(jax.ShapeDtypeStruct((384, 128), f32),) * 2,
        scratch_shapes=[pltpu.VMEM((128, 640), f32), pltpu.VMEM((2, 384, 128), f32)],
        compiler_params=params(),
        name="side_sums",
    )(mid, dlogits, first, core)


def outer_sums_kernel(
    cols, dmid_ref, prod_ref, core_ref, mine_ref, other_ref, outer_ref, whole_ref
):
    t = pl.program_id(0)

    @pl.when(t == 0)
    def _():
        outer_ref[...] = jnp.zeros_like(outer_ref)

    dmid = halves(jnp.transpose(read_rows(dmid_ref, four_rows(t, cols))))
    for g in range(4):
        outer_ref[:, g * 256 : (g + 1) * 256] += tall3(dmid, pair_of(prod_ref, 0, g))

    @pl.when(t == 7)
    def _():
        for g in range(4):
            tile = jnp.transpose(outer_ref[:, g * 256 : (g + 1) * 256]).reshape(32, 8, 128)
            for p in range(32):
                start = p % 16 * 32 + g * 8
                whole_ref[p // 16, start : start + 8] = tile[p]
        give_halves(core_ref, whole_ref, mine_ref, other_ref)


def call_outer_sums(dmid, prods, core, cols):
    return pl.pallas_call(
        functools.partial(outer_sums_kernel, cols),
        grid=(8,),
        in_specs=[full(dmid), step_block(prods.shape), pl.BlockSpec(memory_space=pltpu.SMEM)],
        out_specs=(pl.BlockSpec((512, 128), lambda t: (0, 0)),) * 2,
        out_shape=(jax.ShapeDtypeStruct((512, 128), f32),) * 2,
        scratch_shapes=[pltpu.VMEM((128, 1024), f32), pltpu.VMEM((2, 512, 128), f32)],
        compiler_params=params(),
        name="outer_sums",
    )(dmid, prods, core)


def pack_heads(y, store):
    lane = iota((1, 1, 128), 2) >> 5
    for tile in range(y.shape[1] // 128):
        part = y[:, tile * 128 : (tile + 1) * 128]
        turned = [part] + [pltpu.roll(part, 32 * n, 1) for n in range(1, 4)]
        turned = [x.reshape(-1, 4, 8, 128) for x in turned]
        for head in range(4):
            out = turned[-head % 4][:, 0]
            for chain in range(1, 4):
                out = jnp.where(lane == chain, turned[(chain - head) % 4][:, chain], out)
            store(tile * 4 + head, out)


def unpack_heads(load, heads):
    lane = iota((1, 1, 128), 2) >> 5
    tiles = []
    for tile in range(heads // 4):
        turned = []
        for head in range(4):
            part = load(tile * 4 + head)
            flat = part.reshape(-1, 128)
            turned.append(
                [part] + [pltpu.roll(flat, 32 * n, 1).reshape(part.shape) for n in range(1, 4)]
            )
        chains = []
        for chain in range(4):
            out = turned[0][-chain % 4]
            for head in range(1, 4):
                out = jnp.where(lane == head, turned[head][(head - chain) % 4], out)
            chains.append(out[:, None])
        tiles.append(jnp.concatenate(chains, 1).reshape(-1, 128))
    return jnp.concatenate(tiles, 1)


def head_lanes(tile, n):
    return jnp.where((iota((1, 128), 1) >> 5) == n, tile, 0.0)


def stack_heads(tile):
    return jnp.concatenate([head_lanes(tile, n) for n in range(4)], 0)


def join_heads(stacked):
    size = stacked.shape[0] // 4
    lane = iota((1, 128), 1) >> 5
    out = stacked[:size]
    for n in range(1, 4):
        out = jnp.where(lane == n, stacked[n * size : (n + 1) * size], out)
    return out


def soft(scores, seen=None):
    if seen is not None:
        scores = jnp.where(seen, scores, -1e30)
    weights = jnp.exp(scores - jnp.max(scores, axis=-1, keepdims=True))
    if seen is not None:
        weights = jnp.where(seen, weights, 0.0)
    return weights * (1.0 / jnp.sum(weights, axis=-1, keepdims=True))


def soft_back(weights, grad):
    return weights * (grad - jnp.sum(weights * grad, axis=-1, keepdims=True))


def stripe_seen(present_ref):
    tokens = present_ref.shape[1]
    shape = (tokens, tokens)
    same = (iota(shape, 0) & 7) == (iota(shape, 1) & 7)
    return same & (present_ref[...] > 0.0)


def column_attention(q, k, v, seen):
    weights, tiles = [], []
    for tile in range(q.shape[1] // 128):
        lanes = slice(tile * 128, (tile + 1) * 128)
        keys, values = halves(k[:, lanes]), halves(v[:, lanes])
        blend = 0.0
        for n in range(4):
            weights.append(soft(dot3(head_lanes(q[:, lanes], n), keys, NT), seen))
            blend = blend + head_lanes(dot3(weights[-1], values), n)
        tiles.append(blend)
    return weights, jnp.concatenate(tiles, 1)


def columns_kernel(
    scale,
    x_ref,
    present_ref,
    bias_ref,
    q_ref,
    k_ref,
    v_ref,
    o_ref,
    q2_ref,
    k2_ref,
    v2_ref,
    out_ref,
    qkv_ref,
):
    x = x_ref[...]
    normed, _ = norm_parts(x)
    normed = halves(normed)
    q, k, v = (dot3(normed, halves(w[...])) for w in (q_ref, k_ref, v_ref))
    _, blend = column_attention(q * scale, k, v, stripe_seen(present_ref))
    out = x + dot3(blend, halves(o_ref[...]))
    out_ref[...] = out
    normed, _ = norm_parts(out)
    normed = halves(normed)
    groups, size = qkv_ref.shape[0] // 8, (qkv_ref.shape[1] - 16) // 3
    qkv_ref[:, -16:] = bias_ref[...]

    def store(kind):
        def put(head, value):
            place = slice(head * groups, (head + 1) * groups)
            rows = slice(kind * size, (kind + 1) * size)
            qkv_ref[place, rows] = value.reshape(groups, size, 128)

        return put

    for kind, w in enumerate((q2_ref, k2_ref, v2_ref)):
        pack_heads(dot3(normed, halves(w[...])), store(kind))


def call_columns(x, present, bias, weights, group_chains, scale):
    return pl.pallas_call(
        functools.partial(columns_kernel, scale),
        out_shape=(
            jax.ShapeDtypeStruct(x.shape, f32),
            jax.ShapeDtypeStruct((bias.shape[0], 6 * group_chains + 16, 128), f32),
        ),
        compiler_params=params(24),
        name="columns",
    )(x, present, bias, *weights)


def packed_parts(ref):
    parts = (ref.shape[1] - 16) // 24
    for half in range(parts):
        places = [(kind * parts + half) * 8 for kind in range(3)]
        yield half, places, [ref[:, p : p + 8].reshape(-1, 128) for p in places]


def rows_kernel(mesh_rows, mesh_cols, scale, qkv_ref, out_ref, whole_ref):
    join_tiles(qkv_ref[:, -16:], mesh_rows, mesh_cols, whole_ref)
    bias = whole_ref[...]
    for half, _, (q, k, v) in packed_parts(qkv_ref):
        k, v, q = halves(k), halves(v), q * scale
        blend = 0.0
        for n in range(4):
            weights = soft(dot3(head_lanes(q, n), k, NT) + bias)
            blend = blend + head_lanes(dot3(weights, v), n)
        out_ref[:, half] = blend.reshape(-1, 8, 128)


def call_rows(qkv, mesh_rows, mesh_cols, scale):
    devices, parts = qkv.shape[0], (qkv.shape[1] - 16) // 24
    span = mesh_rows * 32
    return pl.pallas_call(
        functools.partial(rows_kernel, mesh_rows, mesh_cols, scale),
        out_shape=jax.ShapeDtypeStruct((devices, parts, 8, 128), f32),
        scratch_shapes=[pltpu.VMEM((span, span), f32)],
        compiler_params=params(24),
        name="rows",
    )(qkv)


def load_heads(ref, kind=None):
    def load(head):
        groups = ref.shape[0] // 8
        place = slice(head * groups, (head + 1) * groups)
        part = ref[place] if kind is None else ref[place, kind]
        return part.reshape(-1, 8, 128)

    return load


def side_copies(source_ref, target_ref):
    both = halves(jnp.concatenate([source_ref[...], target_ref[...]], 0))
    shape = (640, 64)
    place = iota(shape, 0) - 128
    feature = jnp.where(place < 0, place & 31, 32 + ((place >> 7) << 3) + (place & 7))
    copies = jnp.where(iota(shape, 1) == feature, 1.0, 0.0).astype(bf16)
    return tuple(one_pass(copies, part).astype(bf16) for part in both)


def rows_out_kernel(
    blend_ref, mid_ref, share_ref, o_ref, source_ref, target_ref, out_ref, left_ref, right_ref
):
    blend = unpack_heads(load_heads(blend_ref), 8)
    out = mid_ref[...] + dot3(blend, halves(o_ref[...]))
    out_ref[...] = out
    normed, _ = norm_parts(out)
    wide = dot3(normed, side_copies(source_ref, target_ref), NT)
    left = (wide[:, :128] * share_ref[...]).reshape(-1, 4, 8, 128)
    lane = iota((1, 1, 128), 2)
    packed = left[:, 0]
    for chain in range(1, 4):
        packed = jnp.where((lane >> 5) == chain, left[:, chain], packed)
    for n in range(packed.shape[0]):
        left_ref[:, n, :] = packed[n]
    for g in range(4):
        right = wide[:, (g + 1) * 128 : (g + 2) * 128].reshape(-1, 16, 8, 128)
        packed = right[:, 0]
        for chain in range(1, 16):
            packed = jnp.where((lane >> 3) == chain, right[:, chain], packed)
        right_ref[g] = packed


def call_rows_out(blend, mid, share, weight, source, target):
    chains = mid.shape[0] // 8
    return pl.pallas_call(
        rows_out_kernel,
        out_shape=(
            jax.ShapeDtypeStruct(mid.shape, f32),
            jax.ShapeDtypeStruct((8, chains // 4, 128), f32),
            jax.ShapeDtypeStruct((4, chains // 16, 8, 128), f32),
        ),
        compiler_params=params(),
        name="rows_out",
    )(blend, mid, share, weight, source, target)


def rows_out_back_kernel(*refs):
    *dleft_refs, dright_ref, grad_ref, out_ref, blend_ref, share_ref = refs[:-10]
    o_ref, source_ref, target_ref = refs[-10:-7]
    core_ref, dout_ref, dblend_ref, thin_ref, mine_ref, other_ref, sum_ref = refs[-7:]
    lane = iota((1, 1, 128), 2)
    chains = grad_ref.shape[0] // 8
    dleft = functools.reduce(jnp.add, [ref[...] for ref in dleft_refs])
    shape = (chains * 8, 128)
    slot = iota(shape, 0) & 7
    copy = (chains * 8, chains)
    copy = jnp.where((iota(copy, 0) >> 3) == iota(copy, 1), 1.0, 0.0).astype(bf16)
    left = 0.0
    for n in range(2):
        high, low = halves(dleft[n])
        spot = (slot >> 2 == n) & (slot & 3 == iota(shape, 1) >> 5)
        left = left + jnp.where(spot, one_pass(copy, high) + one_pass(copy, low), 0.0)
    wide = [left * share_ref[...]]
    dright = dright_ref[...]
    for g in range(4):
        part = [jnp.where((lane >> 3) == n, dright[g], 0.0)[:, None] for n in range(16)]
        wide.append(jnp.concatenate(part, 1).reshape(-1, 128))
    wide = halves(jnp.concatenate(wide, 1))
    normed, inverse = norm_parts(out_ref[...])
    dsides = halves(dot3(halves(jnp.transpose(normed)), wide))
    shape = (640, 128)
    place, spot = iota(shape, 0) - 128, iota(shape, 1)
    target = jnp.where(place < 0, place & 31, 32 + ((place >> 7) << 3) + (place & 7))
    fold = jnp.where(target == spot, 1.0, 0.0).astype(bf16)
    thin_ref[...] = one_pass(dsides[0], fold) + one_pass(dsides[1], fold)
    dout = grad_ref[...] + norm_back(normed, inverse, dot3(wide, side_copies(source_ref, target_ref)))
    dout_ref[...] = dout
    dout = halves(dout)
    groups = dblend_ref.shape[0] // 8

    def store(head, value):
        dblend_ref[head * groups : (head + 1) * groups] = value.reshape(groups, -1, 8, 128)

    pack_heads(dot3(dout, halves(o_ref[...]), NT), store)
    blend = unpack_heads(load_heads(blend_ref), 8)
    write_halves(sum_ref, 0, dot3(halves(jnp.transpose(blend)), dout))
    give_halves(core_ref, sum_ref, mine_ref, other_ref)


def call_rows_out_back(dlefts, dright, grad, out, blend, share, weight, source, target, core):
    shapes, scratch = halves_shapes([weight])
    return pl.pallas_call(
        rows_out_back_kernel,
        out_shape=(
            jax.ShapeDtypeStruct(grad.shape, f32),
            jax.ShapeDtypeStruct(blend.shape, f32),
            jax.ShapeDtypeStruct((256, 128), f32),
        )
        + shapes,
        in_specs=specs(len(dlefts) + 8),
        scratch_shapes=[scratch],
        compiler_params=params(),
        name="rows_out_back",
    )(*dlefts, dright, grad, out, blend, share, weight, source, target, core)


def rows_back_kernel(
    mesh_rows, mesh_cols, scale, qkv_ref, dblend_ref, out_ref, whole_ref
):
    join_tiles(qkv_ref[:, -16:], mesh_rows, mesh_cols, whole_ref)
    bias = jnp.concatenate([whole_ref[...]] * 4, 0)
    span = whole_ref.shape[0]
    dbias = 0.0
    for half, places, (q, k, v) in packed_parts(qkv_ref):
        k, query = halves(k), halves(stack_heads(q * scale))
        dblend = halves(stack_heads(dblend_ref[:, half].reshape(-1, 128)))
        weights = soft(dot3(query, k, NT) + bias)
        dv = dot3(halves(jnp.transpose(weights)), dblend)
        dscores = soft_back(weights, dot3(dblend, halves(v), NT))
        for n in range(4):
            dbias = dbias + dscores[n * span : (n + 1) * span]
        dk = dot3(halves(jnp.transpose(dscores)), query)
        dq = join_heads(dot3(dscores, k))
        for place, value in zip(places, (dq * scale, dk, dv)):
            out_ref[:, place : place + 8] = value.reshape(-1, 8, 128)

    def store(d, tile):
        out_ref[d, -16:] = tile

    cut_tiles(dbias, mesh_rows, mesh_cols, store)


def call_rows_back(qkv, dblend, mesh_rows, mesh_cols, scale):
    span = mesh_rows * 32
    return pl.pallas_call(
        functools.partial(rows_back_kernel, mesh_rows, mesh_cols, scale),
        out_shape=jax.ShapeDtypeStruct(qkv.shape, f32),
        scratch_shapes=[pltpu.VMEM((span, span), f32)],
        compiler_params=params(24),
        name="rows_back",
    )(qkv, dblend)


def write_halves(ref, n, value):
    height = value.shape[0]
    for half in range(2):
        ref[half, n * height : (n + 1) * height] = value[:, half * 128 : (half + 1) * 128]


def projections_back(normed, inverse, grads, weight_refs, sum_ref):
    turned = halves(jnp.transpose(normed))
    dnormed = 0.0
    for n, (grad, w) in enumerate(zip(grads, weight_refs)):
        grad = halves(grad)
        write_halves(sum_ref, n, dot3(turned, grad))
        dnormed = dnormed + dot3(grad, halves(w[...]), NT)
    return norm_back(normed, inverse, dnormed)


def rows_in_back_kernel(
    dqkv_ref, mid_ref, grad_ref, q_ref, k_ref, v_ref, core_ref, dmid_ref, mine_ref, other_ref, sum_ref
):
    groups, size = dqkv_ref.shape[0] // 8, (dqkv_ref.shape[1] - 16) // 3

    def load(kind):
        place = slice(kind * size, (kind + 1) * size)
        return lambda head: dqkv_ref[head * groups : (head + 1) * groups, place].reshape(-1, 8, 128)

    grads = [unpack_heads(load(kind), 8) for kind in range(3)]
    normed, inverse = norm_parts(mid_ref[...])
    dmid_ref[...] = grad_ref[...] + projections_back(
        normed, inverse, grads, (q_ref, k_ref, v_ref), sum_ref
    )
    give_halves(core_ref, sum_ref, mine_ref, other_ref)


def halves_shapes(weights):
    rows = sum(w.size for w in weights) // 256
    return (jax.ShapeDtypeStruct((rows, 128), f32),) * 2, pltpu.VMEM((2, rows, 128), f32)


def specs(count):
    vmem = pl.BlockSpec(memory_space=pltpu.VMEM)
    return [vmem] * count + [pl.BlockSpec(memory_space=pltpu.SMEM)]


def call_rows_in_back(dqkv, mid, grad, weights, core):
    shapes, scratch = halves_shapes(weights)
    return pl.pallas_call(
        rows_in_back_kernel,
        in_specs=specs(6),
        out_shape=(jax.ShapeDtypeStruct(mid.shape, f32),) + shapes,
        scratch_shapes=[scratch],
        compiler_params=params(24),
        name="rows_in_back",
    )(dqkv, mid, grad, *weights, core)


def columns_back_kernel(
    scale,
    x_ref,
    present_ref,
    grad_ref,
    q_ref,
    k_ref,
    v_ref,
    o_ref,
    core_ref,
    dx_ref,
    mine_ref,
    other_ref,
    sum_ref,
):
    normed, inverse = norm_parts(x_ref[...])
    normed_halves = halves(normed)
    q, k, v = (dot3(normed_halves, halves(w[...])) for w in (q_ref, k_ref, v_ref))
    q = q * scale
    weights, blend = column_attention(q, k, v, stripe_seen(present_ref))
    grad = grad_ref[...]
    grad_halves = halves(grad)
    write_halves(sum_ref, 3, dot3(halves(jnp.transpose(blend)), grad_halves))
    dblend = dot3(grad_halves, halves(o_ref[...]), NT)
    tiles = [[], [], []]
    for tile in range(q.shape[1] // 128):
        lanes = slice(tile * 128, (tile + 1) * 128)
        keys, values = halves(k[:, lanes]), halves(v[:, lanes])
        dq, dk, dv = 0.0, 0.0, 0.0
        for n in range(4):
            query = halves(head_lanes(q[:, lanes], n))
            dhead = halves(head_lanes(dblend[:, lanes], n))
            share = weights[tile * 4 + n]
            dv = dv + dot3(halves(jnp.transpose(share)), dhead)
            dscores = soft_back(share, dot3(dhead, values, NT))
            dk = dk + dot3(halves(jnp.transpose(dscores)), query)
            dq = dq + head_lanes(dot3(dscores, keys), n)
        for kind, value in enumerate((dq * scale, dk, dv)):
            tiles[kind].append(value)
    grads = [jnp.concatenate(t, 1) for t in tiles]
    dx_ref[...] = grad + projections_back(
        normed, inverse, grads, (q_ref, k_ref, v_ref), sum_ref
    )
    give_halves(core_ref, sum_ref, mine_ref, other_ref)


def call_columns_back(x, present, grad, weights, core, scale):
    shapes, scratch = halves_shapes(weights)
    return pl.pallas_call(
        functools.partial(columns_back_kernel, scale),
        in_specs=specs(7),
        out_shape=(jax.ShapeDtypeStruct(x.shape, f32),) + shapes,
        scratch_shapes=[scratch],
        compiler_params=params(24),
        name="columns_back",
    )(x, present, grad, *weights, core)


def bias_kernel(cols, pair_ref, weight_ref, out_ref):
    weight = halves(weight_ref[...])

    def step(t, carry):
        rows = halves(read_rows(pair_ref, four_rows(t, cols)))
        heads = dot3(weight, rows, NT)
        for v in range(2):
            tile = heads[:, v * 128 : (v + 1) * 128][:, None, :]
            for g in range(out_ref.shape[1]):
                out_ref[:, g, pl.ds(2 * t + v, 1), :] = tile
        return carry

    lax.fori_loop(0, 8, step, 0)


def call_bias(pair, weight, copies, cols):
    return pl.pallas_call(
        functools.partial(bias_kernel, cols),
        out_shape=jax.ShapeDtypeStruct((weight.shape[0], copies, 16, 128), f32),
        compiler_params=params(24),
        name="bias",
    )(pair, weight)


def bias_rows(dbias):
    heads, groups, rows = dbias.shape[:3]
    return pl.BlockSpec((heads, groups, 16, 128), lambda t: (0, 0, rows // 16 - 1, 0))


def head_rows(ref, t):
    heads = [ref[:, pl.ds(2 * t + v, 1), :].reshape(-1, 128) for v in range(2)]
    return jnp.concatenate(heads, 1)


def bias_sums_kernel(
    cols, dbias_ref, pair_ref, thin_ref, core_ref, mine_ref, other_ref, whole_ref, sum_ref, dweight_ref
):
    sum_ref[...] = jnp.sum(dbias_ref[...], axis=1)
    dweight_ref[...] = jnp.zeros_like(dweight_ref)

    def step(t, carry):
        dweight_ref[...] += dot3(head_rows(sum_ref, t), read_rows(pair_ref, four_rows(t, cols)))
        return carry

    lax.fori_loop(0, 8, step, 0)
    whole_ref[0], whole_ref[1] = thin_ref[:128], thin_ref[128:]
    whole_ref[0, :, 64 : 64 + dweight_ref.shape[0]] = jnp.transpose(dweight_ref[...])
    give_halves(core_ref, whole_ref, mine_ref, other_ref)


def call_bias_sums(dbias, pair, thin, core, cols):
    heads = dbias.shape[0]
    return pl.pallas_call(
        functools.partial(bias_sums_kernel, cols),
        grid=(1,),
        in_specs=[bias_rows(dbias), full(pair), full(thin), pl.BlockSpec(memory_space=pltpu.SMEM)],
        out_specs=(pl.BlockSpec((128, 128), lambda t: (0, 0)),) * 2,
        out_shape=(jax.ShapeDtypeStruct((128, 128), f32),) * 2,
        scratch_shapes=[
            pltpu.VMEM((2, 128, 128), f32),
            pltpu.VMEM((heads, 16, 128), f32),
            pltpu.VMEM((heads, 128), f32),
        ],
        compiler_params=params(24),
        name="bias_sums",
    )(dbias, pair, thin, core)


def bias_back_kernel(cols, dbias_ref, dmid_ref, weight_ref, out_ref, sum_ref):
    weight = halves(weight_ref[...])
    sum_ref[...] = jnp.sum(dbias_ref[...], axis=1)

    def step(t, carry):
        places = four_rows(t, cols)
        dpair = dot3(jnp.transpose(head_rows(sum_ref, t)), weight)
        write_rows(out_ref, places, read_rows(dmid_ref, places) + dpair)
        return carry

    lax.fori_loop(0, 8, step, 0)


def call_bias_back(dbias, dmid, weight, cols):
    return pl.pallas_call(
        functools.partial(bias_back_kernel, cols),
        grid=(1,),
        in_specs=[bias_rows(dbias), full(dmid), full(weight)],
        out_specs=full(dmid),
        out_shape=jax.ShapeDtypeStruct(dmid.shape, f32),
        scratch_shapes=[pltpu.VMEM((dbias.shape[0], 16, 128), f32)],
        compiler_params=params(24),
        name="bias_back",
    )(dbias, dmid, weight)


def spread_sums_kernel(
    half, cols, mine_ref, early_ref, other_ref, other_early_ref, place_ref, *refs
):
    *outs, whole_ref = refs
    size = early_ref.shape[0] // (half * cols)
    for part, ref in enumerate((early_ref, other_early_ref)):
        for n in range(half * cols):
            row = lax.rem(place_ref[1] + half - n // cols, half)
            chip = row * cols + lax.rem(place_ref[2] + cols - n % cols, cols)
            target = pl.ds(pl.multiple_of(chip * size, 8), size)
            whole_ref[part, target] = ref[n * size : (n + 1) * size]

    def place(first, second, order):
        for half, ref in enumerate((first, second)):
            lanes = slice(half * 128, (half + 1) * 128)
            for n, target in enumerate((0, 1, 2, 3, 4, 5, 6)):
                outs[target][:, lanes] = ref[n * 256 : (n + 1) * 256]
            outs[8][:, lanes] = whole_ref[order[half], 512:768]
            for n, target in enumerate(((13, 15, 12), (14, 16, 17))[half]):
                outs[target][...] = ref[1920 + n * 128 : 2048 + n * 128]
            outs[11][half * 512 : (half + 1) * 512] = whole_ref[order[half], :512]
        thin = jnp.transpose(jnp.concatenate([first[1792:1920], second[1792:1920]], 0))
        outs[7][...] = thin[64 : 64 + outs[7].shape[0], :128]
        outs[9][...] = thin[:32]
        outs[10][...] = thin[32:64]

    @pl.when(place_ref[0] == 0)
    def _():
        place(mine_ref, other_ref, (0, 1))

    @pl.when(place_ref[0] != 0)
    def _():
        place(other_ref, mine_ref, (1, 0))


def call_spread_sums(mine, early, other, other_early, place, half, cols, shapes):
    thin = (7, 9, 10)
    shapes = [shape[::-1] if n in thin else shape for n, shape in enumerate(shapes)]
    sums = pl.pallas_call(
        functools.partial(spread_sums_kernel, half, cols),
        in_specs=specs(4),
        out_shape=tuple(jax.ShapeDtypeStruct(shape, f32) for shape in shapes),
        scratch_shapes=[pltpu.VMEM((2,) + early.shape, f32)],
        compiler_params=params(24),
        name="spread_sums",
    )(mine, early, other, other_early, place)
    return [jnp.transpose(x) if n in thin else x for n, x in enumerate(sums)]


precise = lax.Precision.HIGH
everyone = ("half", "core", "col")
row = ("half", "core")
chips = ("half", "col")


def affine_map(tensor, weight):
    return jnp.einsum("...a,ab->...b", tensor, weight, precision=precise)


def exchange(chunks, axis):
    shape = chunks.shape
    flat = chunks.reshape(shape[0], -1, 128)
    return lax.all_to_all(flat, axis, 0, 0, tiled=True).reshape(shape)


def collect(block, axis, count):
    return exchange(jnp.broadcast_to(block[None], (count,) + block.shape), axis)


def tall(weight):
    return jnp.concatenate([weight[:, :128], weight[:, 128:]], 0)


def together(*arrays):
    return lax.optimization_barrier(arrays)


class Layout:
    def __init__(self, mesh_rows, mesh_cols, pair, chains, heads, head_width):
        self.mesh_rows, self.mesh_cols = mesh_rows, mesh_cols
        self.devices = mesh_rows * mesh_cols
        self.rows_here, self.cols_here, self.pair_width = pair
        self.span = self.rows_here * mesh_rows
        self.slim = self.span // self.devices
        self.chains, self.heads, self.head_width = chains, heads, head_width
        self.chain_groups = self.devices // heads
        self.group_chains = chains // self.chain_groups
        self.channels_here = self.pair_width // self.devices
        self.scale = head_width ** (-0.5)
        self.turn = [
            (g, (g % mesh_rows) * mesh_cols + g // mesh_rows) for g in range(self.devices)
        ]
        self.turn_back = [(b, a) for a, b in self.turn]

        self.swap = [(0, 1), (1, 0)]
        self.core = lax.axis_index("core").reshape(1)

    def to_slim(self, x):
        return lax.all_to_all(x, "col", 1, 0, tiled=True)

    def both_views(self, grad, out):
        count, slim, width = self.mesh_cols, self.slim, grad.shape[2]
        grad = jnp.transpose(grad.reshape(-1, count, slim, width), (1, 0, 2, 3))
        both = jnp.stack([grad, out.reshape(count, -1, slim, width)], 1)
        return both.reshape(count, -1, width)

    def split_views(self, both):
        count, slim, width = self.mesh_cols, self.slim, both.shape[2]
        both = both.reshape(count, 2, -1, slim, width)
        out = jnp.transpose(both[:, 1], (1, 0, 2, 3)).reshape(-1, count * slim, width)
        return both[:, 0].reshape(-1, slim, width), out

    def from_slim_permuted(self, x):
        count, slim = self.mesh_cols, x.shape[1]
        here = lax.axis_index("col")
        blocks = x.reshape(count, -1, slim, x.shape[2])
        out = jnp.zeros((blocks.shape[1], count * slim, x.shape[2]), f32)
        for n in range(count):
            block = lax.dynamic_index_in_dim(blocks, lax.rem(here + n, count), 0, False)
            if n:
                block = lax.ppermute(block, "col", [(s, (s + n) % count) for s in range(count)])
            source = lax.rem(here + count - n, count)
            out = lax.dynamic_update_slice_in_dim(out, block, source * slim, 1)
        return out

    def from_others(self, arrays, axis="col"):
        count = len(arrays)
        return [
            lax.ppermute(x, axis, [(s, (s + n) % count) for s in range(count)]) if n else x
            for n, x in enumerate(arrays)
        ]

    def share_sum(self, x, axis, count):
        here = lax.axis_index(axis)
        x = x.reshape(count, -1, 128)
        parts = [
            lax.dynamic_index_in_dim(x, lax.rem(here + n, count), 0, False) for n in range(count)
        ]
        return functools.reduce(jnp.add, self.from_others(parts, axis))

    def all_parts(self, x, axis, count):
        return jnp.concatenate(self.from_others([x] * count, axis), 0)

    def core_sum(self, sums):
        sums = [
            part[0] + lax.ppermute(part[1], "core", self.swap) if len(part) == 2 else part[0]
            for part in sums
        ]
        return jnp.concatenate(sums, 0)

    def half_sum(self, early):
        early = self.core_sum(early)
        pad = -early.shape[0] % (4 * self.devices)
        early = jnp.pad(early, ((0, pad), (0, 0))) if pad else early
        return self.share_sum(early, "half", self.mesh_rows // 2)

    def sum_all(self, late, early, *beside):
        half, cols = self.mesh_rows // 2, self.mesh_cols
        late, early = together(self.core_sum(late), early)
        late = exchange(late.reshape(half, -1, 128), "half")
        late, early = together(late, self.share_sum(early, "col", cols))
        late = exchange(late.sum(0).reshape(cols, -1, 128), "col")
        late, early, *beside = together(late, self.all_parts(early, "col", cols), *beside)
        late = collect(late.sum(0), "col", cols).reshape(-1, 128)
        late, early = together(late, self.all_parts(early, "half", half))
        late = collect(late, "half", half).reshape(-1, 128)
        late, other_early = together(late, lax.ppermute(early, "core", self.swap))
        return (late, early, lax.ppermute(late, "core", self.swap), other_early), beside


def msa_plain(size, alignment_features, residue_couplings, present, weights):
    chains, slim, heads, head_width = size.chains, size.slim, size.heads, size.head_width
    devices, groups, group_chains = size.devices, size.chain_groups, size.group_chains
    rows_here, cols_here, span = size.rows_here, size.cols_here, size.span
    mesh_rows, mesh_cols = size.mesh_rows, size.mesh_cols
    bias = jnp.transpose(affine_map(residue_couplings, weights[7]), (2, 0, 1))
    bias = jnp.broadcast_to(bias[:, None], (heads, groups, rows_here, cols_here))
    bias = exchange(bias.reshape(devices, rows_here, cols_here), everyone)
    bias = bias.reshape(mesh_rows, mesh_cols, rows_here, cols_here)
    bias = jnp.transpose(bias, (0, 2, 1, 3)).reshape(span, span)

    stripe = size.to_slim(alignment_features)
    normed, _ = norm_parts(stripe)
    col_q, col_k, col_v = (
        affine_map(normed, w).reshape(chains, slim, heads, head_width) for w in weights[:3]
    )
    scores = jnp.einsum("sihd,tihd->ihst", col_q, col_k, precision=precise) * size.scale
    scores = jnp.where(present[None, None, None, :] > 0, scores, -1000000000.0)
    blend = jnp.einsum(
        "ihst,tihd->sihd", jax.nn.softmax(scores, axis=-1), col_v, precision=precise
    )
    msa_col = stripe + affine_map(blend.reshape(chains, slim, heads * head_width), weights[3])

    normed, _ = norm_parts(msa_col)
    qkv = jnp.stack([affine_map(normed, w) for w in weights[4:7]])
    qkv = qkv.reshape(3, groups, group_chains, slim, heads, head_width)
    qkv = jnp.transpose(qkv, (4, 1, 0, 2, 3, 5))
    qkv = exchange(qkv.reshape(devices, 3, group_chains, slim, head_width), everyone)
    qkv = jnp.transpose(qkv, (1, 2, 0, 3, 4)).reshape(3, group_chains, span, head_width)
    scores = jnp.einsum("sid,sjd->sij", qkv[0], qkv[1], precision=precise) * size.scale
    shares = jax.nn.softmax(scores + bias[None], axis=-1)
    blend = jnp.einsum("sij,sjd->sid", shares, qkv[2], precision=precise)
    blend = blend.reshape(group_chains, devices, slim, head_width)
    blend = exchange(jnp.transpose(blend, (1, 0, 2, 3)), everyone)
    blend = blend.reshape(heads, chains, slim, head_width)
    blend = jnp.transpose(blend, (1, 2, 0, 3)).reshape(chains, slim, heads * head_width)
    msa_out = msa_col + affine_map(blend, weights[8])

    normed, _ = norm_parts(msa_out)
    left = affine_map(normed, weights[9]) * (present / jnp.sum(present))[:, None, None]
    left = jnp.transpose(left.reshape(chains // 4, 4, slim, 32), (2, 0, 1, 3))
    left = collect(left.reshape(slim, chains // 4, 128), "col", mesh_cols).reshape(-1, 128)
    right = affine_map(normed, weights[10]).reshape(chains // 16, 16, slim, 4, 8)
    right = jnp.transpose(right, (3, 0, 2, 1, 4)).reshape(-1, 128)
    right = collect(lax.ppermute(right, everyone, size.turn), row, mesh_rows)
    right = right.reshape(mesh_rows, 4, chains // 16, slim, 128)
    right = jnp.transpose(right, (1, 0, 3, 2, 4)).reshape(4, cols_here // 8, 8, chains // 16, 128)
    return msa_out, [left], jnp.transpose(right, (1, 0, 3, 2, 4))


def msa_forward(size, alignment_features, residue_couplings, present, weights, prepare, raw):
    chains, slim, devices = size.chains, size.slim, size.devices
    mesh_rows, mesh_cols = size.mesh_rows, size.mesh_cols
    pair_flat = residue_couplings.reshape(-1, size.pair_width)
    tokens = chains * slim
    seen = jnp.repeat(present, slim)[None]
    share = jnp.repeat(present / jnp.sum(present), slim)[:, None]
    source, target = jnp.transpose(weights[9]), jnp.transpose(weights[10])
    offset = jnp.transpose(weights[7])
    stripe = size.to_slim(alignment_features).reshape(tokens, -1)
    bias = call_bias(pair_flat, offset, size.chain_groups, size.cols_here)
    bias = bias.reshape(devices, 16, 128)
    msa_col, qkv = call_columns(stripe, seen, bias, weights[:7], size.group_chains, size.scale)
    qkv = exchange(qkv, everyone)
    blend = call_rows(qkv, mesh_rows, mesh_cols, size.scale)
    raw, blend = together(raw, blend)
    blend, ready = together(exchange(blend, everyone), prepare(raw))
    msa_out, left, right = call_rows_out(blend, msa_col, share, weights[8], source, target)
    left = size.from_others([left.reshape(-1, 128)] * mesh_cols)
    right, *left = together(lax.ppermute(right, everyone, size.turn), *left)
    right = collect(right, row, mesh_rows)

    def back(grad, d_lefts, d_right, d_mid, pair_mid, side_sums, outer_sums):
        d_lefts = size.from_others(d_lefts)
        d_right = exchange(d_right, row).sum(0)
        d_right = lax.ppermute(d_right, everyone, size.turn_back)
        d_out, d_blend, thin, *out_sums = call_rows_out_back(
            d_lefts,
            d_right,
            grad.reshape(tokens, -1),
            msa_out,
            blend,
            share,
            weights[8],
            source,
            target,
            size.core,
        )
        d_mid, d_blend = together(d_mid, d_blend)
        outer_sums = outer_sums(d_mid)
        d_blend, *outer_sums = together(exchange(d_blend, everyone), *outer_sums)
        d_qkv = call_rows_back(qkv, d_blend, mesh_rows, mesh_cols, size.scale)
        pair_mid, d_qkv = together(pair_mid, d_qkv)
        side_sums = side_sums(pair_mid)
        early = size.half_sum((outer_sums, out_sums))
        side_sum = size.core_sum([side_sums])
        d_qkv, early, side_sum = together(exchange(d_qkv, everyone), early, side_sum)
        d_col, *in_sums = call_rows_in_back(d_qkv, msa_col, d_out, weights[4:7], size.core)
        d_stripe, *col_sums = call_columns_back(
            stripe, seen, d_col, weights[:4], size.core, size.scale
        )
        d_bias = d_qkv.reshape(size.heads, size.chain_groups, -1, 128)
        thin_sums = call_bias_sums(d_bias, pair_flat, thin, size.core, size.cols_here)
        d_pair = call_bias_back(d_bias, d_mid, offset, size.cols_here)
        d_features = size.from_slim_permuted(d_stripe.reshape(chains, slim, -1))
        late = (col_sums, in_sums, thin_sums, (side_sum,))
        return d_features, d_pair, late, early

    return (msa_out.reshape(chains, slim, -1), left, right), ready, back


def msa_plain_forward(
    size, alignment_features, residue_couplings, present, weights, prepare, raw
):
    chains, rows_here = size.chains, size.rows_here
    outputs, pull = jax.vjp(
        lambda x, y, w: msa_plain(size, x, y, present, w),
        alignment_features,
        residue_couplings,
        weights,
    )

    def back(grad, d_lefts, d_right, d_mid, pair_mid, side_sums, outer_sums):
        d_left = d_lefts[0].reshape(rows_here // 4, chains // 4, 4, 4, 32)
        d_left = jnp.transpose(d_left, (0, 3, 1, 2, 4)).reshape(-1, 128)
        d_features, d_pair, d_weights = pull((grad, [d_left], d_right))
        d_pair = d_pair.reshape(-1, size.pair_width) + d_mid
        thin = [d_weights[9], d_weights[10], jnp.pad(d_weights[7], ((0, 128), (0, 0)))]
        thin = jnp.pad(jnp.concatenate(thin, 1), ((0, 0), (0, 64 - size.heads)))
        core = size.core[0]
        pick = lambda x, n: lax.dynamic_index_in_dim(x, n, 0, False)
        own = lambda x: (pick(x, core), pick(x, 1 - core))
        cut = lambda ws: own(
            jnp.stack([jnp.concatenate([w[:, n : n + 128] for w in ws], 0) for n in (0, 128)])
        )
        late = (cut(d_weights[:4]), cut(d_weights[4:7]), own(thin.reshape(2, -1, 128)))
        late = (*late, side_sums(pair_mid))
        early = (outer_sums(d_mid), cut(d_weights[8:9]))
        return d_features, d_pair, late, size.half_sum(early)

    return outputs, prepare(raw), back


def per_device(mesh_rows, mesh_cols, *arguments):
    (
        alignment_features,
        residue_couplings,
        chain_indicator,
        alignment_result_adjoint,
        coupling_result_adjoint,
        *weights,
    ) = arguments
    present = chain_indicator.astype(jnp.float32)
    heads = weights[7].shape[1]
    size = Layout(
        mesh_rows,
        mesh_cols,
        residue_couplings.shape,
        present.shape[0],
        heads,
        weights[4].shape[1] // heads,
    )
    devices, channels_here = size.devices, size.channels_here
    cols_here, pair_width = size.cols_here, size.pair_width
    (
        tensor_result_matrix,
        source_side_matrix,
        source_side_switch,
        target_side_matrix,
        target_side_switch,
        trilateral_result_switch,
        trilateral_result_matrix,
    ) = weights[11:]

    sides = (source_side_switch, target_side_switch, source_side_matrix, target_side_matrix)
    shift = channels_here.bit_length() - 1
    def prepare(raw):
        return call_prepare(raw[0], raw[1:], shift)

    forward = msa_forward if size.slim == 8 else msa_plain_forward
    (msa_slim, left_rows, right_rows), (outer_halves, sides_halves), msa_back = forward(
        size,
        alignment_features,
        residue_couplings,
        present,
        tuple(weights[:11]),
        prepare,
        (tensor_result_matrix, *sides, trilateral_result_switch),
    )
    pair_flat = residue_couplings.reshape(-1, pair_width)
    grad_flat = coupling_result_adjoint.reshape(-1, pair_width)
    count = len(left_rows)
    first = (lax.axis_index("col") if count > 1 else jnp.int32(0)).reshape(1)
    blocks = call_blocks(first, left_rows)
    pair_mid, edges, prods = call_edges(
        blocks, right_rows, outer_halves, sides_halves, pair_flat, cols_here
    )
    edges = exchange(edges.reshape(devices, 2, channels_here, 16, 128), everyone)
    triangle = exchange(call_triangle(edges, mesh_rows, mesh_cols), everyone)
    pair_out, d_triangle, d_logit, g_tri_out = call_finish(
        triangle.reshape(pair_width, 16, 128),
        pair_mid,
        grad_flat,
        trilateral_result_switch,
        trilateral_result_matrix,
        cols_here,
    )
    views = (alignment_result_adjoint, msa_slim)
    *views, d_triangle = together(*views, d_triangle)
    views = size.both_views(*views)
    d_triangle = exchange(d_triangle.reshape(devices, channels_here, 16, 128), everyone)
    d_edges = call_triangle_back(edges, d_triangle, mesh_rows, mesh_cols)
    d_edges, mid_again = together(d_edges, pair_mid)
    factors = call_factors(mid_again, sides_halves, cols_here)
    d_edges, factors = together(exchange(d_edges, everyone), factors)
    d_edges, views = together(d_edges, views)
    views = lax.all_to_all(views, "col", 0, 0, tiled=True)
    d_mid, d_logits, d_right, *d_lefts = call_edges_back(
        d_edges.reshape(2 * pair_width, 16, 128),
        pair_mid,
        grad_flat,
        d_logit,
        sides_halves,
        right_rows,
        outer_halves,
        factors,
        blocks,
        first,
        count,
        cols_here,
    )
    d_right, views = together(d_right, views)
    msa_grad, msa_out = size.split_views(views)

    def side_sums(pair_mid):
        return call_side_sums(pair_mid, d_logits, g_tri_out, size.core, cols_here, shift)

    def outer_sums(d_mid):
        return call_outer_sums(d_mid, prods, size.core, cols_here)

    alignment_adjoint, coupling_adjoint, late, early = msa_back(
        msa_grad, d_lefts, d_right, d_mid, pair_mid, side_sums, outer_sums
    )
    sums, (alignment_adjoint, coupling_adjoint) = size.sum_all(
        late, early, alignment_adjoint, coupling_adjoint
    )
    place = jnp.stack([lax.axis_index(axis) for axis in ("core", "half", "col")])
    summed = call_spread_sums(*sums, place, mesh_rows // 2, mesh_cols, [w.shape for w in weights])
    return (
        msa_out,
        pair_out.reshape(residue_couplings.shape),
        alignment_adjoint,
        coupling_adjoint.reshape(residue_couplings.shape),
        *summed,
    )


def solution(mesh):
    mesh_rows, mesh_cols = mesh.shape["row"], mesh.shape["col"]

    def local(*arguments):
        return per_device(mesh_rows, mesh_cols, *arguments)

    split = jax.sharding.Mesh(
        mesh.devices.reshape(mesh_rows // 2, 2, mesh_cols), ("half", "core", "col")
    )
    whole = P()
    msa = P("col", row, None)
    pair = P(row, "col", None)
    return jax.shard_map(
        local,
        mesh=split,
        in_specs=(msa, pair, whole, msa, pair) + (whole,) * 18,
        out_specs=(msa, pair, msa, pair) + (whole,) * 18,
        check_vma=False,
    )
```
